32 devices in a mesh: seq: 16 (over z, y, core), dp: 2 (over x).
Axes of the slice: x: 2, y: 2, z: 4, core: 2. Of those that a mesh axis runs over, the one named last changes fastest.
Arguments:
- source: bfloat16 [2, 8192, 768], P('dp', 'seq'), may hold values from -6 to 6
- target: bfloat16 [2, 512, 768], P('dp', 'seq'), may hold values from -6 to 6
- cotangent: bfloat16 [2, 512, 768], P('dp', 'seq'), may hold values from -6 to 6
- src_len: int32 [2], P('dp'), may hold values from 4096 to 8192, as said below
- dec_len: int32 [2], P('dp'), may hold values from 256 to 512, as said below
- global_pos: int32 [2, 64], P('dp'), may hold values from 0 to 4095, as said below
- enc_query: bfloat16 [768, 768], replicated, may hold values from -0.21875 to 0.21875
- enc_key: bfloat16 [768, 768], replicated, may hold values from -0.21875 to 0.21875
- enc_value: bfloat16 [768, 768], replicated, may hold values from -0.21875 to 0.21875
- glob_query: bfloat16 [768, 768], replicated, may hold values from -0.21875 to 0.21875
- glob_key: bfloat16 [768, 768], replicated, may hold values from -0.21875 to 0.21875
- glob_value: bfloat16 [768, 768], replicated, may hold values from -0.21875 to 0.21875
- enc_out: bfloat16 [768, 768], replicated, may hold values from -6 to 6
- enc_attn_gain: bfloat16 [768], replicated, may hold values from 0.5 to 1.5
- enc_attn_shift: bfloat16 [768], replicated, may hold values from -3 to 3
- enc_up: bfloat16 [768, 3072], replicated, may hold values from -0.21875 to 0.21875
- enc_down: bfloat16 [3072, 768], replicated, may hold values from -0.109375 to 0.109375
- enc_ffn_gain: bfloat16 [768], replicated, may hold values from 0.5 to 1.5
- enc_ffn_shift: bfloat16 [768], replicated, may hold values from -3 to 3
- self_query: bfloat16 [768, 768], replicated, may hold values from -0.21875 to 0.21875
- self_key: bfloat16 [768, 768], replicated, may hold values from -0.21875 to 0.21875
- self_value: bfloat16 [768, 768], replicated, may hold values from -0.21875 to 0.21875
- self_out: bfloat16 [768, 768], replicated, may hold values from -0.875 to 0.875
- dec_self_gain: bfloat16 [768], replicated, may hold values from 0.5 to 1.5
- dec_self_shift: bfloat16 [768], replicated, may hold values from -3 to 3
- cross_query: bfloat16 [768, 768], replicated, may hold values from -0.21875 to 0.21875
- cross_key: bfloat16 [768, 768], replicated, may hold values from -0.21875 to 0.21875
- cross_value: bfloat16 [768, 768], replicated, may hold values from -0.21875 to 0.21875
- cross_out: bfloat16 [768, 768], replicated, may hold values from -6 to 6
- dec_cross_gain: bfloat16 [768], replicated, may hold values from 0.5 to 1.5
- dec_cross_shift: bfloat16 [768], replicated, may hold values from -3 to 3
- dec_up: bfloat16 [768, 3072], replicated, may hold values from -0.21875 to 0.21875
- dec_down: bfloat16 [3072, 768], replicated, may hold values from -0.109375 to 0.109375
- dec_ffn_gain: bfloat16 [768], replicated, may hold values from 0.5 to 1.5
- dec_ffn_shift: bfloat16 [768], replicated, may hold values from -3 to 3
Outputs:
- decoded: bfloat16 [2, 512, 768], P('dp', 'seq')
- grad_source: float32 [2, 8192, 768], P('dp', 'seq')
- grad_target: float32 [2, 512, 768], P('dp', 'seq')
- grad_enc_query: float32 [768, 768], P('seq', 'dp')
- grad_enc_key: float32 [768, 768], P('seq', 'dp')
- grad_enc_value: float32 [768, 768], P('seq', 'dp')
- grad_glob_query: float32 [768, 768], P('seq', 'dp')
- grad_glob_key: float32 [768, 768], P('seq', 'dp')
- grad_glob_value: float32 [768, 768], P('seq', 'dp')
- grad_enc_out: float32 [768, 768], P('seq', 'dp')
- grad_enc_attn_gain: float32 [768], P('seq')
- grad_enc_attn_shift: float32 [768], P('seq')
- grad_enc_up: float32 [768, 3072], P('seq', 'dp')
- grad_enc_down: float32 [3072, 768], P('seq', 'dp')
- grad_enc_ffn_gain: float32 [768], P('seq')
- grad_enc_ffn_shift: float32 [768], P('seq')
- grad_self_query: float32 [768, 768], P('seq', 'dp')
- grad_self_key: float32 [768, 768], P('seq', 'dp')
- grad_self_value: float32 [768, 768], P('seq', 'dp')
- grad_self_out: float32 [768, 768], P('seq', 'dp')
- grad_dec_self_gain: float32 [768], P('seq')
- grad_dec_self_shift: float32 [768], P('seq')
- grad_cross_query: float32 [768, 768], P('seq', 'dp')
- grad_cross_key: float32 [768, 768], P('seq', 'dp')
- grad_cross_value: float32 [768, 768], P('seq', 'dp')
- grad_cross_out: float32 [768, 768], P('seq', 'dp')
- grad_dec_cross_gain: float32 [768], P('seq')
- grad_dec_cross_shift: float32 [768], P('seq')
- grad_dec_up: float32 [768, 3072], P('seq', 'dp')
- grad_dec_down: float32 [3072, 768], P('seq', 'dp')
- grad_dec_ffn_gain: float32 [768], P('seq')
- grad_dec_ffn_shift: float32 [768], P('seq')
The draws below stay inside these ranges and needn't reach their ends.
Inputs may be any that keep to these rules, and one draw needn't show every extreme that they name: `src_len`: one sequence fills all 8192 positions; the others are shorter. `dec_len`: one sequence fills all 512 positions; the others are shorter. `global_pos`: each row holds 64 distinct positions, 0 among them and 4095 too.
All inputs are finite; a program needn't handle non-finite values.
Results may differ from the reference program's by a relative error of at most 0.038.
Values may be sent and summed in bfloat16 or wider, within the bound.
A program may use at most 384 MiB of HBM per device.

```python
import math
import jax
import jax.numpy as jnp
from jax import lax

D = 768
HEADS = 12
HEAD_DIM = 64
FF = 3072
HALF = 512
NGLOB = 64
SEQS = 2
SRC = 8192
DEC = 512


def draw_src_len(key, part):
    key = jax.random.fold_in(key, 11)
    lengths = jax.random.randint(key, (SEQS,), SRC // 2, SRC)
    chosen = jax.random.randint(jax.random.fold_in(key, 1), (), 0, SEQS)
    return jnp.where(jnp.arange(SEQS) == chosen, SRC, lengths).astype(jnp.int32)


def draw_dec_len(key, part):
    key = jax.random.fold_in(key, 12)
    lengths = jax.random.randint(key, (SEQS,), DEC // 2, DEC)
    chosen = jax.random.randint(jax.random.fold_in(key, 1), (), 0, SEQS)
    return jnp.where(jnp.arange(SEQS) == chosen, DEC, lengths).astype(jnp.int32)


def draw_global_pos(key, part):
    key = jax.random.fold_in(key, 13)
    upper_end = SRC // 2
    rows_list = []
    for seq_row in range(SEQS):
        picks = jax.random.permutation(jax.random.fold_in(key, seq_row), upper_end - 2)[:NGLOB - 2] + 1
        rows_list.append(jnp.concatenate([jnp.zeros((1,), jnp.int32), picks.astype(jnp.int32), jnp.full((1,), upper_end - 1, jnp.int32)]))
    return jnp.stack(rows_list)


def levels(stream_key, extent, cuts, low, largest):
    factor_of = 1.0
    for position, parts in cuts:
        draws = jax.random.uniform(jax.random.fold_in(jax.random.fold_in(stream_key, 6), position), (parts,), jnp.float32, low / len(cuts), largest / len(cuts))
        factor_of = factor_of * jnp.repeat(jnp.exp(draws), extent[position] // parts).reshape((-1,) + (1,) * (len(extent) - 1 - position))
    return factor_of


def gaussian(rng, extent, width, limit, split=(), kind=jnp.bfloat16):
    gain = levels(rng, extent, split, -0.22, 0.18) if split else 1.0
    entries = jax.random.normal(rng, extent, jnp.float32) * width * gain
    return jnp.minimum(jnp.maximum(entries, -limit), limit).astype(kind)


def setup_inputs(seed: int = 0) -> dict:
    key_list = jax.random.split(jax.random.key(seed), 36)
    source = gaussian(key_list[0], (SEQS, SRC, D), 1.0, 6.0, ((0, 2), (1, 16)))
    target = gaussian(key_list[1], (SEQS, DEC, D), 1.0, 6.0, ((0, 2), (1, 16)))
    cotangent = gaussian(key_list[2], (SEQS, DEC, D), 1.0, 6.0, ((0, 2), (1, 16)))
    src_len = draw_src_len(jax.random.fold_in(key_list[35], 71), 0)
    dec_len = draw_dec_len(jax.random.fold_in(key_list[35], 71), 0)
    global_pos = draw_global_pos(jax.random.fold_in(key_list[35], 71), 0)
    enc_query = gaussian(key_list[6], (D, D), D ** -0.5, 0.21875)
    enc_key = gaussian(key_list[7], (D, D), D ** -0.5, 0.21875)
    enc_value = gaussian(key_list[8], (D, D), D ** -0.5, 0.21875)
    glob_query = gaussian(key_list[9], (D, D), D ** -0.5, 0.21875)
    glob_key = gaussian(key_list[10], (D, D), D ** -0.5, 0.21875)
    glob_value = gaussian(key_list[11], (D, D), D ** -0.5, 0.21875)
    enc_out = gaussian(key_list[12], (D, D), 1 ** -0.5, 6.0)
    enc_attn_gain = jnp.clip(1.0 + 0.1 * jax.random.normal(key_list[13], (D,), jnp.float32), 0.5, 1.5).astype(jnp.bfloat16)
    enc_attn_shift = gaussian(key_list[14], (D,), 0.3, 3.0)
    enc_up = gaussian(key_list[15], (D, FF), D ** -0.5, 0.21875)
    enc_down = gaussian(key_list[16], (FF, D), FF ** -0.5, 0.109375)
    enc_ffn_gain = jnp.clip(1.0 + 0.1 * jax.random.normal(key_list[17], (D,), jnp.float32), 0.5, 1.5).astype(jnp.bfloat16)
    enc_ffn_shift = gaussian(key_list[18], (D,), 0.3, 3.0)
    self_query = gaussian(key_list[19], (D, D), D ** -0.5, 0.21875)
    self_key = gaussian(key_list[20], (D, D), D ** -0.5, 0.21875)
    self_value = gaussian(key_list[21], (D, D), D ** -0.5, 0.21875)
    self_out = gaussian(key_list[22], (D, D), (D // 16) ** -0.5, 0.875)
    dec_self_gain = jnp.clip(1.0 + 0.1 * jax.random.normal(key_list[23], (D,), jnp.float32), 0.5, 1.5).astype(jnp.bfloat16)
    dec_self_shift = gaussian(key_list[24], (D,), 0.3, 3.0)
    cross_query = gaussian(key_list[25], (D, D), D ** -0.5, 0.21875)
    cross_key = gaussian(key_list[26], (D, D), D ** -0.5, 0.21875)
    cross_value = gaussian(key_list[27], (D, D), D ** -0.5, 0.21875)
    cross_out = gaussian(key_list[28], (D, D), 1 ** -0.5, 6.0)
    dec_cross_gain = jnp.clip(1.0 + 0.1 * jax.random.normal(key_list[29], (D,), jnp.float32), 0.5, 1.5).astype(jnp.bfloat16)
    dec_cross_shift = gaussian(key_list[30], (D,), 0.3, 3.0)
    dec_up = gaussian(key_list[31], (D, FF), D ** -0.5, 0.21875)
    dec_down = gaussian(key_list[32], (FF, D), FF ** -0.5, 0.109375)
    dec_ffn_gain = jnp.clip(1.0 + 0.1 * jax.random.normal(key_list[33], (D,), jnp.float32), 0.5, 1.5).astype(jnp.bfloat16)
    dec_ffn_shift = gaussian(key_list[34], (D,), 0.3, 3.0)
    return {"source": source, "target": target, "cotangent": cotangent, "src_len": src_len, "dec_len": dec_len, "global_pos": global_pos, "enc_query": enc_query, "enc_key": enc_key, "enc_value": enc_value, "glob_query": glob_query, "glob_key": glob_key, "glob_value": glob_value, "enc_out": enc_out, "enc_attn_gain": enc_attn_gain, "enc_attn_shift": enc_attn_shift, "enc_up": enc_up, "enc_down": enc_down, "enc_ffn_gain": enc_ffn_gain, "enc_ffn_shift": enc_ffn_shift, "self_query": self_query, "self_key": self_key, "self_value": self_value, "self_out": self_out, "dec_self_gain": dec_self_gain, "dec_self_shift": dec_self_shift, "cross_query": cross_query, "cross_key": cross_key, "cross_value": cross_value, "cross_out": cross_out, "dec_cross_gain": dec_cross_gain, "dec_cross_shift": dec_cross_shift, "dec_up": dec_up, "dec_down": dec_down, "dec_ffn_gain": dec_ffn_gain, "dec_ffn_shift": dec_ffn_shift}


@jax.custom_vjp
def low(v):
    return lax.optimization_barrier(v.astype(jnp.bfloat16)).astype(jnp.float32)

@jax.custom_vjp
def low_back(v):
    return v

def low_keep(v):
    return (low(v), None)

def low_pass(kept, grad):
    return (grad,)

def back_keep(v):
    return (v, None)

def back_low(kept, grad):
    return (low(grad),)
low.defvjp(low_keep, low_pass)
low_back.defvjp(back_keep, back_low)
masked_score = -1e+30
eps_norm = 1e-05

def rounded(value):
    return low(low_back(value))

def matmul(left, right):
    return jnp.dot(left, right, precision=lax.Precision.HIGHEST, preferred_element_type=jnp.float32)

def layer_norm(value, scale_vec, shift_vec):
    average = lax.optimization_barrier(jnp.mean(value, axis=-1, keepdims=True))
    centred = value - average
    spread = lax.optimization_barrier(jnp.mean(centred * centred, axis=-1, keepdims=True))
    return centred * lax.rsqrt(spread + eps_norm) * scale_vec + shift_vec

def heads_of(value):
    return value.reshape(value.shape[0], HEADS, HEAD_DIM)

def scores_of(queries, keys):
    return jnp.einsum('qhe,khe->hqk', queries, keys, precision=lax.Precision.HIGHEST)

def mix_values(weights_p, values):
    return jnp.einsum('hqk,khe->qhe', weights_p, values, precision=lax.Precision.HIGHEST)

def gelu_exact(value):
    return jax.nn.gelu(value, approximate=False)

def encoder(inputs, src_limit, glob_places, params):
    w_query, w_key, w_value, w_gquery, w_gkey, w_gvalue, w_out, gain_one, shift_one, w_up, w_down, gain_two, shift_two = params
    queries = heads_of(rounded(matmul(inputs, w_query) * 0.125))
    keys = heads_of(rounded(matmul(inputs, w_key)))
    values = heads_of(rounded(matmul(inputs, w_value)))
    glob_q = heads_of(rounded(matmul(inputs, w_gquery) * 0.125))
    glob_k = heads_of(rounded(matmul(inputs, w_gkey)))
    glob_v = heads_of(rounded(matmul(inputs, w_gvalue)))
    places = jnp.arange(SRC, dtype=jnp.int32)
    is_glob = jnp.any(places[:, None] == glob_places[None, :], axis=1)
    valid = places < src_limit
    usable = valid & jnp.logical_not(is_glob)
    key_glob = keys[glob_places]
    val_glob = values[glob_places]
    pad_keys = jnp.pad(keys, ((HALF, HALF), (0, 0), (0, 0)))
    pad_vals = jnp.pad(values, ((HALF, HALF), (0, 0), (0, 0)))
    pad_use = jnp.pad(usable, (HALF, HALF))
    offsets = jnp.arange(HALF, dtype=jnp.int32)[:, None] - jnp.arange(3 * HALF, dtype=jnp.int32)[None, :] + HALF
    near = jnp.abs(offsets) <= HALF

    def window_block(block_index):
        start = (block_index * HALF).astype(jnp.int32)
        query_block = lax.dynamic_slice_in_dim(queries, start, HALF, 0)
        key_block = lax.dynamic_slice_in_dim(pad_keys, start, 3 * HALF, 0)
        val_block = lax.dynamic_slice_in_dim(pad_vals, start, 3 * HALF, 0)
        use_block = lax.dynamic_slice_in_dim(pad_use, start, 3 * HALF, 0)
        allowed = near & use_block[None, :]
        window_scores = jnp.where(allowed[None], scores_of(query_block, key_block), masked_score)
        all_scores = low_back(jnp.concatenate([window_scores, scores_of(query_block, key_glob)], axis=2))
        weights_p = low(jax.nn.softmax(all_scores, axis=-1))
        return mix_values(weights_p[:, :, :3 * HALF], val_block) + mix_values(weights_p[:, :, 3 * HALF:], val_glob)
    local = lax.map(jax.checkpoint(window_block), jnp.arange(SRC // HALF, dtype=jnp.int32)).reshape(SRC, D)
    glob_scores = jnp.where(valid[None, None, :], scores_of(glob_q[glob_places], glob_k), masked_score)
    glob_weights = low(jax.nn.softmax(low_back(glob_scores), axis=-1))
    glob_out = mix_values(glob_weights, glob_v).reshape(NGLOB, D)
    placed = jnp.zeros((SRC, D), jnp.float32).at[glob_places].set(glob_out)
    attn = rounded(jnp.where(is_glob[:, None], placed, local))
    first = layer_norm(inputs + low_back(matmul(attn, w_out)), gain_one, shift_one)
    hidden = low(gelu_exact(low_back(matmul(low(first), w_up))))
    second = first + low_back(matmul(hidden, w_down))
    return layer_norm(second, gain_two, shift_two)

def decoder(inputs, memory, src_limit, dec_limit, params):
    w_sq, w_sk, w_sv, w_so, gain_one, shift_one, w_cq, w_ck, w_cv, w_co, gain_two, shift_two, w_up, w_down, gain_three, shift_three = params
    rows_block = math.gcd(DEC, 512)
    self_q = heads_of(rounded(matmul(inputs, w_sq) * 0.125))
    self_k = heads_of(rounded(matmul(inputs, w_sk)))
    self_v = heads_of(rounded(matmul(inputs, w_sv)))
    key_places = jnp.arange(DEC, dtype=jnp.int32)
    live = key_places < dec_limit

    def self_block(block_index):
        start = (block_index * rows_block).astype(jnp.int32)
        query_block = lax.dynamic_slice_in_dim(self_q, start, rows_block, 0)
        query_places = start + jnp.arange(rows_block, dtype=jnp.int32)
        allowed = (key_places[None, :] <= query_places[:, None]) & live[None, :]
        block_scores = low_back(jnp.where(allowed[None], scores_of(query_block, self_k), masked_score))
        return mix_values(low(jax.nn.softmax(block_scores, axis=-1)), self_v)
    self_attn = lax.map(jax.checkpoint(self_block), jnp.arange(DEC // rows_block, dtype=jnp.int32)).reshape(DEC, D)
    first = layer_norm(inputs + low_back(matmul(rounded(self_attn), w_so)), gain_one, shift_one)
    cross_q = heads_of(rounded(matmul(low(first), w_cq) * 0.125))
    memory_low = low(memory)
    cross_k = heads_of(rounded(matmul(memory_low, w_ck)))
    cross_v = heads_of(rounded(matmul(memory_low, w_cv)))
    src_live = jnp.arange(SRC, dtype=jnp.int32) < src_limit

    def cross_block(block_index):
        start = (block_index * rows_block).astype(jnp.int32)
        query_block = lax.dynamic_slice_in_dim(cross_q, start, rows_block, 0)
        block_scores = low_back(jnp.where(src_live[None, None, :], scores_of(query_block, cross_k), masked_score))
        return mix_values(low(jax.nn.softmax(block_scores, axis=-1)), cross_v)
    cross_attn = lax.map(jax.checkpoint(cross_block), jnp.arange(DEC // rows_block, dtype=jnp.int32)).reshape(DEC, D)
    second = layer_norm(first + low_back(matmul(rounded(cross_attn), w_co)), gain_two, shift_two)
    hidden = low(gelu_exact(low_back(matmul(low(second), w_up))))
    third = second + low_back(matmul(hidden, w_down))
    return layer_norm(third, gain_three, shift_three)

def reference(source, target, cotangent, src_len, dec_len, global_pos, enc_query, enc_key, enc_value, glob_query, glob_key, glob_value, enc_out, enc_attn_gain, enc_attn_shift, enc_up, enc_down, enc_ffn_gain, enc_ffn_shift, self_query, self_key, self_value, self_out, dec_self_gain, dec_self_shift, cross_query, cross_key, cross_value, cross_out, dec_cross_gain, dec_cross_shift, dec_up, dec_down, dec_ffn_gain, dec_ffn_shift):
    enc_params = tuple((weight_arr.astype(jnp.float32) for weight_arr in (enc_query, enc_key, enc_value, glob_query, glob_key, glob_value, enc_out, enc_attn_gain, enc_attn_shift, enc_up, enc_down, enc_ffn_gain, enc_ffn_shift)))
    dec_params = tuple((weight_arr.astype(jnp.float32) for weight_arr in (self_query, self_key, self_value, self_out, dec_self_gain, dec_self_shift, cross_query, cross_key, cross_value, cross_out, dec_cross_gain, dec_cross_shift, dec_up, dec_down, dec_ffn_gain, dec_ffn_shift)))

    def forward(enc_weights, dec_weights, src_in, tgt_in):
        results = []
        for seq_row in range(SEQS):
            memory = encoder(src_in[seq_row], src_len[seq_row], global_pos[seq_row], enc_weights)
            results.append(decoder(tgt_in[seq_row], memory, src_len[seq_row], dec_len[seq_row], dec_weights))
        return jnp.stack(results)
    decoded, pullback = jax.vjp(forward, enc_params, dec_params, source.astype(jnp.float32), target.astype(jnp.float32))
    grad_enc, grad_dec, grad_src, grad_tgt = pullback(cotangent.astype(jnp.float32))
    return (decoded.astype(jnp.bfloat16), grad_src, grad_tgt, grad_enc[0], grad_enc[1], grad_enc[2], grad_enc[3], grad_enc[4], grad_enc[5], grad_enc[6], grad_enc[7], grad_enc[8], grad_enc[9], grad_enc[10], grad_enc[11], grad_enc[12], grad_dec[0], grad_dec[1], grad_dec[2], grad_dec[3], grad_dec[4], grad_dec[5], grad_dec[6], grad_dec[7], grad_dec[8], grad_dec[9], grad_dec[10], grad_dec[11], grad_dec[12], grad_dec[13], grad_dec[14], grad_dec[15])
```

```python
import functools

import jax
import jax.numpy as jnp
from jax import lax
from jax.experimental import pallas as pl
from jax.experimental.pallas import tpu as pltpu
from jax.sharding import PartitionSpec as P

HEADS = 12
HEAD_DIM = 64
HALF = 512
PAIRS = HEADS // 2
LANES = 2 * HEAD_DIM
SLOT = 16

masked_score = -1e30
eps_norm = 1e-05
low_type = jnp.bfloat16
vmem_bytes = 56 * 2**20


def dot_plain(left, right):
    return jnp.dot(left, right, preferred_element_type=jnp.float32)


def dot_left(left, right):
    return lax.dot_general(
        left, right, (((0,), (0,)), ((), ())), preferred_element_type=jnp.float32
    )


def dot_right(left, right):
    return lax.dot_general(
        left, right, (((1,), (1,)), ((), ())), preferred_element_type=jnp.float32
    )


def exact_dot(left, right):
    return jnp.dot(
        left, right, precision=lax.Precision.HIGHEST, preferred_element_type=jnp.float32
    )


def layer_norm(value, scale_vec, shift_vec):
    average = jnp.mean(value, axis=-1, keepdims=True)
    centred = value - average
    spread = jnp.mean(centred * centred, axis=-1, keepdims=True)
    return centred * lax.rsqrt(spread + eps_norm) * scale_vec + shift_vec


def gelu_pair(value):
    cdf = 0.5 * (1.0 + lax.erf(value * 0.7071067811865476))
    slope = cdf + value * (0.3989422804014327 * jnp.exp(-0.5 * value * value))
    return (value * cdf).astype(low_type), slope.astype(low_type)


def head_spread():
    heads = lax.broadcasted_iota(jnp.int32, (SLOT, HEADS * HEAD_DIM), 0)
    columns = lax.broadcasted_iota(jnp.int32, (SLOT, HEADS * HEAD_DIM), 1)
    return (columns // HEAD_DIM == heads).astype(jnp.float32)


def head_mask(which):
    lanes = lax.broadcasted_iota(jnp.int32, (1, LANES), 1)
    return ((lanes // HEAD_DIM) == which).astype(low_type)


def forward_body(parts, rows_block, blocks, normalize, q_ref, k_ref, v_ref, bias_ref, o_ref, st_ref):
    pair = pl.program_id(1)
    lane = lax.broadcasted_iota(jnp.int32, (1, LANES), 1)

    @pl.when(pair == 0)
    def _():
        st_ref[...] = jnp.zeros_like(st_ref)

    for block in range(blocks):
        rows = pl.ds(block * rows_block, rows_block)
        q_two = q_ref[rows, :]
        stats = st_ref[rows, :]
        outs = []
        for which in range(2):
            head = 2 * pair + which
            q_one = q_two * head_mask(which)
            scores = []
            for start, size in parts[block]:
                bias = bias_ref[:, start : start + size]
                if bias_ref.shape[0] > 1:
                    bias = bias_ref[rows, start : start + size]
                scores.append(dot_right(q_one, k_ref[start : start + size, :]) + bias)
            top = functools.reduce(
                jnp.maximum, [jnp.max(part, axis=1, keepdims=True) for part in scores]
            )
            total = jnp.zeros((rows_block, 1), jnp.float32)
            mixed = jnp.zeros((rows_block, LANES), jnp.float32)
            for (start, size), part in zip(parts[block], scores):
                weights = jnp.exp(part - top)
                total = total + jnp.sum(weights, axis=1, keepdims=True)
                mixed = mixed + dot_plain(weights.astype(low_type), v_ref[start : start + size, :])
            if normalize:
                mixed = mixed / total
                stats = jnp.where(lane == head, top + jnp.log(total), stats)
            else:
                stats = jnp.where(lane == head, top, stats)
                stats = jnp.where(lane == head + SLOT, total, stats)
            outs.append(mixed)
        st_ref[rows, :] = stats
        o_ref[rows, :] = jnp.where(lane < HEAD_DIM, outs[0], outs[1])


def attend(queries, keys, values, bias, parts, rows_block, normalize):
    count, width = queries.shape
    key_count = keys.shape[0]
    big = min(count, 512)
    blocks = big // rows_block
    parts = parts or [((0, key_count),)] * blocks
    bias_rows = bias.shape[0]
    flops = 4 * count * key_count * width
    return pl.pallas_call(
        functools.partial(forward_body, parts, rows_block, blocks, normalize),
        grid=(count // big, PAIRS),
        in_specs=[
            pl.BlockSpec((big, LANES), lambda i, p: (i, p)),
            pl.BlockSpec((key_count, LANES), lambda i, p: (0, p)),
            pl.BlockSpec((key_count, LANES), lambda i, p: (0, p)),
            pl.BlockSpec((min(bias_rows, big), key_count), lambda i, p: (0, 0)),
        ],
        out_specs=[
            pl.BlockSpec((big, LANES), lambda i, p: (i, p)),
            pl.BlockSpec((big, LANES), lambda i, p: (i, 0)),
        ],
        out_shape=[
            jax.ShapeDtypeStruct((count, width), jnp.float32),
            jax.ShapeDtypeStruct((count, LANES), jnp.float32),
        ],
        compiler_params=pltpu.CompilerParams(vmem_limit_bytes=vmem_bytes),
        cost_estimate=pl.CostEstimate(
            flops=4 * flops,
            bytes_accessed=2 * (count + 2 * key_count) * width + 4 * count * width,
            transcendentals=count * key_count * HEADS,
        ),
    )(queries, keys, values, bias)


def backward_body(
    parts, rows_block, blocks, q_ref, k_ref, v_ref, d_ref, st_ref, bias_ref,
    dq_ref, dk_ref, dv_ref, key_sum, val_sum,
):
    pair = pl.program_id(0)
    turn = pl.program_id(1)

    @pl.when(turn == 0)
    def _():
        key_sum[...] = jnp.zeros_like(key_sum)
        val_sum[...] = jnp.zeros_like(val_sum)

    for block in range(blocks):
        rows = pl.ds(block * rows_block, rows_block)
        q_two = q_ref[rows, :]
        d_two = d_ref[rows, :]
        turned = []
        for which in range(2):
            head = 2 * pair + which
            q_one = q_two * head_mask(which)
            d_one = d_two * head_mask(which)
            lse = st_ref[pl.ds(head, 1), rows]
            delta = st_ref[pl.ds(head + SLOT, 1), rows]
            q_grad = jnp.zeros((LANES, rows_block), jnp.float32)
            for start, size in parts[block]:
                keys = slice(start, start + size)
                bias = bias_ref[keys, :]
                if bias_ref.shape[1] > 1:
                    bias = bias_ref[keys, rows]
                k_two = k_ref[keys, :]
                scores = dot_right(k_two, q_one) + bias
                weights = jnp.exp(scores - lse)
                slopes = dot_right(v_ref[keys, :], d_one)
                diffs = (weights * (slopes - delta)).astype(low_type)
                val_sum[keys, :] += dot_plain(weights.astype(low_type), d_one)
                key_sum[keys, :] += dot_plain(diffs, q_one)
                q_grad = q_grad + dot_left(k_two, diffs)
            turned.append(q_grad[which * HEAD_DIM : (which + 1) * HEAD_DIM, :])
        dq_ref[rows, :] = jnp.concatenate(turned, axis=0).T

    @pl.when(turn == pl.num_programs(1) - 1)
    def _():
        dk_ref[...] = key_sum[...].astype(low_type)
        dv_ref[...] = val_sum[...].astype(low_type)


def attend_back(queries, keys, values, grads, stats, bias, parts, rows_block):
    count, width = queries.shape
    key_count = keys.shape[0]
    big = min(count, 512)
    blocks = big // rows_block
    parts = parts or [((0, key_count),)] * blocks
    bias_cols = bias.shape[1]
    flops = 10 * count * key_count * width
    return pl.pallas_call(
        functools.partial(backward_body, parts, rows_block, blocks),
        grid=(PAIRS, count // big),
        in_specs=[
            pl.BlockSpec((big, LANES), lambda p, i: (i, p)),
            pl.BlockSpec((key_count, LANES), lambda p, i: (0, p)),
            pl.BlockSpec((key_count, LANES), lambda p, i: (0, p)),
            pl.BlockSpec((big, LANES), lambda p, i: (i, p)),
            pl.BlockSpec((2 * SLOT, big), lambda p, i: (0, i)),
            pl.BlockSpec((key_count, min(bias_cols, big)), lambda p, i: (0, 0)),
        ],
        out_specs=[
            pl.BlockSpec((big, LANES), lambda p, i: (i, p)),
            pl.BlockSpec((key_count, LANES), lambda p, i: (0, p)),
            pl.BlockSpec((key_count, LANES), lambda p, i: (0, p)),
        ],
        out_shape=[
            jax.ShapeDtypeStruct((count, width), jnp.float32),
            jax.ShapeDtypeStruct((key_count, width), low_type),
            jax.ShapeDtypeStruct((key_count, width), low_type),
        ],
        scratch_shapes=[
            pltpu.VMEM((key_count, LANES), jnp.float32),
            pltpu.VMEM((key_count, LANES), jnp.float32),
        ],
        compiler_params=pltpu.CompilerParams(vmem_limit_bytes=vmem_bytes),
        cost_estimate=pl.CostEstimate(
            flops=4 * flops,
            bytes_accessed=2 * (2 * count + 4 * key_count) * width + 4 * count * width,
            transcendentals=count * key_count * HEADS,
        ),
    )(queries, keys, values, grads, stats, bias)


def seq_bits():
    count = lax.axis_size("seq")
    return [1 << k for k in range(count.bit_length() - 1)]


def swap(value, bit):
    pairs = [(i, i ^ bit) for i in range(lax.axis_size("seq"))]
    return jax.tree.map(lambda part: lax.ppermute(part, "seq", pairs), value)


def swap_dp(value):
    pairs = [(i, i ^ 1) for i in range(lax.axis_size("dp"))]
    return lax.ppermute(value, "dp", pairs)


def bit_set(bit):
    return (lax.axis_index("seq") & bit) != 0


def gather_rows(value):
    rows, width = value.shape
    held = value[None]
    for bit in reversed(seq_bits()):
        other = swap(held, bit)
        upper = bit_set(bit)
        held = jnp.stack(
            [jnp.where(upper, other, held), jnp.where(upper, held, other)], axis=1
        ).reshape(2 * held.shape[0], rows, width)
    return held.reshape(-1, width)


def add_all(value):
    for bit in seq_bits():
        value = value + swap(value, bit)
    return value


def pick_half(value, chosen, axis):
    return lax.dynamic_index_in_dim(value, chosen, axis, keepdims=False)


def scatter_rows(value):
    bits = seq_bits()
    held = value.reshape((2,) * len(bits) + (-1, value.shape[1]))
    for step, bit in enumerate(bits):
        axis = len(bits) - 1 - step
        mine = bit_set(bit).astype(jnp.int32)
        other = swap(pick_half(held, 1 - mine, axis).astype(low_type), bit)
        held = pick_half(held, mine, axis) + other.astype(jnp.float32)
    return held


def merge_body(acc_a, st_a, acc_b, st_b, acc_o, st_o):
    top_a, top_b = st_a[:, :SLOT], st_b[:, :SLOT]
    top = jnp.maximum(top_a, top_b)
    keep_a = jnp.exp(top_a - top)
    keep_b = jnp.exp(top_b - top)
    total = st_a[:, SLOT : 2 * SLOT] * keep_a + st_b[:, SLOT : 2 * SLOT] * keep_b
    spread = head_spread()
    acc_o[...] = acc_a[...] * exact_dot(keep_a, spread) + acc_b[...].astype(
        jnp.float32
    ) * exact_dot(keep_b, spread)
    rest = jnp.zeros((top.shape[0], LANES - 2 * SLOT), jnp.float32)
    st_o[...] = jnp.concatenate([top, total, rest], axis=1)


def merge_soft(held, other):
    rows = held[0].shape[0]
    return pl.pallas_call(
        merge_body,
        out_shape=[
            jax.ShapeDtypeStruct((rows, held[0].shape[1]), jnp.float32),
            jax.ShapeDtypeStruct((rows, LANES), jnp.float32),
        ],
        compiler_params=pltpu.CompilerParams(vmem_limit_bytes=vmem_bytes),
    )(*held, *other)


def merge_all(held):
    for bit in seq_bits():
        held = merge_soft(held, swap((held[0].astype(low_type), held[1]), bit))
    return held


def merge_scatter(held):
    bits = seq_bits()
    for step, bit in enumerate(bits):
        inner = len(bits) - 1 - step
        mine = bit_set(bit).astype(jnp.int32)

        def halves(value, chosen):
            split = value.reshape(1 << inner, 2, -1, value.shape[1])
            return pick_half(split, chosen, 1).reshape(-1, value.shape[1])

        away = (halves(held[0], 1 - mine).astype(low_type), halves(held[1], 1 - mine))
        held = merge_soft((halves(held[0], mine), halves(held[1], mine)), swap(away, bit))
    return held


def share_grads(grads, dp_first):
    bits = seq_bits()
    width = grads[0].shape[1]
    half = width // 2
    rows = [grad.shape[0] >> len(bits) for grad in grads]
    dp_mine = lax.axis_index("dp")
    laid = [
        grad.astype(low_type).reshape((2,) * len(bits) + (count, width))
        for grad, count in zip(grads, rows)
    ]
    steps = [(1, False)]
    rest = [(bit, False) for bit in bits[1:]]
    steps += [(0, True)] + rest if dp_first else rest[:1] + [(0, True)] + rest[1:]
    held = None
    axis = len(bits)
    for bit, is_dp in steps:
        if is_dp:
            own = lax.dynamic_slice_in_dim(held, dp_mine * half, half, held.ndim - 1)
            away = lax.dynamic_slice_in_dim(held, (1 - dp_mine) * half, half, held.ndim - 1)
            held = own + swap_dp(away)
            continue
        axis -= 1
        mine = bit_set(bit).astype(jnp.int32)
        if held is None:
            away = jnp.concatenate([pick_half(v, 1 - mine, axis) for v in laid], axis=-2)
            own = jnp.concatenate([pick_half(v, mine, axis) for v in laid], axis=-2)
        else:
            away = pick_half(held, 1 - mine, axis)
            own = pick_half(held, mine, axis)
        held = own + swap(away, bit)
    result = []
    start = 0
    for count in rows:
        result.append(held[start : start + count].astype(jnp.float32))
        start += count
    return result


def share_vectors(vectors):
    stacked = jnp.concatenate([jnp.stack(vectors), jnp.zeros((6, vectors[0].shape[0]))], axis=0)
    total = add_all(stacked)
    total = total + swap_dp(total)
    length = stacked.shape[1] // lax.axis_size("seq")
    mine = lax.dynamic_slice_in_dim(total, lax.axis_index("seq") * length, length, 1)
    return [mine[k] for k in range(len(vectors))]


def pad_rows(value, count):
    return jnp.pad(value, ((0, count - value.shape[0]), (0, 0)))


def per_device(
    source,
    target,
    cotangent,
    src_len,
    dec_len,
    global_pos,
    enc_query,
    enc_key,
    enc_value,
    glob_query,
    glob_key,
    glob_value,
    enc_out,
    enc_attn_gain,
    enc_attn_shift,
    enc_up,
    enc_down,
    enc_ffn_gain,
    enc_ffn_shift,
    self_query,
    self_key,
    self_value,
    self_out,
    dec_self_gain,
    dec_self_shift,
    cross_query,
    cross_key,
    cross_value,
    cross_out,
    dec_cross_gain,
    dec_cross_shift,
    dec_up,
    dec_down,
    dec_ffn_gain,
    dec_ffn_shift,
):
    full = jnp.float32
    src_x = source[0]
    dec_x = target[0]
    src_count = src_x.shape[0]
    dec_count = dec_x.shape[0]
    seq_index = lax.axis_index("seq")
    peers = lax.axis_size("seq")
    src_limit = src_len[0]
    dec_limit = dec_len[0]
    glob_places = global_pos[0]
    glob_count = glob_places.shape[0]
    src_places = seq_index * src_count + jnp.arange(src_count, dtype=jnp.int32)
    select_glob = glob_places[:, None] == src_places[None, :]
    select_low = select_glob.astype(low_type)
    is_global = jnp.any(select_glob, axis=0)
    spread = head_spread()

    upward = [(i, i + 1) for i in range(peers - 1)]
    downward = [(i + 1, i) for i in range(peers - 1)]
    before = lax.ppermute(src_x[src_count - HALF :], "seq", upward)
    after = lax.ppermute(src_x[:HALF], "seq", downward)
    dec_all = gather_rows(dec_x)
    glob_x = add_all(dot_plain(select_low, src_x).astype(low_type))

    query_loc = (dot_plain(src_x, enc_query) * 0.125).astype(low_type)
    glob_keys_loc = dot_plain(src_x, glob_key).astype(low_type)
    glob_vals_loc = dot_plain(src_x, glob_value).astype(low_type)

    self_q = (dot_plain(dec_x, self_query) * 0.125).astype(low_type)
    self_k = dot_plain(dec_all, self_key).astype(low_type)
    self_v = dot_plain(dec_all, self_value).astype(low_type)
    dec_total = dec_all.shape[0]
    dec_places = seq_index * dec_count + jnp.arange(dec_count, dtype=jnp.int32)
    all_dec = jnp.arange(dec_total, dtype=jnp.int32)
    self_allowed = (all_dec[None, :] <= dec_places[:, None]) & (all_dec < dec_limit)[None, :]
    self_bias = jnp.where(self_allowed, 0.0, masked_score)
    self_out_full, self_stats = attend(self_q, self_k, self_v, self_bias, None, dec_count, True)
    self_attn = self_out_full.astype(low_type)
    dec_res_one = dec_x.astype(full) + dot_plain(self_attn, self_out)
    dec_first, dec_first_back = jax.vjp(
        layer_norm, dec_res_one, dec_self_gain.astype(full), dec_self_shift.astype(full)
    )
    dec_first_low = dec_first.astype(low_type)
    cross_q = (dot_plain(dec_first_low, cross_query) * 0.125).astype(low_type)
    all_cross_q = gather_rows(cross_q)

    glob_queries = (dot_plain(glob_x, glob_query) * 0.125).astype(low_type)
    live_bias = jnp.where(src_places < src_limit, 0.0, masked_score)
    glob_acc, glob_stats = merge_all(
        attend(
            glob_queries, glob_keys_loc, glob_vals_loc, live_bias[None, :], None, glob_count, False
        )
    )
    glob_total = glob_stats[:, SLOT : 2 * SLOT]
    glob_out = glob_acc / exact_dot(glob_total, spread)
    glob_lse = glob_stats[:, :SLOT] + jnp.log(jnp.maximum(glob_total, 1e-30))

    x_all = jnp.concatenate([before, src_x, after, glob_x], axis=0)
    keys_all = dot_plain(x_all, enc_key).astype(low_type)
    vals_all = dot_plain(x_all, enc_value).astype(low_type)
    pad_count = src_count + 2 * HALF
    pad_places = seq_index * src_count - HALF + jnp.arange(pad_count, dtype=jnp.int32)
    pad_glob = jnp.any(glob_places[:, None] == pad_places[None, :], axis=0)
    pad_use = (pad_places >= 0) & (pad_places < src_limit) & jnp.logical_not(pad_glob)
    near = jnp.abs(src_places[:, None] - pad_places[None, :]) <= HALF
    win_bias = jnp.concatenate(
        [
            jnp.where(near & pad_use[None, :], 0.0, masked_score),
            jnp.zeros((src_count, glob_count), full),
        ],
        axis=1,
    )
    near_turned = jnp.abs(src_places[None, :] - pad_places[:, None]) <= HALF
    win_bias_turned = jnp.concatenate(
        [
            jnp.where(near_turned & pad_use[:, None], 0.0, masked_score),
            jnp.zeros((glob_count, src_count), full),
        ],
        axis=0,
    )
    rows_block = 256
    reach = rows_block + 2 * HALF
    win_parts = [
        ((block * rows_block, reach), (pad_count, glob_count))
        for block in range(src_count // rows_block)
    ]
    win_out, win_stats = attend(
        query_loc, keys_all, vals_all, win_bias, win_parts, rows_block, True
    )
    placed = dot_left(select_low, glob_out.astype(low_type))
    enc_attn = jnp.where(is_global[:, None], placed, win_out).astype(low_type)
    enc_res = src_x.astype(full) + dot_plain(enc_attn, enc_out)
    enc_first, enc_first_back = jax.vjp(
        layer_norm, enc_res, enc_attn_gain.astype(full), enc_attn_shift.astype(full)
    )
    enc_first_low = enc_first.astype(low_type)
    enc_hidden, enc_slope = gelu_pair(dot_plain(enc_first_low, enc_up))
    enc_second = enc_first + dot_plain(enc_hidden, enc_down)
    memory, enc_final_back = jax.vjp(
        layer_norm, enc_second, enc_ffn_gain.astype(full), enc_ffn_shift.astype(full)
    )
    memory_low = memory.astype(low_type)

    cross_k = dot_plain(memory_low, cross_key).astype(low_type)
    cross_v = dot_plain(memory_low, cross_value).astype(low_type)
    cross_acc, cross_stats = merge_scatter(
        attend(all_cross_q, cross_k, cross_v, live_bias[None, :], None, 256, False)
    )
    cross_total = cross_stats[:, SLOT : 2 * SLOT]
    cross_out_full = cross_acc / exact_dot(cross_total, spread)
    cross_lse = cross_stats[:, :SLOT] + jnp.log(jnp.maximum(cross_total, 1e-30))
    cross_attn = cross_out_full.astype(low_type)
    dec_res_two = dec_first + dot_plain(cross_attn, cross_out)
    dec_second, dec_second_back = jax.vjp(
        layer_norm, dec_res_two, dec_cross_gain.astype(full), dec_cross_shift.astype(full)
    )
    dec_second_low = dec_second.astype(low_type)
    dec_hidden, dec_slope = gelu_pair(dot_plain(dec_second_low, dec_up))
    dec_third = dec_second + dot_plain(dec_hidden, dec_down)
    decoded, dec_final_back = jax.vjp(
        layer_norm, dec_third, dec_ffn_gain.astype(full), dec_ffn_shift.astype(full)
    )

    d_third, g_dec_ffn_gain, g_dec_ffn_shift = dec_final_back(cotangent[0].astype(full))
    d_down_low = d_third.astype(low_type)
    d_pre_low = (dot_right(d_down_low, dec_down) * dec_slope.astype(full)).astype(low_type)
    d_second = d_third + dot_right(d_pre_low, dec_up)
    d_res_two, g_dec_cross_gain, g_dec_cross_shift = dec_second_back(d_second)
    d_cross_o = d_res_two.astype(low_type)
    d_cross_attn = dot_right(d_cross_o, cross_out).astype(low_type)
    cross_delta = exact_dot(d_cross_attn.astype(full) * cross_out_full, spread.T)
    all_dout = gather_rows(d_cross_attn)
    all_stats = gather_rows(
        jnp.concatenate(
            [cross_lse, cross_delta, jnp.zeros((dec_count, LANES - 2 * SLOT), full)], axis=1
        )
    )[:, : 2 * SLOT].T
    live_turned = jnp.broadcast_to(live_bias[:, None], (src_count, 512))
    query_parts, ck_low, cv_low = attend_back(
        all_cross_q, cross_k, cross_v, all_dout, all_stats, live_turned, None, 256
    )
    d_memory = dot_right(ck_low, cross_key) + dot_right(cv_low, cross_value)

    g_dec_down = dot_left(dec_hidden, d_down_low)
    g_dec_up = dot_left(dec_second_low, d_pre_low)
    g_cross_out = dot_left(cross_attn, d_cross_o)
    g_cross_key = dot_left(memory_low, ck_low)
    g_cross_value = dot_left(memory_low, cv_low)

    d_enc_second, g_enc_ffn_gain, g_enc_ffn_shift = enc_final_back(d_memory)
    d_enc_down = d_enc_second.astype(low_type)
    d_enc_pre = (dot_right(d_enc_down, enc_down) * enc_slope.astype(full)).astype(low_type)
    d_enc_first = d_enc_second + dot_right(d_enc_pre, enc_up)
    d_enc_res, g_enc_attn_gain, g_enc_attn_shift = enc_first_back(d_enc_first)
    d_attn_o = d_enc_res.astype(low_type)
    d_attn = dot_right(d_attn_o, enc_out).astype(low_type)
    g_enc_down = dot_left(enc_hidden, d_enc_down)
    g_enc_up = dot_left(enc_first_low, d_enc_pre)
    g_enc_out = dot_left(enc_attn, d_attn_o)

    d_cross_q = scatter_rows(query_parts).astype(low_type) * 0.125
    g_cross_query = dot_left(dec_first_low, d_cross_q)
    d_first = d_res_two + dot_right(d_cross_q, cross_query)
    d_res_one, g_dec_self_gain, g_dec_self_shift = dec_first_back(d_first)
    d_self_o = d_res_one.astype(low_type)
    g_self_out = dot_left(self_attn, d_self_o)
    d_self_attn = dot_right(d_self_o, self_out).astype(low_type)
    self_delta = exact_dot(d_self_attn.astype(full) * self_out_full, spread.T)
    wide = max(dec_count, LANES)
    self_pair = jnp.concatenate([self_stats[:, :SLOT], self_delta], axis=1)
    self_query_parts, d_self_k, d_self_v = attend_back(
        pad_rows(self_q, wide),
        self_k,
        self_v,
        pad_rows(d_self_attn, wide),
        pad_rows(self_pair, wide).T,
        pad_rows(self_bias, wide).T,
        None,
        wide,
    )
    d_self_q = self_query_parts[:dec_count].astype(low_type) * 0.125
    g_self_query = dot_left(dec_x, d_self_q)
    g_self_key = dot_left(dec_all, d_self_k)
    g_self_value = dot_left(dec_all, d_self_v)
    d_target = (
        d_res_one
        + dot_right(d_self_q, self_query)
        + scatter_rows(dot_right(d_self_k, self_key) + dot_right(d_self_v, self_value))
    )

    glob_dout = add_all(dot_plain(select_low, d_attn).astype(low_type))
    d_window = jnp.where(is_global[:, None], jnp.zeros_like(d_attn), d_attn)
    win_delta = exact_dot(d_window.astype(full) * win_out, spread.T)
    win_pair = jnp.concatenate([win_stats[:, :SLOT], win_delta], axis=1).T
    d_query, d_keys_all, d_vals_all = attend_back(
        query_loc, keys_all, vals_all, d_window, win_pair, win_bias_turned, win_parts, rows_block
    )
    d_query_low = d_query.astype(low_type) * 0.125

    wide = max(glob_count, LANES)
    glob_delta = exact_dot(glob_dout.astype(full) * glob_out, spread.T)
    glob_pair = jnp.concatenate([glob_lse, glob_delta], axis=1)
    glob_query_parts, gk_low, gv_low = attend_back(
        pad_rows(glob_queries, wide),
        glob_keys_loc,
        glob_vals_loc,
        pad_rows(glob_dout, wide),
        pad_rows(glob_pair, wide).T,
        live_turned[:, :wide],
        None,
        wide,
    )
    d_gq = glob_query_parts[:glob_count].astype(low_type) * 0.125

    g_enc_query = dot_left(src_x, d_query_low)
    g_enc_key = dot_left(x_all, d_keys_all)
    g_enc_value = dot_left(x_all, d_vals_all)
    g_glob_query = dot_left(glob_x, d_gq)
    g_glob_key = dot_left(src_x, gk_low)
    g_glob_value = dot_left(src_x, gv_low)

    d_x_all = dot_right(d_keys_all, enc_key) + dot_right(d_vals_all, enc_value)
    from_after = lax.ppermute(d_x_all[:HALF].astype(low_type), "seq", downward)
    from_before = lax.ppermute(d_x_all[HALF + src_count : pad_count].astype(low_type), "seq", upward)
    d_glob_x = add_all((d_x_all[pad_count:] + dot_right(d_gq, glob_query)).astype(low_type))
    d_source = (
        d_enc_res
        + dot_right(d_query_low, enc_query)
        + d_x_all[HALF : HALF + src_count]
        + dot_right(gk_low, glob_key)
        + dot_right(gv_low, glob_value)
        + dot_left(select_low, d_glob_x)
    )
    d_source = d_source + jnp.pad(
        from_after.astype(full), ((src_count - HALF, 0), (0, 0))
    )
    d_source = d_source + jnp.pad(
        from_before.astype(full), ((0, src_count - HALF), (0, 0))
    )

    (s_dec_up,) = share_grads([g_dec_up], True)
    s_dec_down, s_cross_out = share_grads([g_dec_down, g_cross_out], False)
    s_cross_key, s_cross_value = share_grads([g_cross_key, g_cross_value], True)
    (s_enc_up,) = share_grads([g_enc_up], True)
    s_enc_down, s_enc_out = share_grads([g_enc_down, g_enc_out], False)
    s_self_query, s_self_key, s_self_value, s_self_out, s_cross_query = share_grads(
        [g_self_query, g_self_key, g_self_value, g_self_out, g_cross_query], False
    )
    s_enc_query, s_enc_key, s_enc_value = share_grads([g_enc_query, g_enc_key, g_enc_value], True)
    s_glob_query, s_glob_key, s_glob_value = share_grads(
        [g_glob_query, g_glob_key, g_glob_value], False
    )
    vectors = share_vectors(
        [
            g_enc_attn_gain,
            g_enc_attn_shift,
            g_enc_ffn_gain,
            g_enc_ffn_shift,
            g_dec_self_gain,
            g_dec_self_shift,
            g_dec_cross_gain,
            g_dec_cross_shift,
            g_dec_ffn_gain,
            g_dec_ffn_shift,
        ]
    )
    return (
        decoded.astype(low_type)[None],
        d_source[None],
        d_target[None],
        s_enc_query,
        s_enc_key,
        s_enc_value,
        s_glob_query,
        s_glob_key,
        s_glob_value,
        s_enc_out,
        vectors[0],
        vectors[1],
        s_enc_up,
        s_enc_down,
        vectors[2],
        vectors[3],
        s_self_query,
        s_self_key,
        s_self_value,
        s_self_out,
        vectors[4],
        vectors[5],
        s_cross_query,
        s_cross_key,
        s_cross_value,
        s_cross_out,
        vectors[6],
        vectors[7],
        s_dec_up,
        s_dec_down,
        vectors[8],
        vectors[9],
    )


def solution(mesh):
    rows = P("dp", "seq", None)
    tile = P("seq", "dp")
    part = P("seq")
    layer = (tile,) * 7 + (part,) * 2 + (tile,) * 2 + (part,) * 2
    decoder = (tile,) * 4 + (part,) * 2 + (tile,) * 4 + (part,) * 2 + (tile,) * 2 + (part,) * 2
    return jax.shard_map(
        per_device,
        mesh=mesh,
        in_specs=(rows, rows, rows, P("dp"), P("dp"), P("dp", None)) + (P(),) * 29,
        out_specs=(rows, rows, rows) + layer + decoder,
        check_vma=False,
    )
```

```python
import functools

import jax
import jax.numpy as jnp
import numpy as np
from jax import lax
from jax.experimental import pallas as pl
from jax.experimental.pallas import tpu as pltpu
from jax.sharding import PartitionSpec as P

HEADS = 12
HEAD_DIM = 64
HALF = 512
PAIRS = HEADS // 2
LANES = 2 * HEAD_DIM
SLOT = 16

masked_score = -1e30
eps_norm = 1e-05
low_type = jnp.bfloat16
vmem_bytes = 56 * 2**20


def dot_plain(left, right):
    return jnp.dot(left, right, preferred_element_type=jnp.float32)


def dot_left(left, right):
    return lax.dot_general(
        left, right, (((0,), (0,)), ((), ())), preferred_element_type=jnp.float32
    )


def dot_right(left, right):
    return lax.dot_general(
        left, right, (((1,), (1,)), ((), ())), preferred_element_type=jnp.float32
    )


def exact_dot(left, right):
    return jnp.dot(
        left, right, precision=lax.Precision.HIGHEST, preferred_element_type=jnp.float32
    )


def layer_norm(value, scale_vec, shift_vec):
    average = jnp.mean(value, axis=-1, keepdims=True)
    centred = value - average
    spread = jnp.mean(centred * centred, axis=-1, keepdims=True)
    return centred * lax.rsqrt(spread + eps_norm) * scale_vec + shift_vec


def gelu_pair(value):
    cdf = 0.5 * (1.0 + lax.erf(value * 0.7071067811865476))
    slope = cdf + value * (0.3989422804014327 * jnp.exp(-0.5 * value * value))
    return (value * cdf).astype(low_type), slope.astype(low_type)


def head_spread():
    heads = lax.broadcasted_iota(jnp.int32, (SLOT, HEADS * HEAD_DIM), 0)
    columns = lax.broadcasted_iota(jnp.int32, (SLOT, HEADS * HEAD_DIM), 1)
    return (columns // HEAD_DIM == heads).astype(jnp.float32)


def head_mask(which):
    lanes = lax.broadcasted_iota(jnp.int32, (1, LANES), 1)
    return ((lanes // HEAD_DIM) == which).astype(low_type)


def forward_body(parts, rows_block, blocks, normalize, q_ref, k_ref, v_ref, bias_ref, o_ref, st_ref):
    pair = pl.program_id(1)
    lane = lax.broadcasted_iota(jnp.int32, (1, LANES), 1)

    @pl.when(pair == 0)
    def _():
        st_ref[...] = jnp.zeros_like(st_ref)

    for block in range(blocks):
        rows = pl.ds(block * rows_block, rows_block)
        q_two = q_ref[rows, :]
        stats = st_ref[rows, :]
        outs = []
        for which in range(2):
            head = 2 * pair + which
            q_one = q_two * head_mask(which)
            scores = []
            for start, size in parts[block]:
                bias = bias_ref[:, start : start + size]
                if bias_ref.shape[0] > 1:
                    bias = bias_ref[rows, start : start + size]
                scores.append(dot_right(q_one, k_ref[start : start + size, :]) + bias)
            top = functools.reduce(
                jnp.maximum, [jnp.max(part, axis=1, keepdims=True) for part in scores]
            )
            total = jnp.zeros((rows_block, 1), jnp.float32)
            mixed = jnp.zeros((rows_block, LANES), jnp.float32)
            for (start, size), part in zip(parts[block], scores):
                weights = jnp.exp(part - top)
                total = total + jnp.sum(weights, axis=1, keepdims=True)
                mixed = mixed + dot_plain(weights.astype(low_type), v_ref[start : start + size, :])
            if normalize:
                mixed = mixed / total
                stats = jnp.where(lane == head, top + jnp.log(total), stats)
            else:
                stats = jnp.where(lane == head, top, stats)
                stats = jnp.where(lane == head + SLOT, total, stats)
            outs.append(mixed)
        st_ref[rows, :] = stats
        o_ref[rows, :] = jnp.where(lane < HEAD_DIM, outs[0], outs[1])


def attend(queries, keys, values, bias, parts, rows_block, normalize):
    count, width = queries.shape
    key_count = keys.shape[0]
    big = min(count, 512)
    blocks = big // rows_block
    parts = parts or [((0, key_count),)] * blocks
    bias_rows = bias.shape[0]
    flops = 4 * count * key_count * width
    return pl.pallas_call(
        functools.partial(forward_body, parts, rows_block, blocks, normalize),
        grid=(count // big, PAIRS),
        in_specs=[
            pl.BlockSpec((big, LANES), lambda i, p: (i, p)),
            pl.BlockSpec((key_count, LANES), lambda i, p: (0, p)),
            pl.BlockSpec((key_count, LANES), lambda i, p: (0, p)),
            pl.BlockSpec((min(bias_rows, big), key_count), lambda i, p: (0, 0)),
        ],
        out_specs=[
            pl.BlockSpec((big, LANES), lambda i, p: (i, p)),
            pl.BlockSpec((big, LANES), lambda i, p: (i, 0)),
        ],
        out_shape=[
            jax.ShapeDtypeStruct((count, width), jnp.float32),
            jax.ShapeDtypeStruct((count, LANES), jnp.float32),
        ],
        compiler_params=pltpu.CompilerParams(vmem_limit_bytes=vmem_bytes),
        cost_estimate=pl.CostEstimate(
            flops=4 * flops,
            bytes_accessed=2 * (count + 2 * key_count) * width + 4 * count * width,
            transcendentals=count * key_count * HEADS,
        ),
    )(queries, keys, values, bias)


def backward_body(
    parts, rows_block, blocks, q_ref, k_ref, v_ref, d_ref, st_ref, bias_ref,
    dq_ref, dk_ref, dv_ref, key_sum, val_sum,
):
    pair = pl.program_id(0)
    turn = pl.program_id(1)

    @pl.when(turn == 0)
    def _():
        key_sum[...] = jnp.zeros_like(key_sum)
        val_sum[...] = jnp.zeros_like(val_sum)

    for block in range(blocks):
        rows = pl.ds(block * rows_block, rows_block)
        q_two = q_ref[rows, :]
        d_two = d_ref[rows, :]
        turned = []
        for which in range(2):
            head = 2 * pair + which
            q_one = q_two * head_mask(which)
            d_one = d_two * head_mask(which)
            lse = st_ref[pl.ds(head, 1), rows]
            delta = st_ref[pl.ds(head + SLOT, 1), rows]
            q_grad = jnp.zeros((LANES, rows_block), jnp.float32)
            for start, size in parts[block]:
                keys = slice(start, start + size)
                bias = bias_ref[keys, :]
                if bias_ref.shape[1] > 1:
                    bias = bias_ref[keys, rows]
                k_two = k_ref[keys, :]
                scores = dot_right(k_two, q_one) + bias
                weights = jnp.exp(scores - lse)
                slopes = dot_right(v_ref[keys, :], d_one)
                diffs = (weights * (slopes - delta)).astype(low_type)
                val_sum[keys, :] += dot_plain(weights.astype(low_type), d_one)
                key_sum[keys, :] += dot_plain(diffs, q_one)
                q_grad = q_grad + dot_left(k_two, diffs)
            turned.append(q_grad[which * HEAD_DIM : (which + 1) * HEAD_DIM, :])
        dq_ref[rows, :] = jnp.concatenate(turned, axis=0).T

    @pl.when(turn == pl.num_programs(1) - 1)
    def _():
        dk_ref[...] = key_sum[...].astype(low_type)
        dv_ref[...] = val_sum[...].astype(low_type)


def attend_back(queries, keys, values, grads, stats, bias, parts, rows_block):
    count, width = queries.shape
    key_count = keys.shape[0]
    big = min(count, 512)
    blocks = big // rows_block
    parts = parts or [((0, key_count),)] * blocks
    bias_cols = bias.shape[1]
    flops = 10 * count * key_count * width
    return pl.pallas_call(
        functools.partial(backward_body, parts, rows_block, blocks),
        grid=(PAIRS, count // big),
        in_specs=[
            pl.BlockSpec((big, LANES), lambda p, i: (i, p)),
            pl.BlockSpec((key_count, LANES), lambda p, i: (0, p)),
            pl.BlockSpec((key_count, LANES), lambda p, i: (0, p)),
            pl.BlockSpec((big, LANES), lambda p, i: (i, p)),
            pl.BlockSpec((2 * SLOT, big), lambda p, i: (0, i)),
            pl.BlockSpec((key_count, min(bias_cols, big)), lambda p, i: (0, 0)),
        ],
        out_specs=[
            pl.BlockSpec((big, LANES), lambda p, i: (i, p)),
            pl.BlockSpec((key_count, LANES), lambda p, i: (0, p)),
            pl.BlockSpec((key_count, LANES), lambda p, i: (0, p)),
        ],
        out_shape=[
            jax.ShapeDtypeStruct((count, width), jnp.float32),
            jax.ShapeDtypeStruct((key_count, width), low_type),
            jax.ShapeDtypeStruct((key_count, width), low_type),
        ],
        scratch_shapes=[
            pltpu.VMEM((key_count, LANES), jnp.float32),
            pltpu.VMEM((key_count, LANES), jnp.float32),
        ],
        compiler_params=pltpu.CompilerParams(vmem_limit_bytes=vmem_bytes),
        cost_estimate=pl.CostEstimate(
            flops=4 * flops,
            bytes_accessed=2 * (2 * count + 4 * key_count) * width + 4 * count * width,
            transcendentals=count * key_count * HEADS,
        ),
    )(queries, keys, values, grads, stats, bias)


def seq_bits():
    count = lax.axis_size("seq")
    return [1 << k for k in range(count.bit_length() - 1)]


def swap(value, bit):
    pairs = [(i, i ^ bit) for i in range(lax.axis_size("seq"))]
    return jax.tree.map(lambda part: lax.ppermute(part, "seq", pairs), value)


def swap_dp(value):
    pairs = [(i, i ^ 1) for i in range(lax.axis_size("dp"))]
    return lax.ppermute(value, "dp", pairs)


def bit_set(bit):
    return (lax.axis_index("seq") & bit) != 0


def gather_rows(value):
    rows, width = value.shape
    held = value[None]
    for bit in reversed(seq_bits()):
        other = swap(held, bit)
        upper = bit_set(bit)
        held = jnp.stack(
            [jnp.where(upper, other, held), jnp.where(upper, held, other)], axis=1
        ).reshape(2 * held.shape[0], rows, width)
    return held.reshape(-1, width)


def add_all(value):
    for bit in seq_bits():
        value = value + swap(value, bit)
    return value


def pick_half(value, chosen, axis):
    return lax.dynamic_index_in_dim(value, chosen, axis, keepdims=False)


def scatter_rows(value):
    bits = seq_bits()
    held = value.reshape((2,) * len(bits) + (-1, value.shape[1]))
    for step, bit in enumerate(bits):
        axis = len(bits) - 1 - step
        mine = bit_set(bit).astype(jnp.int32)
        other = swap(pick_half(held, 1 - mine, axis).astype(low_type), bit)
        held = pick_half(held, mine, axis) + other.astype(jnp.float32)
    return held


def merge_body(acc_a, st_a, acc_b, st_b, acc_o, st_o):
    top_a, top_b = st_a[:, :SLOT], st_b[:, :SLOT]
    top = jnp.maximum(top_a, top_b)
    keep_a = jnp.exp(top_a - top)
    keep_b = jnp.exp(top_b - top)
    total = st_a[:, SLOT : 2 * SLOT] * keep_a + st_b[:, SLOT : 2 * SLOT] * keep_b
    spread = head_spread()
    acc_o[...] = acc_a[...] * exact_dot(keep_a, spread) + acc_b[...].astype(
        jnp.float32
    ) * exact_dot(keep_b, spread)
    rest = jnp.zeros((top.shape[0], LANES - 2 * SLOT), jnp.float32)
    st_o[...] = jnp.concatenate([top, total, rest], axis=1)


def merge_soft(held, other):
    rows = held[0].shape[0]
    return pl.pallas_call(
        merge_body,
        out_shape=[
            jax.ShapeDtypeStruct((rows, held[0].shape[1]), jnp.float32),
            jax.ShapeDtypeStruct((rows, LANES), jnp.float32),
        ],
        compiler_params=pltpu.CompilerParams(vmem_limit_bytes=vmem_bytes),
    )(*held, *other)


def merge_all(held):
    for bit in seq_bits():
        held = merge_soft(held, swap((held[0].astype(low_type), held[1]), bit))
    return held


def merge_scatter(held):
    bits = seq_bits()
    for step, bit in enumerate(bits):
        inner = len(bits) - 1 - step
        mine = bit_set(bit).astype(jnp.int32)

        def halves(value, chosen):
            split = value.reshape(1 << inner, 2, -1, value.shape[1])
            return pick_half(split, chosen, 1).reshape(-1, value.shape[1])

        away = (halves(held[0], 1 - mine).astype(low_type), halves(held[1], 1 - mine))
        held = merge_soft((halves(held[0], mine), halves(held[1], mine)), swap(away, bit))
    return held


def share_grads(grads, dp_first):
    bits = seq_bits()
    width = grads[0].shape[1]
    half = width // 2
    rows = [grad.shape[0] >> len(bits) for grad in grads]
    dp_mine = lax.axis_index("dp")
    laid = [
        grad.astype(low_type).reshape((2,) * len(bits) + (count, width))
        for grad, count in zip(grads, rows)
    ]
    steps = [(1, False)]
    rest = [(bit, False) for bit in bits[1:]]
    steps += [(0, True)] + rest if dp_first else rest[:1] + [(0, True)] + rest[1:]
    held = None
    axis = len(bits)
    for bit, is_dp in steps:
        if is_dp:
            own = lax.dynamic_slice_in_dim(held, dp_mine * half, half, held.ndim - 1)
            away = lax.dynamic_slice_in_dim(held, (1 - dp_mine) * half, half, held.ndim - 1)
            held = own + swap_dp(away)
            continue
        axis -= 1
        mine = bit_set(bit).astype(jnp.int32)
        if held is None:
            away = jnp.concatenate([pick_half(v, 1 - mine, axis) for v in laid], axis=-2)
            own = jnp.concatenate([pick_half(v, mine, axis) for v in laid], axis=-2)
        else:
            away = pick_half(held, 1 - mine, axis)
            own = pick_half(held, mine, axis)
        held = own + swap(away, bit)
    result = []
    start = 0
    for count in rows:
        result.append(held[start : start + count].astype(jnp.float32))
        start += count
    return result


def other_of(place, bit):
    return place + bit * (1 - 2 * ((place // bit) % 2))


def greet(partners):
    barrier = pltpu.get_barrier_semaphore()
    for partner in partners:
        pl.semaphore_signal(
            barrier, inc=1, device_id=partner, device_id_type=pl.DeviceIdType.MESH
        )
    pl.semaphore_wait(barrier, len(partners))


def remote(src, dst, sems, k, partner):
    return pltpu.make_async_remote_copy(
        src_ref=src,
        dst_ref=dst,
        send_sem=sems[0].at[k],
        recv_sem=sems[1].at[k],
        device_id=partner,
        device_id_type=pl.DeviceIdType.MESH,
    )


def piece_stages(peers, dp_first):
    bits = [1 << k for k in range(1, peers.bit_length() - 1)]
    return [1] + (["dp"] + bits if dp_first else bits[:1] + ["dp"] + bits[1:])


def piece_shapes(peers, piece):
    dp_first, mats, width = piece
    rows = sum(count for _, count in mats)
    free = peers.bit_length() - 1
    shapes = []
    for stage in piece_stages(peers, dp_first):
        if stage == "dp":
            width = width // 2
        else:
            free -= 1
        shapes.append((2,) * free + (rows, width))
    return shapes


def reduce_body(peers, pieces, mat_count, *refs):
    mats = refs[:mat_count]
    outs = refs[mat_count : mat_count + len(pieces)]
    send, recv, load = refs[mat_count + len(pieces) : mat_count + len(pieces) + 3]
    rest = list(refs[mat_count + len(pieces) + 3 :])
    stages = [piece_stages(peers, piece[0]) for piece in pieces]
    count = len(stages[0])
    held = [[rest.pop(0) for _ in range(count)] for _ in pieces]
    own = [rest.pop(0) for _ in pieces]
    me = lax.axis_index("seq")
    mine_dp = lax.axis_index("dp")
    free = peers.bit_length() - 2

    def partner(stage):
        if stage == "dp":
            return {"dp": 1 - mine_dp}
        return {"seq": other_of(me, stage)}

    greet([partner(stage) for stage in stages[0]])
    core = me % 2
    numbers = {}

    def number(*key):
        return numbers.setdefault(key, len(numbers))

    def first_copies(p):
        result = []
        start = 0
        for mat, rows in pieces[p][1]:
            k = number(p, 0, mat)
            spot = (slice(None),) * free + (pl.ds(start, rows),)
            theirs = mats[mat].at[(slice(None),) * free + (1 - core,)]
            ours = mats[mat].at[(slice(None),) * free + (core,)]
            result.append(remote(theirs, held[p][0].at[spot], (send, recv), k, partner(1)))
            result.append(pltpu.make_async_copy(ours, own[p].at[spot], load.at[mat]))
            start += rows
        return result

    def later_copy(p, s):
        stage = stages[p][s]
        source = held[p][s - 1]
        if stage == "dp":
            half = source.shape[-1] // 2
            away = pl.multiple_of((1 - mine_dp) * half, LANES)
            view = source.at[(slice(None),) * (len(source.shape) - 1) + (pl.ds(away, half),)]
        else:
            bits = len(source.shape) - 2
            view = source.at[(slice(None),) * (bits - 1) + (1 - (me // stage) % 2,)]
        return remote(view, held[p][s], (send, recv), number(p, s), partner(stage))

    def begin(p, s):
        for copy in first_copies(p) if s == 0 else [later_copy(p, s)]:
            copy.start()

    def end(p, s):
        for copy in first_copies(p) if s == 0 else [later_copy(p, s)]:
            copy.wait()
        target = held[p][s]
        bits = len(target.shape) - 2
        for place in np.ndindex(*(2,) * bits):
            if s == 0:
                more = own[p][place]
            elif stages[p][s] == "dp":
                half = target.shape[-1]
                start = pl.multiple_of(mine_dp * half, LANES)
                more = held[p][s - 1][place + (slice(None), pl.ds(start, half))]
            else:
                more = held[p][s - 1][place + ((me // stages[p][s]) % 2,)]
            total = target[place] + more
            if s == count - 1:
                outs[p][...] = total.astype(jnp.float32)
            else:
                target[place] = total

    turns = [list(range(k, min(k + 2, len(pieces)))) for k in range(0, len(pieces), 2)]
    for turn in turns[:2]:
        for p in turn:
            begin(p, 0)
    for now in range(len(turns) + count - 1):
        for age in range(count):
            if not 0 <= now - age < len(turns):
                continue
            for p in turns[now - age]:
                end(p, age)
                if age < count - 1:
                    begin(p, age + 1)
        if now + 2 < len(turns):
            for p in turns[now + 2]:
                begin(p, 0)


def reduce_grads(grads, groups):
    peers = lax.axis_size("seq")
    free = peers.bit_length() - 1
    mats = [
        grad.reshape((2,) * free + (grad.shape[0] // peers, grad.shape[1])) for grad in grads
    ]
    pieces = [
        (
            bool(k % 2),
            tuple((mat, mats[mat].shape[-2]) for mat in group),
            grads[group[0]].shape[1],
        )
        for k, group in enumerate(groups)
    ]
    shapes = [piece_shapes(peers, piece) for piece in pieces]
    copies = len(grads) + sum(len(stages) - 1 for stages in shapes)
    sent = sum(grad.size for grad in grads)
    sums = pl.pallas_call(
        functools.partial(reduce_body, peers, pieces, len(grads)),
        in_specs=[pl.BlockSpec(memory_space=pl.ANY)] * len(grads),
        out_specs=[pl.BlockSpec(memory_space=pltpu.VMEM)] * len(pieces),
        out_shape=[jax.ShapeDtypeStruct(stages[-1], jnp.float32) for stages in shapes],
        scratch_shapes=[
            pltpu.SemaphoreType.DMA((copies,)),
            pltpu.SemaphoreType.DMA((copies,)),
            pltpu.SemaphoreType.DMA((len(grads),)),
        ]
        + [pltpu.VMEM(shape, low_type) for stages in shapes for shape in stages]
        + [pltpu.VMEM(stages[0], low_type) for stages in shapes],
        compiler_params=pltpu.CompilerParams(
            collective_id=1, has_side_effects=True, vmem_limit_bytes=62 * 2**20
        ),
        cost_estimate=pl.CostEstimate(flops=sent, bytes_accessed=2 * sent, transcendentals=0),
    )(*mats)
    result = [None] * len(grads)
    for piece, total in zip(pieces, sums):
        start = 0
        for mat, rows in piece[1]:
            result[mat] = total[start : start + rows]
            start += rows
    return result


def share_vectors(vectors):
    stacked = jnp.concatenate([jnp.stack(vectors), jnp.zeros((6, vectors[0].shape[0]))], axis=0)
    total = add_all(stacked)
    total = total + swap_dp(total)
    length = stacked.shape[1] // lax.axis_size("seq")
    mine = lax.dynamic_slice_in_dim(total, lax.axis_index("seq") * length, length, 1)
    return [mine[k] for k in range(len(vectors))]


def pad_rows(value, count):
    return jnp.pad(value, ((0, count - value.shape[0]), (0, 0)))


def per_device(
    source,
    target,
    cotangent,
    src_len,
    dec_len,
    global_pos,
    enc_query,
    enc_key,
    enc_value,
    glob_query,
    glob_key,
    glob_value,
    enc_out,
    enc_attn_gain,
    enc_attn_shift,
    enc_up,
    enc_down,
    enc_ffn_gain,
    enc_ffn_shift,
    self_query,
    self_key,
    self_value,
    self_out,
    dec_self_gain,
    dec_self_shift,
    cross_query,
    cross_key,
    cross_value,
    cross_out,
    dec_cross_gain,
    dec_cross_shift,
    dec_up,
    dec_down,
    dec_ffn_gain,
    dec_ffn_shift,
):
    full = jnp.float32
    src_x = source[0]
    dec_x = target[0]
    src_count = src_x.shape[0]
    dec_count = dec_x.shape[0]
    seq_index = lax.axis_index("seq")
    peers = lax.axis_size("seq")
    src_limit = src_len[0]
    dec_limit = dec_len[0]
    glob_places = global_pos[0]
    glob_count = glob_places.shape[0]
    src_places = seq_index * src_count + jnp.arange(src_count, dtype=jnp.int32)
    select_glob = glob_places[:, None] == src_places[None, :]
    select_low = select_glob.astype(low_type)
    is_global = jnp.any(select_glob, axis=0)
    spread = head_spread()

    upward = [(i, i + 1) for i in range(peers - 1)]
    downward = [(i + 1, i) for i in range(peers - 1)]
    before = lax.ppermute(src_x[src_count - HALF :], "seq", upward)
    after = lax.ppermute(src_x[:HALF], "seq", downward)
    dec_all = gather_rows(dec_x)
    glob_x = add_all(dot_plain(select_low, src_x).astype(low_type))

    query_loc = (dot_plain(src_x, enc_query) * 0.125).astype(low_type)
    glob_keys_loc = dot_plain(src_x, glob_key).astype(low_type)
    glob_vals_loc = dot_plain(src_x, glob_value).astype(low_type)

    self_q = (dot_plain(dec_x, self_query) * 0.125).astype(low_type)
    self_k = dot_plain(dec_all, self_key).astype(low_type)
    self_v = dot_plain(dec_all, self_value).astype(low_type)
    dec_total = dec_all.shape[0]
    dec_places = seq_index * dec_count + jnp.arange(dec_count, dtype=jnp.int32)
    all_dec = jnp.arange(dec_total, dtype=jnp.int32)
    self_allowed = (all_dec[None, :] <= dec_places[:, None]) & (all_dec < dec_limit)[None, :]
    self_bias = jnp.where(self_allowed, 0.0, masked_score)
    self_out_full, self_stats = attend(self_q, self_k, self_v, self_bias, None, dec_count, True)
    self_attn = self_out_full.astype(low_type)
    dec_res_one = dec_x.astype(full) + dot_plain(self_attn, self_out)
    dec_first, dec_first_back = jax.vjp(
        layer_norm, dec_res_one, dec_self_gain.astype(full), dec_self_shift.astype(full)
    )
    dec_first_low = dec_first.astype(low_type)
    cross_q = (dot_plain(dec_first_low, cross_query) * 0.125).astype(low_type)
    all_cross_q = gather_rows(cross_q)

    glob_queries = (dot_plain(glob_x, glob_query) * 0.125).astype(low_type)
    live_bias = jnp.where(src_places < src_limit, 0.0, masked_score)
    glob_acc, glob_stats = merge_all(
        attend(
            glob_queries, glob_keys_loc, glob_vals_loc, live_bias[None, :], None, glob_count, False
        )
    )
    glob_total = glob_stats[:, SLOT : 2 * SLOT]
    glob_out = glob_acc / exact_dot(glob_total, spread)
    glob_lse = glob_stats[:, :SLOT] + jnp.log(jnp.maximum(glob_total, 1e-30))

    x_all = jnp.concatenate([before, src_x, after, glob_x], axis=0)
    keys_all = dot_plain(x_all, enc_key).astype(low_type)
    vals_all = dot_plain(x_all, enc_value).astype(low_type)
    pad_count = src_count + 2 * HALF
    pad_places = seq_index * src_count - HALF + jnp.arange(pad_count, dtype=jnp.int32)
    pad_glob = jnp.any(glob_places[:, None] == pad_places[None, :], axis=0)
    pad_use = (pad_places >= 0) & (pad_places < src_limit) & jnp.logical_not(pad_glob)
    near = jnp.abs(src_places[:, None] - pad_places[None, :]) <= HALF
    win_bias = jnp.concatenate(
        [
            jnp.where(near & pad_use[None, :], 0.0, masked_score),
            jnp.zeros((src_count, glob_count), full),
        ],
        axis=1,
    )
    near_turned = jnp.abs(src_places[None, :] - pad_places[:, None]) <= HALF
    win_bias_turned = jnp.concatenate(
        [
            jnp.where(near_turned & pad_use[:, None], 0.0, masked_score),
            jnp.zeros((glob_count, src_count), full),
        ],
        axis=0,
    )
    rows_block = 256
    reach = rows_block + 2 * HALF
    win_parts = [
        ((block * rows_block, reach), (pad_count, glob_count))
        for block in range(src_count // rows_block)
    ]
    win_out, win_stats = attend(
        query_loc, keys_all, vals_all, win_bias, win_parts, rows_block, True
    )
    placed = dot_left(select_low, glob_out.astype(low_type))
    enc_attn = jnp.where(is_global[:, None], placed, win_out).astype(low_type)
    enc_res = src_x.astype(full) + dot_plain(enc_attn, enc_out)
    enc_first, enc_first_back = jax.vjp(
        layer_norm, enc_res, enc_attn_gain.astype(full), enc_attn_shift.astype(full)
    )
    enc_first_low = enc_first.astype(low_type)
    enc_hidden, enc_slope = gelu_pair(dot_plain(enc_first_low, enc_up))
    enc_second = enc_first + dot_plain(enc_hidden, enc_down)
    memory, enc_final_back = jax.vjp(
        layer_norm, enc_second, enc_ffn_gain.astype(full), enc_ffn_shift.astype(full)
    )
    memory_low = memory.astype(low_type)

    cross_k = dot_plain(memory_low, cross_key).astype(low_type)
    cross_v = dot_plain(memory_low, cross_value).astype(low_type)
    cross_acc, cross_stats = merge_scatter(
        attend(all_cross_q, cross_k, cross_v, live_bias[None, :], None, 256, False)
    )
    cross_total = cross_stats[:, SLOT : 2 * SLOT]
    cross_out_full = cross_acc / exact_dot(cross_total, spread)
    cross_lse = cross_stats[:, :SLOT] + jnp.log(jnp.maximum(cross_total, 1e-30))
    cross_attn = cross_out_full.astype(low_type)
    dec_res_two = dec_first + dot_plain(cross_attn, cross_out)
    dec_second, dec_second_back = jax.vjp(
        layer_norm, dec_res_two, dec_cross_gain.astype(full), dec_cross_shift.astype(full)
    )
    dec_second_low = dec_second.astype(low_type)
    dec_hidden, dec_slope = gelu_pair(dot_plain(dec_second_low, dec_up))
    dec_third = dec_second + dot_plain(dec_hidden, dec_down)
    decoded, dec_final_back = jax.vjp(
        layer_norm, dec_third, dec_ffn_gain.astype(full), dec_ffn_shift.astype(full)
    )

    d_third, g_dec_ffn_gain, g_dec_ffn_shift = dec_final_back(cotangent[0].astype(full))
    d_down_low = d_third.astype(low_type)
    d_pre_low = (dot_right(d_down_low, dec_down) * dec_slope.astype(full)).astype(low_type)
    d_second = d_third + dot_right(d_pre_low, dec_up)
    d_res_two, g_dec_cross_gain, g_dec_cross_shift = dec_second_back(d_second)
    d_cross_o = d_res_two.astype(low_type)
    d_cross_attn = dot_right(d_cross_o, cross_out).astype(low_type)
    cross_delta = exact_dot(d_cross_attn.astype(full) * cross_out_full, spread.T)
    all_dout = gather_rows(d_cross_attn)
    all_stats = gather_rows(
        jnp.concatenate(
            [cross_lse, cross_delta, jnp.zeros((dec_count, LANES - 2 * SLOT), full)], axis=1
        )
    )[:, : 2 * SLOT].T
    live_turned = jnp.broadcast_to(live_bias[:, None], (src_count, 512))
    query_parts, ck_low, cv_low = attend_back(
        all_cross_q, cross_k, cross_v, all_dout, all_stats, live_turned, None, 256
    )
    d_memory = dot_right(ck_low, cross_key) + dot_right(cv_low, cross_value)

    g_dec_down = dot_left(dec_hidden, d_down_low)
    g_dec_up = dot_left(dec_second_low, d_pre_low)
    g_cross_out = dot_left(cross_attn, d_cross_o)
    g_cross_key = dot_left(memory_low, ck_low)
    g_cross_value = dot_left(memory_low, cv_low)

    d_enc_second, g_enc_ffn_gain, g_enc_ffn_shift = enc_final_back(d_memory)
    d_enc_down = d_enc_second.astype(low_type)
    d_enc_pre = (dot_right(d_enc_down, enc_down) * enc_slope.astype(full)).astype(low_type)
    d_enc_first = d_enc_second + dot_right(d_enc_pre, enc_up)
    d_enc_res, g_enc_attn_gain, g_enc_attn_shift = enc_first_back(d_enc_first)
    d_attn_o = d_enc_res.astype(low_type)
    d_attn = dot_right(d_attn_o, enc_out).astype(low_type)
    g_enc_down = dot_left(enc_hidden, d_enc_down)
    g_enc_up = dot_left(enc_first_low, d_enc_pre)
    g_enc_out = dot_left(enc_attn, d_attn_o)

    d_cross_q = scatter_rows(query_parts).astype(low_type) * 0.125
    g_cross_query = dot_left(dec_first_low, d_cross_q)
    d_first = d_res_two + dot_right(d_cross_q, cross_query)
    d_res_one, g_dec_self_gain, g_dec_self_shift = dec_first_back(d_first)
    d_self_o = d_res_one.astype(low_type)
    g_self_out = dot_left(self_attn, d_self_o)
    d_self_attn = dot_right(d_self_o, self_out).astype(low_type)
    self_delta = exact_dot(d_self_attn.astype(full) * self_out_full, spread.T)
    wide = max(dec_count, LANES)
    self_pair = jnp.concatenate([self_stats[:, :SLOT], self_delta], axis=1)
    self_query_parts, d_self_k, d_self_v = attend_back(
        pad_rows(self_q, wide),
        self_k,
        self_v,
        pad_rows(d_self_attn, wide),
        pad_rows(self_pair, wide).T,
        pad_rows(self_bias, wide).T,
        None,
        wide,
    )
    d_self_q = self_query_parts[:dec_count].astype(low_type) * 0.125
    g_self_query = dot_left(dec_x, d_self_q)
    g_self_key = dot_left(dec_all, d_self_k)
    g_self_value = dot_left(dec_all, d_self_v)
    d_target = (
        d_res_one
        + dot_right(d_self_q, self_query)
        + scatter_rows(dot_right(d_self_k, self_key) + dot_right(d_self_v, self_value))
    )

    glob_dout = add_all(dot_plain(select_low, d_attn).astype(low_type))
    d_window = jnp.where(is_global[:, None], jnp.zeros_like(d_attn), d_attn)
    win_delta = exact_dot(d_window.astype(full) * win_out, spread.T)
    win_pair = jnp.concatenate([win_stats[:, :SLOT], win_delta], axis=1).T
    d_query, d_keys_all, d_vals_all = attend_back(
        query_loc, keys_all, vals_all, d_window, win_pair, win_bias_turned, win_parts, rows_block
    )
    d_query_low = d_query.astype(low_type) * 0.125

    wide = max(glob_count, LANES)
    glob_delta = exact_dot(glob_dout.astype(full) * glob_out, spread.T)
    glob_pair = jnp.concatenate([glob_lse, glob_delta], axis=1)
    glob_query_parts, gk_low, gv_low = attend_back(
        pad_rows(glob_queries, wide),
        glob_keys_loc,
        glob_vals_loc,
        pad_rows(glob_dout, wide),
        pad_rows(glob_pair, wide).T,
        live_turned[:, :wide],
        None,
        wide,
    )
    d_gq = glob_query_parts[:glob_count].astype(low_type) * 0.125

    g_enc_query = dot_left(src_x, d_query_low)
    g_enc_key = dot_left(x_all, d_keys_all)
    g_enc_value = dot_left(x_all, d_vals_all)
    g_glob_query = dot_left(glob_x, d_gq)
    g_glob_key = dot_left(src_x, gk_low)
    g_glob_value = dot_left(src_x, gv_low)

    d_x_all = dot_right(d_keys_all, enc_key) + dot_right(d_vals_all, enc_value)
    from_after = lax.ppermute(d_x_all[:HALF].astype(low_type), "seq", downward)
    from_before = lax.ppermute(d_x_all[HALF + src_count : pad_count].astype(low_type), "seq", upward)
    d_glob_x = add_all((d_x_all[pad_count:] + dot_right(d_gq, glob_query)).astype(low_type))
    d_source = (
        d_enc_res
        + dot_right(d_query_low, enc_query)
        + d_x_all[HALF : HALF + src_count]
        + dot_right(gk_low, glob_key)
        + dot_right(gv_low, glob_value)
        + dot_left(select_low, d_glob_x)
    )
    d_source = d_source + jnp.pad(
        from_after.astype(full), ((src_count - HALF, 0), (0, 0))
    )
    d_source = d_source + jnp.pad(
        from_before.astype(full), ((0, src_count - HALF), (0, 0))
    )

    big = [g_dec_up, g_dec_down, g_enc_up, g_enc_down]
    small = [
        g_cross_out,
        g_cross_key,
        g_cross_value,
        g_enc_out,
        g_cross_query,
        g_self_out,
        g_self_query,
        g_self_key,
        g_self_value,
        g_enc_query,
        g_enc_key,
        g_enc_value,
        g_glob_key,
        g_glob_value,
        g_glob_query,
    ]
    grads = big + small
    if (small[0].shape[0] // peers) % 16 == 0:
        groups = [[0], [1], [2], [3], [4, 5], [6, 7], [8, 9], [10, 11], [12, 13], [14, 15], [16, 17], [18]]
        shared = reduce_grads([grad.astype(low_type) for grad in grads], groups)
    else:
        shared = [share_grads([grad], k % 2 == 0)[0] for k, grad in enumerate(grads)]
    (
        s_dec_up, s_dec_down, s_enc_up, s_enc_down,
        s_cross_out, s_cross_key, s_cross_value, s_enc_out, s_cross_query,
        s_self_out, s_self_query, s_self_key, s_self_value,
        s_enc_query, s_enc_key, s_enc_value, s_glob_key, s_glob_value, s_glob_query,
    ) = shared
    vectors = share_vectors(
        [
            g_enc_attn_gain,
            g_enc_attn_shift,
            g_enc_ffn_gain,
            g_enc_ffn_shift,
            g_dec_self_gain,
            g_dec_self_shift,
            g_dec_cross_gain,
            g_dec_cross_shift,
            g_dec_ffn_gain,
            g_dec_ffn_shift,
        ]
    )
    return (
        decoded.astype(low_type)[None],
        d_source[None],
        d_target[None],
        s_enc_query,
        s_enc_key,
        s_enc_value,
        s_glob_query,
        s_glob_key,
        s_glob_value,
        s_enc_out,
        vectors[0],
        vectors[1],
        s_enc_up,
        s_enc_down,
        vectors[2],
        vectors[3],
        s_self_query,
        s_self_key,
        s_self_value,
        s_self_out,
        vectors[4],
        vectors[5],
        s_cross_query,
        s_cross_key,
        s_cross_value,
        s_cross_out,
        vectors[6],
        vectors[7],
        s_dec_up,
        s_dec_down,
        vectors[8],
        vectors[9],
    )


def solution(mesh):
    rows = P("dp", "seq", None)
    tile = P("seq", "dp")
    part = P("seq")
    layer = (tile,) * 7 + (part,) * 2 + (tile,) * 2 + (part,) * 2
    decoder = (tile,) * 4 + (part,) * 2 + (tile,) * 4 + (part,) * 2 + (tile,) * 2 + (part,) * 2
    return jax.shard_map(
        per_device,
        mesh=mesh,
        in_specs=(rows, rows, rows, P("dp"), P("dp"), P("dp", None)) + (P(),) * 29,
        out_specs=(rows, rows, rows) + layer + decoder,
        check_vma=False,
    )
```

```python
import functools

import jax
import jax.numpy as jnp
import numpy as np
from jax import lax
from jax.experimental import pallas as pl
from jax.experimental.pallas import tpu as pltpu
from jax.sharding import PartitionSpec as P

HEADS = 12
HEAD_DIM = 64
HALF = 512
PAIRS = HEADS // 2
LANES = 2 * HEAD_DIM
SLOT = 16

masked_score = -1e30
eps_norm = 1e-05
low_type = jnp.bfloat16
vmem_bytes = 56 * 2**20


def dot_plain(left, right):
    return jnp.dot(left, right, preferred_element_type=jnp.float32)


def dot_left(left, right):
    return lax.dot_general(
        left, right, (((0,), (0,)), ((), ())), preferred_element_type=jnp.float32
    )


def dot_right(left, right):
    return lax.dot_general(
        left, right, (((1,), (1,)), ((), ())), preferred_element_type=jnp.float32
    )


def exact_dot(left, right):
    return jnp.dot(
        left, right, precision=lax.Precision.HIGHEST, preferred_element_type=jnp.float32
    )


def layer_norm(value, scale_vec, shift_vec):
    average = jnp.mean(value, axis=-1, keepdims=True)
    centred = value - average
    spread = jnp.mean(centred * centred, axis=-1, keepdims=True)
    return centred * lax.rsqrt(spread + eps_norm) * scale_vec + shift_vec


def gelu_pair(value):
    cdf = 0.5 * (1.0 + lax.erf(value * 0.7071067811865476))
    slope = cdf + value * (0.3989422804014327 * jnp.exp(-0.5 * value * value))
    return (value * cdf).astype(low_type), slope.astype(low_type)


def head_spread():
    heads = lax.broadcasted_iota(jnp.int32, (SLOT, HEADS * HEAD_DIM), 0)
    columns = lax.broadcasted_iota(jnp.int32, (SLOT, HEADS * HEAD_DIM), 1)
    return (columns // HEAD_DIM == heads).astype(jnp.float32)


def head_mask(which):
    lanes = lax.broadcasted_iota(jnp.int32, (1, LANES), 1)
    return ((lanes // HEAD_DIM) == which).astype(low_type)


def forward_body(
    parts, rows_block, blocks, normalize, group, q_ref, k_ref, v_ref, bias_ref, o_ref, st_ref
):
    first = pl.program_id(1) * (2 * group)
    lane = lax.broadcasted_iota(jnp.int32, (1, LANES), 1)

    @pl.when(first == 0)
    def _():
        st_ref[...] = jnp.zeros_like(st_ref)

    for block in range(blocks):
        rows = pl.ds(block * rows_block, rows_block)
        stats = st_ref[rows, :]
        for pair in range(group):
            columns = pl.ds(pair * LANES, LANES)
            q_two = q_ref[rows, columns]
            outs = []
            for which in range(2):
                head = first + 2 * pair + which
                q_one = q_two * head_mask(which)
                scores = []
                for start, size in parts[block]:
                    keys = pl.ds(start, size)
                    bias = bias_ref[rows, keys] if bias_ref.shape[0] > 1 else bias_ref[:, keys]
                    scores.append(dot_right(q_one, k_ref[keys, columns]) + bias)
                top = functools.reduce(
                    jnp.maximum, [jnp.max(part, axis=1, keepdims=True) for part in scores]
                )
                total = jnp.zeros((rows_block, 1), jnp.float32)
                mixed = jnp.zeros((rows_block, LANES), jnp.float32)
                for (start, size), part in zip(parts[block], scores):
                    weights = jnp.exp(part - top)
                    total = total + jnp.sum(weights, axis=1, keepdims=True)
                    mixed = mixed + dot_plain(
                        weights.astype(low_type), v_ref[pl.ds(start, size), columns]
                    )
                if normalize:
                    mixed = mixed / total
                    stats = jnp.where(lane == head, top + jnp.log(total), stats)
                else:
                    stats = jnp.where(lane == head, top, stats)
                    stats = jnp.where(lane == head + SLOT, total, stats)
                outs.append(mixed)
            o_ref[rows, columns] = jnp.where(lane < HEAD_DIM, outs[0], outs[1])
        st_ref[rows, :] = stats


def attend(queries, keys, values, bias, parts, rows_block, normalize, group=1):
    count, width = queries.shape
    key_count = keys.shape[0]
    big = min(count, 512)
    blocks = big // rows_block
    parts = parts or [((0, key_count),)] * blocks
    bias_rows = bias.shape[0]
    flops = 4 * count * key_count * width
    wide = group * LANES
    return pl.pallas_call(
        functools.partial(forward_body, parts, rows_block, blocks, normalize, group),
        grid=(count // big, PAIRS // group),
        in_specs=[
            pl.BlockSpec((big, wide), lambda i, p: (i, p)),
            pl.BlockSpec((key_count, wide), lambda i, p: (0, p)),
            pl.BlockSpec((key_count, wide), lambda i, p: (0, p)),
            pl.BlockSpec(
                (min(bias_rows, big), key_count), lambda i, p: (i if bias_rows > big else 0, 0)
            ),
        ],
        out_specs=[
            pl.BlockSpec((big, wide), lambda i, p: (i, p)),
            pl.BlockSpec((big, LANES), lambda i, p: (i, 0)),
        ],
        out_shape=[
            jax.ShapeDtypeStruct((count, width), jnp.float32),
            jax.ShapeDtypeStruct((count, LANES), jnp.float32),
        ],
        compiler_params=pltpu.CompilerParams(vmem_limit_bytes=vmem_bytes),
        cost_estimate=pl.CostEstimate(
            flops=4 * flops,
            bytes_accessed=2 * (count + 2 * key_count) * width + 4 * count * width,
            transcendentals=count * key_count * HEADS,
        ),
    )(queries, keys, values, bias)


def backward_body(
    parts, rows_block, blocks, group, q_ref, k_ref, v_ref, d_ref, st_ref, bias_ref,
    dq_ref, dk_ref, dv_ref, key_sum, val_sum,
):
    first = pl.program_id(0) * (2 * group)
    turn = pl.program_id(1)

    @pl.when(turn == 0)
    def _():
        key_sum[...] = jnp.zeros_like(key_sum)
        val_sum[...] = jnp.zeros_like(val_sum)

    for block in range(blocks):
        rows = pl.ds(block * rows_block, rows_block)
        for pair in range(group):
            columns = pl.ds(pair * LANES, LANES)
            q_two = q_ref[rows, columns]
            d_two = d_ref[rows, columns]
            turned = []
            for which in range(2):
                head = first + 2 * pair + which
                q_one = q_two * head_mask(which)
                d_one = d_two * head_mask(which)
                lse = st_ref[pl.ds(head, 1), rows]
                delta = st_ref[pl.ds(head + SLOT, 1), rows]
                q_grad = jnp.zeros((LANES, rows_block), jnp.float32)
                for start, size in parts[block]:
                    keys = pl.ds(start, size)
                    bias = bias_ref[keys, rows] if bias_ref.shape[1] > 1 else bias_ref[keys, :]
                    k_two = k_ref[keys, columns]
                    scores = dot_right(k_two, q_one) + bias
                    weights = jnp.exp(scores - lse)
                    slopes = dot_right(v_ref[keys, columns], d_one)
                    diffs = (weights * (slopes - delta)).astype(low_type)
                    val_sum[keys, columns] += dot_plain(weights.astype(low_type), d_one)
                    key_sum[keys, columns] += dot_plain(diffs, q_one)
                    q_grad = q_grad + dot_left(k_two, diffs)
                turned.append(q_grad[which * HEAD_DIM : (which + 1) * HEAD_DIM, :])
            dq_ref[rows, columns] = jnp.concatenate(turned, axis=0).T

    @pl.when(turn == pl.num_programs(1) - 1)
    def _():
        dk_ref[...] = key_sum[...].astype(low_type)
        dv_ref[...] = val_sum[...].astype(low_type)


def attend_back(queries, keys, values, grads, stats, bias, parts, rows_block, group=1):
    count, width = queries.shape
    key_count = keys.shape[0]
    big = min(count, 512)
    blocks = big // rows_block
    parts = parts or [((0, key_count),)] * blocks
    bias_cols = bias.shape[1]
    flops = 10 * count * key_count * width
    wide = group * LANES
    return pl.pallas_call(
        functools.partial(backward_body, parts, rows_block, blocks, group),
        grid=(PAIRS // group, count // big),
        in_specs=[
            pl.BlockSpec((big, wide), lambda p, i: (i, p)),
            pl.BlockSpec((key_count, wide), lambda p, i: (0, p)),
            pl.BlockSpec((key_count, wide), lambda p, i: (0, p)),
            pl.BlockSpec((big, wide), lambda p, i: (i, p)),
            pl.BlockSpec((2 * SLOT, big), lambda p, i: (0, i)),
            pl.BlockSpec((key_count, min(bias_cols, big)), lambda p, i: (0, 0)),
        ],
        out_specs=[
            pl.BlockSpec((big, wide), lambda p, i: (i, p)),
            pl.BlockSpec((key_count, wide), lambda p, i: (0, p)),
            pl.BlockSpec((key_count, wide), lambda p, i: (0, p)),
        ],
        out_shape=[
            jax.ShapeDtypeStruct((count, width), jnp.float32),
            jax.ShapeDtypeStruct((key_count, width), low_type),
            jax.ShapeDtypeStruct((key_count, width), low_type),
        ],
        scratch_shapes=[
            pltpu.VMEM((key_count, wide), jnp.float32),
            pltpu.VMEM((key_count, wide), jnp.float32),
        ],
        compiler_params=pltpu.CompilerParams(vmem_limit_bytes=vmem_bytes),
        cost_estimate=pl.CostEstimate(
            flops=4 * flops,
            bytes_accessed=2 * (2 * count + 4 * key_count) * width + 4 * count * width,
            transcendentals=count * key_count * HEADS,
        ),
    )(queries, keys, values, grads, stats, bias)


def seq_bits():
    count = lax.axis_size("seq")
    return [1 << k for k in range(count.bit_length() - 1)]


def swap(value, bit):
    pairs = [(i, i ^ bit) for i in range(lax.axis_size("seq"))]
    return jax.tree.map(lambda part: lax.ppermute(part, "seq", pairs), value)


def swap_dp(value):
    pairs = [(i, i ^ 1) for i in range(lax.axis_size("dp"))]
    return lax.ppermute(value, "dp", pairs)


def bit_set(bit):
    return (lax.axis_index("seq") & bit) != 0


def add_all(value):
    for bit in seq_bits():
        value = value + swap(value, bit)
    return value


def pick_half(value, chosen, axis):
    return lax.dynamic_index_in_dim(value, chosen, axis, keepdims=False)


def scatter_step(held, step):
    bits = seq_bits()
    axis = len(bits) - 1 - step
    mine = bit_set(bits[step]).astype(jnp.int32)
    other = swap(pick_half(held, 1 - mine, axis).astype(low_type), bits[step])
    return pick_half(held, mine, axis) + other.astype(jnp.float32)


def scatter_start(value):
    return value.reshape((2,) * len(seq_bits()) + (-1, value.shape[1]))


def scatter_rows(value, done=0):
    for step in range(done, len(seq_bits())):
        value = scatter_step(scatter_start(value) if step == 0 else value, step)
    return value


def share_grads(grads, dp_first):
    bits = seq_bits()
    width = grads[0].shape[1]
    half = width // 2
    rows = [grad.shape[0] >> len(bits) for grad in grads]
    dp_mine = lax.axis_index("dp")
    laid = [
        grad.astype(low_type).reshape((2,) * len(bits) + (count, width))
        for grad, count in zip(grads, rows)
    ]
    steps = [(1, False)]
    rest = [(bit, False) for bit in bits[1:]]
    steps += [(0, True)] + rest if dp_first else rest[:1] + [(0, True)] + rest[1:]
    held = None
    axis = len(bits)
    for bit, is_dp in steps:
        if is_dp:
            own = lax.dynamic_slice_in_dim(held, dp_mine * half, half, held.ndim - 1)
            away = lax.dynamic_slice_in_dim(held, (1 - dp_mine) * half, half, held.ndim - 1)
            held = own + swap_dp(away)
            continue
        axis -= 1
        mine = bit_set(bit).astype(jnp.int32)
        if held is None:
            away = jnp.concatenate([pick_half(v, 1 - mine, axis) for v in laid], axis=-2)
            own = jnp.concatenate([pick_half(v, mine, axis) for v in laid], axis=-2)
        else:
            away = pick_half(held, 1 - mine, axis)
            own = pick_half(held, mine, axis)
        held = own + swap(away, bit)
    result = []
    start = 0
    for count in rows:
        result.append(held[start : start + count].astype(jnp.float32))
        start += count
    return result


def other_of(place, bit):
    return place + bit * (1 - 2 * ((place // bit) % 2))


def greet(partners):
    barrier = pltpu.get_barrier_semaphore()
    for partner in partners:
        pl.semaphore_signal(
            barrier, inc=1, device_id=partner, device_id_type=pl.DeviceIdType.MESH
        )
    pl.semaphore_wait(barrier, len(partners))


def remote(src, dst, sems, k, partner):
    return pltpu.make_async_remote_copy(
        src_ref=src,
        dst_ref=dst,
        send_sem=sems[0].at[k],
        recv_sem=sems[1].at[k],
        device_id=partner,
        device_id_type=pl.DeviceIdType.MESH,
    )


def piece_stages(peers, kind):
    bits = [1 << k for k in range(1, peers.bit_length() - 1)]
    if kind == "x":
        return [1, "dp"] + bits
    if kind == "y":
        return [1] + bits[:1] + ["dp"] + bits[1:]
    return [1] + bits[1:] + ["dp"] + bits[:1]


def piece_shapes(peers, rows, width, stages):
    free = peers.bit_length() - 1
    shapes = []
    for stage in stages:
        if stage == "dp":
            width = width // 2
        else:
            free -= 1
        shapes.append((2,) * free + (rows, width))
    return shapes


def bit_axis(peers, stages, s):
    rest = [bit for bit in reversed([1 << k for k in range(peers.bit_length() - 1)])]
    for stage in stages[:s]:
        if stage != "dp":
            rest.remove(stage)
    return rest.index(stages[s])


def last_body(peers, plan, *refs):
    refs = list(refs)

    def take(count):
        result = refs[:count]
        del refs[:count]
        return result

    mats = take(plan["mats"])
    factors = take(plan["factors"])
    target_part, glob_part, vec_part, rim = take(4)
    outs = take(len(plan["pieces"]))
    target_out, glob_out, vec_out, from_after, from_before = take(5)
    send, recv, load = take(3)
    pieces = plan["pieces"]
    held = [take(len(shapes)) for shapes in plan["shapes"]]
    own = take(plan["mats"])
    staging = take(plan["slots"])
    target_held = take(len(plan["target_shapes"]))
    glob_held = take(plan["glob_steps"])
    vec_held = take(plan["vec_steps"])
    me = lax.axis_index("seq")
    mine_dp = lax.axis_index("dp")
    free = peers.bit_length() - 1
    bits = [1 << k for k in range(free)]
    every = slice(None)

    def partner(stage):
        if stage == "dp":
            return {"dp": 1 - mine_dp}
        return {"seq": other_of(me, stage)}

    numbers = {}

    def number(*key):
        return numbers.setdefault(key, len(numbers))

    left_one = {"seq": lax.rem(me + peers - 1, peers)}
    right_one = {"seq": lax.rem(me + 1, peers)}
    greet([partner(stage) for stage in bits + ["dp"]] + [left_one, right_one])
    to_left = remote(rim.at[0], from_after, (send, recv), number("left"), left_one)
    to_right = remote(rim.at[1], from_before, (send, recv), number("right"), right_one)

    def halved(source, stages, s, mine):
        if stages[s] == "dp":
            half = source.shape[-1] // 2
            where = mine_dp if mine else 1 - mine_dp
            start = pl.multiple_of(where * half, LANES)
            return (every,) * (len(source.shape) - 1) + (pl.ds(start, half),)
        digit = (me // stages[s]) % 2
        return (every,) * bit_axis(peers, stages, s) + (digit if mine else 1 - digit,)

    def copies(name, stages, source, buffers, s):
        origin = source if s == 0 else buffers[s - 1]
        view = origin.at[halved(origin, stages, s, False)]
        return remote(view, buffers[s], (send, recv), number(name, s), partner(stages[s]))

    def fold(stages, source, buffers, s, finish):
        origin = source if s == 0 else buffers[s - 1]
        target = buffers[s]
        spot = halved(origin, stages, s, True)
        for place in np.ndindex(*target.shape[:-2]):
            if stages[s] == "dp":
                more = origin[place + spot[-2:]]
            else:
                axis = len(spot) - 1
                more = origin[place[:axis] + spot[-1:] + place[axis:]]
            total = target[place] + more
            if s == len(stages) - 1:
                finish[...] = total.astype(finish.dtype)
            else:
                target[place] = total

    def source_of(p):
        kind, which = pieces[p]["from"]
        return mats[which] if kind == "mat" else staging[which]

    def compute(p):
        x, y = (factors[k] for k in pieces[p]["pair"])
        target = staging[pieces[p]["from"][1]]
        step = x.shape[1] // 2
        for block in range(2):
            product = dot_left(x[:, block * step : (block + 1) * step], y[...])
            target[block] = product.astype(low_type).reshape(target.shape[1:])

    def begin(p, s):
        if s == 0:
            kind, which = pieces[p]["from"]
            if kind == "mat":
                origin = mats[which]
                ours = origin.at[halved(origin, pieces[p]["stages"], 0, True)]
                pltpu.make_async_copy(ours, own[which], load.at[which]).start()
        copies(p, pieces[p]["stages"], source_of(p), held[p], s).start()

    def end(p, s):
        stages = pieces[p]["stages"]
        copies(p, stages, source_of(p), held[p], s).wait()
        kind, which = pieces[p]["from"]
        if s == 0 and kind == "mat":
            origin = mats[which]
            ours = origin.at[halved(origin, pieces[p]["stages"], 0, True)]
            pltpu.make_async_copy(ours, own[which], load.at[which]).wait()
            for place in np.ndindex(*held[p][0].shape[:-2]):
                held[p][0][place] = held[p][0][place] + own[which][place]
        else:
            fold(stages, source_of(p), held[p], s, outs[p])

    target_stages = bits
    vec_stages = bits + ["dp"]

    def small_begin(s):
        if s < len(target_stages):
            copies("t", target_stages, target_part, target_held, s).start()
        if s < len(bits):
            origin = glob_part if s == 0 else glob_out
            remote(
                origin, glob_held[s], (send, recv), number("g", s), partner(bits[s])
            ).start()
        if s < len(vec_stages):
            origin = vec_part if s == 0 else vec_out
            remote(
                origin, vec_held[s], (send, recv), number("v", s), partner(vec_stages[s])
            ).start()

    def small_end(s):
        if s < len(target_stages):
            copies("t", target_stages, target_part, target_held, s).wait()
            fold(target_stages, target_part, target_held, s, target_out)
        if s < len(bits):
            origin = glob_part if s == 0 else glob_out
            remote(
                origin, glob_held[s], (send, recv), number("g", s), partner(bits[s])
            ).wait()
            glob_out[...] = origin[...] + glob_held[s][...]
        if s < len(vec_stages):
            origin = vec_part if s == 0 else vec_out
            remote(
                origin, vec_held[s], (send, recv), number("v", s), partner(vec_stages[s])
            ).wait()
            vec_out[...] = origin[...] + vec_held[s][...]

    turns = plan["turns"]
    count = len(pieces[0]["stages"])

    def open_turn(turn):
        for p in turns[turn]:
            if "pair" in pieces[p]:
                compute(p)
            begin(p, 0)

    for turn in range(min(2, len(turns))):
        open_turn(turn)

    @pl.when(me > 0)
    def _():
        to_left.start()

    @pl.when(me < peers - 1)
    def _():
        to_right.start()

    small_begin(0)
    for now in range(len(turns) + count - 1):
        for age in range(count):
            if not 0 <= now - age < len(turns):
                continue
            for p in turns[now - age]:
                end(p, age)
                if age < count - 1:
                    begin(p, age + 1)
        if 1 <= now <= len(vec_stages):
            small_end(now - 1)
            if now < len(vec_stages):
                small_begin(now)
        if now + 2 < len(turns):
            open_turn(now + 2)

    @pl.when(me > 0)
    def _():
        to_left.wait_send()
        to_right_in = remote(rim.at[1], from_before, (send, recv), number("right"), left_one)
        to_right_in.wait_recv()

    @pl.when(me < peers - 1)
    def _():
        to_right.wait_send()
        to_left_in = remote(rim.at[0], from_after, (send, recv), number("left"), right_one)
        to_left_in.wait_recv()


KINDS = "xyzxyxxyxxyxxy"


def last_exchange(made, pairs, target_part, glob_part, vec_part, rim):
    peers = lax.axis_size("seq")
    free = peers.bit_length() - 1
    lead = (2,) * free
    factors = []
    places = []
    for pair in pairs:
        spots = []
        for factor in pair:
            known = [k for k, other in enumerate(factors) if other is factor]
            if not known:
                factors.append(factor)
                known = [len(factors) - 1]
            spots.append(known[0])
        places.append(tuple(spots))
    mats = [grad.reshape(lead + (grad.shape[0] // peers, grad.shape[1])) for grad in made]
    slots = 6
    pieces = []
    for mat, kind in zip(mats, "xy"):
        stages = piece_stages(peers, kind)
        place = len(pieces)
        pieces.append({"from": ("mat", place), "stages": stages, "rows": mat.shape[-2:]})
    kinds = KINDS[: len(places)]
    turns = [[2 + k for k in range(3)], [0, 1]]
    turns += [list(range(k, min(k + 3, len(places) + 2))) for k in range(5, len(places) + 2, 3)]
    for k, (pair, kind) in enumerate(zip(places, kinds)):
        x, y = (factors[spot] for spot in pair)
        pieces.append(
            {
                "from": ("made", k % slots),
                "pair": pair,
                "stages": piece_stages(peers, kind),
                "rows": (x.shape[1] // peers, y.shape[1]),
            }
        )
    shapes = [piece_shapes(peers, *piece["rows"], piece["stages"]) for piece in pieces]
    target_shapes = piece_shapes(
        peers, target_part.shape[0] // peers, target_part.shape[1], [1 << k for k in range(free)]
    )
    plan = {
        "mats": len(mats),
        "factors": len(factors),
        "pieces": pieces,
        "shapes": shapes,
        "slots": slots,
        "turns": turns,
        "target_shapes": target_shapes,
        "glob_steps": free,
        "vec_steps": free + 1,
    }
    width = pairs[0][1].shape[1]
    rows = pairs[0][0].shape[1] // peers
    sems = sum(len(stages) for stages in shapes) + len(target_shapes) + 2 * free + 3
    whole = pl.BlockSpec(memory_space=pltpu.VMEM)
    far = pl.BlockSpec(memory_space=pl.ANY)
    sent = sum(grad.size for grad in made) + len(pairs) * rows * peers * width
    outs = pl.pallas_call(
        functools.partial(last_body, peers, plan),
        in_specs=[far] * len(mats) + [whole] * (len(factors) + 3) + [far],
        out_specs=[whole] * (len(pieces) + 3) + [far] * 2,
        out_shape=[jax.ShapeDtypeStruct(stages[-1], jnp.float32) for stages in shapes]
        + [
            jax.ShapeDtypeStruct(target_shapes[-1], jnp.float32),
            jax.ShapeDtypeStruct(glob_part.shape, glob_part.dtype),
            jax.ShapeDtypeStruct(vec_part.shape, vec_part.dtype),
            jax.ShapeDtypeStruct(rim.shape[1:], rim.dtype),
            jax.ShapeDtypeStruct(rim.shape[1:], rim.dtype),
        ],
        scratch_shapes=[
            pltpu.SemaphoreType.DMA((sems,)),
            pltpu.SemaphoreType.DMA((sems,)),
            pltpu.SemaphoreType.DMA((max(len(mats), 1),)),
        ]
        + [pltpu.VMEM(shape, low_type) for stages in shapes for shape in stages]
        + [pltpu.VMEM(shapes[k][0], low_type) for k in range(len(mats))]
        + [pltpu.VMEM(lead + (rows, width), low_type)] * slots
        + [pltpu.VMEM(shape, low_type) for shape in target_shapes]
        + [pltpu.VMEM(glob_part.shape, glob_part.dtype)] * free
        + [pltpu.VMEM(vec_part.shape, vec_part.dtype)] * (free + 1),
        compiler_params=pltpu.CompilerParams(
            collective_id=1, has_side_effects=True, vmem_limit_bytes=62 * 2**20
        ),
        cost_estimate=pl.CostEstimate(flops=sent, bytes_accessed=2 * sent, transcendentals=0),
    )(
        *mats,
        *factors,
        target_part.reshape(lead + (-1, target_part.shape[1])),
        glob_part,
        vec_part,
        rim,
    )
    return outs[: len(pieces)], outs[len(pieces) :]


def place_bits(peers):
    me = lax.axis_index("seq")
    bits = [1 << k for k in reversed(range(peers.bit_length() - 1))]
    return bits, [(me // bit) % 2 for bit in bits]


def block_at(peers, ref, place):
    return ref.at[tuple((place // bit) % 2 for bit in place_bits(peers)[0])]


def chip_copies(peers, refs, sems, k):
    me = lax.axis_index("seq")
    half = peers // 2
    return [
        remote(
            block_at(peers, ref, me),
            block_at(peers, ref, me),
            sems,
            which * peers + k,
            {"seq": lax.rem(me + 2 * k, peers)},
        )
        for which, ref in enumerate(refs)
    ]


def core_copies(peers, refs, sems, k):
    me = lax.axis_index("seq")
    place = lax.rem(me + peers - 2 * k, peers)
    return [
        remote(
            block_at(peers, ref, place),
            block_at(peers, ref, place),
            sems,
            which * peers + peers // 2 + k,
            {"seq": other_of(me, 1)},
        )
        for which, ref in enumerate(refs)
    ]


def reach_out(peers, refs, sems):
    for k in range(1, peers // 2):
        for copy in chip_copies(peers, refs, sems, k):
            copy.start()
    for copy in core_copies(peers, refs, sems, 0):
        copy.start()


def pass_on(peers, refs, sems):
    half = peers // 2
    for k in range(1, half):
        for copy in chip_copies(peers, refs, sems, k):
            copy.wait_recv()
        for copy in core_copies(peers, refs, sems, k):
            copy.start()
    for k in range(half):
        for copy in core_copies(peers, refs, sems, k):
            copy.wait()
    for k in range(1, half):
        for copy in chip_copies(peers, refs, sems, k):
            copy.wait_send()


def gather_body(peers, count, *refs):
    ins, outs, sems = refs[:count], refs[count : 2 * count], refs[2 * count :]
    me = lax.axis_index("seq")
    bits, digits = place_bits(peers)
    greet([{"seq": lax.rem(me + 2 * k, peers)} for k in range(1, peers // 2)] + [{"seq": other_of(me, 1)}])
    for source, target in zip(ins, outs):
        target[tuple(digits)] = source[...]
    reach_out(peers, outs, sems)
    pass_on(peers, outs, sems)


def gather_all(values, number):
    peers = lax.axis_size("seq")
    free = peers.bit_length() - 1
    whole = pl.BlockSpec(memory_space=pltpu.VMEM)
    copies = peers * len(values)
    outs = pl.pallas_call(
        functools.partial(gather_body, peers, len(values)),
        in_specs=[whole] * len(values),
        out_specs=[whole] * len(values),
        out_shape=[
            jax.ShapeDtypeStruct((2,) * free + value.shape, value.dtype) for value in values
        ],
        scratch_shapes=[pltpu.SemaphoreType.DMA((copies,)), pltpu.SemaphoreType.DMA((copies,))],
        compiler_params=pltpu.CompilerParams(
            collective_id=number, has_side_effects=True, vmem_limit_bytes=vmem_bytes
        ),
    )(*values)
    return [out.reshape(-1, value.shape[1]) for out, value in zip(outs, values)]


OWNERS = 4


def everyone(peers):
    me = lax.axis_index("seq")
    return [{"seq": lax.rem(me + k, peers)} for k in range(1, peers)]


def send_in(peers, parts, slots, sems):
    me = lax.axis_index("seq")
    apart = peers // OWNERS
    for o in range(OWNERS):
        for k, (part, slot) in enumerate(zip(parts, slots)):
            copy = pltpu.make_async_remote_copy(
                src_ref=part.at[o],
                dst_ref=slot.at[me],
                send_sem=sems[0].at[k, o],
                recv_sem=sems[1].at[k, me],
                device_id={"seq": o * apart},
                device_id_type=pl.DeviceIdType.MESH,
            )

            @pl.when(me != o * apart)
            def _():
                copy.start()

            @pl.when(me == o * apart)
            def _():
                slot[me] = part[o]


def arrive(peers, parts, slots, sems):
    me = lax.axis_index("seq")
    for j in range(peers):
        for k, (part, slot) in enumerate(zip(parts, slots)):

            @pl.when(me != j)
            def _():
                pltpu.make_async_remote_copy(
                    src_ref=part.at[0],
                    dst_ref=slot.at[j],
                    send_sem=sems[0].at[k, 0],
                    recv_sem=sems[1].at[k, j],
                    device_id={"seq": j},
                    device_id_type=pl.DeviceIdType.MESH,
                ).wait_recv()


def left(peers, parts, slots, sems):
    me = lax.axis_index("seq")
    apart = peers // OWNERS
    for o in range(OWNERS):
        for k, (part, slot) in enumerate(zip(parts, slots)):

            @pl.when(me != o * apart)
            def _():
                pltpu.make_async_remote_copy(
                    src_ref=part.at[o],
                    dst_ref=slot.at[me],
                    send_sem=sems[0].at[k, o],
                    recv_sem=sems[1].at[k, me],
                    device_id={"seq": o * apart},
                    device_id_type=pl.DeviceIdType.MESH,
                ).wait_send()


def out_copies(results, sems, o, j):
    return [
        pltpu.make_async_remote_copy(
            src_ref=result.at[o],
            dst_ref=result.at[o],
            send_sem=sems[2].at[k, j],
            recv_sem=sems[3].at[k, o],
            device_id={"seq": j},
            device_id_type=pl.DeviceIdType.MESH,
        )
        for k, result in enumerate(results)
    ]


def send_out(peers, results, sems):
    me = lax.axis_index("seq")
    apart = peers // OWNERS
    for o in range(OWNERS):
        owner = o * apart

        @pl.when(me == owner)
        def _():
            for j in range(peers):
                if j != owner:
                    for copy in out_copies(results, sems, o, j):
                        copy.start()


def take_out(peers, results, sems):
    me = lax.axis_index("seq")
    apart = peers // OWNERS
    for o in range(OWNERS):
        owner = o * apart

        @pl.when(me != owner)
        def _():
            for copy in out_copies(results, sems, o, owner):
                copy.wait_recv()

        @pl.when(me == owner)
        def _():
            for j in range(peers):
                if j != owner:
                    for copy in out_copies(results, sems, o, j):
                        copy.wait_send()


def owner_sems(peers, count):
    return [
        pltpu.SemaphoreType.DMA((count, OWNERS)),
        pltpu.SemaphoreType.DMA((count, peers)),
        pltpu.SemaphoreType.DMA((count, peers)),
        pltpu.SemaphoreType.DMA((count, OWNERS)),
    ]


def sum_at_owner(peers, part_ref, slot, sum_ref, sems):
    me = lax.axis_index("seq")
    apart = peers // OWNERS
    for o in range(OWNERS):

        @pl.when(me == o * apart)
        def _():
            arrive(peers, [part_ref], [slot], sems)
            total = slot[0].astype(jnp.float32)
            for j in range(1, peers):
                total = total + slot[j].astype(jnp.float32)
            sum_ref[o] = total.astype(low_type)


def begin_body(peers, dec_ref, part_ref, all_ref, glob_ref, slot, send, recv, *sems):
    me = lax.axis_index("seq")
    bits, digits = place_bits(peers)
    apart = peers // OWNERS
    greet(everyone(peers))
    send_in(peers, [part_ref], [slot], sems)
    all_ref[tuple(digits)] = dec_ref[...]
    reach_out(peers, [all_ref], (send, recv))
    sum_at_owner(peers, part_ref, slot, glob_ref, sems)
    send_out(peers, [glob_ref], sems)
    pass_on(peers, [all_ref], (send, recv))
    take_out(peers, [glob_ref], sems)
    left(peers, [part_ref], [slot], sems)


def begin_exchange(dec_x, glob_part):
    peers = lax.axis_size("seq")
    free = peers.bit_length() - 1
    whole = pl.BlockSpec(memory_space=pltpu.VMEM)
    rows = glob_part.shape[0] // OWNERS
    width = dec_x.shape[1]
    dec_all, glob_x = pl.pallas_call(
        functools.partial(begin_body, peers),
        in_specs=[whole] * 2,
        out_specs=[whole] * 2,
        out_shape=[
            jax.ShapeDtypeStruct((2,) * free + dec_x.shape, dec_x.dtype),
            jax.ShapeDtypeStruct((OWNERS, rows, width), low_type),
        ],
        scratch_shapes=[
            pltpu.VMEM((peers, rows, width), low_type),
            pltpu.SemaphoreType.DMA((peers,)),
            pltpu.SemaphoreType.DMA((peers,)),
        ]
        + owner_sems(peers, 1),
        compiler_params=pltpu.CompilerParams(
            collective_id=2, has_side_effects=True, vmem_limit_bytes=vmem_bytes
        ),
    )(dec_x, glob_part.reshape(OWNERS, rows, width))
    return dec_all.reshape(-1, width), glob_x.reshape(-1, width)


def merge_parts(accs, stats):
    tops = [part[:, :SLOT] for part in stats]
    top = functools.reduce(jnp.maximum, tops)
    spread = head_spread()
    total = jnp.zeros_like(top)
    acc = jnp.zeros(accs[0].shape, jnp.float32)
    for part, stat, own_top in zip(accs, stats, tops):
        keep = jnp.exp(own_top - top)
        total = total + stat[:, SLOT : 2 * SLOT] * keep
        acc = acc + part.astype(jnp.float32) * exact_dot(keep, spread)
    return acc, top, total


def finish_parts(acc, top, total):
    lanes = lax.broadcasted_iota(jnp.int32, total.shape, 1)
    total = jnp.where(lanes < HEADS, total, 1.0)
    lse = top + jnp.log(total)
    rest = jnp.zeros((top.shape[0], LANES - SLOT), jnp.float32)
    return acc * exact_dot(1.0 / total, head_spread()), jnp.concatenate([lse, rest], axis=1)


def window_body(
    peers, parts, rows_block, blocks, q_ref, k_ref, v_ref, use_ref, acc_ref, part_ref,
    o_ref, st_ref, out_copy, lse_copy, bias_ref, low_ref, acc_in, st_in, out_ref, lse_ref, *sems
):
    step = pl.program_id(1)
    me = lax.axis_index("seq")
    apart = peers // OWNERS

    @pl.when(step == 0)
    def _():
        greet(everyone(peers))
        low_ref[...] = acc_ref[...].astype(low_type)
        send_in(peers, [low_ref, part_ref], [acc_in, st_in], sems)
        rows = lax.broadcasted_iota(jnp.int32, bias_ref.shape, 0)
        keys = lax.broadcasted_iota(jnp.int32, bias_ref.shape, 1)
        apart_by = rows + HALF - keys
        near = (jnp.abs(apart_by) <= HALF) | (keys >= bias_ref.shape[0] + 2 * HALF)
        bias_ref[...] = jnp.where(near, use_ref[...], masked_score)

    @pl.when(step == 2)
    def _():
        for o in range(OWNERS):

            @pl.when(me == o * apart)
            def _():
                arrive(peers, [low_ref, part_ref], [acc_in, st_in], sems)
                acc, top, total = merge_parts(
                    [acc_in[j] for j in range(peers)], [st_in[j] for j in range(peers)]
                )
                out_ref[o], lse_ref[o] = finish_parts(acc, top, total)

        send_out(peers, [out_ref, lse_ref], sems)

    forward_body(
        parts, rows_block, blocks, True, 1, q_ref, k_ref, v_ref, bias_ref, o_ref, st_ref
    )

    @pl.when(step == PAIRS - 1)
    def _():
        take_out(peers, [out_ref, lse_ref], sems)
        left(peers, [low_ref, part_ref], [acc_in, st_in], sems)
        out_copy[...] = out_ref[...]
        lse_copy[...] = lse_ref[...]


def window_attend(queries, keys, values, use, parts, rows_block, glob_acc, glob_stats):
    peers = lax.axis_size("seq")
    count, width = queries.shape
    key_count = keys.shape[0]
    rows = glob_acc.shape[0] // OWNERS
    flops = 4 * count * key_count * width

    def pair_block(size):
        return pl.BlockSpec((size, LANES), lambda i, p: (0, p))

    def whole(*shape):
        return pl.BlockSpec(shape, lambda i, p: (0,) * len(shape))

    out, stats, glob_out, lse = pl.pallas_call(
        functools.partial(window_body, peers, parts, rows_block, count // rows_block),
        grid=(1, PAIRS),
        in_specs=[
            pair_block(count),
            pair_block(key_count),
            pair_block(key_count),
            whole(1, key_count),
            whole(OWNERS, rows, width),
            whole(OWNERS, rows, LANES),
        ],
        out_specs=[
            pair_block(count),
            whole(count, LANES),
            whole(OWNERS, rows, width),
            whole(OWNERS, rows, LANES),
        ],
        out_shape=[
            jax.ShapeDtypeStruct((count, width), jnp.float32),
            jax.ShapeDtypeStruct((count, LANES), jnp.float32),
            jax.ShapeDtypeStruct((OWNERS, rows, width), jnp.float32),
            jax.ShapeDtypeStruct((OWNERS, rows, LANES), jnp.float32),
        ],
        scratch_shapes=[
            pltpu.VMEM((count, key_count), jnp.float32),
            pltpu.VMEM((OWNERS, rows, width), low_type),
            pltpu.VMEM((peers, rows, width), low_type),
            pltpu.VMEM((peers, rows, LANES), jnp.float32),
            pltpu.VMEM((OWNERS, rows, width), jnp.float32),
            pltpu.VMEM((OWNERS, rows, LANES), jnp.float32),
        ]
        + owner_sems(peers, 2),
        compiler_params=pltpu.CompilerParams(
            collective_id=3, has_side_effects=True, vmem_limit_bytes=vmem_bytes
        ),
        cost_estimate=pl.CostEstimate(
            flops=4 * flops,
            bytes_accessed=2 * (count + 2 * key_count) * width + 4 * count * width,
            transcendentals=count * key_count * HEADS,
        ),
    )(
        queries, keys, values, use,
        glob_acc.reshape(OWNERS, rows, width), glob_stats.reshape(OWNERS, rows, LANES),
    )
    return out, stats, glob_out.reshape(-1, width), lse.reshape(-1, LANES)[:, :SLOT]


def window_back_body(
    peers, parts, rows_block, blocks, q_ref, k_ref, v_ref, d_ref, st_ref, use_ref, part_ref,
    dq_ref, dk_ref, dv_ref, sum_copy, key_sum, val_sum, bias_ref, slot, sum_ref, *sems
):
    step = pl.program_id(0)

    @pl.when(step == 0)
    def _():
        greet(everyone(peers))
        send_in(peers, [part_ref], [slot], sems)
        keys = lax.broadcasted_iota(jnp.int32, bias_ref.shape, 0)
        rows = lax.broadcasted_iota(jnp.int32, bias_ref.shape, 1)
        near = (jnp.abs(rows + HALF - keys) <= HALF) | (keys >= bias_ref.shape[1] + 2 * HALF)
        bias_ref[...] = jnp.where(near, use_ref[...], masked_score)

    @pl.when(step == 1)
    def _():
        sum_at_owner(peers, part_ref, slot, sum_ref, sems)
        send_out(peers, [sum_ref], sems)

    backward_body(
        parts, rows_block, blocks, 1, q_ref, k_ref, v_ref, d_ref, st_ref, bias_ref,
        dq_ref, dk_ref, dv_ref, key_sum, val_sum,
    )

    @pl.when(step == PAIRS - 1)
    def _():
        take_out(peers, [sum_ref], sems)
        left(peers, [part_ref], [slot], sems)
        sum_copy[...] = sum_ref[...]


def window_attend_back(queries, keys, values, grads, stats, use, parts, rows_block, glob_part):
    peers = lax.axis_size("seq")
    count, width = queries.shape
    key_count = keys.shape[0]
    rows = glob_part.shape[0] // OWNERS
    flops = 10 * count * key_count * width

    def pair_block(size):
        return pl.BlockSpec((size, LANES), lambda p, i: (0, p))

    def whole(*shape):
        return pl.BlockSpec(shape, lambda p, i: (0,) * len(shape))

    dq, dk, dv, total = pl.pallas_call(
        functools.partial(window_back_body, peers, parts, rows_block, count // rows_block),
        grid=(PAIRS, 1),
        in_specs=[
            pair_block(count),
            pair_block(key_count),
            pair_block(key_count),
            pair_block(count),
            whole(2 * SLOT, count),
            whole(key_count, 1),
            whole(OWNERS, rows, width),
        ],
        out_specs=[
            pair_block(count),
            pair_block(key_count),
            pair_block(key_count),
            whole(OWNERS, rows, width),
        ],
        out_shape=[
            jax.ShapeDtypeStruct((count, width), jnp.float32),
            jax.ShapeDtypeStruct((key_count, width), low_type),
            jax.ShapeDtypeStruct((key_count, width), low_type),
            jax.ShapeDtypeStruct((OWNERS, rows, width), low_type),
        ],
        scratch_shapes=[
            pltpu.VMEM((key_count, LANES), jnp.float32),
            pltpu.VMEM((key_count, LANES), jnp.float32),
            pltpu.VMEM((key_count, count), jnp.float32),
            pltpu.VMEM((peers, rows, width), low_type),
            pltpu.VMEM((OWNERS, rows, width), low_type),
        ]
        + owner_sems(peers, 1),
        compiler_params=pltpu.CompilerParams(
            collective_id=7, has_side_effects=True, vmem_limit_bytes=vmem_bytes
        ),
        cost_estimate=pl.CostEstimate(
            flops=4 * flops,
            bytes_accessed=2 * (2 * count + 4 * key_count) * width + 4 * count * width,
            transcendentals=count * key_count * HEADS,
        ),
    )(queries, keys, values, grads, stats, use, glob_part.reshape(OWNERS, rows, width))
    return dq, dk, dv, total.reshape(-1, width)


def end_body(counts, *refs):
    shared = refs[: counts[0]]
    (early, source_own, after, before, select, glob,
     target_own, target_sum, flags) = refs[counts[0] : counts[0] + 9]
    outs = refs[counts[0] + 9 :]
    for source, target in zip(shared, outs):
        target[...] = source[...].astype(jnp.float32)
    outs = outs[counts[0] :]
    full = jnp.float32
    start = 0
    for (rows, count), target in zip(counts[1], outs):
        wide = target.shape[1] // count
        for k in range(count):
            target[:, k * wide : (k + 1) * wide] = early[start : start + rows, :].astype(full)
            start += rows
    d_source, d_target = outs[len(counts[1]) :]
    d_target[...] = target_own[...] + target_sum[...]
    has_after = flags[:, :1] > 0
    has_before = flags[:, 1:2] > 0
    total = source_own[...] + dot_left(select[...], glob[...])
    total = total + jnp.where(has_after, after[...].astype(full), 0.0)
    d_source[...] = total + jnp.where(has_before, before[...].astype(full), 0.0)


def end_outputs(shared, early, early_rows, source_parts, target_parts):
    half = early.shape[1]
    shapes = [part.shape for part in shared]
    shapes += [(rows, half * count) for rows, count in early_rows]
    shapes += [source_parts[0].shape, target_parts[0].shape]
    return pl.pallas_call(
        functools.partial(end_body, (len(shared), early_rows)),
        out_shape=[jax.ShapeDtypeStruct(shape, jnp.float32) for shape in shapes],
        compiler_params=pltpu.CompilerParams(vmem_limit_bytes=vmem_bytes),
    )(*shared, early, *source_parts[:5], *target_parts, source_parts[5])


def cross_merge_body(
    peers, acc_ref, st_ref, out_ref, lse_ref, away, acc_one, st_one, low_out, st_out,
    acc_in, st_in, send, recv, send_two, recv_two,
):
    me = lax.axis_index("seq")
    core = me % 2
    pair = me // 2
    half = peers // 2
    mate = {"seq": other_of(me, 1)}
    others = [{"seq": lax.rem(me + 2 * k, peers)} for k in range(1, half)]
    greet([mate] + others)
    for j in range(half):
        away[j] = acc_ref[j, 1 - core].astype(low_type)
    first = [
        remote(away, acc_one, (send, recv), 0, mate),
        remote(st_ref.at[:, 1 - core], st_one, (send, recv), 1, mate),
    ]
    for copy in first:
        copy.start()
    for copy in first:
        copy.wait()
    rest = jnp.zeros((st_one.shape[1], LANES - 2 * SLOT), jnp.float32)

    def join(j):
        acc, top, total = merge_parts(
            [acc_ref[j, core], acc_one[j]], [st_ref[j, core], st_one[j]]
        )
        return acc, jnp.concatenate([top, total, rest], axis=1)

    def ship(k):
        j = lax.rem(pair + k, half)
        target = {"seq": lax.rem(me + 2 * k, peers)}
        copies = []
        for which, (source, slot) in enumerate(((low_out, acc_in), (st_out, st_in))):
            copies.append(
                pltpu.make_async_remote_copy(
                    src_ref=source.at[j],
                    dst_ref=slot.at[half - k],
                    send_sem=send_two.at[which, k],
                    recv_sem=recv_two.at[which, half - k],
                    device_id=target,
                    device_id_type=pl.DeviceIdType.MESH,
                )
            )
        return copies

    for k in range(1, half):
        j = lax.rem(pair + k, half)
        acc, stat = join(j)
        low_out[j] = acc.astype(low_type)
        st_out[j] = stat
        for copy in ship(k):
            copy.start()
    own_acc, own_stat = join(pair)
    for k in range(1, half):
        for copy in ship(k):
            copy.wait()
    acc, top, total = merge_parts(
        [own_acc] + [acc_in[k] for k in range(1, half)],
        [own_stat] + [st_in[k] for k in range(1, half)],
    )
    out_ref[...], lse_ref[...] = finish_parts(acc, top, total)


def cross_merge(acc, stats):
    peers = lax.axis_size("seq")
    half = peers // 2
    rows = acc.shape[0] // peers
    width = acc.shape[1]
    whole = pl.BlockSpec(memory_space=pltpu.VMEM)
    out, lse = pl.pallas_call(
        functools.partial(cross_merge_body, peers),
        in_specs=[whole] * 2,
        out_specs=[whole] * 2,
        out_shape=[
            jax.ShapeDtypeStruct((rows, width), jnp.float32),
            jax.ShapeDtypeStruct((rows, LANES), jnp.float32),
        ],
        scratch_shapes=[
            pltpu.VMEM((half, rows, width), low_type),
            pltpu.VMEM((half, rows, width), low_type),
            pltpu.VMEM((half, rows, LANES), jnp.float32),
            pltpu.VMEM((half, rows, width), low_type),
            pltpu.VMEM((half, rows, LANES), jnp.float32),
            pltpu.VMEM((half, rows, width), low_type),
            pltpu.VMEM((half, rows, LANES), jnp.float32),
            pltpu.SemaphoreType.DMA((2,)),
            pltpu.SemaphoreType.DMA((2,)),
            pltpu.SemaphoreType.DMA((2, half)),
            pltpu.SemaphoreType.DMA((2, half)),
        ],
        compiler_params=pltpu.CompilerParams(
            collective_id=4, has_side_effects=True, vmem_limit_bytes=vmem_bytes
        ),
    )(acc.reshape(half, 2, rows, width), stats.reshape(half, 2, rows, LANES))
    return out, lse[:, :SLOT]


def lay_early(grads):
    peers = lax.axis_size("seq")
    width = min(grad.shape[1] for grad in grads)
    half = width // 2
    dp_count = lax.axis_size("dp")
    parts = [[] for _ in range(dp_count)]
    rows = []
    for grad in grads:
        own = grad.shape[1] // dp_count
        low_grad = grad.astype(low_type).reshape(peers, -1, grad.shape[1])
        for k in range(own // half):
            for d in range(dp_count):
                start = d * own + k * half
                parts[d].append(low_grad[:, :, start : start + half])
        rows.append((low_grad.shape[1], own // half))
    laid = jnp.stack([jnp.concatenate(part, axis=1) for part in parts], axis=1)
    return laid.reshape(-1, half), rows


def share_vectors(total, vectors):
    length = total.shape[1] // lax.axis_size("seq")
    mine = lax.dynamic_slice_in_dim(total, lax.axis_index("seq") * length, length, 1)
    return [mine[k] for k in range(len(vectors))]


def pad_rows(value, count):
    return jnp.pad(value, ((0, count - value.shape[0]), (0, 0)))


def per_device(
    source,
    target,
    cotangent,
    src_len,
    dec_len,
    global_pos,
    enc_query,
    enc_key,
    enc_value,
    glob_query,
    glob_key,
    glob_value,
    enc_out,
    enc_attn_gain,
    enc_attn_shift,
    enc_up,
    enc_down,
    enc_ffn_gain,
    enc_ffn_shift,
    self_query,
    self_key,
    self_value,
    self_out,
    dec_self_gain,
    dec_self_shift,
    cross_query,
    cross_key,
    cross_value,
    cross_out,
    dec_cross_gain,
    dec_cross_shift,
    dec_up,
    dec_down,
    dec_ffn_gain,
    dec_ffn_shift,
):
    full = jnp.float32
    src_x = source[0]
    dec_x = target[0]
    src_count = src_x.shape[0]
    dec_count = dec_x.shape[0]
    seq_index = lax.axis_index("seq")
    peers = lax.axis_size("seq")
    src_limit = src_len[0]
    dec_limit = dec_len[0]
    glob_places = global_pos[0]
    glob_count = glob_places.shape[0]
    src_places = seq_index * src_count + jnp.arange(src_count, dtype=jnp.int32)
    select_glob = glob_places[:, None] == src_places[None, :]
    select_low = select_glob.astype(low_type)
    is_global = jnp.any(select_glob, axis=0)
    spread = head_spread()

    upward = [(i, i + 1) for i in range(peers - 1)]
    downward = [(i + 1, i) for i in range(peers - 1)]
    dec_all, glob_x = begin_exchange(dec_x, dot_plain(select_low, src_x).astype(low_type))
    rim_x, _ = lax.optimization_barrier((src_x, glob_x))
    before = lax.ppermute(rim_x[src_count - HALF :], "seq", upward)
    after = lax.ppermute(rim_x[:HALF], "seq", downward)

    query_loc = (dot_plain(src_x, enc_query) * 0.125).astype(low_type)
    glob_keys_loc = dot_plain(src_x, glob_key).astype(low_type)
    glob_vals_loc = dot_plain(src_x, glob_value).astype(low_type)

    dec_total = dec_all.shape[0]
    dec_start = seq_index * dec_count
    all_dec = jnp.arange(dec_total, dtype=jnp.int32)
    few = dec_total <= 2 * HALF
    row_x = dec_all if few else dec_x
    row_places = all_dec if few else dec_start + jnp.arange(dec_count, dtype=jnp.int32)
    rows_q = (dot_plain(row_x, self_query) * 0.125).astype(low_type)
    self_k = dot_plain(dec_all, self_key).astype(low_type)
    self_v = dot_plain(dec_all, self_value).astype(low_type)
    row_allowed = (all_dec[None, :] <= row_places[:, None]) & (all_dec < dec_limit)[None, :]
    row_bias = jnp.where(row_allowed, 0.0, masked_score)
    row_out, row_stats = attend(
        rows_q, self_k, self_v, row_bias, None, min(row_x.shape[0], 256), True, 2
    )
    row_attn = row_out.astype(low_type)
    row_res = row_x.astype(full) + dot_plain(row_attn, self_out)
    row_first = layer_norm(row_res, dec_self_gain.astype(full), dec_self_shift.astype(full))
    row_cross_q = (dot_plain(row_first.astype(low_type), cross_query) * 0.125).astype(low_type)

    def own_rows(value):
        return lax.dynamic_slice_in_dim(value, dec_start, dec_count, 0) if few else value

    all_cross_q = row_cross_q if few else gather_all([row_cross_q], 6)[0]
    self_q = own_rows(rows_q)
    self_bias = own_rows(row_bias)
    self_out_full = own_rows(row_out)
    self_stats = own_rows(row_stats)
    self_attn = own_rows(row_attn)
    dec_first, dec_first_back = jax.vjp(
        layer_norm, own_rows(row_res), dec_self_gain.astype(full), dec_self_shift.astype(full)
    )
    dec_first_low = dec_first.astype(low_type)

    glob_queries = (dot_plain(glob_x, glob_query) * 0.125).astype(low_type)
    live_bias = jnp.where(src_places < src_limit, 0.0, masked_score)
    glob_acc, glob_stats = attend(
        glob_queries, glob_keys_loc, glob_vals_loc, live_bias[None, :], None, glob_count, False, 6
    )

    x_all = jnp.concatenate([before, src_x, after, glob_x], axis=0)
    keys_all = dot_plain(x_all, enc_key).astype(low_type)
    vals_all = dot_plain(x_all, enc_value).astype(low_type)
    pad_count = src_count + 2 * HALF
    pad_places = seq_index * src_count - HALF + jnp.arange(pad_count, dtype=jnp.int32)
    pad_glob = jnp.any(glob_places[:, None] == pad_places[None, :], axis=0)
    pad_use = (pad_places >= 0) & (pad_places < src_limit) & jnp.logical_not(pad_glob)
    win_use = jnp.concatenate(
        [jnp.where(pad_use, 0.0, masked_score), jnp.zeros((glob_count,), full)]
    )
    rows_block = 256
    reach = rows_block + 2 * HALF
    win_parts = [
        ((block * rows_block, reach), (pad_count, glob_count))
        for block in range(src_count // rows_block)
    ]
    win_out, win_stats, glob_out, glob_lse = window_attend(
        query_loc, keys_all, vals_all, win_use[None, :], win_parts, rows_block, glob_acc, glob_stats
    )
    placed = dot_left(select_low, glob_out.astype(low_type))
    enc_attn = jnp.where(is_global[:, None], placed, win_out).astype(low_type)
    enc_res = src_x.astype(full) + dot_plain(enc_attn, enc_out)
    enc_first, enc_first_back = jax.vjp(
        layer_norm, enc_res, enc_attn_gain.astype(full), enc_attn_shift.astype(full)
    )
    enc_first_low = enc_first.astype(low_type)
    enc_hidden, enc_slope = gelu_pair(dot_plain(enc_first_low, enc_up))
    enc_second = enc_first + dot_plain(enc_hidden, enc_down)
    memory, enc_final_back = jax.vjp(
        layer_norm, enc_second, enc_ffn_gain.astype(full), enc_ffn_shift.astype(full)
    )
    memory_low = memory.astype(low_type)

    cross_k = dot_plain(memory_low, cross_key).astype(low_type)
    cross_v = dot_plain(memory_low, cross_value).astype(low_type)
    cross_out_full, cross_lse = cross_merge(
        *attend(all_cross_q, cross_k, cross_v, live_bias[None, :], None, 256, False, 2)
    )
    cross_attn = cross_out_full.astype(low_type)
    dec_res_two = dec_first + dot_plain(cross_attn, cross_out)
    dec_second, dec_second_back = jax.vjp(
        layer_norm, dec_res_two, dec_cross_gain.astype(full), dec_cross_shift.astype(full)
    )
    dec_second_low = dec_second.astype(low_type)
    dec_hidden, dec_slope = gelu_pair(dot_plain(dec_second_low, dec_up))
    dec_third = dec_second + dot_plain(dec_hidden, dec_down)
    decoded, dec_final_back = jax.vjp(
        layer_norm, dec_third, dec_ffn_gain.astype(full), dec_ffn_shift.astype(full)
    )

    d_third, g_dec_ffn_gain, g_dec_ffn_shift = dec_final_back(cotangent[0].astype(full))
    d_down_low = d_third.astype(low_type)
    d_pre_low = (dot_right(d_down_low, dec_down) * dec_slope.astype(full)).astype(low_type)
    d_second = d_third + dot_right(d_pre_low, dec_up)
    d_res_two, g_dec_cross_gain, g_dec_cross_shift = dec_second_back(d_second)
    d_cross_o = d_res_two.astype(low_type)
    d_cross_attn = dot_right(d_cross_o, cross_out).astype(low_type)
    early = [
        dot_left(dec_second_low, d_pre_low),
        dot_left(dec_hidden, d_down_low),
        dot_left(cross_attn, d_cross_o),
    ]
    early_laid, early_rows = lay_early(early)
    cross_delta = exact_dot(d_cross_attn.astype(full) * cross_out_full, spread.T)
    all_dout, all_stats = gather_all(
        [
            d_cross_attn,
            jnp.concatenate(
                [cross_lse, cross_delta, jnp.zeros((dec_count, LANES - 2 * SLOT), full)], axis=1
            ),
        ],
        5,
    )
    all_dout, early_laid = lax.optimization_barrier((all_dout, early_laid))
    early_mine = lax.psum_scatter(early_laid, ("seq", "dp"), scatter_dimension=0, tiled=True)
    all_stats = all_stats[:, : 2 * SLOT].T
    live_turned = jnp.broadcast_to(live_bias[:, None], (src_count, 512))
    query_parts, ck_low, cv_low = attend_back(
        all_cross_q, cross_k, cross_v, all_dout, all_stats, live_turned, None, 256, 2
    )
    d_memory = dot_right(ck_low, cross_key) + dot_right(cv_low, cross_value)


    cross_held = scatter_step(scatter_start(query_parts), 0)
    d_enc_second, g_enc_ffn_gain, g_enc_ffn_shift = enc_final_back(d_memory)
    d_enc_second, cross_held = lax.optimization_barrier((d_enc_second, cross_held))
    cross_held = scatter_step(cross_held, 1)
    d_enc_down = d_enc_second.astype(low_type)
    d_enc_pre = (dot_right(d_enc_down, enc_down) * enc_slope.astype(full)).astype(low_type)
    d_enc_pre, cross_held = lax.optimization_barrier((d_enc_pre, cross_held))
    cross_held = scatter_step(cross_held, 2)
    d_enc_first = d_enc_second + dot_right(d_enc_pre, enc_up)
    d_enc_first, cross_held = lax.optimization_barrier((d_enc_first, cross_held))
    cross_held = scatter_step(cross_held, 3)
    d_enc_res, g_enc_attn_gain, g_enc_attn_shift = enc_first_back(d_enc_first)
    d_attn_o = d_enc_res.astype(low_type)
    d_attn = dot_right(d_attn_o, enc_out).astype(low_type)
    g_enc_down = dot_left(enc_hidden, d_enc_down)
    g_enc_up = dot_left(enc_first_low, d_enc_pre)

    d_cross_q = scatter_rows(cross_held, 4).astype(low_type) * 0.125
    d_first = d_res_two + dot_right(d_cross_q, cross_query)
    d_res_one, g_dec_self_gain, g_dec_self_shift = dec_first_back(d_first)
    d_self_o = d_res_one.astype(low_type)
    d_self_attn = dot_right(d_self_o, self_out).astype(low_type)
    self_delta = exact_dot(d_self_attn.astype(full) * self_out_full, spread.T)
    wide = max(dec_count, LANES)
    self_pair = jnp.concatenate([self_stats[:, :SLOT], self_delta], axis=1)
    self_query_parts, d_self_k, d_self_v = attend_back(
        pad_rows(self_q, wide),
        self_k,
        self_v,
        pad_rows(d_self_attn, wide),
        pad_rows(self_pair, wide).T,
        pad_rows(self_bias, wide).T,
        None,
        wide,
        6,
    )
    d_self_q = self_query_parts[:dec_count].astype(low_type) * 0.125
    d_target_own = d_res_one + dot_right(d_self_q, self_query)
    d_target_part = dot_right(d_self_k, self_key) + dot_right(d_self_v, self_value)

    d_window = jnp.where(is_global[:, None], jnp.zeros_like(d_attn), d_attn)
    win_delta = exact_dot(d_window.astype(full) * win_out, spread.T)
    win_pair = jnp.concatenate([win_stats[:, :SLOT], win_delta], axis=1).T
    d_query, d_keys_all, d_vals_all, glob_dout = window_attend_back(
        query_loc, keys_all, vals_all, d_window, win_pair, win_use[:, None], win_parts, rows_block,
        dot_plain(select_low, d_attn).astype(low_type),
    )
    d_query_low = d_query.astype(low_type) * 0.125

    wide = max(glob_count, LANES)
    glob_delta = exact_dot(glob_dout.astype(full) * glob_out, spread.T)
    glob_pair = jnp.concatenate([glob_lse, glob_delta], axis=1)
    glob_query_parts, gk_low, gv_low = attend_back(
        pad_rows(glob_queries, wide),
        glob_keys_loc,
        glob_vals_loc,
        pad_rows(glob_dout, wide),
        pad_rows(glob_pair, wide).T,
        live_turned[:, :wide],
        None,
        wide,
        6,
    )
    d_gq = glob_query_parts[:glob_count].astype(low_type) * 0.125

    d_x_all = dot_right(d_keys_all, enc_key) + dot_right(d_vals_all, enc_value)
    rim = jnp.stack([d_x_all[:HALF], d_x_all[HALF + src_count : pad_count]]).astype(low_type)
    d_glob_part = (d_x_all[pad_count:] + dot_right(d_gq, glob_query)).astype(low_type)
    d_source_own = (
        d_enc_res
        + dot_right(d_query_low, enc_query)
        + d_x_all[HALF : HALF + src_count]
        + dot_right(gk_low, glob_key)
        + dot_right(gv_low, glob_value)
    )
    vectors = [
        g_enc_attn_gain,
        g_enc_attn_shift,
        g_enc_ffn_gain,
        g_enc_ffn_shift,
        g_dec_self_gain,
        g_dec_self_shift,
        g_dec_cross_gain,
        g_dec_cross_shift,
        g_dec_ffn_gain,
        g_dec_ffn_shift,
    ]
    vec_part = jnp.concatenate([jnp.stack(vectors), jnp.zeros((6, vectors[0].shape[0]))], axis=0)

    made = [g_enc_up, g_enc_down]
    pairs = [
        (memory_low, ck_low),
        (memory_low, cv_low),
        (enc_attn, d_attn_o),
        (dec_first_low, d_cross_q),
        (self_attn, d_self_o),
        (dec_x, d_self_q),
        (dec_all, d_self_k),
        (dec_all, d_self_v),
        (src_x, d_query_low),
        (x_all, d_keys_all),
        (x_all, d_vals_all),
        (src_x, gk_low),
        (src_x, gv_low),
        (glob_x, d_gq),
    ]
    if (src_x.shape[1] // peers) % 16 == 0:
        shared, (d_target_sum, d_glob_x, vec_sum, from_after, from_before) = last_exchange(
            [grad.astype(low_type) for grad in made], pairs, d_target_part.astype(low_type),
            d_glob_part, vec_part, rim,
        )
    else:
        every = made + [dot_left(*pair) for pair in pairs]
        shared = [share_grads([grad], k % 2 == 0)[0] for k, grad in enumerate(every)]
        d_target_sum = scatter_rows(d_target_part)
        d_glob_x = add_all(d_glob_part)
        vec_sum = add_all(vec_part)
        vec_sum = vec_sum + swap_dp(vec_sum)
        from_after = lax.ppermute(rim[0], "seq", downward)
        from_before = lax.ppermute(rim[1], "seq", upward)
    vectors = share_vectors(vec_sum, vectors)
    early_mine, d_glob_x = lax.optimization_barrier((early_mine, d_glob_x))
    flags = jnp.stack([seq_index < peers - 1, seq_index > 0]).astype(jnp.int32)[None, :]
    (
        s_enc_up, s_enc_down,
        s_cross_key, s_cross_value, s_enc_out, s_cross_query, s_self_out,
        s_self_query, s_self_key, s_self_value,
        s_enc_query, s_enc_key, s_enc_value, s_glob_key, s_glob_value, s_glob_query,
        s_dec_up, s_dec_down, s_cross_out, d_source, d_target,
    ) = end_outputs(
        shared,
        early_mine,
        early_rows,
        (d_source_own, from_after, from_before, select_low, d_glob_x, flags),
        (d_target_own, d_target_sum),
    )
    return (
        decoded.astype(low_type)[None],
        d_source[None],
        d_target[None],
        s_enc_query,
        s_enc_key,
        s_enc_value,
        s_glob_query,
        s_glob_key,
        s_glob_value,
        s_enc_out,
        vectors[0],
        vectors[1],
        s_enc_up,
        s_enc_down,
        vectors[2],
        vectors[3],
        s_self_query,
        s_self_key,
        s_self_value,
        s_self_out,
        vectors[4],
        vectors[5],
        s_cross_query,
        s_cross_key,
        s_cross_value,
        s_cross_out,
        vectors[6],
        vectors[7],
        s_dec_up,
        s_dec_down,
        vectors[8],
        vectors[9],
    )


def solution(mesh):
    rows = P("dp", "seq", None)
    tile = P("seq", "dp")
    part = P("seq")
    layer = (tile,) * 7 + (part,) * 2 + (tile,) * 2 + (part,) * 2
    decoder = (tile,) * 4 + (part,) * 2 + (tile,) * 4 + (part,) * 2 + (tile,) * 2 + (part,) * 2
    return jax.shard_map(
        per_device,
        mesh=mesh,
        in_specs=(rows, rows, rows, P("dp"), P("dp"), P("dp", None)) + (P(),) * 29,
        out_specs=(rows, rows, rows) + layer + decoder,
        check_vma=False,
    )
```

```python
import functools

import jax
import jax.numpy as jnp
import numpy as np
from jax import lax
from jax.experimental import pallas as pl
from jax.experimental.pallas import tpu as pltpu
from jax.sharding import PartitionSpec as P

HEADS = 12
HEAD_DIM = 64
HALF = 512
PAIRS = HEADS // 2
LANES = 2 * HEAD_DIM
SLOT = 16

masked_score = -1e30
eps_norm = 1e-05
low_type = jnp.bfloat16
vmem_bytes = 56 * 2**20


def dot_plain(left, right):
    return jnp.dot(left, right, preferred_element_type=jnp.float32)


def dot_left(left, right):
    return lax.dot_general(
        left, right, (((0,), (0,)), ((), ())), preferred_element_type=jnp.float32
    )


def dot_right(left, right):
    return lax.dot_general(
        left, right, (((1,), (1,)), ((), ())), preferred_element_type=jnp.float32
    )


def exact_dot(left, right):
    return jnp.dot(
        left, right, precision=lax.Precision.HIGHEST, preferred_element_type=jnp.float32
    )


def layer_norm(value, scale_vec, shift_vec):
    average = jnp.mean(value, axis=-1, keepdims=True)
    centred = value - average
    spread = jnp.mean(centred * centred, axis=-1, keepdims=True)
    return centred * lax.rsqrt(spread + eps_norm) * scale_vec + shift_vec


def gelu_pair(value):
    cdf = 0.5 * (1.0 + lax.erf(value * 0.7071067811865476))
    slope = cdf + value * (0.3989422804014327 * jnp.exp(-0.5 * value * value))
    return (value * cdf).astype(low_type), slope.astype(low_type)


def head_spread():
    heads = lax.broadcasted_iota(jnp.int32, (SLOT, HEADS * HEAD_DIM), 0)
    columns = lax.broadcasted_iota(jnp.int32, (SLOT, HEADS * HEAD_DIM), 1)
    return (columns // HEAD_DIM == heads).astype(jnp.float32)


def head_mask(which):
    lanes = lax.broadcasted_iota(jnp.int32, (1, LANES), 1)
    return ((lanes // HEAD_DIM) == which).astype(low_type)


def attend_heads(
    first, group, parts, rows_block, blocks, normalize, q_ref, k_ref, v_ref, bias_ref, o_ref, st_ref
):
    lane = lax.broadcasted_iota(jnp.int32, (1, LANES), 1)
    for block in range(blocks):
        rows = pl.ds(block * rows_block, rows_block)
        stats = st_ref[rows, :]
        for pair in range(group):
            columns = pl.ds(pair * LANES, LANES)
            q_two = q_ref[rows, columns]
            outs = []
            for which in range(2):
                head = first + 2 * pair + which
                q_one = q_two * head_mask(which)
                scores = []
                for start, size in parts[block]:
                    keys = pl.ds(start, size)
                    bias = bias_ref[rows, keys] if bias_ref.shape[0] > 1 else bias_ref[:, keys]
                    scores.append(dot_right(q_one, k_ref[keys, columns]) + bias)
                top = functools.reduce(
                    jnp.maximum, [jnp.max(part, axis=1, keepdims=True) for part in scores]
                )
                total = jnp.zeros((rows_block, 1), jnp.float32)
                mixed = jnp.zeros((rows_block, LANES), jnp.float32)
                for (start, size), part in zip(parts[block], scores):
                    weights = jnp.exp(part - top)
                    total = total + jnp.sum(weights, axis=1, keepdims=True)
                    mixed = mixed + dot_plain(
                        weights.astype(low_type), v_ref[pl.ds(start, size), columns]
                    )
                if normalize:
                    mixed = mixed / total
                    stats = jnp.where(lane == head, top + jnp.log(total), stats)
                else:
                    stats = jnp.where(lane == head, top, stats)
                    stats = jnp.where(lane == head + SLOT, total, stats)
                outs.append(mixed)
            o_ref[rows, columns] = jnp.where(lane < HEAD_DIM, outs[0], outs[1])
        st_ref[rows, :] = stats


def forward_body(
    parts, rows_block, blocks, normalize, group, q_ref, k_ref, v_ref, bias_ref, o_ref, st_ref
):
    first = pl.program_id(1) * (2 * group)

    @pl.when(first == 0)
    def _():
        st_ref[...] = jnp.zeros_like(st_ref)

    attend_heads(
        first, group, parts, rows_block, blocks, normalize, q_ref, k_ref, v_ref, bias_ref,
        o_ref, st_ref,
    )


def attend(queries, keys, values, bias, parts, rows_block, normalize, group=1):
    count, width = queries.shape
    key_count = keys.shape[0]
    big = min(count, 512)
    blocks = big // rows_block
    parts = parts or [((0, key_count),)] * blocks
    bias_rows = bias.shape[0]
    flops = 4 * count * key_count * width
    wide = group * LANES
    return pl.pallas_call(
        functools.partial(forward_body, parts, rows_block, blocks, normalize, group),
        grid=(count // big, PAIRS // group),
        in_specs=[
            pl.BlockSpec((big, wide), lambda i, p: (i, p)),
            pl.BlockSpec((key_count, wide), lambda i, p: (0, p)),
            pl.BlockSpec((key_count, wide), lambda i, p: (0, p)),
            pl.BlockSpec(
                (min(bias_rows, big), key_count), lambda i, p: (i if bias_rows > big else 0, 0)
            ),
        ],
        out_specs=[
            pl.BlockSpec((big, wide), lambda i, p: (i, p)),
            pl.BlockSpec((big, LANES), lambda i, p: (i, 0)),
        ],
        out_shape=[
            jax.ShapeDtypeStruct((count, width), jnp.float32),
            jax.ShapeDtypeStruct((count, LANES), jnp.float32),
        ],
        compiler_params=pltpu.CompilerParams(vmem_limit_bytes=vmem_bytes),
        cost_estimate=pl.CostEstimate(
            flops=4 * flops,
            bytes_accessed=2 * (count + 2 * key_count) * width + 4 * count * width,
            transcendentals=count * key_count * HEADS,
        ),
    )(queries, keys, values, bias)


def back_heads(
    first, group, parts, rows_block, blocks, q_ref, k_ref, v_ref, d_ref, st_ref, bias_ref,
    dq_ref, key_sum, val_sum,
):
    for block in range(blocks):
        rows = pl.ds(block * rows_block, rows_block)
        for pair in range(group):
            columns = pl.ds(pair * LANES, LANES)
            q_two = q_ref[rows, columns]
            d_two = d_ref[rows, columns]
            turned = []
            for which in range(2):
                head = first + 2 * pair + which
                q_one = q_two * head_mask(which)
                d_one = d_two * head_mask(which)
                lse = st_ref[pl.ds(head, 1), rows]
                delta = st_ref[pl.ds(head + SLOT, 1), rows]
                q_grad = jnp.zeros((LANES, rows_block), jnp.float32)
                for start, size in parts[block]:
                    keys = pl.ds(start, size)
                    bias = bias_ref[keys, rows] if bias_ref.shape[1] > 1 else bias_ref[keys, :]
                    k_two = k_ref[keys, columns]
                    scores = dot_right(k_two, q_one) + bias
                    weights = jnp.exp(scores - lse)
                    slopes = dot_right(v_ref[keys, columns], d_one)
                    diffs = (weights * (slopes - delta)).astype(low_type)
                    val_sum[keys, columns] += dot_plain(weights.astype(low_type), d_one)
                    key_sum[keys, columns] += dot_plain(diffs, q_one)
                    q_grad = q_grad + dot_left(k_two, diffs)
                turned.append(q_grad[which * HEAD_DIM : (which + 1) * HEAD_DIM, :])
            dq_ref[rows, columns] = jnp.concatenate(turned, axis=0).T


def backward_body(
    parts, rows_block, blocks, group, q_ref, k_ref, v_ref, d_ref, st_ref, bias_ref,
    dq_ref, dk_ref, dv_ref, key_sum, val_sum,
):
    first = pl.program_id(0) * (2 * group)
    turn = pl.program_id(1)

    @pl.when(turn == 0)
    def _():
        key_sum[...] = jnp.zeros_like(key_sum)
        val_sum[...] = jnp.zeros_like(val_sum)

    back_heads(
        first, group, parts, rows_block, blocks, q_ref, k_ref, v_ref, d_ref, st_ref, bias_ref,
        dq_ref, key_sum, val_sum,
    )

    @pl.when(turn == pl.num_programs(1) - 1)
    def _():
        dk_ref[...] = key_sum[...].astype(low_type)
        dv_ref[...] = val_sum[...].astype(low_type)


def attend_back(queries, keys, values, grads, stats, bias, parts, rows_block, group=1):
    count, width = queries.shape
    key_count = keys.shape[0]
    big = min(count, 512)
    blocks = big // rows_block
    parts = parts or [((0, key_count),)] * blocks
    bias_cols = bias.shape[1]
    flops = 10 * count * key_count * width
    wide = group * LANES
    return pl.pallas_call(
        functools.partial(backward_body, parts, rows_block, blocks, group),
        grid=(PAIRS // group, count // big),
        in_specs=[
            pl.BlockSpec((big, wide), lambda p, i: (i, p)),
            pl.BlockSpec((key_count, wide), lambda p, i: (0, p)),
            pl.BlockSpec((key_count, wide), lambda p, i: (0, p)),
            pl.BlockSpec((big, wide), lambda p, i: (i, p)),
            pl.BlockSpec((2 * SLOT, big), lambda p, i: (0, i)),
            pl.BlockSpec((key_count, min(bias_cols, big)), lambda p, i: (0, 0)),
        ],
        out_specs=[
            pl.BlockSpec((big, wide), lambda p, i: (i, p)),
            pl.BlockSpec((key_count, wide), lambda p, i: (0, p)),
            pl.BlockSpec((key_count, wide), lambda p, i: (0, p)),
        ],
        out_shape=[
            jax.ShapeDtypeStruct((count, width), jnp.float32),
            jax.ShapeDtypeStruct((key_count, width), low_type),
            jax.ShapeDtypeStruct((key_count, width), low_type),
        ],
        scratch_shapes=[
            pltpu.VMEM((key_count, wide), jnp.float32),
            pltpu.VMEM((key_count, wide), jnp.float32),
        ],
        compiler_params=pltpu.CompilerParams(vmem_limit_bytes=vmem_bytes),
        cost_estimate=pl.CostEstimate(
            flops=4 * flops,
            bytes_accessed=2 * (2 * count + 4 * key_count) * width + 4 * count * width,
            transcendentals=count * key_count * HEADS,
        ),
    )(queries, keys, values, grads, stats, bias)


def seq_bits():
    count = lax.axis_size("seq")
    return [1 << k for k in range(count.bit_length() - 1)]


def swap(value, bit):
    pairs = [(i, i ^ bit) for i in range(lax.axis_size("seq"))]
    return jax.tree.map(lambda part: lax.ppermute(part, "seq", pairs), value)


def bit_set(bit):
    return (lax.axis_index("seq") & bit) != 0


def pick_half(value, chosen, axis):
    return lax.dynamic_index_in_dim(value, chosen, axis, keepdims=False)


def other_of(place, bit):
    return place + bit * (1 - 2 * ((place // bit) % 2))


def greet(partners):
    barrier = pltpu.get_barrier_semaphore()
    for partner in partners:
        pl.semaphore_signal(
            barrier, inc=1, device_id=partner, device_id_type=pl.DeviceIdType.MESH
        )
    pl.semaphore_wait(barrier, len(partners))


def remote(src, dst, sems, k, partner):
    return pltpu.make_async_remote_copy(
        src_ref=src,
        dst_ref=dst,
        send_sem=sems[0].at[k],
        recv_sem=sems[1].at[k],
        device_id=partner,
        device_id_type=pl.DeviceIdType.MESH,
    )


def piece_stages(peers, kind):
    bits = [1 << k for k in range(1, peers.bit_length() - 1)]
    if kind == "x":
        return [1, "dp"] + bits
    if kind == "y":
        return [1] + bits[:1] + ["dp"] + bits[1:]
    return [1] + bits[1:] + ["dp"] + bits[:1]


def piece_shapes(peers, rows, width, stages):
    free = peers.bit_length() - 1
    shapes = []
    for stage in stages:
        if stage == "dp":
            width = width // 2
        else:
            free -= 1
        shapes.append((2,) * free + (rows, width))
    return shapes


def bit_axis(peers, stages, s):
    rest = [bit for bit in reversed([1 << k for k in range(peers.bit_length() - 1)])]
    for stage in stages[:s]:
        if stage != "dp":
            rest.remove(stage)
    return rest.index(stages[s])


def last_body(peers, plan, *refs):
    refs = list(refs)

    def take(count):
        result = refs[:count]
        del refs[:count]
        return result

    mats = take(plan["mats"])
    factors = take(plan["factors"])
    target_part, glob_part, vec_part, rim = take(4)
    outs = take(len(plan["pieces"]))
    target_out, glob_out, vec_out, from_after, from_before = take(5)
    send, recv, load = take(3)
    pieces = plan["pieces"]
    held = [take(len(shapes)) for shapes in plan["shapes"]]
    own = take(plan["mats"])
    staging = take(plan["slots"])
    target_held = take(len(plan["target_shapes"]))
    glob_held = take(plan["glob_steps"])
    vec_held = take(plan["vec_steps"])
    me = lax.axis_index("seq")
    mine_dp = lax.axis_index("dp")
    free = peers.bit_length() - 1
    bits = [1 << k for k in range(free)]
    every = slice(None)

    def partner(stage):
        if stage == "dp":
            return {"dp": 1 - mine_dp}
        return {"seq": other_of(me, stage)}

    numbers = {}

    def number(*key):
        return numbers.setdefault(key, len(numbers))

    left_one = {"seq": lax.rem(me + peers - 1, peers)}
    right_one = {"seq": lax.rem(me + 1, peers)}
    greet([partner(stage) for stage in bits + ["dp"]] + [left_one, right_one])
    to_left = remote(rim.at[0], from_after, (send, recv), number("left"), left_one)
    to_right = remote(rim.at[1], from_before, (send, recv), number("right"), right_one)

    def halved(source, stages, s, mine):
        if stages[s] == "dp":
            half = source.shape[-1] // 2
            where = mine_dp if mine else 1 - mine_dp
            start = pl.multiple_of(where * half, LANES)
            return (every,) * (len(source.shape) - 1) + (pl.ds(start, half),)
        digit = (me // stages[s]) % 2
        return (every,) * bit_axis(peers, stages, s) + (digit if mine else 1 - digit,)

    def copies(name, stages, source, buffers, s):
        origin = source if s == 0 else buffers[s - 1]
        view = origin.at[halved(origin, stages, s, False)]
        return remote(view, buffers[s], (send, recv), number(name, s), partner(stages[s]))

    def fold(stages, source, buffers, s, finish):
        origin = source if s == 0 else buffers[s - 1]
        target = buffers[s]
        spot = halved(origin, stages, s, True)
        for place in np.ndindex(*target.shape[:-2]):
            if stages[s] == "dp":
                more = origin[place + spot[-2:]]
            else:
                axis = len(spot) - 1
                more = origin[place[:axis] + spot[-1:] + place[axis:]]
            total = target[place] + more
            if s == len(stages) - 1:
                finish[...] = total.astype(finish.dtype)
            else:
                target[place] = total

    def source_of(p):
        kind, which = pieces[p]["from"]
        return mats[which] if kind == "mat" else staging[which]

    def compute(p):
        x, y = (factors[k] for k in pieces[p]["pair"])
        target = staging[pieces[p]["from"][1]]
        step = x.shape[1] // 2
        for block in range(2):
            product = dot_left(x[:, block * step : (block + 1) * step], y[...])
            target[block] = product.astype(low_type).reshape(target.shape[1:])

    def begin(p, s):
        if s == 0:
            kind, which = pieces[p]["from"]
            if kind == "mat":
                origin = mats[which]
                ours = origin.at[halved(origin, pieces[p]["stages"], 0, True)]
                pltpu.make_async_copy(ours, own[which], load.at[which]).start()
        copies(p, pieces[p]["stages"], source_of(p), held[p], s).start()

    def end(p, s):
        stages = pieces[p]["stages"]
        copies(p, stages, source_of(p), held[p], s).wait()
        kind, which = pieces[p]["from"]
        if s == 0 and kind == "mat":
            origin = mats[which]
            ours = origin.at[halved(origin, pieces[p]["stages"], 0, True)]
            pltpu.make_async_copy(ours, own[which], load.at[which]).wait()
            for place in np.ndindex(*held[p][0].shape[:-2]):
                held[p][0][place] = held[p][0][place] + own[which][place]
        else:
            fold(stages, source_of(p), held[p], s, outs[p])

    target_stages = bits
    vec_stages = bits + ["dp"]

    def small_begin(s):
        if s < len(target_stages):
            copies("t", target_stages, target_part, target_held, s).start()
        if s < len(bits):
            origin = glob_part if s == 0 else glob_out
            remote(
                origin, glob_held[s], (send, recv), number("g", s), partner(bits[s])
            ).start()
        if s < len(vec_stages):
            origin = vec_part if s == 0 else vec_out
            remote(
                origin, vec_held[s], (send, recv), number("v", s), partner(vec_stages[s])
            ).start()

    def small_end(s):
        if s < len(target_stages):
            copies("t", target_stages, target_part, target_held, s).wait()
            fold(target_stages, target_part, target_held, s, target_out)
        if s < len(bits):
            origin = glob_part if s == 0 else glob_out
            remote(
                origin, glob_held[s], (send, recv), number("g", s), partner(bits[s])
            ).wait()
            glob_out[...] = origin[...] + glob_held[s][...]
        if s < len(vec_stages):
            origin = vec_part if s == 0 else vec_out
            remote(
                origin, vec_held[s], (send, recv), number("v", s), partner(vec_stages[s])
            ).wait()
            vec_out[...] = origin[...] + vec_held[s][...]

    turns = plan["turns"]
    count = len(pieces[0]["stages"])

    def open_turn(turn):
        for p in turns[turn]:
            if "pair" in pieces[p]:
                compute(p)
            begin(p, 0)

    for turn in range(min(2, len(turns))):
        open_turn(turn)

    @pl.when(me > 0)
    def _():
        to_left.start()

    @pl.when(me < peers - 1)
    def _():
        to_right.start()

    small_begin(0)
    for now in range(len(turns) + count - 1):
        for age in range(count):
            if not 0 <= now - age < len(turns):
                continue
            for p in turns[now - age]:
                end(p, age)
                if age < count - 1:
                    begin(p, age + 1)
        if 1 <= now <= len(vec_stages):
            small_end(now - 1)
            if now < len(vec_stages):
                small_begin(now)
        if now + 2 < len(turns):
            open_turn(now + 2)

    @pl.when(me > 0)
    def _():
        to_left.wait_send()
        to_right_in = remote(rim.at[1], from_before, (send, recv), number("right"), left_one)
        to_right_in.wait_recv()

    @pl.when(me < peers - 1)
    def _():
        to_right.wait_send()
        to_left_in = remote(rim.at[0], from_after, (send, recv), number("left"), right_one)
        to_left_in.wait_recv()


KINDS = "xyzxyxxyxxyxxy"


def last_exchange(made, pairs, target_part, glob_part, vec_part, rim):
    peers = lax.axis_size("seq")
    free = peers.bit_length() - 1
    lead = (2,) * free
    factors = []
    places = []
    for pair in pairs:
        spots = []
        for factor in pair:
            known = [k for k, other in enumerate(factors) if other is factor]
            if not known:
                factors.append(factor)
                known = [len(factors) - 1]
            spots.append(known[0])
        places.append(tuple(spots))
    mats = [grad.reshape(lead + (grad.shape[0] // peers, grad.shape[1])) for grad in made]
    slots = 6
    pieces = []
    for mat, kind in zip(mats, "xy"):
        stages = piece_stages(peers, kind)
        place = len(pieces)
        pieces.append({"from": ("mat", place), "stages": stages, "rows": mat.shape[-2:]})
    kinds = KINDS[: len(places)]
    turns = [[2 + k for k in range(3)], [0, 1]]
    turns += [list(range(k, min(k + 3, len(places) + 2))) for k in range(5, len(places) + 2, 3)]
    for k, (pair, kind) in enumerate(zip(places, kinds)):
        x, y = (factors[spot] for spot in pair)
        pieces.append(
            {
                "from": ("made", k % slots),
                "pair": pair,
                "stages": piece_stages(peers, kind),
                "rows": (x.shape[1] // peers, y.shape[1]),
            }
        )
    shapes = [piece_shapes(peers, *piece["rows"], piece["stages"]) for piece in pieces]
    target_shapes = piece_shapes(
        peers, target_part.shape[0] // peers, target_part.shape[1], [1 << k for k in range(free)]
    )
    plan = {
        "mats": len(mats),
        "factors": len(factors),
        "pieces": pieces,
        "shapes": shapes,
        "slots": slots,
        "turns": turns,
        "target_shapes": target_shapes,
        "glob_steps": free,
        "vec_steps": free + 1,
    }
    width = pairs[0][1].shape[1]
    rows = pairs[0][0].shape[1] // peers
    sems = sum(len(stages) for stages in shapes) + len(target_shapes) + 2 * free + 3
    whole = pl.BlockSpec(memory_space=pltpu.VMEM)
    far = pl.BlockSpec(memory_space=pl.ANY)
    sent = sum(grad.size for grad in made) + len(pairs) * rows * peers * width
    outs = pl.pallas_call(
        functools.partial(last_body, peers, plan),
        in_specs=[far] * len(mats) + [whole] * (len(factors) + 3) + [far],
        out_specs=[whole] * (len(pieces) + 3) + [far] * 2,
        out_shape=[jax.ShapeDtypeStruct(stages[-1], jnp.float32) for stages in shapes]
        + [
            jax.ShapeDtypeStruct(target_shapes[-1], jnp.float32),
            jax.ShapeDtypeStruct(glob_part.shape, glob_part.dtype),
            jax.ShapeDtypeStruct(vec_part.shape, vec_part.dtype),
            jax.ShapeDtypeStruct(rim.shape[1:], rim.dtype),
            jax.ShapeDtypeStruct(rim.shape[1:], rim.dtype),
        ],
        scratch_shapes=[
            pltpu.SemaphoreType.DMA((sems,)),
            pltpu.SemaphoreType.DMA((sems,)),
            pltpu.SemaphoreType.DMA((max(len(mats), 1),)),
        ]
        + [pltpu.VMEM(shape, low_type) for stages in shapes for shape in stages]
        + [pltpu.VMEM(shapes[k][0], low_type) for k in range(len(mats))]
        + [pltpu.VMEM(lead + (rows, width), low_type)] * slots
        + [pltpu.VMEM(shape, low_type) for shape in target_shapes]
        + [pltpu.VMEM(glob_part.shape, glob_part.dtype)] * free
        + [pltpu.VMEM(vec_part.shape, vec_part.dtype)] * (free + 1),
        compiler_params=pltpu.CompilerParams(
            collective_id=1, has_side_effects=True, vmem_limit_bytes=62 * 2**20
        ),
        cost_estimate=pl.CostEstimate(flops=sent, bytes_accessed=2 * sent, transcendentals=0),
    )(
        *mats,
        *factors,
        target_part.reshape(lead + (-1, target_part.shape[1])),
        glob_part,
        vec_part,
        rim,
    )
    return outs[: len(pieces)], outs[len(pieces) :]


def place_bits(peers):
    me = lax.axis_index("seq")
    bits = [1 << k for k in reversed(range(peers.bit_length() - 1))]
    return bits, [(me // bit) % 2 for bit in bits]


def block_at(peers, ref, place):
    return ref.at[tuple((place // bit) % 2 for bit in place_bits(peers)[0])]


def chip_copies(peers, refs, sems, k):
    me = lax.axis_index("seq")
    half = peers // 2
    return [
        remote(
            block_at(peers, ref, me),
            block_at(peers, ref, me),
            sems,
            which * peers + k,
            {"seq": lax.rem(me + 2 * k, peers)},
        )
        for which, ref in enumerate(refs)
    ]


def core_copies(peers, refs, sems, k):
    me = lax.axis_index("seq")
    place = lax.rem(me + peers - 2 * k, peers)
    return [
        remote(
            block_at(peers, ref, place),
            block_at(peers, ref, place),
            sems,
            which * peers + peers // 2 + k,
            {"seq": other_of(me, 1)},
        )
        for which, ref in enumerate(refs)
    ]


def reach_out(peers, refs, sems):
    for k in range(1, peers // 2):
        for copy in chip_copies(peers, refs, sems, k):
            copy.start()
    for copy in core_copies(peers, refs, sems, 0):
        copy.start()


def pass_on(peers, refs, sems):
    half = peers // 2
    for k in range(1, half):
        for copy in chip_copies(peers, refs, sems, k):
            copy.wait_recv()
        for copy in core_copies(peers, refs, sems, k):
            copy.start()
    for k in range(half):
        for copy in core_copies(peers, refs, sems, k):
            copy.wait()
    for k in range(1, half):
        for copy in chip_copies(peers, refs, sems, k):
            copy.wait_send()


OWNERS = 4


def everyone(peers):
    me = lax.axis_index("seq")
    return [{"seq": lax.rem(me + k, peers)} for k in range(1, peers)]


def send_in(peers, parts, slots, sems):
    me = lax.axis_index("seq")
    apart = peers // OWNERS
    for o in range(OWNERS):
        for k, (part, slot) in enumerate(zip(parts, slots)):
            copy = pltpu.make_async_remote_copy(
                src_ref=part.at[o],
                dst_ref=slot.at[me],
                send_sem=sems[0].at[k, o],
                recv_sem=sems[1].at[k, me],
                device_id={"seq": o * apart},
                device_id_type=pl.DeviceIdType.MESH,
            )

            @pl.when(me != o * apart)
            def _():
                copy.start()

            @pl.when(me == o * apart)
            def _():
                slot[me] = part[o]


def arrive(peers, parts, slots, sems):
    me = lax.axis_index("seq")
    for j in range(peers):
        for k, (part, slot) in enumerate(zip(parts, slots)):

            @pl.when(me != j)
            def _():
                pltpu.make_async_remote_copy(
                    src_ref=part.at[0],
                    dst_ref=slot.at[j],
                    send_sem=sems[0].at[k, 0],
                    recv_sem=sems[1].at[k, j],
                    device_id={"seq": j},
                    device_id_type=pl.DeviceIdType.MESH,
                ).wait_recv()


def left(peers, parts, slots, sems):
    me = lax.axis_index("seq")
    apart = peers // OWNERS
    for o in range(OWNERS):
        for k, (part, slot) in enumerate(zip(parts, slots)):

            @pl.when(me != o * apart)
            def _():
                pltpu.make_async_remote_copy(
                    src_ref=part.at[o],
                    dst_ref=slot.at[me],
                    send_sem=sems[0].at[k, o],
                    recv_sem=sems[1].at[k, me],
                    device_id={"seq": o * apart},
                    device_id_type=pl.DeviceIdType.MESH,
                ).wait_send()


def out_copies(results, sems, o, j):
    return [
        pltpu.make_async_remote_copy(
            src_ref=result.at[o],
            dst_ref=result.at[o],
            send_sem=sems[2].at[k, j],
            recv_sem=sems[3].at[k, o],
            device_id={"seq": j},
            device_id_type=pl.DeviceIdType.MESH,
        )
        for k, result in enumerate(results)
    ]


def send_out(peers, results, sems):
    me = lax.axis_index("seq")
    apart = peers // OWNERS
    for o in range(OWNERS):
        owner = o * apart

        @pl.when(me == owner)
        def _():
            for j in range(peers):
                if j != owner:
                    for copy in out_copies(results, sems, o, j):
                        copy.start()


def take_out(peers, results, sems):
    me = lax.axis_index("seq")
    apart = peers // OWNERS
    for o in range(OWNERS):
        owner = o * apart

        @pl.when(me != owner)
        def _():
            for copy in out_copies(results, sems, o, owner):
                copy.wait_recv()

        @pl.when(me == owner)
        def _():
            for j in range(peers):
                if j != owner:
                    for copy in out_copies(results, sems, o, j):
                        copy.wait_send()


def owner_sems(peers, count):
    return [
        pltpu.SemaphoreType.DMA((count, OWNERS)),
        pltpu.SemaphoreType.DMA((count, peers)),
        pltpu.SemaphoreType.DMA((count, peers)),
        pltpu.SemaphoreType.DMA((count, OWNERS)),
    ]


def sum_at_owner(peers, part_ref, slot, sum_ref, sems):
    me = lax.axis_index("seq")
    apart = peers // OWNERS
    for o in range(OWNERS):

        @pl.when(me == o * apart)
        def _():
            arrive(peers, [part_ref], [slot], sems)
            total = slot[0].astype(jnp.float32)
            for j in range(1, peers):
                total = total + slot[j].astype(jnp.float32)
            sum_ref[o] = total.astype(low_type)


def expand_heads(stat):
    lane = lax.broadcasted_iota(jnp.int32, (1, LANES), 1)
    return jnp.concatenate(
        [
            jnp.where(lane < HEAD_DIM, stat[:, 2 * p : 2 * p + 1], stat[:, 2 * p + 1 : 2 * p + 2])
            for p in range(PAIRS)
        ],
        axis=1,
    )


def merge_parts(accs, stats):
    tops = [part[:, :SLOT] for part in stats]
    top = functools.reduce(jnp.maximum, tops)
    total = jnp.zeros_like(top)
    acc = jnp.zeros(accs[0].shape, jnp.float32)
    for part, stat, own_top in zip(accs, stats, tops):
        keep = jnp.exp(own_top - top)
        total = total + stat[:, SLOT : 2 * SLOT] * keep
        acc = acc + part.astype(jnp.float32) * expand_heads(keep)
    return acc, top, total


def finish_parts(acc, top, total):
    lanes = lax.broadcasted_iota(jnp.int32, total.shape, 1)
    total = jnp.where(lanes < HEADS, total, 1.0)
    lse = top + jnp.log(total)
    rest = jnp.zeros((top.shape[0], LANES - SLOT), jnp.float32)
    return acc * expand_heads(1.0 / total), jnp.concatenate([lse, rest], axis=1)


def window_body(
    peers, parts, rows_block, blocks, q_ref, k_ref, v_ref, use_ref, acc_ref, part_ref,
    o_ref, st_ref, out_copy, lse_copy, bias_ref, low_ref, acc_in, st_in, out_ref, lse_ref, *sems
):
    step = pl.program_id(1)
    me = lax.axis_index("seq")
    apart = peers // OWNERS

    @pl.when(step == 0)
    def _():
        greet(everyone(peers))
        low_ref[...] = acc_ref[...].astype(low_type)
        send_in(peers, [low_ref, part_ref], [acc_in, st_in], sems)
        rows = lax.broadcasted_iota(jnp.int32, bias_ref.shape, 0)
        keys = lax.broadcasted_iota(jnp.int32, bias_ref.shape, 1)
        apart_by = rows + HALF - keys
        near = (jnp.abs(apart_by) <= HALF) | (keys >= bias_ref.shape[0] + 2 * HALF)
        bias_ref[...] = jnp.where(near, use_ref[...], masked_score)

    @pl.when(step == 2)
    def _():
        for o in range(OWNERS):

            @pl.when(me == o * apart)
            def _():
                arrive(peers, [low_ref, part_ref], [acc_in, st_in], sems)
                acc, top, total = merge_parts(
                    [acc_in[j] for j in range(peers)], [st_in[j] for j in range(peers)]
                )
                out_ref[o], lse_ref[o] = finish_parts(acc, top, total)

        send_out(peers, [out_ref, lse_ref], sems)

    forward_body(
        parts, rows_block, blocks, True, 1, q_ref, k_ref, v_ref, bias_ref, o_ref, st_ref
    )

    @pl.when(step == PAIRS - 1)
    def _():
        take_out(peers, [out_ref, lse_ref], sems)
        left(peers, [low_ref, part_ref], [acc_in, st_in], sems)
        out_copy[...] = out_ref[...]
        lse_copy[...] = lse_ref[...]


def window_attend(queries, keys, values, use, parts, rows_block, glob_acc, glob_stats):
    peers = lax.axis_size("seq")
    count, width = queries.shape
    key_count = keys.shape[0]
    rows = glob_acc.shape[0] // OWNERS
    flops = 4 * count * key_count * width

    def pair_block(size):
        return pl.BlockSpec((size, LANES), lambda i, p: (0, p))

    def whole(*shape):
        return pl.BlockSpec(shape, lambda i, p: (0,) * len(shape))

    out, stats, glob_out, lse = pl.pallas_call(
        functools.partial(window_body, peers, parts, rows_block, count // rows_block),
        grid=(1, PAIRS),
        in_specs=[
            pair_block(count),
            pair_block(key_count),
            pair_block(key_count),
            whole(1, key_count),
            whole(OWNERS, rows, width),
            whole(OWNERS, rows, LANES),
        ],
        out_specs=[
            pair_block(count),
            whole(count, LANES),
            whole(OWNERS, rows, width),
            whole(OWNERS, rows, LANES),
        ],
        out_shape=[
            jax.ShapeDtypeStruct((count, width), jnp.float32),
            jax.ShapeDtypeStruct((count, LANES), jnp.float32),
            jax.ShapeDtypeStruct((OWNERS, rows, width), jnp.float32),
            jax.ShapeDtypeStruct((OWNERS, rows, LANES), jnp.float32),
        ],
        scratch_shapes=[
            pltpu.VMEM((count, key_count), jnp.float32),
            pltpu.VMEM((OWNERS, rows, width), low_type),
            pltpu.VMEM((peers, rows, width), low_type),
            pltpu.VMEM((peers, rows, LANES), jnp.float32),
            pltpu.VMEM((OWNERS, rows, width), jnp.float32),
            pltpu.VMEM((OWNERS, rows, LANES), jnp.float32),
        ]
        + owner_sems(peers, 2),
        compiler_params=pltpu.CompilerParams(
            collective_id=3, has_side_effects=True, vmem_limit_bytes=vmem_bytes
        ),
        cost_estimate=pl.CostEstimate(
            flops=4 * flops,
            bytes_accessed=2 * (count + 2 * key_count) * width + 4 * count * width,
            transcendentals=count * key_count * HEADS,
        ),
    )(
        queries, keys, values, use,
        glob_acc.reshape(OWNERS, rows, width), glob_stats.reshape(OWNERS, rows, LANES),
    )
    return out, stats, glob_out.reshape(-1, width), lse.reshape(-1, LANES)


def window_back_body(
    peers, parts, rows_block, blocks, q_ref, k_ref, v_ref, d_ref, st_ref, use_ref, part_ref,
    dq_ref, dk_ref, dv_ref, sum_copy, key_sum, val_sum, bias_ref, slot, sum_ref, *sems
):
    step = pl.program_id(0)

    @pl.when(step == 0)
    def _():
        greet(everyone(peers))
        send_in(peers, [part_ref], [slot], sems)
        keys = lax.broadcasted_iota(jnp.int32, bias_ref.shape, 0)
        rows = lax.broadcasted_iota(jnp.int32, bias_ref.shape, 1)
        near = (jnp.abs(rows + HALF - keys) <= HALF) | (keys >= bias_ref.shape[1] + 2 * HALF)
        bias_ref[...] = jnp.where(near, use_ref[...], masked_score)

    @pl.when(step == 1)
    def _():
        sum_at_owner(peers, part_ref, slot, sum_ref, sems)
        send_out(peers, [sum_ref], sems)

    backward_body(
        parts, rows_block, blocks, 1, q_ref, k_ref, v_ref, d_ref, st_ref, bias_ref,
        dq_ref, dk_ref, dv_ref, key_sum, val_sum,
    )

    @pl.when(step == PAIRS - 1)
    def _():
        take_out(peers, [sum_ref], sems)
        left(peers, [part_ref], [slot], sems)
        sum_copy[...] = sum_ref[...]


def window_attend_back(queries, keys, values, grads, stats, use, parts, rows_block, glob_part):
    peers = lax.axis_size("seq")
    count, width = queries.shape
    key_count = keys.shape[0]
    rows = glob_part.shape[0] // OWNERS
    flops = 10 * count * key_count * width

    def pair_block(size):
        return pl.BlockSpec((size, LANES), lambda p, i: (0, p))

    def whole(*shape):
        return pl.BlockSpec(shape, lambda p, i: (0,) * len(shape))

    dq, dk, dv, total = pl.pallas_call(
        functools.partial(window_back_body, peers, parts, rows_block, count // rows_block),
        grid=(PAIRS, 1),
        in_specs=[
            pair_block(count),
            pair_block(key_count),
            pair_block(key_count),
            pair_block(count),
            whole(2 * SLOT, count),
            whole(key_count, 1),
            whole(OWNERS, rows, width),
        ],
        out_specs=[
            pair_block(count),
            pair_block(key_count),
            pair_block(key_count),
            whole(OWNERS, rows, width),
        ],
        out_shape=[
            jax.ShapeDtypeStruct((count, width), jnp.float32),
            jax.ShapeDtypeStruct((key_count, width), low_type),
            jax.ShapeDtypeStruct((key_count, width), low_type),
            jax.ShapeDtypeStruct((OWNERS, rows, width), low_type),
        ],
        scratch_shapes=[
            pltpu.VMEM((key_count, LANES), jnp.float32),
            pltpu.VMEM((key_count, LANES), jnp.float32),
            pltpu.VMEM((key_count, count), jnp.float32),
            pltpu.VMEM((peers, rows, width), low_type),
            pltpu.VMEM((OWNERS, rows, width), low_type),
        ]
        + owner_sems(peers, 1),
        compiler_params=pltpu.CompilerParams(
            collective_id=7, has_side_effects=True, vmem_limit_bytes=vmem_bytes
        ),
        cost_estimate=pl.CostEstimate(
            flops=4 * flops,
            bytes_accessed=2 * (2 * count + 4 * key_count) * width + 4 * count * width,
            transcendentals=count * key_count * HEADS,
        ),
    )(queries, keys, values, grads, stats, use, glob_part.reshape(OWNERS, rows, width))
    return dq, dk, dv, total.reshape(-1, width)


def end_body(counts, *refs):
    shared = refs[: counts[0]]
    (early, source_own, after, before, select, glob,
     target_own, target_sum, flags) = refs[counts[0] : counts[0] + 9]
    outs = refs[counts[0] + 9 :]
    for source, target in zip(shared, outs):
        target[...] = source[...].astype(jnp.float32)
    outs = outs[counts[0] :]
    full = jnp.float32
    start = 0
    for (rows, count), target in zip(counts[1], outs):
        wide = target.shape[1] // count
        for k in range(count):
            target[:, k * wide : (k + 1) * wide] = early[start : start + rows, :].astype(full)
            start += rows
    d_source, d_target = outs[len(counts[1]) :]
    d_target[...] = target_own[...] + target_sum[...]
    has_after = flags[:, :1] > 0
    has_before = flags[:, 1:2] > 0
    total = source_own[...] + dot_left(select[...], glob[...])
    total = total + jnp.where(has_after, after[...].astype(full), 0.0)
    d_source[...] = total + jnp.where(has_before, before[...].astype(full), 0.0)


def end_outputs(shared, early, early_rows, source_parts, target_parts):
    half = early.shape[1]
    shapes = [part.shape for part in shared]
    shapes += [(rows, half * count) for rows, count in early_rows]
    shapes += [source_parts[0].shape, target_parts[0].shape]
    return pl.pallas_call(
        functools.partial(end_body, (len(shared), early_rows)),
        out_shape=[jax.ShapeDtypeStruct(shape, jnp.float32) for shape in shapes],
        compiler_params=pltpu.CompilerParams(vmem_limit_bytes=vmem_bytes),
    )(*shared, early, *source_parts[:5], *target_parts, source_parts[5])


def share_vectors(total, count):
    length = total.shape[1] // lax.axis_size("seq")
    mine = lax.dynamic_slice_in_dim(total, lax.axis_index("seq") * length, length, 1)
    return [mine[k] for k in range(count)]


def pad_rows(value, count):
    return jnp.pad(value, ((0, count - value.shape[0]), (0, 0)))


def ln_parts(value):
    average = jnp.mean(value, axis=-1, keepdims=True)
    centred = value - average
    spread = jnp.mean(centred * centred, axis=-1, keepdims=True)
    rate = lax.rsqrt(spread + eps_norm)
    return centred * rate, rate


def ln_back(grad, unit, rate, gain):
    scaled = grad * gain
    pull = jnp.mean(scaled, axis=-1, keepdims=True)
    twist = jnp.mean(scaled * unit, axis=-1, keepdims=True)
    return (
        rate * (scaled - pull - unit * twist),
        jnp.sum(grad * unit, axis=0, keepdims=True),
        jnp.sum(grad, axis=0, keepdims=True),
    )


def call_whole(body, inputs, shapes, scratch=(), **params):
    whole = pl.BlockSpec(memory_space=pltpu.VMEM)
    return pl.pallas_call(
        body,
        in_specs=[whole] * len(inputs),
        out_specs=[whole] * len(shapes),
        out_shape=[jax.ShapeDtypeStruct(shape, kind) for shape, kind in shapes],
        scratch_shapes=list(scratch),
        compiler_params=pltpu.CompilerParams(vmem_limit_bytes=vmem_bytes, **params),
    )(*inputs)


ENC_ATTN, ENC_FFN, DEC_SELF, DEC_CROSS, DEC_FFN = 0, 2, 4, 6, 8


def scale_shift(norms, which):
    return norms[which : which + 1, :], norms[which + 1 : which + 2, :]


def start_body(
    peers, dec_ref, part_ref, x_ref, wq, wgk, wgv, all_ref, glob_ref, q_ref, gk_ref, gv_ref,
    slot, send, recv, *sems
):
    bits, digits = place_bits(peers)
    greet(everyone(peers))
    send_in(peers, [part_ref], [slot], sems)
    all_ref[tuple(digits)] = dec_ref[...]
    reach_out(peers, [all_ref], (send, recv))
    x = x_ref[...]
    gk_ref[...] = dot_plain(x, wgk[...]).astype(low_type)
    sum_at_owner(peers, part_ref, slot, glob_ref, sems)
    send_out(peers, [glob_ref], sems)
    q_ref[...] = (dot_plain(x, wq[...]) * 0.125).astype(low_type)
    pass_on(peers, [all_ref], (send, recv))
    gv_ref[...] = dot_plain(x, wgv[...]).astype(low_type)
    take_out(peers, [glob_ref], sems)
    left(peers, [part_ref], [slot], sems)


def start_exchange(dec_x, glob_part, src_x, weights):
    peers = lax.axis_size("seq")
    free = peers.bit_length() - 1
    rows = glob_part.shape[0] // OWNERS
    width = dec_x.shape[1]
    dec_all, glob_x, q, gk, gv = call_whole(
        functools.partial(start_body, peers),
        [dec_x, glob_part.reshape(OWNERS, rows, width), src_x, *weights],
        [((2,) * free + dec_x.shape, dec_x.dtype), ((OWNERS, rows, width), low_type)]
        + [(src_x.shape, low_type)] * 3,
        [
            pltpu.VMEM((peers, rows, width), low_type),
            pltpu.SemaphoreType.DMA((peers,)),
            pltpu.SemaphoreType.DMA((peers,)),
        ]
        + owner_sems(peers, 1),
        collective_id=2,
        has_side_effects=True,
    )
    return dec_all.reshape(-1, width), glob_x.reshape(-1, width), q, gk, gv


def project_body(*refs):
    sources = refs[:4]
    wk, wv, x_all, k_all, v_all = refs[4:]
    start = 0
    for source in sources:
        rows = pl.ds(start, source.shape[0])
        x = source[...]
        x_all[rows, :] = x
        k_all[rows, :] = dot_plain(x, wk[...]).astype(low_type)
        v_all[rows, :] = dot_plain(x, wv[...]).astype(low_type)
        start += source.shape[0]


def project_all(sources, wk, wv):
    total = sum(source.shape[0] for source in sources)
    return call_whole(
        project_body, [*sources, wk, wv], [((total, sources[0].shape[1]), low_type)] * 3
    )


def dec_front_body(
    limit_ref, x_ref, wq, wk, wv, wo, wcq, norms, k_ref, v_ref, cq_ref, q_own, out_own, attn_own,
    st_own, first_own, unit_own, rate_own, q_ref, o_ref, st_ref, bias_ref,
):
    x = x_ref[...]
    count = x.shape[0]
    half = count // 2
    q_ref[...] = (dot_plain(x, wq[...]) * 0.125).astype(low_type)
    k_ref[...] = dot_plain(x, wk[...]).astype(low_type)
    v_ref[...] = dot_plain(x, wv[...]).astype(low_type)
    rows = lax.broadcasted_iota(jnp.int32, (count, count), 0)
    keys = lax.broadcasted_iota(jnp.int32, (count, count), 1)
    bias_ref[...] = jnp.where((keys <= rows) & (keys < limit_ref[0]), 0.0, masked_score)
    st_ref[...] = jnp.zeros_like(st_ref)
    attend_heads(
        0, PAIRS, [((0, half),), ((0, count),)], half, 2, True, q_ref, k_ref, v_ref, bias_ref,
        o_ref, st_ref,
    )
    gain, shift = scale_shift(norms, DEC_SELF)
    res = x.astype(jnp.float32) + dot_plain(o_ref[...].astype(low_type), wo[...])
    unit, _ = ln_parts(res)
    first = unit * gain + shift
    cq_ref[...] = (dot_plain(first.astype(low_type), wcq[...]) * 0.125).astype(low_type)
    mine = q_own.shape[0]
    start = pl.multiple_of(lax.axis_index("seq") * mine, mine)
    own = pl.ds(start, mine)
    q_own[...] = q_ref[own, :]
    out_own[...] = o_ref[own, :]
    attn = o_ref[own, :].astype(low_type)
    attn_own[...] = attn
    st_own[...] = st_ref[own, :]
    res_own = x_ref[own, :].astype(jnp.float32) + dot_plain(attn, wo[...])
    unit, rate = ln_parts(res_own)
    unit_own[...] = unit
    rate_own[...] = rate
    first_own[...] = unit * gain + shift


def dec_front(limit, dec_all, weights, norms, mine):
    count, width = dec_all.shape
    full = jnp.float32
    whole = pl.BlockSpec(memory_space=pltpu.VMEM)
    shapes = [
        ((count, width), low_type),
        ((count, width), low_type),
        ((count, width), low_type),
        ((mine, width), low_type),
        ((mine, width), full),
        ((mine, width), low_type),
        ((mine, LANES), full),
        ((mine, width), full),
        ((mine, width), full),
        ((mine, 1), full),
    ]
    return pl.pallas_call(
        dec_front_body,
        in_specs=[pl.BlockSpec(memory_space=pltpu.SMEM)] + [whole] * 7,
        out_specs=[whole] * len(shapes),
        out_shape=[jax.ShapeDtypeStruct(shape, kind) for shape, kind in shapes],
        scratch_shapes=[
            pltpu.VMEM((count, width), low_type),
            pltpu.VMEM((count, width), full),
            pltpu.VMEM((count, LANES), full),
            pltpu.VMEM((count, count), full),
        ],
        compiler_params=pltpu.CompilerParams(vmem_limit_bytes=vmem_bytes),
    )(limit, dec_all, *weights, norms)


def enc_front_body(
    win_ref, keep_ref, select, glob, x_ref, wo, wu, wd, wck, wcv, norms, attn_ref, unit_one,
    rate_one, low_one, hidden_ref, slope_ref, unit_two, rate_two, low_two, ck_ref, cv_ref,
):
    rows_block = x_ref.shape[0] // 2
    width = x_ref.shape[1]
    for block in range(2):
        rows = pl.ds(block * rows_block, rows_block)
        placed = dot_left(select[:, block * rows_block : (block + 1) * rows_block], glob[...])
        attn = jnp.where(keep_ref[rows, :] > 0, win_ref[rows, :], placed).astype(low_type)
        attn_ref[rows, :] = attn
        unit, rate = ln_parts(x_ref[rows, :].astype(jnp.float32) + dot_plain(attn, wo[...]))
        unit_one[rows, :] = unit
        rate_one[rows, :] = rate
        gain, shift = scale_shift(norms, ENC_ATTN)
        second = unit * gain + shift
        first = second.astype(low_type)
        low_one[rows, :] = first
        for k in range(wu.shape[1] // width):
            columns = pl.ds(k * width, width)
            hidden, slope = gelu_pair(dot_plain(first, wu[:, columns]))
            hidden_ref[rows, columns] = hidden
            slope_ref[rows, columns] = slope
            second = second + dot_plain(hidden, wd[columns, :])
        unit, rate = ln_parts(second)
        unit_two[rows, :] = unit
        rate_two[rows, :] = rate
        gain, shift = scale_shift(norms, ENC_FFN)
        memory = (unit * gain + shift).astype(low_type)
        low_two[rows, :] = memory
        ck_ref[rows, :] = dot_plain(memory, wck[...]).astype(low_type)
        cv_ref[rows, :] = dot_plain(memory, wcv[...]).astype(low_type)


def enc_front(win_out, keep, select, glob, x, weights, norms):
    count, width = x.shape
    wide = weights[1].shape[1]
    full = jnp.float32
    narrow = (count, width)
    return call_whole(
        enc_front_body,
        [win_out, keep, select, glob, x, *weights, norms],
        [
            (narrow, low_type),
            (narrow, full),
            ((count, 1), full),
            (narrow, low_type),
            ((count, wide), low_type),
            ((count, wide), low_type),
            (narrow, full),
            ((count, 1), full),
            (narrow, low_type),
            (narrow, low_type),
            (narrow, low_type),
        ],
    )


def row_sum_steps(peers, whole_ref, out_ref, buffers, send, recv):
    me = lax.axis_index("seq")
    free = peers.bit_length() - 1
    every = slice(None)
    sends, takes, helds = buffers[:free], buffers[free : 2 * free], buffers[2 * free :]

    def source(k):
        return whole_ref if k == 0 else helds[k - 1]

    def copy(k):
        return remote(sends[k], takes[k], (send, recv), k, {"seq": other_of(me, 1 << k)})

    def begin(k):
        digit = (me // (1 << k)) % 2
        lead = (every,) * (free - 1 - k)
        sends[k][...] = source(k)[lead + (1 - digit,)].astype(low_type)
        copy(k).start()

    def end(k):
        copy(k).wait()
        digit = (me // (1 << k)) % 2
        lead = (every,) * (free - 1 - k)
        total = source(k)[lead + (digit,)] + takes[k][...].astype(jnp.float32)
        target = out_ref if k == free - 1 else helds[k]
        target[...] = total

    def step(k):
        if k > 0:
            end(k - 1)
        if k < free:
            begin(k)

    return [functools.partial(step, k) for k in range(free + 1)]


def enc_back_body(
    peers, parts_ref, dck, dcv, unit_two, rate_two, slope_ref, unit_one, rate_one, win_ref, keep_ref, select,
    wck, wcv, wd, wu, wo, norms, down_ref, pre_ref, res_ref, out_ref, window_ref, delta_ref,
    glob_ref, vec_ref, sum_ref, send, recv, *buffers
):
    me = lax.axis_index("seq")
    free = peers.bit_length() - 1
    greet([{"seq": other_of(me, 1 << k)} for k in range(free)])
    steps = row_sum_steps(peers, parts_ref, sum_ref, buffers, send, recv)
    steps[0]()
    rows_block = dck.shape[0] // 2
    width = dck.shape[1]
    vec_ref[...] = jnp.zeros_like(vec_ref)
    glob = jnp.zeros(glob_ref.shape, jnp.float32)
    for block in range(2):
        rows = pl.ds(block * rows_block, rows_block)
        d_memory = dot_right(dck[rows, :], wck[...]) + dot_right(dcv[rows, :], wcv[...])
        gain, _ = scale_shift(norms, ENC_FFN)
        d_second, d_gain, d_shift = ln_back(d_memory, unit_two[rows, :], rate_two[rows, :], gain)
        vec_ref[2:3, :] += d_gain
        vec_ref[3:4, :] += d_shift
        d_down = d_second.astype(low_type)
        down_ref[rows, :] = d_down
        steps[2 * block + 1]()
        for k in range(wu.shape[1] // width):
            columns = pl.ds(k * width, width)
            d_hidden = dot_right(d_down, wd[columns, :])
            d_pre = (d_hidden * slope_ref[rows, columns].astype(jnp.float32)).astype(low_type)
            pre_ref[rows, columns] = d_pre
            d_second = d_second + dot_right(d_pre, wu[:, columns])
        gain, _ = scale_shift(norms, ENC_ATTN)
        d_res, d_gain, d_shift = ln_back(d_second, unit_one[rows, :], rate_one[rows, :], gain)
        vec_ref[0:1, :] += d_gain
        vec_ref[1:2, :] += d_shift
        res_ref[rows, :] = d_res
        d_out = d_res.astype(low_type)
        out_ref[rows, :] = d_out
        d_attn = dot_right(d_out, wo[...]).astype(low_type)
        glob = glob + dot_plain(
            select[:, block * rows_block : (block + 1) * rows_block], d_attn
        )
        d_window = jnp.where(keep_ref[rows, :] > 0, d_attn.astype(jnp.float32), 0.0)
        window_ref[rows, :] = d_window.astype(low_type)
        delta_ref[rows, :] = head_sums(d_window * win_ref[rows, :])
        steps[2 * block + 2]()
    for step in steps[5:]:
        step()
    glob_ref[...] = glob.astype(low_type)


def head_sums(value):
    lane = lax.broadcasted_iota(jnp.int32, (1, LANES), 1)
    result = jnp.zeros((value.shape[0], LANES), jnp.float32)
    for pair in range(PAIRS):
        two = value[:, pair * LANES : (pair + 1) * LANES]
        for which in range(2):
            inside = (lane // HEAD_DIM) == which
            total = jnp.sum(jnp.where(inside, two, 0.0), axis=1, keepdims=True)
            result = jnp.where(lane == SLOT + 2 * pair + which, total, result)
    return result


def enc_back(query_parts, dck, dcv, kept, weights, norms):
    peers = lax.axis_size("seq")
    free = peers.bit_length() - 1
    count, width = dck.shape
    full = jnp.float32
    narrow = (count, width)
    wide = weights[3].shape[1]
    glob_count = kept[-1].shape[0]
    rows = query_parts.shape[0] // peers
    shapes = [(2,) * (free - 1 - k) + (rows, width) for k in range(free)]
    return call_whole(
        functools.partial(enc_back_body, peers),
        [query_parts.reshape((2,) * free + (rows, width)), dck, dcv, *kept, *weights, norms],
        [
            (narrow, low_type),
            ((count, wide), low_type),
            (narrow, full),
            (narrow, low_type),
            (narrow, low_type),
            ((count, LANES), full),
            ((glob_count, width), low_type),
            ((4, width), full),
            ((rows, width), full),
        ],
        [pltpu.SemaphoreType.DMA((free,))] * 2
        + [pltpu.VMEM(shape, low_type) for shape in shapes] * 2
        + [pltpu.VMEM(shape, full) for shape in shapes[:-1]],
        collective_id=8,
        has_side_effects=True,
    )


def turned_stats(stats, padded):
    padded[...] = jnp.zeros_like(padded)
    padded[: stats.shape[0], :] = stats
    return padded[...].T


def dec_back_body(
    limit_ref, sum_ref, res_ref, unit_ref, rate_ref, q_ref, k_ref, v_ref, o_ref, st_ref,
    wcq, wso, wsq, wsk, wsv, norms, dcq_ref, dso_ref, dsq_ref, dsk_ref, dsv_ref, own_ref,
    part_ref, vec_ref, q_pad, d_pad, st_pad, st_turned, bias_ref, dq_ref, key_sum, val_sum,
):
    full = jnp.float32
    mine = q_ref.shape[0]
    d_cq = sum_ref[...].astype(low_type) * 0.125
    dcq_ref[...] = d_cq
    gain, _ = scale_shift(norms, DEC_SELF)
    d_first = res_ref[...] + dot_right(d_cq, wcq[...])
    d_res, d_gain, d_shift = ln_back(d_first, unit_ref[...], rate_ref[...], gain)
    vec_ref[0:1, :] = d_gain
    vec_ref[1:2, :] = d_shift
    d_out = d_res.astype(low_type)
    dso_ref[...] = d_out
    d_attn = dot_right(d_out, wso[...]).astype(low_type)
    st_turned[...] = turned_stats(
        st_ref[...] + head_sums(d_attn.astype(full) * o_ref[...]), st_pad
    )
    q_pad[...] = jnp.zeros_like(q_pad)
    d_pad[...] = jnp.zeros_like(d_pad)
    q_pad[:mine, :] = q_ref[...]
    d_pad[:mine, :] = d_attn
    keys = lax.broadcasted_iota(jnp.int32, bias_ref.shape, 0)
    rows = lax.axis_index("seq") * mine + lax.broadcasted_iota(jnp.int32, bias_ref.shape, 1)
    bias_ref[...] = jnp.where((keys <= rows) & (keys < limit_ref[0]), 0.0, masked_score)
    key_sum[...] = jnp.zeros_like(key_sum)
    val_sum[...] = jnp.zeros_like(val_sum)
    back_heads(
        0, PAIRS, [((0, k_ref.shape[0]),)], LANES, 1, q_pad, k_ref, v_ref, d_pad, st_turned,
        bias_ref, dq_ref, key_sum, val_sum,
    )
    d_q = dq_ref[:mine, :].astype(low_type) * 0.125
    d_k = key_sum[...].astype(low_type)
    d_v = val_sum[...].astype(low_type)
    dsq_ref[...] = d_q
    dsk_ref[...] = d_k
    dsv_ref[...] = d_v
    own_ref[...] = d_res + dot_right(d_q, wsq[...])
    part_ref[...] = (dot_right(d_k, wsk[...]) + dot_right(d_v, wsv[...])).astype(low_type)


def dec_back(limit, inputs, weights, norms):
    full = jnp.float32
    mine, width = inputs[0].shape
    count = inputs[5].shape[0]
    whole = pl.BlockSpec(memory_space=pltpu.VMEM)
    shapes = [((mine, width), low_type)] * 3 + [((count, width), low_type)] * 2
    shapes += [((mine, width), full), ((count, width), low_type), ((2, width), full)]
    return pl.pallas_call(
        dec_back_body,
        in_specs=[pl.BlockSpec(memory_space=pltpu.SMEM)]
        + [whole] * (len(inputs) + len(weights) + 1),
        out_specs=[whole] * len(shapes),
        out_shape=[jax.ShapeDtypeStruct(shape, kind) for shape, kind in shapes],
        scratch_shapes=[
            pltpu.VMEM((LANES, width), low_type),
            pltpu.VMEM((LANES, width), low_type),
            pltpu.VMEM((LANES, LANES), full),
            pltpu.VMEM((LANES, LANES), full),
            pltpu.VMEM((count, LANES), full),
            pltpu.VMEM((LANES, width), full),
            pltpu.VMEM((count, width), full),
            pltpu.VMEM((count, width), full),
        ],
        compiler_params=pltpu.CompilerParams(vmem_limit_bytes=vmem_bytes),
    )(limit, *inputs, *weights, norms)


def enc_last_body(
    gq_ref, gk_ref, gv_ref, gd_ref, go_ref, gs_ref, live_ref, dq_in, dk_in, dv_in, res_ref,
    wq, wk, wv, wgq, wgk, wgv, dgk_ref, dgv_ref, dgq_ref, dq_low, rim_ref, glob_ref, source_ref,
    q_pad, d_pad, st_pad, st_turned, bias_ref, dq_ref, key_sum, val_sum,
):
    full = jnp.float32
    few = gq_ref.shape[0]
    count = gk_ref.shape[0]
    q_pad[...] = jnp.zeros_like(q_pad)
    d_pad[...] = jnp.zeros_like(d_pad)
    q_pad[:few, :] = gq_ref[...]
    d_pad[:few, :] = gd_ref[...]
    st_turned[...] = turned_stats(
        gs_ref[...] + head_sums(gd_ref[...].astype(full) * go_ref[...]), st_pad
    )
    bias_ref[...] = jnp.broadcast_to(live_ref[...], bias_ref.shape)
    key_sum[...] = jnp.zeros_like(key_sum)
    val_sum[...] = jnp.zeros_like(val_sum)
    back_heads(
        0, PAIRS, [((0, count),)], LANES, 1, q_pad, gk_ref, gv_ref, d_pad, st_turned, bias_ref,
        dq_ref, key_sum, val_sum,
    )
    d_gq = dq_ref[:few, :].astype(low_type) * 0.125
    d_gk = key_sum[...].astype(low_type)
    d_gv = val_sum[...].astype(low_type)
    dgq_ref[...] = d_gq
    dgk_ref[...] = d_gk
    dgv_ref[...] = d_gv
    d_q = dq_in[...].astype(low_type) * 0.125
    dq_low[...] = d_q

    def keys_part(start, size):
        rows = pl.ds(start, size)
        return dot_right(dk_in[rows, :], wk[...]) + dot_right(dv_in[rows, :], wv[...])

    rim_ref[0] = keys_part(0, HALF).astype(low_type)
    rim_ref[1] = keys_part(HALF + count, HALF).astype(low_type)
    glob_ref[...] = (keys_part(2 * HALF + count, few) + dot_right(d_gq, wgq[...])).astype(low_type)
    total = res_ref[...] + keys_part(HALF, count) + dot_right(d_q, wq[...])
    source_ref[...] = total + dot_right(d_gk, wgk[...]) + dot_right(d_gv, wgv[...])


def enc_last(inputs, weights):
    full = jnp.float32
    few, width = inputs[0].shape
    count = inputs[1].shape[0]
    narrow = (count, width)
    return call_whole(
        enc_last_body,
        [*inputs, *weights],
        [
            (narrow, low_type),
            (narrow, low_type),
            ((few, width), low_type),
            (narrow, low_type),
            ((2, HALF, width), low_type),
            ((few, width), low_type),
            (narrow, full),
        ],
        [
            pltpu.VMEM((LANES, width), low_type),
            pltpu.VMEM((LANES, width), low_type),
            pltpu.VMEM((LANES, LANES), full),
            pltpu.VMEM((LANES, LANES), full),
            pltpu.VMEM((count, LANES), full),
            pltpu.VMEM((LANES, width), full),
            pltpu.VMEM(narrow, full),
            pltpu.VMEM(narrow, full),
        ],
    )


def dec_middle_body(
    peers, acc_ref, st_ref, first_ref, cot_ref, norms, wo_far, wu_far, wd_far,
    decoded_ref, res_ref, dout_ref, stats_ref, laid_ref, vec_ref,
    wo, wu, wd, away, acc_one, st_one, low_out, st_out, acc_in, st_in,
    load, send, recv, send_two, recv_two, send_all, recv_all,
):
    full = jnp.float32
    me = lax.axis_index("seq")
    bits, digits = place_bits(peers)
    loads = [
        pltpu.make_async_copy(far, near, load.at[k])
        for k, (far, near) in enumerate(((wo_far, wo), (wu_far, wu), (wd_far, wd)))
    ]
    for copy in loads:
        copy.start()
    acc, top, total = merge_cross(
        peers, acc_ref, st_ref, away, acc_one, st_one, low_out, st_out, acc_in, st_in,
        send, recv, send_two, recv_two,
    )
    cross, lse = finish_parts(acc, top, total)
    cross_low = cross.astype(low_type)
    loads[0].wait()
    unit_one, rate_one = ln_parts(first_ref[...] + dot_plain(cross_low, wo[...]))
    gain, shift = scale_shift(norms, DEC_CROSS)
    second = unit_one * gain + shift
    second_low = second.astype(low_type)
    loads[1].wait()
    hidden, slope = gelu_pair(dot_plain(second_low, wu[...]))
    loads[2].wait()
    unit_two, rate_two = ln_parts(second + dot_plain(hidden, wd[...]))
    gain, shift = scale_shift(norms, DEC_FFN)
    decoded_ref[...] = (unit_two * gain + shift).astype(low_type)
    d_third, d_gain, d_shift = ln_back(cot_ref[...].astype(full), unit_two, rate_two, gain)
    vec_ref[2:3, :] = d_gain
    vec_ref[3:4, :] = d_shift
    d_down = d_third.astype(low_type)
    d_pre = (dot_right(d_down, wd[...]) * slope.astype(full)).astype(low_type)
    d_second = d_third + dot_right(d_pre, wu[...])
    gain, _ = scale_shift(norms, DEC_CROSS)
    d_res, d_gain, d_shift = ln_back(d_second, unit_one, rate_one, gain)
    vec_ref[0:1, :] = d_gain
    vec_ref[1:2, :] = d_shift
    res_ref[...] = d_res
    d_out = d_res.astype(low_type)
    d_cross = dot_right(d_out, wo[...]).astype(low_type)
    dout_ref[tuple(digits)] = d_cross
    stats_ref[tuple(digits)] = lse + head_sums(d_cross.astype(full) * cross)
    refs = [dout_ref, stats_ref]
    sems = (send_all, recv_all)
    reach_out(peers, refs, sems)

    half = d_out.shape[1] // 2
    wide_rows = second_low.shape[1] // peers
    count = d_pre.shape[1] // (2 * half)
    start = 0
    for k in range(count):
        for d in range(2):
            columns = (d * count + k) * half
            product = dot_left(second_low, d_pre[:, columns : columns + half]).astype(low_type)
            laid_ref[:, d, pl.ds(start, wide_rows), :] = product.reshape(peers, wide_rows, half)
        start += wide_rows
    pass_on(peers, refs, sems)
    tall_rows = hidden.shape[1] // peers
    few = second_low.shape[1] // tall_rows
    for k in range(peers // few):
        step = few * tall_rows
        product = dot_left(hidden[:, k * step : (k + 1) * step], d_down).astype(low_type)
        for d in range(2):
            part = product[:, d * half : (d + 1) * half].reshape(few, tall_rows, half)
            laid_ref[k * few : (k + 1) * few, d, pl.ds(start, tall_rows), :] = part
    start += tall_rows
    product = dot_left(cross_low, d_out).astype(low_type)
    for d in range(2):
        part = product[:, d * half : (d + 1) * half].reshape(peers, wide_rows, half)
        laid_ref[:, d, pl.ds(start, wide_rows), :] = part


def merge_cross(
    peers, acc_ref, st_ref, away, acc_one, st_one, low_out, st_out, acc_in, st_in,
    send, recv, send_two, recv_two,
):
    me = lax.axis_index("seq")
    core = me % 2
    pair = me // 2
    half = peers // 2
    mate = {"seq": other_of(me, 1)}
    greet([mate] + [{"seq": lax.rem(me + 2 * k, peers)} for k in range(1, half)])
    for j in range(half):
        away[j] = acc_ref[j, 1 - core].astype(low_type)
    first = [
        remote(away, acc_one, (send, recv), 0, mate),
        remote(st_ref.at[:, 1 - core], st_one, (send, recv), 1, mate),
    ]
    for copy in first:
        copy.start()
    for copy in first:
        copy.wait()
    rest = jnp.zeros((st_one.shape[1], LANES - 2 * SLOT), jnp.float32)

    def join(j):
        acc, top, total = merge_parts([acc_ref[j, core], acc_one[j]], [st_ref[j, core], st_one[j]])
        return acc, jnp.concatenate([top, total, rest], axis=1)

    def ship(k):
        j = lax.rem(pair + k, half)
        return [
            pltpu.make_async_remote_copy(
                src_ref=source.at[j],
                dst_ref=slot.at[half - k],
                send_sem=send_two.at[which, k],
                recv_sem=recv_two.at[which, half - k],
                device_id={"seq": lax.rem(me + 2 * k, peers)},
                device_id_type=pl.DeviceIdType.MESH,
            )
            for which, (source, slot) in enumerate(((low_out, acc_in), (st_out, st_in)))
        ]

    for k in range(1, half):
        j = lax.rem(pair + k, half)
        acc, stat = join(j)
        low_out[j] = acc.astype(low_type)
        st_out[j] = stat
        for copy in ship(k):
            copy.start()
    own_acc, own_stat = join(pair)
    for k in range(1, half):
        for copy in ship(k):
            copy.wait()
    return merge_parts(
        [own_acc] + [acc_in[k] for k in range(1, half)],
        [own_stat] + [st_in[k] for k in range(1, half)],
    )


def dec_middle(acc, stats, dec_first, cotangent, norms, weights):
    peers = lax.axis_size("seq")
    free = peers.bit_length() - 1
    half = peers // 2
    rows, width = dec_first.shape
    full = jnp.float32
    whole = pl.BlockSpec(memory_space=pltpu.VMEM)
    far = pl.BlockSpec(memory_space=pl.ANY)
    wide = weights[1].shape[1]
    early_rows = ((width // peers, wide // width), (wide // peers, 1), (width // peers, 1))
    laid_rows = sum(count * times for count, times in early_rows)
    lead = (2,) * free
    shapes = [
        ((rows, width), low_type),
        ((rows, width), full),
        (lead + (rows, width), low_type),
        (lead + (rows, LANES), full),
        ((peers, 2, laid_rows, width // 2), low_type),
        ((4, width), full),
    ]
    sem = pltpu.SemaphoreType.DMA
    decoded, d_res, dout, all_stats, laid, vec = pl.pallas_call(
        functools.partial(dec_middle_body, peers),
        in_specs=[whole] * 5 + [far] * 3,
        out_specs=[whole] * len(shapes),
        out_shape=[jax.ShapeDtypeStruct(shape, kind) for shape, kind in shapes],
        scratch_shapes=[pltpu.VMEM(weight.shape, low_type) for weight in weights]
        + [
            pltpu.VMEM((half, rows, width), low_type),
            pltpu.VMEM((half, rows, width), low_type),
            pltpu.VMEM((half, rows, LANES), full),
            pltpu.VMEM((half, rows, width), low_type),
            pltpu.VMEM((half, rows, LANES), full),
            pltpu.VMEM((half, rows, width), low_type),
            pltpu.VMEM((half, rows, LANES), full),
            sem((3,)),
            sem((2,)),
            sem((2,)),
            sem((2, half)),
            sem((2, half)),
            sem((2 * peers,)),
            sem((2 * peers,)),
        ],
        compiler_params=pltpu.CompilerParams(
            collective_id=4, has_side_effects=True, vmem_limit_bytes=vmem_bytes
        ),
    )(
        acc.reshape(half, 2, rows, width), stats.reshape(half, 2, rows, LANES),
        dec_first, cotangent, norms, *weights,
    )
    return (
        decoded, d_res, dout.reshape(-1, width), all_stats.reshape(-1, LANES),
        laid.reshape(-1, width // 2), early_rows, vec,
    )


def per_device(
    source,
    target,
    cotangent,
    src_len,
    dec_len,
    global_pos,
    enc_query,
    enc_key,
    enc_value,
    glob_query,
    glob_key,
    glob_value,
    enc_out,
    enc_attn_gain,
    enc_attn_shift,
    enc_up,
    enc_down,
    enc_ffn_gain,
    enc_ffn_shift,
    self_query,
    self_key,
    self_value,
    self_out,
    dec_self_gain,
    dec_self_shift,
    cross_query,
    cross_key,
    cross_value,
    cross_out,
    dec_cross_gain,
    dec_cross_shift,
    dec_up,
    dec_down,
    dec_ffn_gain,
    dec_ffn_shift,
):
    full = jnp.float32
    src_x = source[0]
    dec_x = target[0]
    src_count = src_x.shape[0]
    dec_count = dec_x.shape[0]
    seq_index = lax.axis_index("seq")
    peers = lax.axis_size("seq")
    src_limit = src_len[0]
    glob_places = global_pos[0]
    glob_count = glob_places.shape[0]
    src_places = seq_index * src_count + jnp.arange(src_count, dtype=jnp.int32)
    select_glob = glob_places[:, None] == src_places[None, :]
    select_low = select_glob.astype(low_type)
    norms = jnp.concatenate(
        [
            enc_attn_gain, enc_attn_shift, enc_ffn_gain, enc_ffn_shift, dec_self_gain,
            dec_self_shift, dec_cross_gain, dec_cross_shift, dec_ffn_gain, dec_ffn_shift,
        ]
    ).astype(full).reshape(10, -1)

    upward = [(i, i + 1) for i in range(peers - 1)]
    downward = [(i + 1, i) for i in range(peers - 1)]
    dec_all, glob_x, query_loc, glob_keys_loc, glob_vals_loc = start_exchange(
        dec_x,
        dot_plain(select_low, src_x).astype(low_type),
        src_x,
        (enc_query, glob_key, glob_value),
    )
    rim_x, _ = lax.optimization_barrier((src_x, glob_x))
    before = lax.ppermute(rim_x[src_count - HALF :], "seq", upward)
    after = lax.ppermute(rim_x[:HALF], "seq", downward)

    (self_k, self_v, all_cross_q, self_q, self_out_full, self_attn, self_stats, dec_first,
     self_unit, self_rate) = dec_front(
        dec_len,
        dec_all,
        (self_query, self_key, self_value, self_out, cross_query),
        norms,
        dec_count,
    )

    glob_queries = (dot_plain(glob_x, glob_query) * 0.125).astype(low_type)
    live_bias = jnp.where(src_places < src_limit, 0.0, masked_score)
    glob_acc, glob_stats = attend(
        glob_queries, glob_keys_loc, glob_vals_loc, live_bias[None, :], None, glob_count, False, 6
    )

    x_all, keys_all, vals_all = project_all((before, src_x, after, glob_x), enc_key, enc_value)
    pad_count = src_count + 2 * HALF
    pad_places = seq_index * src_count - HALF + jnp.arange(pad_count, dtype=jnp.int32)
    pad_glob = jnp.any(glob_places[:, None] == pad_places[None, :], axis=0)
    pad_use = (pad_places >= 0) & (pad_places < src_limit) & jnp.logical_not(pad_glob)
    win_use = jnp.concatenate(
        [jnp.where(pad_use, 0.0, masked_score), jnp.zeros((glob_count,), full)]
    )
    keep = jnp.where(pad_glob[HALF : HALF + src_count], 0.0, 1.0)[:, None]
    rows_block = 256
    reach = rows_block + 2 * HALF
    win_parts = [
        ((block * rows_block, reach), (pad_count, glob_count))
        for block in range(src_count // rows_block)
    ]
    win_out, win_stats, glob_out, glob_lse = window_attend(
        query_loc, keys_all, vals_all, win_use[None, :], win_parts, rows_block, glob_acc, glob_stats
    )
    (enc_attn, unit_one, rate_one, enc_first_low, enc_hidden, enc_slope, unit_two, rate_two,
     memory_low, cross_k, cross_v) = enc_front(
        win_out,
        keep,
        select_low,
        glob_out.astype(low_type),
        src_x,
        (enc_out, enc_up, enc_down, cross_key, cross_value),
        norms,
    )

    cross_acc, cross_stats = attend(
        all_cross_q, cross_k, cross_v, live_bias[None, :], None, 256, False, 2
    )
    decoded, d_res_two, all_dout, all_stats, early_laid, early_rows, dec_vec = dec_middle(
        cross_acc, cross_stats, dec_first, cotangent[0], norms, (cross_out, dec_up, dec_down)
    )
    early_mine = lax.psum_scatter(early_laid, ("seq", "dp"), scatter_dimension=0, tiled=True)
    query_parts, ck_low, cv_low = attend_back(
        all_cross_q,
        cross_k,
        cross_v,
        all_dout,
        all_stats[:, : 2 * SLOT].T,
        jnp.broadcast_to(live_bias[:, None], (src_count, 512)),
        None,
        256,
        2,
    )

    (d_enc_down, d_enc_pre, d_enc_res, d_attn_o, d_window, win_delta, glob_part, enc_vec,
     d_cross_sum) = enc_back(
        query_parts,
        ck_low,
        cv_low,
        (unit_two, rate_two, enc_slope, unit_one, rate_one, win_out, keep, select_low),
        (cross_key, cross_value, enc_down, enc_up, enc_out),
        norms,
    )
    g_enc_down = dot_left(enc_hidden, d_enc_down).astype(low_type)
    g_enc_up = dot_left(enc_first_low, d_enc_pre).astype(low_type)

    win_pair = (win_stats + win_delta)[:, : 2 * SLOT].T
    d_query, d_keys_all, d_vals_all, glob_dout = window_attend_back(
        query_loc, keys_all, vals_all, d_window, win_pair, win_use[:, None], win_parts, rows_block,
        glob_part,
    )

    (d_cross_q, d_self_o, d_self_q, d_self_k, d_self_v, d_target_own, d_target_part,
     self_vec) = dec_back(
        dec_len,
        (d_cross_sum, d_res_two, self_unit, self_rate, self_q, self_k, self_v, self_out_full,
         self_stats),
        (cross_query, self_out, self_query, self_key, self_value),
        norms,
    )
    gk_low, gv_low, d_gq, d_query_low, rim, d_glob_part, d_source_own = enc_last(
        (glob_queries, glob_keys_loc, glob_vals_loc, glob_dout, glob_out, glob_lse,
         live_bias[:, None], d_query, d_keys_all, d_vals_all, d_enc_res),
        (enc_query, enc_key, enc_value, glob_query, glob_key, glob_value),
    )
    vec_part = jnp.concatenate(
        [enc_vec, self_vec, dec_vec, jnp.zeros((6, enc_vec.shape[1]), full)], axis=0
    )

    pairs = [
        (memory_low, ck_low),
        (memory_low, cv_low),
        (enc_attn, d_attn_o),
        (dec_first.astype(low_type), d_cross_q),
        (self_attn, d_self_o),
        (dec_x, d_self_q),
        (dec_all, d_self_k),
        (dec_all, d_self_v),
        (src_x, d_query_low),
        (x_all, d_keys_all),
        (x_all, d_vals_all),
        (src_x, gk_low),
        (src_x, gv_low),
        (glob_x, d_gq),
    ]
    shared, (d_target_sum, d_glob_x, vec_sum, from_after, from_before) = last_exchange(
        [g_enc_up, g_enc_down], pairs, d_target_part, d_glob_part, vec_part, rim
    )
    vectors = share_vectors(vec_sum, 10)
    early_mine, d_glob_x = lax.optimization_barrier((early_mine, d_glob_x))
    flags = jnp.stack([seq_index < peers - 1, seq_index > 0]).astype(jnp.int32)[None, :]
    (
        s_enc_up, s_enc_down,
        s_cross_key, s_cross_value, s_enc_out, s_cross_query, s_self_out,
        s_self_query, s_self_key, s_self_value,
        s_enc_query, s_enc_key, s_enc_value, s_glob_key, s_glob_value, s_glob_query,
        s_dec_up, s_dec_down, s_cross_out, d_source, d_target,
    ) = end_outputs(
        shared,
        early_mine,
        early_rows,
        (d_source_own, from_after, from_before, select_low, d_glob_x, flags),
        (d_target_own, d_target_sum),
    )
    return (
        decoded[None],
        d_source[None],
        d_target[None],
        s_enc_query,
        s_enc_key,
        s_enc_value,
        s_glob_query,
        s_glob_key,
        s_glob_value,
        s_enc_out,
        vectors[0],
        vectors[1],
        s_enc_up,
        s_enc_down,
        vectors[2],
        vectors[3],
        s_self_query,
        s_self_key,
        s_self_value,
        s_self_out,
        vectors[4],
        vectors[5],
        s_cross_query,
        s_cross_key,
        s_cross_value,
        s_cross_out,
        vectors[6],
        vectors[7],
        s_dec_up,
        s_dec_down,
        vectors[8],
        vectors[9],
    )


def swap_dp(value):
    pairs = [(i, i ^ 1) for i in range(lax.axis_size("dp"))]
    return lax.ppermute(value, "dp", pairs)


def gather_rows(value):
    rows, width = value.shape
    held = value[None]
    for bit in reversed(seq_bits()):
        other = swap(held, bit)
        upper = bit_set(bit)
        held = jnp.stack(
            [jnp.where(upper, other, held), jnp.where(upper, held, other)], axis=1
        ).reshape(2 * held.shape[0], rows, width)
    return held.reshape(-1, width)


def add_all(value):
    for bit in seq_bits():
        value = value + swap(value, bit)
    return value


def scatter_all(value):
    bits = seq_bits()
    held = value.reshape((2,) * len(bits) + (-1, value.shape[1]))
    for step, bit in enumerate(bits):
        axis = len(bits) - 1 - step
        mine = bit_set(bit).astype(jnp.int32)
        other = swap(pick_half(held, 1 - mine, axis).astype(low_type), bit)
        held = pick_half(held, mine, axis) + other.astype(jnp.float32)
    return held


def merge_body(acc_a, st_a, acc_b, st_b, acc_o, st_o):
    top_a, top_b = st_a[:, :SLOT], st_b[:, :SLOT]
    top = jnp.maximum(top_a, top_b)
    keep_a = jnp.exp(top_a - top)
    keep_b = jnp.exp(top_b - top)
    total = st_a[:, SLOT : 2 * SLOT] * keep_a + st_b[:, SLOT : 2 * SLOT] * keep_b
    spread = head_spread()
    acc_o[...] = acc_a[...] * exact_dot(keep_a, spread) + acc_b[...].astype(
        jnp.float32
    ) * exact_dot(keep_b, spread)
    rest = jnp.zeros((top.shape[0], LANES - 2 * SLOT), jnp.float32)
    st_o[...] = jnp.concatenate([top, total, rest], axis=1)


def merge_soft(held, other):
    rows = held[0].shape[0]
    return pl.pallas_call(
        merge_body,
        out_shape=[
            jax.ShapeDtypeStruct((rows, held[0].shape[1]), jnp.float32),
            jax.ShapeDtypeStruct((rows, LANES), jnp.float32),
        ],
        compiler_params=pltpu.CompilerParams(vmem_limit_bytes=vmem_bytes),
    )(*held, *other)


def merge_all(held):
    for bit in seq_bits():
        held = merge_soft(held, swap((held[0].astype(low_type), held[1]), bit))
    return held


def merge_scatter(held):
    bits = seq_bits()
    for step, bit in enumerate(bits):
        inner = len(bits) - 1 - step
        mine = bit_set(bit).astype(jnp.int32)

        def halves(value, chosen):
            split = value.reshape(1 << inner, 2, -1, value.shape[1])
            return pick_half(split, chosen, 1).reshape(-1, value.shape[1])

        away = (halves(held[0], 1 - mine).astype(low_type), halves(held[1], 1 - mine))
        held = merge_soft((halves(held[0], mine), halves(held[1], mine)), swap(away, bit))
    return held


def share_grads(grads, dp_first):
    bits = seq_bits()
    width = grads[0].shape[1]
    half = width // 2
    rows = [grad.shape[0] >> len(bits) for grad in grads]
    dp_mine = lax.axis_index("dp")
    laid = [
        grad.astype(low_type).reshape((2,) * len(bits) + (count, width))
        for grad, count in zip(grads, rows)
    ]
    steps = [(1, False)]
    rest = [(bit, False) for bit in bits[1:]]
    steps += [(0, True)] + rest if dp_first else rest[:1] + [(0, True)] + rest[1:]
    held = None
    axis = len(bits)
    for bit, is_dp in steps:
        if is_dp:
            own = lax.dynamic_slice_in_dim(held, dp_mine * half, half, held.ndim - 1)
            away = lax.dynamic_slice_in_dim(held, (1 - dp_mine) * half, half, held.ndim - 1)
            held = own + swap_dp(away)
            continue
        axis -= 1
        mine = bit_set(bit).astype(jnp.int32)
        if held is None:
            away = jnp.concatenate([pick_half(v, 1 - mine, axis) for v in laid], axis=-2)
            own = jnp.concatenate([pick_half(v, mine, axis) for v in laid], axis=-2)
        else:
            away = pick_half(held, 1 - mine, axis)
            own = pick_half(held, mine, axis)
        held = own + swap(away, bit)
    result = []
    start = 0
    for count in rows:
        result.append(held[start : start + count].astype(jnp.float32))
        start += count
    return result


def share_norms(vectors):
    stacked = jnp.concatenate([jnp.stack(vectors), jnp.zeros((6, vectors[0].shape[0]))], axis=0)
    total = add_all(stacked)
    total = total + swap_dp(total)
    length = stacked.shape[1] // lax.axis_size("seq")
    mine = lax.dynamic_slice_in_dim(total, lax.axis_index("seq") * length, length, 1)
    return [mine[k] for k in range(len(vectors))]


def per_device_wide(
    source,
    target,
    cotangent,
    src_len,
    dec_len,
    global_pos,
    enc_query,
    enc_key,
    enc_value,
    glob_query,
    glob_key,
    glob_value,
    enc_out,
    enc_attn_gain,
    enc_attn_shift,
    enc_up,
    enc_down,
    enc_ffn_gain,
    enc_ffn_shift,
    self_query,
    self_key,
    self_value,
    self_out,
    dec_self_gain,
    dec_self_shift,
    cross_query,
    cross_key,
    cross_value,
    cross_out,
    dec_cross_gain,
    dec_cross_shift,
    dec_up,
    dec_down,
    dec_ffn_gain,
    dec_ffn_shift,
):
    full = jnp.float32
    src_x = source[0]
    dec_x = target[0]
    src_count = src_x.shape[0]
    dec_count = dec_x.shape[0]
    seq_index = lax.axis_index("seq")
    peers = lax.axis_size("seq")
    src_limit = src_len[0]
    dec_limit = dec_len[0]
    glob_places = global_pos[0]
    glob_count = glob_places.shape[0]
    src_places = seq_index * src_count + jnp.arange(src_count, dtype=jnp.int32)
    select_glob = glob_places[:, None] == src_places[None, :]
    select_low = select_glob.astype(low_type)
    is_global = jnp.any(select_glob, axis=0)
    spread = head_spread()

    upward = [(i, i + 1) for i in range(peers - 1)]
    downward = [(i + 1, i) for i in range(peers - 1)]
    before = lax.ppermute(src_x[src_count - HALF :], "seq", upward)
    after = lax.ppermute(src_x[:HALF], "seq", downward)
    dec_all = gather_rows(dec_x)
    glob_x = add_all(dot_plain(select_low, src_x).astype(low_type))

    query_loc = (dot_plain(src_x, enc_query) * 0.125).astype(low_type)
    glob_keys_loc = dot_plain(src_x, glob_key).astype(low_type)
    glob_vals_loc = dot_plain(src_x, glob_value).astype(low_type)

    self_q = (dot_plain(dec_x, self_query) * 0.125).astype(low_type)
    self_k = dot_plain(dec_all, self_key).astype(low_type)
    self_v = dot_plain(dec_all, self_value).astype(low_type)
    dec_total = dec_all.shape[0]
    dec_places = seq_index * dec_count + jnp.arange(dec_count, dtype=jnp.int32)
    all_dec = jnp.arange(dec_total, dtype=jnp.int32)
    self_allowed = (all_dec[None, :] <= dec_places[:, None]) & (all_dec < dec_limit)[None, :]
    self_bias = jnp.where(self_allowed, 0.0, masked_score)
    self_out_full, self_stats = attend(self_q, self_k, self_v, self_bias, None, dec_count, True)
    self_attn = self_out_full.astype(low_type)
    dec_res_one = dec_x.astype(full) + dot_plain(self_attn, self_out)
    dec_first, dec_first_back = jax.vjp(
        layer_norm, dec_res_one, dec_self_gain.astype(full), dec_self_shift.astype(full)
    )
    dec_first_low = dec_first.astype(low_type)
    cross_q = (dot_plain(dec_first_low, cross_query) * 0.125).astype(low_type)
    all_cross_q = gather_rows(cross_q)

    glob_queries = (dot_plain(glob_x, glob_query) * 0.125).astype(low_type)
    live_bias = jnp.where(src_places < src_limit, 0.0, masked_score)
    glob_acc, glob_stats = merge_all(
        attend(
            glob_queries, glob_keys_loc, glob_vals_loc, live_bias[None, :], None, glob_count, False
        )
    )
    glob_total = glob_stats[:, SLOT : 2 * SLOT]
    glob_out = glob_acc / exact_dot(glob_total, spread)
    glob_lse = glob_stats[:, :SLOT] + jnp.log(jnp.maximum(glob_total, 1e-30))

    x_all = jnp.concatenate([before, src_x, after, glob_x], axis=0)
    keys_all = dot_plain(x_all, enc_key).astype(low_type)
    vals_all = dot_plain(x_all, enc_value).astype(low_type)
    pad_count = src_count + 2 * HALF
    pad_places = seq_index * src_count - HALF + jnp.arange(pad_count, dtype=jnp.int32)
    pad_glob = jnp.any(glob_places[:, None] == pad_places[None, :], axis=0)
    pad_use = (pad_places >= 0) & (pad_places < src_limit) & jnp.logical_not(pad_glob)
    near = jnp.abs(src_places[:, None] - pad_places[None, :]) <= HALF
    win_bias = jnp.concatenate(
        [
            jnp.where(near & pad_use[None, :], 0.0, masked_score),
            jnp.zeros((src_count, glob_count), full),
        ],
        axis=1,
    )
    near_turned = jnp.abs(src_places[None, :] - pad_places[:, None]) <= HALF
    win_bias_turned = jnp.concatenate(
        [
            jnp.where(near_turned & pad_use[:, None], 0.0, masked_score),
            jnp.zeros((glob_count, src_count), full),
        ],
        axis=0,
    )
    rows_block = 256
    reach = rows_block + 2 * HALF
    win_parts = [
        ((block * rows_block, reach), (pad_count, glob_count))
        for block in range(src_count // rows_block)
    ]
    win_out, win_stats = attend(
        query_loc, keys_all, vals_all, win_bias, win_parts, rows_block, True
    )
    placed = dot_left(select_low, glob_out.astype(low_type))
    enc_attn = jnp.where(is_global[:, None], placed, win_out).astype(low_type)
    enc_res = src_x.astype(full) + dot_plain(enc_attn, enc_out)
    enc_first, enc_first_back = jax.vjp(
        layer_norm, enc_res, enc_attn_gain.astype(full), enc_attn_shift.astype(full)
    )
    enc_first_low = enc_first.astype(low_type)
    enc_hidden, enc_slope = gelu_pair(dot_plain(enc_first_low, enc_up))
    enc_second = enc_first + dot_plain(enc_hidden, enc_down)
    memory, enc_final_back = jax.vjp(
        layer_norm, enc_second, enc_ffn_gain.astype(full), enc_ffn_shift.astype(full)
    )
    memory_low = memory.astype(low_type)

    cross_k = dot_plain(memory_low, cross_key).astype(low_type)
    cross_v = dot_plain(memory_low, cross_value).astype(low_type)
    cross_acc, cross_stats = merge_scatter(
        attend(all_cross_q, cross_k, cross_v, live_bias[None, :], None, 256, False)
    )
    cross_total = cross_stats[:, SLOT : 2 * SLOT]
    cross_out_full = cross_acc / exact_dot(cross_total, spread)
    cross_lse = cross_stats[:, :SLOT] + jnp.log(jnp.maximum(cross_total, 1e-30))
    cross_attn = cross_out_full.astype(low_type)
    dec_res_two = dec_first + dot_plain(cross_attn, cross_out)
    dec_second, dec_second_back = jax.vjp(
        layer_norm, dec_res_two, dec_cross_gain.astype(full), dec_cross_shift.astype(full)
    )
    dec_second_low = dec_second.astype(low_type)
    dec_hidden, dec_slope = gelu_pair(dot_plain(dec_second_low, dec_up))
    dec_third = dec_second + dot_plain(dec_hidden, dec_down)
    decoded, dec_final_back = jax.vjp(
        layer_norm, dec_third, dec_ffn_gain.astype(full), dec_ffn_shift.astype(full)
    )

    d_third, g_dec_ffn_gain, g_dec_ffn_shift = dec_final_back(cotangent[0].astype(full))
    d_down_low = d_third.astype(low_type)
    d_pre_low = (dot_right(d_down_low, dec_down) * dec_slope.astype(full)).astype(low_type)
    d_second = d_third + dot_right(d_pre_low, dec_up)
    d_res_two, g_dec_cross_gain, g_dec_cross_shift = dec_second_back(d_second)
    d_cross_o = d_res_two.astype(low_type)
    d_cross_attn = dot_right(d_cross_o, cross_out).astype(low_type)
    cross_delta = exact_dot(d_cross_attn.astype(full) * cross_out_full, spread.T)
    all_dout = gather_rows(d_cross_attn)
    all_stats = gather_rows(
        jnp.concatenate(
            [cross_lse, cross_delta, jnp.zeros((dec_count, LANES - 2 * SLOT), full)], axis=1
        )
    )[:, : 2 * SLOT].T
    live_turned = jnp.broadcast_to(live_bias[:, None], (src_count, 512))
    query_parts, ck_low, cv_low = attend_back(
        all_cross_q, cross_k, cross_v, all_dout, all_stats, live_turned, None, 256
    )
    d_memory = dot_right(ck_low, cross_key) + dot_right(cv_low, cross_value)

    g_dec_down = dot_left(dec_hidden, d_down_low)
    g_dec_up = dot_left(dec_second_low, d_pre_low)
    g_cross_out = dot_left(cross_attn, d_cross_o)
    g_cross_key = dot_left(memory_low, ck_low)
    g_cross_value = dot_left(memory_low, cv_low)

    d_enc_second, g_enc_ffn_gain, g_enc_ffn_shift = enc_final_back(d_memory)
    d_enc_down = d_enc_second.astype(low_type)
    d_enc_pre = (dot_right(d_enc_down, enc_down) * enc_slope.astype(full)).astype(low_type)
    d_enc_first = d_enc_second + dot_right(d_enc_pre, enc_up)
    d_enc_res, g_enc_attn_gain, g_enc_attn_shift = enc_first_back(d_enc_first)
    d_attn_o = d_enc_res.astype(low_type)
    d_attn = dot_right(d_attn_o, enc_out).astype(low_type)
    g_enc_down = dot_left(enc_hidden, d_enc_down)
    g_enc_up = dot_left(enc_first_low, d_enc_pre)
    g_enc_out = dot_left(enc_attn, d_attn_o)

    d_cross_q = scatter_all(query_parts).astype(low_type) * 0.125
    g_cross_query = dot_left(dec_first_low, d_cross_q)
    d_first = d_res_two + dot_right(d_cross_q, cross_query)
    d_res_one, g_dec_self_gain, g_dec_self_shift = dec_first_back(d_first)
    d_self_o = d_res_one.astype(low_type)
    g_self_out = dot_left(self_attn, d_self_o)
    d_self_attn = dot_right(d_self_o, self_out).astype(low_type)
    self_delta = exact_dot(d_self_attn.astype(full) * self_out_full, spread.T)
    wide = max(dec_count, LANES)
    self_pair = jnp.concatenate([self_stats[:, :SLOT], self_delta], axis=1)
    self_query_parts, d_self_k, d_self_v = attend_back(
        pad_rows(self_q, wide),
        self_k,
        self_v,
        pad_rows(d_self_attn, wide),
        pad_rows(self_pair, wide).T,
        pad_rows(self_bias, wide).T,
        None,
        wide,
    )
    d_self_q = self_query_parts[:dec_count].astype(low_type) * 0.125
    g_self_query = dot_left(dec_x, d_self_q)
    g_self_key = dot_left(dec_all, d_self_k)
    g_self_value = dot_left(dec_all, d_self_v)
    d_target = (
        d_res_one
        + dot_right(d_self_q, self_query)
        + scatter_all(dot_right(d_self_k, self_key) + dot_right(d_self_v, self_value))
    )

    glob_dout = add_all(dot_plain(select_low, d_attn).astype(low_type))
    d_window = jnp.where(is_global[:, None], jnp.zeros_like(d_attn), d_attn)
    win_delta = exact_dot(d_window.astype(full) * win_out, spread.T)
    win_pair = jnp.concatenate([win_stats[:, :SLOT], win_delta], axis=1).T
    d_query, d_keys_all, d_vals_all = attend_back(
        query_loc, keys_all, vals_all, d_window, win_pair, win_bias_turned, win_parts, rows_block
    )
    d_query_low = d_query.astype(low_type) * 0.125

    wide = max(glob_count, LANES)
    glob_delta = exact_dot(glob_dout.astype(full) * glob_out, spread.T)
    glob_pair = jnp.concatenate([glob_lse, glob_delta], axis=1)
    glob_query_parts, gk_low, gv_low = attend_back(
        pad_rows(glob_queries, wide),
        glob_keys_loc,
        glob_vals_loc,
        pad_rows(glob_dout, wide),
        pad_rows(glob_pair, wide).T,
        live_turned[:, :wide],
        None,
        wide,
    )
    d_gq = glob_query_parts[:glob_count].astype(low_type) * 0.125

    g_enc_query = dot_left(src_x, d_query_low)
    g_enc_key = dot_left(x_all, d_keys_all)
    g_enc_value = dot_left(x_all, d_vals_all)
    g_glob_query = dot_left(glob_x, d_gq)
    g_glob_key = dot_left(src_x, gk_low)
    g_glob_value = dot_left(src_x, gv_low)

    d_x_all = dot_right(d_keys_all, enc_key) + dot_right(d_vals_all, enc_value)
    from_after = lax.ppermute(d_x_all[:HALF].astype(low_type), "seq", downward)
    from_before = lax.ppermute(d_x_all[HALF + src_count : pad_count].astype(low_type), "seq", upward)
    d_glob_x = add_all((d_x_all[pad_count:] + dot_right(d_gq, glob_query)).astype(low_type))
    d_source = (
        d_enc_res
        + dot_right(d_query_low, enc_query)
        + d_x_all[HALF : HALF + src_count]
        + dot_right(gk_low, glob_key)
        + dot_right(gv_low, glob_value)
        + dot_left(select_low, d_glob_x)
    )
    d_source = d_source + jnp.pad(
        from_after.astype(full), ((src_count - HALF, 0), (0, 0))
    )
    d_source = d_source + jnp.pad(
        from_before.astype(full), ((0, src_count - HALF), (0, 0))
    )

    (s_dec_up,) = share_grads([g_dec_up], True)
    s_dec_down, s_cross_out = share_grads([g_dec_down, g_cross_out], False)
    s_cross_key, s_cross_value = share_grads([g_cross_key, g_cross_value], True)
    (s_enc_up,) = share_grads([g_enc_up], True)
    s_enc_down, s_enc_out = share_grads([g_enc_down, g_enc_out], False)
    s_self_query, s_self_key, s_self_value, s_self_out, s_cross_query = share_grads(
        [g_self_query, g_self_key, g_self_value, g_self_out, g_cross_query], False
    )
    s_enc_query, s_enc_key, s_enc_value = share_grads([g_enc_query, g_enc_key, g_enc_value], True)
    s_glob_query, s_glob_key, s_glob_value = share_grads(
        [g_glob_query, g_glob_key, g_glob_value], False
    )
    vectors = share_norms(
        [
            g_enc_attn_gain,
            g_enc_attn_shift,
            g_enc_ffn_gain,
            g_enc_ffn_shift,
            g_dec_self_gain,
            g_dec_self_shift,
            g_dec_cross_gain,
            g_dec_cross_shift,
            g_dec_ffn_gain,
            g_dec_ffn_shift,
        ]
    )
    return (
        decoded.astype(low_type)[None],
        d_source[None],
        d_target[None],
        s_enc_query,
        s_enc_key,
        s_enc_value,
        s_glob_query,
        s_glob_key,
        s_glob_value,
        s_enc_out,
        vectors[0],
        vectors[1],
        s_enc_up,
        s_enc_down,
        vectors[2],
        vectors[3],
        s_self_query,
        s_self_key,
        s_self_value,
        s_self_out,
        vectors[4],
        vectors[5],
        s_cross_query,
        s_cross_key,
        s_cross_value,
        s_cross_out,
        vectors[6],
        vectors[7],
        s_dec_up,
        s_dec_down,
        vectors[8],
        vectors[9],
    )


def solution(mesh):
    rows = P("dp", "seq", None)
    tile = P("seq", "dp")
    part = P("seq")
    layer = (tile,) * 7 + (part,) * 2 + (tile,) * 2 + (part,) * 2
    decoder = (tile,) * 4 + (part,) * 2 + (tile,) * 4 + (part,) * 2 + (tile,) * 2 + (part,) * 2
    few = mesh.shape["seq"] <= 16
    return jax.shard_map(
        per_device if few else per_device_wide,
        mesh=mesh,
        in_specs=(rows, rows, rows, P("dp"), P("dp"), P("dp", None)) + (P(),) * 29,
        out_specs=(rows, rows, rows) + layer + decoder,
        check_vma=False,
    )
```

```python
import functools

import jax
import jax.numpy as jnp
import numpy as np
from jax import lax
from jax.experimental import pallas as pl
from jax.experimental.pallas import tpu as pltpu
from jax.sharding import PartitionSpec as P

HEADS = 12
HEAD_DIM = 64
HALF = 512
PAIRS = HEADS // 2
LANES = 2 * HEAD_DIM
SLOT = 16

masked_score = -1e30
eps_norm = 1e-05
low_type = jnp.bfloat16
vmem_bytes = 56 * 2**20


def dot_plain(left, right):
    return jnp.dot(left, right, preferred_element_type=jnp.float32)


def dot_left(left, right):
    return lax.dot_general(
        left, right, (((0,), (0,)), ((), ())), preferred_element_type=jnp.float32
    )


def dot_right(left, right):
    return lax.dot_general(
        left, right, (((1,), (1,)), ((), ())), preferred_element_type=jnp.float32
    )


def exact_dot(left, right):
    return jnp.dot(
        left, right, precision=lax.Precision.HIGHEST, preferred_element_type=jnp.float32
    )


def layer_norm(value, scale_vec, shift_vec):
    average = jnp.mean(value, axis=-1, keepdims=True)
    centred = value - average
    spread = jnp.mean(centred * centred, axis=-1, keepdims=True)
    return centred * lax.rsqrt(spread + eps_norm) * scale_vec + shift_vec


def gelu_pair(value):
    cdf = 0.5 * (1.0 + lax.erf(value * 0.7071067811865476))
    slope = cdf + value * (0.3989422804014327 * jnp.exp(-0.5 * value * value))
    return (value * cdf).astype(low_type), slope.astype(low_type)


def head_spread():
    heads = lax.broadcasted_iota(jnp.int32, (SLOT, HEADS * HEAD_DIM), 0)
    columns = lax.broadcasted_iota(jnp.int32, (SLOT, HEADS * HEAD_DIM), 1)
    return (columns // HEAD_DIM == heads).astype(jnp.float32)


def head_mask(which):
    lanes = lax.broadcasted_iota(jnp.int32, (1, LANES), 1)
    return ((lanes // HEAD_DIM) == which).astype(low_type)


def attend_heads(
    first, group, parts, rows_block, blocks, normalize, q_ref, k_ref, v_ref, bias_ref, o_ref, st_ref
):
    lane = lax.broadcasted_iota(jnp.int32, (1, LANES), 1)
    for block in range(blocks):
        rows = pl.ds(block * rows_block, rows_block)
        stats = st_ref[rows, :]
        for pair in range(group):
            columns = pl.ds(pair * LANES, LANES)
            q_two = q_ref[rows, columns]
            outs = []
            for which in range(2):
                head = first + 2 * pair + which
                q_one = q_two * head_mask(which)
                scores = []
                for start, size in parts[block]:
                    keys = pl.ds(start, size)
                    bias = bias_ref[rows, keys] if bias_ref.shape[0] > 1 else bias_ref[:, keys]
                    scores.append(dot_right(q_one, k_ref[keys, columns]) + bias)
                top = functools.reduce(
                    jnp.maximum, [jnp.max(part, axis=1, keepdims=True) for part in scores]
                )
                total = jnp.zeros((rows_block, 1), jnp.float32)
                mixed = jnp.zeros((rows_block, LANES), jnp.float32)
                for (start, size), part in zip(parts[block], scores):
                    weights = jnp.exp(part - top)
                    total = total + jnp.sum(weights, axis=1, keepdims=True)
                    mixed = mixed + dot_plain(
                        weights.astype(low_type), v_ref[pl.ds(start, size), columns]
                    )
                if normalize:
                    mixed = mixed / total
                    stats = jnp.where(lane == head, top + jnp.log(total), stats)
                else:
                    stats = jnp.where(lane == head, top, stats)
                    stats = jnp.where(lane == head + SLOT, total, stats)
                outs.append(mixed)
            o_ref[rows, columns] = jnp.where(lane < HEAD_DIM, outs[0], outs[1])
        st_ref[rows, :] = stats


def forward_body(
    parts, rows_block, blocks, normalize, group, q_ref, k_ref, v_ref, bias_ref, o_ref, st_ref
):
    first = pl.program_id(1) * (2 * group)

    @pl.when(first == 0)
    def _():
        st_ref[...] = jnp.zeros_like(st_ref)

    attend_heads(
        first, group, parts, rows_block, blocks, normalize, q_ref, k_ref, v_ref, bias_ref,
        o_ref, st_ref,
    )


def attend(queries, keys, values, bias, parts, rows_block, normalize, group=1):
    count, width = queries.shape
    key_count = keys.shape[0]
    big = min(count, 512)
    blocks = big // rows_block
    parts = parts or [((0, key_count),)] * blocks
    bias_rows = bias.shape[0]
    flops = 4 * count * key_count * width
    wide = group * LANES
    return pl.pallas_call(
        functools.partial(forward_body, parts, rows_block, blocks, normalize, group),
        grid=(count // big, PAIRS // group),
        in_specs=[
            pl.BlockSpec((big, wide), lambda i, p: (i, p)),
            pl.BlockSpec((key_count, wide), lambda i, p: (0, p)),
            pl.BlockSpec((key_count, wide), lambda i, p: (0, p)),
            pl.BlockSpec(
                (min(bias_rows, big), key_count), lambda i, p: (i if bias_rows > big else 0, 0)
            ),
        ],
        out_specs=[
            pl.BlockSpec((big, wide), lambda i, p: (i, p)),
            pl.BlockSpec((big, LANES), lambda i, p: (i, 0)),
        ],
        out_shape=[
            jax.ShapeDtypeStruct((count, width), jnp.float32),
            jax.ShapeDtypeStruct((count, LANES), jnp.float32),
        ],
        compiler_params=pltpu.CompilerParams(vmem_limit_bytes=vmem_bytes),
        cost_estimate=pl.CostEstimate(
            flops=4 * flops,
            bytes_accessed=2 * (count + 2 * key_count) * width + 4 * count * width,
            transcendentals=count * key_count * HEADS,
        ),
    )(queries, keys, values, bias)


def back_heads(
    first, group, parts, rows_block, blocks, q_ref, k_ref, v_ref, d_ref, st_ref, bias_ref,
    dq_ref, key_sum, val_sum,
):
    for block in range(blocks):
        rows = pl.ds(block * rows_block, rows_block)
        for pair in range(group):
            columns = pl.ds(pair * LANES, LANES)
            q_two = q_ref[rows, columns]
            d_two = d_ref[rows, columns]
            turned = []
            for which in range(2):
                head = first + 2 * pair + which
                q_one = q_two * head_mask(which)
                d_one = d_two * head_mask(which)
                lse = st_ref[pl.ds(head, 1), rows]
                delta = st_ref[pl.ds(head + SLOT, 1), rows]
                q_grad = jnp.zeros((LANES, rows_block), jnp.float32)
                for start, size in parts[block]:
                    keys = pl.ds(start, size)
                    bias = bias_ref[keys, rows] if bias_ref.shape[1] > 1 else bias_ref[keys, :]
                    k_two = k_ref[keys, columns]
                    scores = dot_right(k_two, q_one) + bias
                    weights = jnp.exp(scores - lse)
                    slopes = dot_right(v_ref[keys, columns], d_one)
                    diffs = (weights * (slopes - delta)).astype(low_type)
                    val_sum[keys, columns] += dot_plain(weights.astype(low_type), d_one)
                    key_sum[keys, columns] += dot_plain(diffs, q_one)
                    q_grad = q_grad + dot_left(k_two, diffs)
                turned.append(q_grad[which * HEAD_DIM : (which + 1) * HEAD_DIM, :])
            dq_ref[rows, columns] = jnp.concatenate(turned, axis=0).T.astype(dq_ref.dtype)


def backward_body(
    parts, rows_block, blocks, group, q_ref, k_ref, v_ref, d_ref, st_ref, bias_ref,
    dq_ref, dk_ref, dv_ref, key_sum, val_sum,
):
    first = pl.program_id(0) * (2 * group)
    turn = pl.program_id(1)

    @pl.when(turn == 0)
    def _():
        key_sum[...] = jnp.zeros_like(key_sum)
        val_sum[...] = jnp.zeros_like(val_sum)

    back_heads(
        first, group, parts, rows_block, blocks, q_ref, k_ref, v_ref, d_ref, st_ref, bias_ref,
        dq_ref, key_sum, val_sum,
    )

    @pl.when(turn == pl.num_programs(1) - 1)
    def _():
        dk_ref[...] = key_sum[...].astype(low_type)
        dv_ref[...] = val_sum[...].astype(low_type)


def attend_back(queries, keys, values, grads, stats, bias, parts, rows_block, group=1):
    count, width = queries.shape
    key_count = keys.shape[0]
    big = min(count, 512)
    blocks = big // rows_block
    parts = parts or [((0, key_count),)] * blocks
    bias_cols = bias.shape[1]
    flops = 10 * count * key_count * width
    wide = group * LANES
    return pl.pallas_call(
        functools.partial(backward_body, parts, rows_block, blocks, group),
        grid=(PAIRS // group, count // big),
        in_specs=[
            pl.BlockSpec((big, wide), lambda p, i: (i, p)),
            pl.BlockSpec((key_count, wide), lambda p, i: (0, p)),
            pl.BlockSpec((key_count, wide), lambda p, i: (0, p)),
            pl.BlockSpec((big, wide), lambda p, i: (i, p)),
            pl.BlockSpec((2 * SLOT, big), lambda p, i: (0, i)),
            pl.BlockSpec((key_count, min(bias_cols, big)), lambda p, i: (0, 0)),
        ],
        out_specs=[
            pl.BlockSpec((big, wide), lambda p, i: (i, p)),
            pl.BlockSpec((key_count, wide), lambda p, i: (0, p)),
            pl.BlockSpec((key_count, wide), lambda p, i: (0, p)),
        ],
        out_shape=[
            jax.ShapeDtypeStruct((count, width), jnp.float32),
            jax.ShapeDtypeStruct((key_count, width), low_type),
            jax.ShapeDtypeStruct((key_count, width), low_type),
        ],
        scratch_shapes=[
            pltpu.VMEM((key_count, wide), jnp.float32),
            pltpu.VMEM((key_count, wide), jnp.float32),
        ],
        compiler_params=pltpu.CompilerParams(vmem_limit_bytes=vmem_bytes),
        cost_estimate=pl.CostEstimate(
            flops=4 * flops,
            bytes_accessed=2 * (2 * count + 4 * key_count) * width + 4 * count * width,
            transcendentals=count * key_count * HEADS,
        ),
    )(queries, keys, values, grads, stats, bias)


def seq_bits():
    count = lax.axis_size("seq")
    return [1 << k for k in range(count.bit_length() - 1)]


def swap(value, bit):
    pairs = [(i, i ^ bit) for i in range(lax.axis_size("seq"))]
    return jax.tree.map(lambda part: lax.ppermute(part, "seq", pairs), value)


def bit_set(bit):
    return (lax.axis_index("seq") & bit) != 0


def pick_half(value, chosen, axis):
    return lax.dynamic_index_in_dim(value, chosen, axis, keepdims=False)


def other_of(place, bit):
    return place + bit * (1 - 2 * ((place // bit) % 2))


def greet(partners):
    barrier = pltpu.get_barrier_semaphore()
    for partner in partners:
        pl.semaphore_signal(
            barrier, inc=1, device_id=partner, device_id_type=pl.DeviceIdType.MESH
        )
    pl.semaphore_wait(barrier, len(partners))


def remote(src, dst, sems, k, partner):
    return pltpu.make_async_remote_copy(
        src_ref=src,
        dst_ref=dst,
        send_sem=sems[0].at[k],
        recv_sem=sems[1].at[k],
        device_id=partner,
        device_id_type=pl.DeviceIdType.MESH,
    )


def piece_stages(peers, kind):
    bits = [1 << k for k in range(1, peers.bit_length() - 1)]
    if kind == "x":
        return [1, "dp"] + bits
    if kind == "y":
        return [1] + bits[:1] + ["dp"] + bits[1:]
    return [1] + bits[1:] + ["dp"] + bits[:1]


def piece_shapes(peers, rows, width, stages):
    free = peers.bit_length() - 1
    shapes = []
    for stage in stages:
        if stage == "dp":
            width = width // 2
        else:
            free -= 1
        shapes.append((2,) * free + (rows, width))
    return shapes


def bit_axis(peers, stages, s):
    rest = [bit for bit in reversed([1 << k for k in range(peers.bit_length() - 1)])]
    for stage in stages[:s]:
        if stage != "dp":
            rest.remove(stage)
    return rest.index(stages[s])


def place_bits(peers):
    me = lax.axis_index("seq")
    bits = [1 << k for k in reversed(range(peers.bit_length() - 1))]
    return bits, [(me // bit) % 2 for bit in bits]


def block_at(peers, ref, place):
    return ref.at[tuple((place // bit) % 2 for bit in place_bits(peers)[0])]


def chip_copies(peers, refs, sems, k):
    me = lax.axis_index("seq")
    half = peers // 2
    return [
        remote(
            block_at(peers, ref, me),
            block_at(peers, ref, me),
            sems,
            which * peers + k,
            {"seq": lax.rem(me + 2 * k, peers)},
        )
        for which, ref in enumerate(refs)
    ]


def core_copies(peers, refs, sems, k):
    me = lax.axis_index("seq")
    place = lax.rem(me + peers - 2 * k, peers)
    return [
        remote(
            block_at(peers, ref, place),
            block_at(peers, ref, place),
            sems,
            which * peers + peers // 2 + k,
            {"seq": other_of(me, 1)},
        )
        for which, ref in enumerate(refs)
    ]


def reach_out(peers, refs, sems):
    for k in range(1, peers // 2):
        for copy in chip_copies(peers, refs, sems, k):
            copy.start()
    for copy in core_copies(peers, refs, sems, 0):
        copy.start()


def pass_on(peers, refs, sems):
    half = peers // 2
    for k in range(1, half):
        for copy in chip_copies(peers, refs, sems, k):
            copy.wait_recv()
        for copy in core_copies(peers, refs, sems, k):
            copy.start()
    for k in range(half):
        for copy in core_copies(peers, refs, sems, k):
            copy.wait()
    for k in range(1, half):
        for copy in chip_copies(peers, refs, sems, k):
            copy.wait_send()


OWNERS = 4


def everyone(peers):
    me = lax.axis_index("seq")
    return [{"seq": lax.rem(me + k, peers)} for k in range(1, peers)]


def send_in(peers, parts, slots, sems):
    me = lax.axis_index("seq")
    apart = peers // OWNERS
    for o in range(OWNERS):
        for k, (part, slot) in enumerate(zip(parts, slots)):
            copy = pltpu.make_async_remote_copy(
                src_ref=part.at[o],
                dst_ref=slot.at[me],
                send_sem=sems[0].at[k, o],
                recv_sem=sems[1].at[k, me],
                device_id={"seq": o * apart},
                device_id_type=pl.DeviceIdType.MESH,
            )

            @pl.when(me != o * apart)
            def _():
                copy.start()

            @pl.when(me == o * apart)
            def _():
                slot[me] = part[o]


def arrive(peers, parts, slots, sems):
    me = lax.axis_index("seq")
    for j in range(peers):
        for k, (part, slot) in enumerate(zip(parts, slots)):

            @pl.when(me != j)
            def _():
                pltpu.make_async_remote_copy(
                    src_ref=part.at[0],
                    dst_ref=slot.at[j],
                    send_sem=sems[0].at[k, 0],
                    recv_sem=sems[1].at[k, j],
                    device_id={"seq": j},
                    device_id_type=pl.DeviceIdType.MESH,
                ).wait_recv()


def left(peers, parts, slots, sems):
    me = lax.axis_index("seq")
    apart = peers // OWNERS
    for o in range(OWNERS):
        for k, (part, slot) in enumerate(zip(parts, slots)):

            @pl.when(me != o * apart)
            def _():
                pltpu.make_async_remote_copy(
                    src_ref=part.at[o],
                    dst_ref=slot.at[me],
                    send_sem=sems[0].at[k, o],
                    recv_sem=sems[1].at[k, me],
                    device_id={"seq": o * apart},
                    device_id_type=pl.DeviceIdType.MESH,
                ).wait_send()


def out_copies(results, sems, o, j):
    return [
        pltpu.make_async_remote_copy(
            src_ref=result.at[o],
            dst_ref=result.at[o],
            send_sem=sems[2].at[k, j],
            recv_sem=sems[3].at[k, o],
            device_id={"seq": j},
            device_id_type=pl.DeviceIdType.MESH,
        )
        for k, result in enumerate(results)
    ]


def send_out(peers, results, sems):
    me = lax.axis_index("seq")
    apart = peers // OWNERS
    for o in range(OWNERS):
        owner = o * apart

        @pl.when(me == owner)
        def _():
            for j in range(peers):
                if j != owner:
                    for copy in out_copies(results, sems, o, j):
                        copy.start()


def take_out(peers, results, sems):
    me = lax.axis_index("seq")
    apart = peers // OWNERS
    for o in range(OWNERS):
        owner = o * apart

        @pl.when(me != owner)
        def _():
            for copy in out_copies(results, sems, o, owner):
                copy.wait_recv()

        @pl.when(me == owner)
        def _():
            for j in range(peers):
                if j != owner:
                    for copy in out_copies(results, sems, o, j):
                        copy.wait_send()


def owner_sems(peers, count):
    return [
        pltpu.SemaphoreType.DMA((count, OWNERS)),
        pltpu.SemaphoreType.DMA((count, peers)),
        pltpu.SemaphoreType.DMA((count, peers)),
        pltpu.SemaphoreType.DMA((count, OWNERS)),
    ]


def sum_at_owner(peers, part_ref, slot, sum_ref, sems):
    me = lax.axis_index("seq")
    apart = peers // OWNERS
    for o in range(OWNERS):

        @pl.when(me == o * apart)
        def _():
            arrive(peers, [part_ref], [slot], sems)
            total = slot[0].astype(jnp.float32)
            for j in range(1, peers):
                total = total + slot[j].astype(jnp.float32)
            sum_ref[o] = total.astype(low_type)


def expand_heads(stat):
    lane = lax.broadcasted_iota(jnp.int32, (1, LANES), 1)
    return jnp.concatenate(
        [
            jnp.where(lane < HEAD_DIM, stat[:, 2 * p : 2 * p + 1], stat[:, 2 * p + 1 : 2 * p + 2])
            for p in range(PAIRS)
        ],
        axis=1,
    )


def merge_parts(accs, stats):
    tops = [part[:, :SLOT] for part in stats]
    top = functools.reduce(jnp.maximum, tops)
    total = jnp.zeros_like(top)
    acc = jnp.zeros(accs[0].shape, jnp.float32)
    for part, stat, own_top in zip(accs, stats, tops):
        keep = jnp.exp(own_top - top)
        total = total + stat[:, SLOT : 2 * SLOT] * keep
        acc = acc + part.astype(jnp.float32) * expand_heads(keep)
    return acc, top, total


def finish_parts(acc, top, total):
    lanes = lax.broadcasted_iota(jnp.int32, total.shape, 1)
    total = jnp.where(lanes < HEADS, total, 1.0)
    lse = top + jnp.log(total)
    rest = jnp.zeros((top.shape[0], LANES - SLOT), jnp.float32)
    return acc * expand_heads(1.0 / total), jnp.concatenate([lse, rest], axis=1)


def window_body(
    peers, parts, rows_block, blocks, q_ref, k_ref, v_ref, use_ref, acc_ref, part_ref,
    o_ref, st_ref, out_copy, lse_copy, bias_ref, low_ref, acc_in, st_in, out_ref, lse_ref, *sems
):
    step = pl.program_id(1)
    me = lax.axis_index("seq")
    apart = peers // OWNERS

    @pl.when(step == 0)
    def _():
        greet(everyone(peers))
        low_ref[...] = acc_ref[...].astype(low_type)
        send_in(peers, [low_ref, part_ref], [acc_in, st_in], sems)
        rows = lax.broadcasted_iota(jnp.int32, bias_ref.shape, 0)
        keys = lax.broadcasted_iota(jnp.int32, bias_ref.shape, 1)
        apart_by = rows + HALF - keys
        near = (jnp.abs(apart_by) <= HALF) | (keys >= bias_ref.shape[0] + 2 * HALF)
        bias_ref[...] = jnp.where(near, use_ref[...], masked_score)

    @pl.when(step == 2)
    def _():
        for o in range(OWNERS):

            @pl.when(me == o * apart)
            def _():
                arrive(peers, [low_ref, part_ref], [acc_in, st_in], sems)
                acc, top, total = merge_parts(
                    [acc_in[j] for j in range(peers)], [st_in[j] for j in range(peers)]
                )
                out_ref[o], lse_ref[o] = finish_parts(acc, top, total)

        send_out(peers, [out_ref, lse_ref], sems)

    forward_body(
        parts, rows_block, blocks, True, 1, q_ref, k_ref, v_ref, bias_ref, o_ref, st_ref
    )

    @pl.when(step == PAIRS - 1)
    def _():
        take_out(peers, [out_ref, lse_ref], sems)
        left(peers, [low_ref, part_ref], [acc_in, st_in], sems)
        out_copy[...] = out_ref[...]
        lse_copy[...] = lse_ref[...]


def window_attend(queries, keys, values, use, parts, rows_block, glob_acc, glob_stats):
    peers = lax.axis_size("seq")
    count, width = queries.shape
    key_count = keys.shape[0]
    rows = glob_acc.shape[0] // OWNERS
    flops = 4 * count * key_count * width

    def pair_block(size):
        return pl.BlockSpec((size, LANES), lambda i, p: (0, p))

    def whole(*shape):
        return pl.BlockSpec(shape, lambda i, p: (0,) * len(shape))

    out, stats, glob_out, lse = pl.pallas_call(
        functools.partial(window_body, peers, parts, rows_block, count // rows_block),
        grid=(1, PAIRS),
        in_specs=[
            pair_block(count),
            pair_block(key_count),
            pair_block(key_count),
            whole(1, key_count),
            whole(OWNERS, rows, width),
            whole(OWNERS, rows, LANES),
        ],
        out_specs=[
            pair_block(count),
            whole(count, LANES),
            whole(OWNERS, rows, width),
            whole(OWNERS, rows, LANES),
        ],
        out_shape=[
            jax.ShapeDtypeStruct((count, width), jnp.float32),
            jax.ShapeDtypeStruct((count, LANES), jnp.float32),
            jax.ShapeDtypeStruct((OWNERS, rows, width), jnp.float32),
            jax.ShapeDtypeStruct((OWNERS, rows, LANES), jnp.float32),
        ],
        scratch_shapes=[
            pltpu.VMEM((count, key_count), jnp.float32),
            pltpu.VMEM((OWNERS, rows, width), low_type),
            pltpu.VMEM((peers, rows, width), low_type),
            pltpu.VMEM((peers, rows, LANES), jnp.float32),
            pltpu.VMEM((OWNERS, rows, width), jnp.float32),
            pltpu.VMEM((OWNERS, rows, LANES), jnp.float32),
        ]
        + owner_sems(peers, 2),
        compiler_params=pltpu.CompilerParams(
            collective_id=3, has_side_effects=True, vmem_limit_bytes=vmem_bytes
        ),
        cost_estimate=pl.CostEstimate(
            flops=4 * flops,
            bytes_accessed=2 * (count + 2 * key_count) * width + 4 * count * width,
            transcendentals=count * key_count * HEADS,
        ),
    )(
        queries, keys, values, use,
        glob_acc.reshape(OWNERS, rows, width), glob_stats.reshape(OWNERS, rows, LANES),
    )
    return out, stats, glob_out.reshape(-1, width), lse.reshape(-1, LANES)


def end_body(count, *refs):
    shared = refs[:count]
    (source_own, after, before, select, glob,
     target_own, target_sum, flags) = refs[count : count + 8]
    outs = refs[count + 8 :]
    for source, target in zip(shared, outs):
        target[...] = source[...]
    d_source, d_target = outs[count:]
    full = jnp.float32
    d_target[...] = target_own[...] + target_sum[...]
    has_after = flags[:, :1] > 0
    has_before = flags[:, 1:2] > 0
    total = source_own[...] + dot_left(select[...], glob[...])
    total = total + jnp.where(has_after, after[...].astype(full), 0.0)
    d_source[...] = total + jnp.where(has_before, before[...].astype(full), 0.0)


def end_outputs(shared, source_parts, target_parts):
    shapes = [part.shape for part in shared]
    shapes += [source_parts[0].shape, target_parts[0].shape]
    return pl.pallas_call(
        functools.partial(end_body, len(shared)),
        out_shape=[jax.ShapeDtypeStruct(shape, jnp.float32) for shape in shapes],
        compiler_params=pltpu.CompilerParams(vmem_limit_bytes=vmem_bytes),
    )(*shared, *source_parts[:5], *target_parts, source_parts[5])


def share_vectors(total, count):
    length = total.shape[1] // lax.axis_size("seq")
    mine = lax.dynamic_slice_in_dim(total, lax.axis_index("seq") * length, length, 1)
    return [mine[k] for k in range(count)]


def pad_rows(value, count):
    return jnp.pad(value, ((0, count - value.shape[0]), (0, 0)))


class Pieces:
    def __init__(self, peers, pieces, mats, factors, kept, outs, sems, load, held, own, staging, base):
        self.peers = peers
        self.pieces = pieces
        self.mats = mats
        self.factors = factors
        self.kept = kept
        self.outs = outs
        self.sems = sems
        self.load = load
        self.held = held
        self.own = own
        self.staging = staging
        self.numbers = {}
        self.base = base
        self.me = lax.axis_index("seq")
        self.mine_dp = lax.axis_index("dp")

    def number(self, *key):
        return self.base + self.numbers.setdefault(key, len(self.numbers))

    def partner(self, stage):
        if stage == "dp":
            return {"dp": 1 - self.mine_dp}
        return {"seq": other_of(self.me, stage)}

    def halved(self, source, stages, s, mine):
        if stages[s] == "dp":
            half = source.shape[-1] // 2
            where = self.mine_dp if mine else 1 - self.mine_dp
            start = pl.multiple_of(where * half, LANES)
            return (slice(None),) * (len(source.shape) - 1) + (pl.ds(start, half),)
        digit = (self.me // stages[s]) % 2
        return (slice(None),) * bit_axis(self.peers, stages, s) + (digit if mine else 1 - digit,)

    def copy(self, name, stages, origin, target, s):
        view = origin.at[self.halved(origin, stages, s, False)]
        return remote(view, target, self.sems, self.number(name, s), self.partner(stages[s]))

    def fold(self, stages, origin, target, s, finish):
        spot = self.halved(origin, stages, s, True)
        for place in np.ndindex(*target.shape[:-2]):
            if stages[s] == "dp":
                more = origin[place + spot[-2:]]
            else:
                axis = len(spot) - 1
                more = origin[place[:axis] + spot[-1:] + place[axis:]]
            total = target[place] + more
            if finish is not None:
                if place:
                    finish[place] = total.astype(finish.dtype)
                else:
                    finish[...] = total.astype(finish.dtype)
            else:
                target[place] = total

    def origin(self, p, s):
        piece = self.pieces[p]
        if s > piece["first"]:
            return self.held[p][s - 1 - piece["first"]]
        kind, which = piece["from"]
        return {"mat": self.mats, "made": self.staging, "kept": self.kept}[kind][which]

    def target(self, p, s):
        return self.held[p][s - self.pieces[p]["first"]]

    def local(self, p, c):
        which = self.pieces[p]["from"][1]
        core = self.me % 2
        return pltpu.make_async_copy(
            self.mats[which].at[c // 2, c % 2, :, core],
            self.own[which].at[c % 2],
            self.load.at[2 * which + c % 2],
        )

    def compute(self, p):
        x, y = (self.factors[k] for k in self.pieces[p]["pair"])
        target = self.staging[self.pieces[p]["from"][1]]
        step = x.shape[1] // 2
        for block in range(2):
            product = dot_left(x[:, block * step : (block + 1) * step], y[...])
            target[block] = product.astype(low_type).reshape(target.shape[1:])

    def begin(self, p, s):
        piece = self.pieces[p]
        if s == 0 and piece["from"][0] == "mat":
            for c in range(2):
                self.local(p, c).start()
        self.copy(p, piece["stages"], self.origin(p, s), self.target(p, s), s).start()

    def end(self, p, s):
        piece = self.pieces[p]
        origin, target = self.origin(p, s), self.target(p, s)
        self.copy(p, piece["stages"], origin, target, s).wait()
        finish = self.outs[p] if s == piece["last"] else None
        if s == 0 and piece["from"][0] == "mat":
            mine = self.own[piece["from"][1]]
            for c in range(4):
                self.local(p, c).wait()
                spot = (c // 2, c % 2)
                for k in range(2):
                    target[spot + (k,)] = target[spot + (k,)] + mine[c % 2, k]
                if c < 2:
                    self.local(p, c + 2).start()
        else:
            self.fold(piece["stages"], origin, target, s, finish)

    def open(self, turn):
        for p in turn:
            if "pair" in self.pieces[p]:
                self.compute(p)
            self.begin(p, self.pieces[p]["first"])

    def move(self, turn, s):
        for p in turn:
            self.end(p, s)
            if s < self.pieces[p]["last"]:
                self.begin(p, s + 1)


def piece_plan(peers, source, rows, width, kind, first, last, pair=None):
    stages = piece_stages(peers, kind)
    shapes = piece_shapes(peers, rows, width, stages)
    plan = {"from": source, "stages": stages, "first": first, "last": last}
    if pair is not None:
        plan["pair"] = pair
    return plan, shapes[first : last + 1]


def ln_parts(value):
    average = jnp.mean(value, axis=-1, keepdims=True)
    centred = value - average
    spread = jnp.mean(centred * centred, axis=-1, keepdims=True)
    rate = lax.rsqrt(spread + eps_norm)
    return centred * rate, rate


def ln_back(grad, unit, rate, gain):
    scaled = grad * gain
    pull = jnp.mean(scaled, axis=-1, keepdims=True)
    twist = jnp.mean(scaled * unit, axis=-1, keepdims=True)
    return (
        rate * (scaled - pull - unit * twist),
        jnp.sum(grad * unit, axis=0, keepdims=True),
        jnp.sum(grad, axis=0, keepdims=True),
    )


def call_whole(body, inputs, shapes, scratch=(), **params):
    whole = pl.BlockSpec(memory_space=pltpu.VMEM)
    return pl.pallas_call(
        body,
        in_specs=[whole] * len(inputs),
        out_specs=[whole] * len(shapes),
        out_shape=[jax.ShapeDtypeStruct(shape, kind) for shape, kind in shapes],
        scratch_shapes=list(scratch),
        compiler_params=pltpu.CompilerParams(vmem_limit_bytes=vmem_bytes, **params),
    )(*inputs)


ENC_ATTN, ENC_FFN, DEC_SELF, DEC_CROSS, DEC_FFN = 0, 2, 4, 6, 8


def scale_shift(norms, which):
    return norms[which : which + 1, :], norms[which + 1 : which + 2, :]


def start_body(
    peers, dec_ref, part_ref, x_ref, wq, wgk, wgv, all_ref, glob_ref, q_ref, gk_ref, gv_ref,
    slot, send, recv, *sems
):
    bits, digits = place_bits(peers)
    greet(everyone(peers))
    send_in(peers, [part_ref], [slot], sems)
    all_ref[tuple(digits)] = dec_ref[...]
    reach_out(peers, [all_ref], (send, recv))
    x = x_ref[...]
    gk_ref[...] = dot_plain(x, wgk[...]).astype(low_type)
    sum_at_owner(peers, part_ref, slot, glob_ref, sems)
    send_out(peers, [glob_ref], sems)
    q_ref[...] = (dot_plain(x, wq[...]) * 0.125).astype(low_type)
    pass_on(peers, [all_ref], (send, recv))
    gv_ref[...] = dot_plain(x, wgv[...]).astype(low_type)
    take_out(peers, [glob_ref], sems)
    left(peers, [part_ref], [slot], sems)


def start_exchange(dec_x, glob_part, src_x, weights):
    peers = lax.axis_size("seq")
    free = peers.bit_length() - 1
    rows = glob_part.shape[0] // OWNERS
    width = dec_x.shape[1]
    dec_all, glob_x, q, gk, gv = call_whole(
        functools.partial(start_body, peers),
        [dec_x, glob_part.reshape(OWNERS, rows, width), src_x, *weights],
        [((2,) * free + dec_x.shape, dec_x.dtype), ((OWNERS, rows, width), low_type)]
        + [(src_x.shape, low_type)] * 3,
        [
            pltpu.VMEM((peers, rows, width), low_type),
            pltpu.SemaphoreType.DMA((peers,)),
            pltpu.SemaphoreType.DMA((peers,)),
        ]
        + owner_sems(peers, 1),
        collective_id=2,
        has_side_effects=True,
    )
    return dec_all.reshape(-1, width), glob_x.reshape(-1, width), q, gk, gv


def project_body(*refs):
    sources = refs[:4]
    wk, wv, x_all, k_all, v_all = refs[4:]
    start = 0
    for source in sources:
        rows = pl.ds(start, source.shape[0])
        x = source[...]
        x_all[rows, :] = x
        k_all[rows, :] = dot_plain(x, wk[...]).astype(low_type)
        v_all[rows, :] = dot_plain(x, wv[...]).astype(low_type)
        start += source.shape[0]


def project_all(sources, wk, wv):
    total = sum(source.shape[0] for source in sources)
    return call_whole(
        project_body, [*sources, wk, wv], [((total, sources[0].shape[1]), low_type)] * 3
    )


def dec_front_body(
    limit_ref, x_ref, wq, wk, wv, wo, wcq, norms, k_ref, v_ref, cq_ref, q_own, out_own, attn_own,
    st_own, first_own, unit_own, rate_own, q_ref, o_ref, st_ref, bias_ref,
):
    x = x_ref[...]
    count = x.shape[0]
    half = count // 2
    q_ref[...] = (dot_plain(x, wq[...]) * 0.125).astype(low_type)
    k_ref[...] = dot_plain(x, wk[...]).astype(low_type)
    v_ref[...] = dot_plain(x, wv[...]).astype(low_type)
    rows = lax.broadcasted_iota(jnp.int32, (count, count), 0)
    keys = lax.broadcasted_iota(jnp.int32, (count, count), 1)
    bias_ref[...] = jnp.where((keys <= rows) & (keys < limit_ref[0]), 0.0, masked_score)
    st_ref[...] = jnp.zeros_like(st_ref)
    attend_heads(
        0, PAIRS, [((0, half),), ((0, count),)], half, 2, True, q_ref, k_ref, v_ref, bias_ref,
        o_ref, st_ref,
    )
    gain, shift = scale_shift(norms, DEC_SELF)
    res = x.astype(jnp.float32) + dot_plain(o_ref[...].astype(low_type), wo[...])
    unit, _ = ln_parts(res)
    first = unit * gain + shift
    cq_ref[...] = (dot_plain(first.astype(low_type), wcq[...]) * 0.125).astype(low_type)
    mine = q_own.shape[0]
    start = pl.multiple_of(lax.axis_index("seq") * mine, mine)
    own = pl.ds(start, mine)
    q_own[...] = q_ref[own, :]
    out_own[...] = o_ref[own, :]
    attn = o_ref[own, :].astype(low_type)
    attn_own[...] = attn
    st_own[...] = st_ref[own, :]
    res_own = x_ref[own, :].astype(jnp.float32) + dot_plain(attn, wo[...])
    unit, rate = ln_parts(res_own)
    unit_own[...] = unit
    rate_own[...] = rate
    first_own[...] = unit * gain + shift


def dec_front(limit, dec_all, weights, norms, mine):
    count, width = dec_all.shape
    full = jnp.float32
    whole = pl.BlockSpec(memory_space=pltpu.VMEM)
    shapes = [
        ((count, width), low_type),
        ((count, width), low_type),
        ((count, width), low_type),
        ((mine, width), low_type),
        ((mine, width), full),
        ((mine, width), low_type),
        ((mine, LANES), full),
        ((mine, width), full),
        ((mine, width), full),
        ((mine, 1), full),
    ]
    return pl.pallas_call(
        dec_front_body,
        in_specs=[pl.BlockSpec(memory_space=pltpu.SMEM)] + [whole] * 7,
        out_specs=[whole] * len(shapes),
        out_shape=[jax.ShapeDtypeStruct(shape, kind) for shape, kind in shapes],
        scratch_shapes=[
            pltpu.VMEM((count, width), low_type),
            pltpu.VMEM((count, width), full),
            pltpu.VMEM((count, LANES), full),
            pltpu.VMEM((count, count), full),
        ],
        compiler_params=pltpu.CompilerParams(vmem_limit_bytes=vmem_bytes),
    )(limit, dec_all, *weights, norms)


def enc_front_body(
    win_ref, keep_ref, select, glob, x_ref, wo, wu, wd, wck, wcv, norms, attn_ref, unit_one,
    rate_one, low_one, hidden_ref, slope_ref, unit_two, rate_two, low_two, ck_ref, cv_ref,
):
    rows_block = x_ref.shape[0] // 2
    width = x_ref.shape[1]
    for block in range(2):
        rows = pl.ds(block * rows_block, rows_block)
        placed = dot_left(select[:, block * rows_block : (block + 1) * rows_block], glob[...])
        attn = jnp.where(keep_ref[rows, :] > 0, win_ref[rows, :], placed).astype(low_type)
        attn_ref[rows, :] = attn
        unit, rate = ln_parts(x_ref[rows, :].astype(jnp.float32) + dot_plain(attn, wo[...]))
        unit_one[rows, :] = unit
        rate_one[rows, :] = rate
        gain, shift = scale_shift(norms, ENC_ATTN)
        second = unit * gain + shift
        first = second.astype(low_type)
        low_one[rows, :] = first
        for k in range(wu.shape[1] // width):
            columns = pl.ds(k * width, width)
            hidden, slope = gelu_pair(dot_plain(first, wu[:, columns]))
            hidden_ref[rows, columns] = hidden
            slope_ref[rows, columns] = slope
            second = second + dot_plain(hidden, wd[columns, :])
        unit, rate = ln_parts(second)
        unit_two[rows, :] = unit
        rate_two[rows, :] = rate
        gain, shift = scale_shift(norms, ENC_FFN)
        memory = (unit * gain + shift).astype(low_type)
        low_two[rows, :] = memory
        ck_ref[rows, :] = dot_plain(memory, wck[...]).astype(low_type)
        cv_ref[rows, :] = dot_plain(memory, wcv[...]).astype(low_type)


def enc_front(win_out, keep, select, glob, x, weights, norms):
    count, width = x.shape
    wide = weights[1].shape[1]
    full = jnp.float32
    narrow = (count, width)
    return call_whole(
        enc_front_body,
        [win_out, keep, select, glob, x, *weights, norms],
        [
            (narrow, low_type),
            (narrow, full),
            ((count, 1), full),
            (narrow, low_type),
            ((count, wide), low_type),
            ((count, wide), low_type),
            (narrow, full),
            ((count, 1), full),
            (narrow, low_type),
            (narrow, low_type),
            (narrow, low_type),
        ],
    )


def row_sum_steps(peers, whole_ref, out_ref, buffers, send, recv):
    me = lax.axis_index("seq")
    free = peers.bit_length() - 1
    every = slice(None)
    sends, takes, helds = buffers[:free], buffers[free : 2 * free], buffers[2 * free :]

    def source(k):
        return whole_ref if k == 0 else helds[k - 1]

    def copy(k):
        return remote(sends[k], takes[k], (send, recv), k, {"seq": other_of(me, 1 << k)})

    def begin(k):
        digit = (me // (1 << k)) % 2
        lead = (every,) * (free - 1 - k)
        sends[k][...] = source(k)[lead + (1 - digit,)].astype(low_type)
        copy(k).start()

    def end(k):
        copy(k).wait()
        digit = (me // (1 << k)) % 2
        lead = (every,) * (free - 1 - k)
        total = source(k)[lead + (digit,)] + takes[k][...].astype(jnp.float32)
        target = out_ref if k == free - 1 else helds[k]
        target[...] = total

    def step(k):
        if k > 0:
            end(k - 1)
        if k < free:
            begin(k)

    return [functools.partial(step, k) for k in range(free + 1)]


def bring(fars, nears, sem):
    copies = [
        pltpu.make_async_copy(far, near, sem.at[k]) for k, (far, near) in enumerate(zip(fars, nears))
    ]
    for copy in copies:
        copy.start()
    return copies


def enc_back_body(
    peers, pieces, parts_ref, g_up, g_down, g_out, dck, dcv, unit_two, rate_two, rate_one, keep_ref,
    select, wck, wcv, norms, *refs
):
    refs = list(refs)

    def take(count):
        result = refs[:count]
        del refs[:count]
        return result

    fars = take(8)
    down_ref, pre_ref, res_ref, out_ref, window_ref, delta_ref, glob_ref, vec_ref, sum_ref = take(9)
    made_up, made_down, kept_up, kept_down, kept_out = take(5)
    send, recv, send_two, recv_two, load, fetch = take(6)
    held, own, nears, buffers = take(6), take(3), take(8), refs
    wd, wu, slope_ref, unit_one, wo, win_ref, hidden_ref, first_ref = nears
    work = Pieces(
        peers, pieces, [g_up, g_down, g_out], [], [], [kept_up, kept_down, kept_out],
        (send_two, recv_two), load, [held[:2], held[2:4], held[4:]], own, [], 0,
    )
    turn = [0, 1, 2]
    me = lax.axis_index("seq")
    free = peers.bit_length() - 1
    greet([{"seq": other_of(me, 1 << k)} for k in range(free)] + [work.partner("dp")])
    steps = row_sum_steps(peers, parts_ref, sum_ref, buffers, send, recv)
    steps[0]()
    work.open(turn)
    copies = bring(fars, nears, fetch)
    rows_block = dck.shape[0] // 2
    width = dck.shape[1]
    vec_ref[...] = jnp.zeros_like(vec_ref)
    glob = jnp.zeros(glob_ref.shape, jnp.float32)
    for block in range(2):
        rows = pl.ds(block * rows_block, rows_block)
        d_memory = dot_right(dck[rows, :], wck[...]) + dot_right(dcv[rows, :], wcv[...])
        gain, _ = scale_shift(norms, ENC_FFN)
        d_second, d_gain, d_shift = ln_back(d_memory, unit_two[rows, :], rate_two[rows, :], gain)
        vec_ref[2:3, :] += d_gain
        vec_ref[3:4, :] += d_shift
        d_down = d_second.astype(low_type)
        down_ref[rows, :] = d_down
        steps[2 * block + 1]()
        if block == 0:
            work.move(turn[:2], 0)
            for copy in copies[:6]:
                copy.wait()
        for k in range(wu.shape[1] // width):
            columns = pl.ds(k * width, width)
            d_hidden = dot_right(d_down, wd[columns, :])
            d_pre = (d_hidden * slope_ref[rows, columns].astype(jnp.float32)).astype(low_type)
            pre_ref[rows, columns] = d_pre
            d_second = d_second + dot_right(d_pre, wu[:, columns])
        gain, _ = scale_shift(norms, ENC_ATTN)
        d_res, d_gain, d_shift = ln_back(d_second, unit_one[rows, :], rate_one[rows, :], gain)
        vec_ref[0:1, :] += d_gain
        vec_ref[1:2, :] += d_shift
        res_ref[rows, :] = d_res
        d_out = d_res.astype(low_type)
        out_ref[rows, :] = d_out
        d_attn = dot_right(d_out, wo[...]).astype(low_type)
        glob = glob + dot_plain(
            select[:, block * rows_block : (block + 1) * rows_block], d_attn
        )
        d_window = jnp.where(keep_ref[rows, :] > 0, d_attn.astype(jnp.float32), 0.0)
        window_ref[rows, :] = d_window.astype(low_type)
        delta_ref[rows, :] = head_sums(d_window * win_ref[rows, :])
        steps[2 * block + 2]()
    work.move(turn[2:], 0)
    for copy in copies[6:]:
        copy.wait()
    for k in range(wu.shape[1] // width):
        columns = pl.ds(k * width, width)
        product = dot_left(first_ref[...], pre_ref[:, columns]).astype(low_type)
        made_up[:, :, :, :, :, columns] = product.reshape((2,) * free + (-1, width))
        product = dot_left(hidden_ref[:, columns], down_ref[...]).astype(low_type)
        made_down[k // 2, k % 2] = product.reshape(made_down.shape[2:])
    work.move(turn, 1)
    glob_ref[...] = glob.astype(low_type)


def head_sums(value):
    lane = lax.broadcasted_iota(jnp.int32, (1, LANES), 1)
    result = jnp.zeros((value.shape[0], LANES), jnp.float32)
    for pair in range(PAIRS):
        two = value[:, pair * LANES : (pair + 1) * LANES]
        for which in range(2):
            inside = (lane // HEAD_DIM) == which
            total = jnp.sum(jnp.where(inside, two, 0.0), axis=1, keepdims=True)
            result = jnp.where(lane == SLOT + 2 * pair + which, total, result)
    return result


def enc_back(query_parts, dck, dcv, kept, weights, norms, made, fars):
    peers = lax.axis_size("seq")
    free = peers.bit_length() - 1
    lead = (2,) * free
    count, width = dck.shape
    full = jnp.float32
    narrow = (count, width)
    wide = fars[1].shape[1]
    glob_count = kept[-1].shape[0]
    rows = query_parts.shape[0] // peers
    shapes = [(2,) * (free - 1 - k) + (rows, width) for k in range(free)]
    plans = [
        piece_plan(peers, ("mat", k), *mat.shape[-2:], kind, 0, 1)
        for k, (mat, kind) in enumerate(zip(made, "xyz"))
    ]
    pieces = [plan for plan, _ in plans]
    whole = pl.BlockSpec(memory_space=pltpu.VMEM)
    far = pl.BlockSpec(memory_space=pl.ANY)
    sem = pltpu.SemaphoreType.DMA
    out_shapes = [
        (narrow, low_type),
        ((count, wide), low_type),
        (narrow, full),
        (narrow, low_type),
        (narrow, low_type),
        ((count, LANES), full),
        ((glob_count, width), low_type),
        ((4, width), full),
        ((rows, width), full),
        (lead + (width // peers, wide), low_type),
        (lead + (wide // peers, width), low_type),
    ] + [(shape[-1], low_type) for _, shape in plans]
    outs = pl.pallas_call(
        functools.partial(enc_back_body, peers, pieces),
        in_specs=[whole]
        + [far] * 3
        + [whole] * (3 + len(kept) + len(weights))
        + [far] * len(fars),
        out_specs=[whole] * len(out_shapes),
        out_shape=[jax.ShapeDtypeStruct(shape, kind) for shape, kind in out_shapes],
        scratch_shapes=[sem((free,)), sem((free,)), sem((6,)), sem((6,)), sem((6,))]
        + [sem((len(fars),))]
        + [pltpu.VMEM(one, low_type) for _, shape in plans for one in shape]
        + [pltpu.VMEM((2, 2) + mat.shape[-2:], low_type) for mat in made]
        + [pltpu.VMEM(array.shape, array.dtype) for array in fars]
        + [pltpu.VMEM(shape, low_type) for shape in shapes] * 2
        + [pltpu.VMEM(shape, full) for shape in shapes[:-1]],
        compiler_params=pltpu.CompilerParams(
            collective_id=8, has_side_effects=True, vmem_limit_bytes=62 * 2**20
        ),
    )(
        query_parts.reshape(lead + (rows, width)), *made, dck, dcv, *kept, *weights, norms, *fars
    )
    return outs[:9], outs[9:11], outs[11:], pieces


def turned_stats(stats, padded):
    padded[...] = jnp.zeros_like(padded)
    padded[: stats.shape[0], :] = stats
    return padded[...].T


def dec_back_body(
    limit_ref, sum_ref, res_ref, unit_ref, rate_ref, q_ref, k_ref, v_ref, o_ref, st_ref,
    wcq, wso, wsq, wsk, wsv, norms, dcq_ref, dso_ref, dsq_ref, dsk_ref, dsv_ref, own_ref,
    part_ref, vec_ref, q_pad, d_pad, st_pad, st_turned, bias_ref, dq_ref, key_sum, val_sum,
):
    full = jnp.float32
    mine = q_ref.shape[0]
    d_cq = sum_ref[...].astype(low_type) * 0.125
    dcq_ref[...] = d_cq
    gain, _ = scale_shift(norms, DEC_SELF)
    d_first = res_ref[...] + dot_right(d_cq, wcq[...])
    d_res, d_gain, d_shift = ln_back(d_first, unit_ref[...], rate_ref[...], gain)
    vec_ref[0:1, :] = d_gain
    vec_ref[1:2, :] = d_shift
    d_out = d_res.astype(low_type)
    dso_ref[...] = d_out
    d_attn = dot_right(d_out, wso[...]).astype(low_type)
    st_turned[...] = turned_stats(
        st_ref[...] + head_sums(d_attn.astype(full) * o_ref[...]), st_pad
    )
    q_pad[...] = jnp.zeros_like(q_pad)
    d_pad[...] = jnp.zeros_like(d_pad)
    q_pad[:mine, :] = q_ref[...]
    d_pad[:mine, :] = d_attn
    keys = lax.broadcasted_iota(jnp.int32, bias_ref.shape, 0)
    rows = lax.axis_index("seq") * mine + lax.broadcasted_iota(jnp.int32, bias_ref.shape, 1)
    bias_ref[...] = jnp.where((keys <= rows) & (keys < limit_ref[0]), 0.0, masked_score)
    key_sum[...] = jnp.zeros_like(key_sum)
    val_sum[...] = jnp.zeros_like(val_sum)
    back_heads(
        0, PAIRS, [((0, k_ref.shape[0]),)], LANES, 1, q_pad, k_ref, v_ref, d_pad, st_turned,
        bias_ref, dq_ref, key_sum, val_sum,
    )
    d_q = dq_ref[:mine, :].astype(low_type) * 0.125
    d_k = key_sum[...].astype(low_type)
    d_v = val_sum[...].astype(low_type)
    dsq_ref[...] = d_q
    dsk_ref[...] = d_k
    dsv_ref[...] = d_v
    own_ref[...] = d_res + dot_right(d_q, wsq[...])
    part_ref[...] = (dot_right(d_k, wsk[...]) + dot_right(d_v, wsv[...])).astype(low_type)


def enc_last_body(
    gq_ref, gk_ref, gv_ref, gd_ref, go_ref, gs_ref, live_ref, dq_in, dk_in, dv_in, res_ref,
    wq, wk, wv, wgq, wgk, wgv, dgk_ref, dgv_ref, dgq_ref, dq_low, rim_ref, glob_ref, source_ref,
    q_pad, d_pad, st_pad, st_turned, bias_ref, dq_ref, key_sum, val_sum,
):
    full = jnp.float32
    few = gq_ref.shape[0]
    count = gk_ref.shape[0]
    q_pad[...] = jnp.zeros_like(q_pad)
    d_pad[...] = jnp.zeros_like(d_pad)
    q_pad[:few, :] = gq_ref[...]
    d_pad[:few, :] = gd_ref[...]
    st_turned[...] = turned_stats(
        gs_ref[...] + head_sums(gd_ref[...].astype(full) * go_ref[...]), st_pad
    )
    bias_ref[...] = jnp.broadcast_to(live_ref[...], bias_ref.shape)
    key_sum[...] = jnp.zeros_like(key_sum)
    val_sum[...] = jnp.zeros_like(val_sum)
    back_heads(
        0, PAIRS, [((0, count),)], LANES, 1, q_pad, gk_ref, gv_ref, d_pad, st_turned, bias_ref,
        dq_ref, key_sum, val_sum,
    )
    d_gq = dq_ref[:few, :].astype(low_type) * 0.125
    d_gk = key_sum[...].astype(low_type)
    d_gv = val_sum[...].astype(low_type)
    dgq_ref[...] = d_gq
    dgk_ref[...] = d_gk
    dgv_ref[...] = d_gv
    d_q = dq_in[...].astype(low_type) * 0.125
    dq_low[...] = d_q

    def keys_part(start, size):
        rows = pl.ds(start, size)
        return dot_right(dk_in[rows, :], wk[...]) + dot_right(dv_in[rows, :], wv[...])

    rim_ref[0] = keys_part(0, HALF).astype(low_type)
    rim_ref[1] = keys_part(HALF + count, HALF).astype(low_type)
    glob_ref[...] = (keys_part(2 * HALF + count, few) + dot_right(d_gq, wgq[...])).astype(low_type)
    total = res_ref[...] + keys_part(HALF, count) + dot_right(d_q, wq[...])
    source_ref[...] = total + dot_right(d_gk, wgk[...]) + dot_right(d_gv, wgv[...])


def dec_middle_body(
    peers, acc_ref, st_ref, first_ref, cot_ref, norms, wo_far, wu_far, wd_far,
    decoded_ref, res_ref, dout_ref, stats_ref, g_up, g_down, g_out, vec_ref,
    wo, wu, wd, away, acc_one, st_one, low_out, st_out, acc_in, st_in,
    load, send, recv, send_two, recv_two, send_all, recv_all,
):
    full = jnp.float32
    me = lax.axis_index("seq")
    bits, digits = place_bits(peers)
    loads = [
        pltpu.make_async_copy(far, near, load.at[k])
        for k, (far, near) in enumerate(((wo_far, wo), (wu_far, wu), (wd_far, wd)))
    ]
    for copy in loads:
        copy.start()
    acc, top, total = merge_cross(
        peers, acc_ref, st_ref, away, acc_one, st_one, low_out, st_out, acc_in, st_in,
        send, recv, send_two, recv_two,
    )
    cross, lse = finish_parts(acc, top, total)
    cross_low = cross.astype(low_type)
    loads[0].wait()
    unit_one, rate_one = ln_parts(first_ref[...] + dot_plain(cross_low, wo[...]))
    gain, shift = scale_shift(norms, DEC_CROSS)
    second = unit_one * gain + shift
    second_low = second.astype(low_type)
    loads[1].wait()
    hidden, slope = gelu_pair(dot_plain(second_low, wu[...]))
    loads[2].wait()
    unit_two, rate_two = ln_parts(second + dot_plain(hidden, wd[...]))
    gain, shift = scale_shift(norms, DEC_FFN)
    decoded_ref[...] = (unit_two * gain + shift).astype(low_type)
    d_third, d_gain, d_shift = ln_back(cot_ref[...].astype(full), unit_two, rate_two, gain)
    vec_ref[2:3, :] = d_gain
    vec_ref[3:4, :] = d_shift
    d_down = d_third.astype(low_type)
    d_pre = (dot_right(d_down, wd[...]) * slope.astype(full)).astype(low_type)
    d_second = d_third + dot_right(d_pre, wu[...])
    gain, _ = scale_shift(norms, DEC_CROSS)
    d_res, d_gain, d_shift = ln_back(d_second, unit_one, rate_one, gain)
    vec_ref[0:1, :] = d_gain
    vec_ref[1:2, :] = d_shift
    res_ref[...] = d_res
    d_out = d_res.astype(low_type)
    d_cross = dot_right(d_out, wo[...]).astype(low_type)
    dout_ref[tuple(digits)] = d_cross
    stats_ref[tuple(digits)] = lse + head_sums(d_cross.astype(full) * cross)
    refs = [dout_ref, stats_ref]
    sems = (send_all, recv_all)
    reach_out(peers, refs, sems)

    width = d_out.shape[1]
    for k in range(d_pre.shape[1] // width):
        columns = pl.ds(k * width, width)
        product = dot_left(second_low, d_pre[:, k * width : (k + 1) * width]).astype(low_type)
        g_up[:, :, :, :, :, columns] = product.reshape(g_out.shape)
    pass_on(peers, refs, sems)
    for k in range(hidden.shape[1] // width):
        product = dot_left(hidden[:, k * width : (k + 1) * width], d_down).astype(low_type)
        g_down[k // 2, k % 2] = product.reshape(g_down.shape[2:])
    g_out[...] = dot_left(cross_low, d_out).astype(low_type).reshape(g_out.shape)


def merge_cross(
    peers, acc_ref, st_ref, away, acc_one, st_one, low_out, st_out, acc_in, st_in,
    send, recv, send_two, recv_two,
):
    me = lax.axis_index("seq")
    core = me % 2
    pair = me // 2
    half = peers // 2
    mate = {"seq": other_of(me, 1)}
    greet([mate] + [{"seq": lax.rem(me + 2 * k, peers)} for k in range(1, half)])
    for j in range(half):
        away[j] = acc_ref[j, 1 - core].astype(low_type)
    first = [
        remote(away, acc_one, (send, recv), 0, mate),
        remote(st_ref.at[:, 1 - core], st_one, (send, recv), 1, mate),
    ]
    for copy in first:
        copy.start()
    for copy in first:
        copy.wait()
    rest = jnp.zeros((st_one.shape[1], LANES - 2 * SLOT), jnp.float32)

    def join(j):
        acc, top, total = merge_parts([acc_ref[j, core], acc_one[j]], [st_ref[j, core], st_one[j]])
        return acc, jnp.concatenate([top, total, rest], axis=1)

    def ship(k):
        j = lax.rem(pair + k, half)
        return [
            pltpu.make_async_remote_copy(
                src_ref=source.at[j],
                dst_ref=slot.at[half - k],
                send_sem=send_two.at[which, k],
                recv_sem=recv_two.at[which, half - k],
                device_id={"seq": lax.rem(me + 2 * k, peers)},
                device_id_type=pl.DeviceIdType.MESH,
            )
            for which, (source, slot) in enumerate(((low_out, acc_in), (st_out, st_in)))
        ]

    for k in range(1, half):
        j = lax.rem(pair + k, half)
        acc, stat = join(j)
        low_out[j] = acc.astype(low_type)
        st_out[j] = stat
        for copy in ship(k):
            copy.start()
    own_acc, own_stat = join(pair)
    for k in range(1, half):
        for copy in ship(k):
            copy.wait()
    return merge_parts(
        [own_acc] + [acc_in[k] for k in range(1, half)],
        [own_stat] + [st_in[k] for k in range(1, half)],
    )


def dec_middle(acc, stats, dec_first, cotangent, norms, weights):
    peers = lax.axis_size("seq")
    free = peers.bit_length() - 1
    half = peers // 2
    rows, width = dec_first.shape
    full = jnp.float32
    whole = pl.BlockSpec(memory_space=pltpu.VMEM)
    far = pl.BlockSpec(memory_space=pl.ANY)
    wide = weights[1].shape[1]
    lead = (2,) * free
    shapes = [
        ((rows, width), low_type),
        ((rows, width), full),
        (lead + (rows, width), low_type),
        (lead + (rows, LANES), full),
        (lead + (width // peers, wide), low_type),
        (lead + (wide // peers, width), low_type),
        (lead + (width // peers, width), low_type),
        ((4, width), full),
    ]
    sem = pltpu.SemaphoreType.DMA
    decoded, d_res, dout, all_stats, g_up, g_down, g_out, vec = pl.pallas_call(
        functools.partial(dec_middle_body, peers),
        in_specs=[whole] * 5 + [far] * 3,
        out_specs=[whole] * len(shapes),
        out_shape=[jax.ShapeDtypeStruct(shape, kind) for shape, kind in shapes],
        scratch_shapes=[pltpu.VMEM(weight.shape, low_type) for weight in weights]
        + [
            pltpu.VMEM((half, rows, width), low_type),
            pltpu.VMEM((half, rows, width), low_type),
            pltpu.VMEM((half, rows, LANES), full),
            pltpu.VMEM((half, rows, width), low_type),
            pltpu.VMEM((half, rows, LANES), full),
            pltpu.VMEM((half, rows, width), low_type),
            pltpu.VMEM((half, rows, LANES), full),
            sem((3,)),
            sem((2,)),
            sem((2,)),
            sem((2, half)),
            sem((2, half)),
            sem((2 * peers,)),
            sem((2 * peers,)),
        ],
        compiler_params=pltpu.CompilerParams(
            collective_id=4, has_side_effects=True, vmem_limit_bytes=vmem_bytes
        ),
    )(
        acc.reshape(half, 2, rows, width), stats.reshape(half, 2, rows, LANES),
        dec_first, cotangent, norms, *weights,
    )
    return (
        decoded, d_res, dout.reshape(-1, width), all_stats.reshape(-1, LANES),
        (g_up, g_down, g_out), vec,
    )


def resumed(peers, piece, array, k, first, last):
    stages = piece["stages"]
    width = array.shape[-1] * (2 if "dp" in stages[:first] else 1)
    shapes = piece_shapes(peers, array.shape[-2], width, stages)
    return (
        {"from": ("kept", k), "stages": stages, "first": first, "last": last},
        shapes[first : last + 1],
    )


def window_back_body(
    peers, parts, rows_block, blocks, pieces, held_counts, turns, *refs
):
    refs = list(refs)

    def take(count):
        result = refs[:count]
        del refs[:count]
        return result

    q_ref, k_ref, v_ref, d_ref, st_ref, use_ref, part_ref = take(7)
    factors = take(5)
    kept = take(3)
    mats = take(2)
    dec_in = take(16)
    dq_ref, dk_ref, dv_ref, sum_copy = take(4)
    outs = take(len(pieces))
    dec_out = take(8)
    key_sum, val_sum, bias_ref, slot, sum_ref = take(5)
    sems = take(4)
    send, recv, load = take(3)
    held = [take(count) for count in held_counts]
    own = take(2)
    staging = take(3)
    dec_scratch = take(8)
    step = pl.program_id(0)
    work = Pieces(
        peers, pieces, mats, factors, kept, outs, (send, recv), load, held, own, staging, 0
    )
    for p, piece in enumerate(pieces):
        for s in range(piece["first"], piece["last"] + 1):
            work.number(p, s)

    @pl.when(step == 0)
    def _():
        greet(everyone(peers) + [work.partner("dp")])
        send_in(peers, [part_ref], [slot], sems)
        work.open(turns[0])
        work.open(turns[2])
        work.open(turns[1])
        keys = lax.broadcasted_iota(jnp.int32, bias_ref.shape, 0)
        rows = lax.broadcasted_iota(jnp.int32, bias_ref.shape, 1)
        near = (jnp.abs(rows + HALF - keys) <= HALF) | (keys >= bias_ref.shape[1] + 2 * HALF)
        bias_ref[...] = jnp.where(near, use_ref[...], masked_score)

    @pl.when(step == 1)
    def _():
        work.move(turns[2], 0)
        sum_at_owner(peers, part_ref, slot, sum_ref, sems)
        send_out(peers, [sum_ref], sems)

    @pl.when(step == 2)
    def _():
        work.move(turns[1], 0)

    backward_body(
        parts, rows_block, blocks, 1, q_ref, k_ref, v_ref, d_ref, st_ref, bias_ref,
        dq_ref, dk_ref, dv_ref, key_sum, val_sum,
    )

    @pl.when(step == PAIRS - 1)
    def _():
        take_out(peers, [sum_ref], sems)
        left(peers, [part_ref], [slot], sems)
        sum_copy[...] = sum_ref[...]
        dec_back_body(*dec_in, *dec_out, *dec_scratch)
        work.move(turns[0], 2)
        work.move(turns[2], 1)
        work.move(turns[1], 1)


def window_attend_back(
    queries, keys, values, grads, stats, use, parts, rows_block, glob_part, pairs, made, kept, begun,
    limit, dec_inputs
):
    peers = lax.axis_size("seq")
    free = peers.bit_length() - 1
    lead = (2,) * free
    count, width = queries.shape
    key_count = keys.shape[0]
    rows = glob_part.shape[0] // OWNERS
    flops = 10 * count * key_count * width
    factors = []
    places = []
    for pair in pairs:
        spots = []
        for factor in pair:
            known = [k for k, other in enumerate(factors) if other is factor]
            if not known:
                factors.append(factor)
                known = [len(factors) - 1]
            spots.append(known[0])
        places.append(tuple(spots))
    mats = list(made)
    block_rows = width // peers
    plans = [resumed(peers, piece, array, k, 2, 2) for k, (piece, array) in enumerate(zip(begun, kept))]
    plans += [
        piece_plan(peers, ("made", k), block_rows, width, kind, 0, 1, pair)
        for k, (pair, kind) in enumerate(zip(places, "xyz"))
    ]
    plans += [
        piece_plan(peers, ("mat", k), *mat.shape[-2:], kind, 0, 1)
        for k, (mat, kind) in enumerate(zip(mats, "xy"))
    ]
    pieces = [plan for plan, _ in plans]
    shapes = [shape for _, shape in plans]
    sem_count = sum(len(shape) for shape in shapes)
    mine = dec_inputs[0].shape[0]
    dec_keys = dec_inputs[5].shape[0]
    full = jnp.float32
    dec_shapes = [((mine, width), low_type)] * 3 + [((dec_keys, width), low_type)] * 2
    dec_shapes += [((mine, width), full), ((dec_keys, width), low_type), ((2, width), full)]

    def pair_block(size):
        return pl.BlockSpec((size, LANES), lambda p, i: (0, p))

    def whole(*shape):
        return pl.BlockSpec(
            shape, lambda p, i: (0,) * len(shape), pipeline_mode=pl.Buffered(1)
        )

    def whole_out(*shape):
        return pl.BlockSpec(shape, lambda p, i: (0,) * len(shape))

    outs = pl.pallas_call(
        functools.partial(
            window_back_body, peers, parts, rows_block, count // rows_block, pieces,
            [len(shape) for shape in shapes], [[0, 1, 2], [3, 4, 5], [6, 7]],
        ),
        grid=(PAIRS, 1),
        in_specs=[
            pair_block(count),
            pair_block(key_count),
            pair_block(key_count),
            pair_block(count),
            whole(2 * SLOT, count),
            whole(key_count, 1),
            whole(OWNERS, rows, width),
        ]
        + [whole(*array.shape) for array in factors + list(kept)]
        + [pl.BlockSpec(memory_space=pl.ANY)] * len(mats)
        + [pl.BlockSpec(memory_space=pltpu.SMEM)]
        + [whole(*array.shape) for array in dec_inputs],
        out_specs=[
            pair_block(count),
            pair_block(key_count),
            pair_block(key_count),
            whole_out(OWNERS, rows, width),
        ]
        + [whole_out(*shape[-1]) for shape in shapes]
        + [whole_out(*shape) for shape, _ in dec_shapes],
        out_shape=[
            jax.ShapeDtypeStruct((count, width), low_type),
            jax.ShapeDtypeStruct((key_count, width), low_type),
            jax.ShapeDtypeStruct((key_count, width), low_type),
            jax.ShapeDtypeStruct((OWNERS, rows, width), low_type),
        ]
        + [jax.ShapeDtypeStruct(shape[-1], low_type) for shape in shapes]
        + [jax.ShapeDtypeStruct(shape, kind) for shape, kind in dec_shapes],
        scratch_shapes=[
            pltpu.VMEM((key_count, LANES), jnp.float32),
            pltpu.VMEM((key_count, LANES), jnp.float32),
            pltpu.VMEM((key_count, count), jnp.float32),
            pltpu.VMEM((peers, rows, width), low_type),
            pltpu.VMEM((OWNERS, rows, width), low_type),
        ]
        + owner_sems(peers, 1)
        + [pltpu.SemaphoreType.DMA((sem_count,))] * 2
        + [pltpu.SemaphoreType.DMA((2 * len(mats),))]
        + [pltpu.VMEM(one, low_type) for shape in shapes for one in shape]
        + [pltpu.VMEM((2, 2) + mat.shape[-2:], low_type) for mat in mats]
        + [pltpu.VMEM(lead + (block_rows, width), low_type)] * 3
        + [
            pltpu.VMEM((LANES, width), low_type),
            pltpu.VMEM((LANES, width), low_type),
            pltpu.VMEM((LANES, LANES), full),
            pltpu.VMEM((LANES, LANES), full),
            pltpu.VMEM((dec_keys, LANES), full),
            pltpu.VMEM((LANES, width), full),
            pltpu.VMEM((dec_keys, width), full),
            pltpu.VMEM((dec_keys, width), full),
        ],
        compiler_params=pltpu.CompilerParams(
            collective_id=7, has_side_effects=True, vmem_limit_bytes=62 * 2**20
        ),
        cost_estimate=pl.CostEstimate(
            flops=4 * flops,
            bytes_accessed=2 * (2 * count + 4 * key_count) * width + 4 * count * width,
            transcendentals=count * key_count * HEADS,
        ),
    )(
        queries, keys, values, grads, stats, use, glob_part.reshape(OWNERS, rows, width),
        *factors, *kept, *mats, limit, *dec_inputs,
    )
    last = 4 + len(pieces)
    return outs[:3], outs[3].reshape(-1, width), outs[4:last], pieces, outs[last:]


def last_body(peers, plan, *refs):
    refs = list(refs)

    def take(count):
        result = refs[:count]
        del refs[:count]
        return result

    pieces = plan["pieces"]
    kept = take(plan["kept"])
    factors = take(plan["factors"])
    target_part, vec_part = take(2)
    enc_in = take(plan["enc_in"])
    outs = take(len(pieces))
    target_out, glob_out, vec_out, from_after, from_before, source_ref = take(6)
    send, recv, fetch = take(3)
    held = [take(count) for count in plan["held"]]
    staging = take(plan["slots"])
    tall, late = plan["tall"], enc_in[8:]
    nears = take(len(tall) + len(late))
    fars = [factors[k] for k in tall] + late
    for k, near in zip(tall, nears):
        factors[k] = near
    enc_in[8:] = nears[len(tall) :]
    target_held = take(plan["free"])
    glob_held = take(plan["free"])
    vec_held = take(plan["free"] + 1)
    d_gk, d_gv, d_gq, d_q, rim, glob_part = take(6)
    enc_scratch = take(8)
    me = lax.axis_index("seq")
    bits = [1 << k for k in range(plan["free"])]
    own_x = factors[plan["rows"]].at[pl.ds(HALF, d_q.shape[0]), :]
    work = Pieces(
        peers, pieces, [], factors + [d_gk, d_gv, d_gq, d_q, own_x], kept, outs, (send, recv), None, held,
        [], staging, 0
    )
    left_one = {"seq": lax.rem(me + peers - 1, peers)}
    right_one = {"seq": lax.rem(me + 1, peers)}
    greet([work.partner(stage) for stage in bits + ["dp"]] + [left_one, right_one])
    sems = (send, recv)
    to_left = remote(rim.at[0], from_after, sems, work.number("left"), left_one)
    to_right = remote(rim.at[1], from_before, sems, work.number("right"), right_one)

    target_stages = bits
    vec_stages = bits + ["dp"]

    def target_copy(s):
        origin = target_part if s == 0 else target_held[s - 1]
        return work.copy("t", target_stages, origin, target_held[s], s), origin

    def whole_copy(name, part, result, buffers, stages, s):
        origin = part if s == 0 else result
        copy = remote(
            origin, buffers[s], sems, work.number(name, s), work.partner(stages[s])
        )
        return copy, origin

    def small_begin(s):
        if s < len(bits):
            target_copy(s)[0].start()
            whole_copy("g", glob_part, glob_out, glob_held, bits, s)[0].start()
        whole_copy("v", vec_part, vec_out, vec_held, vec_stages, s)[0].start()

    def small_end(s):
        if s < len(bits):
            copy, origin = target_copy(s)
            copy.wait()
            finish = target_out if s == len(bits) - 1 else None
            work.fold(target_stages, origin, target_held[s], s, finish)
            copy, origin = whole_copy("g", glob_part, glob_out, glob_held, bits, s)
            copy.wait()
            glob_out[...] = origin[...] + glob_held[s][...]
        copy, origin = whole_copy("v", vec_part, vec_out, vec_held, vec_stages, s)
        copy.wait()
        vec_out[...] = origin[...] + vec_held[s][...]

    turns = plan["turns"]
    work.open(turns[0])
    work.open(turns[5])
    fetched = bring(fars, nears, fetch)
    work.open(turns[1])
    work.move(turns[1], 0)
    work.open(turns[2])
    for copy in fetched:
        copy.wait()
    keys, vals = (factors[k] for k in plan["shared"])
    enc_last_body(*enc_in[:8], keys, vals, *enc_in[8:], d_gk, d_gv, d_gq, d_q, rim, glob_part, source_ref, *enc_scratch)

    @pl.when(me > 0)
    def _():
        to_left.start()

    @pl.when(me < peers - 1)
    def _():
        to_right.start()

    small_begin(0)
    work.move(turns[5], 3)
    work.move(turns[2], 0)
    work.move(turns[0], 2)
    work.open(turns[3])
    work.move(turns[5], 4)
    work.move(turns[1], 1)
    work.move(turns[3], 0)
    work.move(turns[2], 1)
    work.move(turns[0], 3)
    small_end(0)
    small_begin(1)
    work.open(turns[4])
    work.move(turns[1], 2)
    work.move(turns[4], 0)
    work.move(turns[3], 1)
    work.move(turns[2], 2)
    work.move(turns[0], 4)
    work.move(turns[1], 3)
    small_end(1)
    small_begin(2)
    work.move(turns[4], 1)
    work.move(turns[3], 2)
    work.move(turns[2], 3)
    work.move(turns[1], 4)
    small_end(2)
    small_begin(3)
    work.move(turns[4], 2)
    work.move(turns[3], 3)
    work.move(turns[2], 4)
    small_end(3)
    small_begin(4)
    work.move(turns[4], 3)
    work.move(turns[3], 4)
    small_end(4)
    work.move(turns[4], 4)

    @pl.when(me > 0)
    def _():
        to_left.wait_send()
        remote(rim.at[1], from_before, sems, work.number("right"), left_one).wait_recv()

    @pl.when(me < peers - 1)
    def _():
        to_right.wait_send()
        remote(rim.at[0], from_after, sems, work.number("left"), right_one).wait_recv()


KINDS = "xyxxyxxxyxx"


def last_exchange(kept, begun, pairs, enc_inputs, target_part, vec_part):
    peers = lax.axis_size("seq")
    free = peers.bit_length() - 1
    lead = (2,) * free
    full = jnp.float32
    factors = []
    spots = []
    for pair in pairs:
        spot = []
        for factor in pair:
            if isinstance(factor, int):
                spot.append(factor - 5)
                continue
            known = [k for k, other in enumerate(factors) if other is factor]
            if not known:
                factors.append(factor)
                known = [len(factors) - 1]
            spot.append(known[0])
        spots.append(tuple(spot))
    width = pairs[0][0].shape[1]
    rows = width // peers
    slots = 6
    last = free
    plans = [
        resumed(peers, piece, array, k, piece["last"] + 1, last)
        for k, (piece, array) in enumerate(zip(begun, kept))
    ]
    order = [0, 1, 2, 3, 4, 5, 6, 7, 8, 9, 10]
    for k, spot in zip(order, spots):
        slot = k if k < 3 else (k if k < 5 else (k - 5) % 6)
        plans.append(piece_plan(peers, ("made", slot), rows, width, KINDS[k], 0, last, spot))
    pieces = [plan for plan, _ in plans]
    shapes = [shape for _, shape in plans]
    begun_count = len(begun)
    made = list(range(begun_count, len(pieces)))
    far_on = [k for k, piece in enumerate(begun) if piece["last"] == 2]
    fresh = [k for k in range(begun_count) if k not in far_on]
    turns = [fresh, made[:3], made[3:5], made[5:8], made[8:], far_on]
    target_shapes = piece_shapes(
        peers, target_part.shape[0] // peers, width, [1 << k for k in range(free)]
    )
    few = enc_inputs[0].shape[0]
    count = enc_inputs[1].shape[0]
    narrow = (count, width)
    tall = [k for k, factor in enumerate(factors) if factor.shape[0] > count]
    late = enc_inputs[8:]
    far = pl.BlockSpec(memory_space=pl.ANY)
    plan = {
        "pieces": pieces,
        "kept": begun_count,
        "factors": len(factors),
        "enc_in": len(enc_inputs),
        "held": [len(shape) for shape in shapes],
        "slots": slots,
        "turns": turns,
        "free": free,
        "shared": (spots[6][1], spots[7][1]),
        "rows": spots[6][0],
        "tall": tall,
    }
    sems = sum(len(shape) for shape in shapes) + free * 3 + 3
    whole = pl.BlockSpec(memory_space=pltpu.VMEM)
    out_shapes = [(shape[-1], full) for shape in shapes] + [
        (target_shapes[-1], full),
        ((few, width), low_type),
        (vec_part.shape, full),
        ((HALF, width), low_type),
        ((HALF, width), low_type),
        (narrow, full),
    ]
    sem = pltpu.SemaphoreType.DMA((sems,))
    outs = pl.pallas_call(
        functools.partial(last_body, peers, plan),
        in_specs=[whole] * begun_count
        + [far if k in tall else whole for k in range(len(factors))]
        + [whole] * 10
        + [far] * len(late),
        out_specs=[whole] * len(out_shapes),
        out_shape=[jax.ShapeDtypeStruct(shape, kind) for shape, kind in out_shapes],
        scratch_shapes=[sem, sem, pltpu.SemaphoreType.DMA((len(tall) + len(late),))]
        + [pltpu.VMEM(one, low_type) for shape in shapes for one in shape]
        + [pltpu.VMEM(lead + (rows, width), low_type)] * slots
        + [pltpu.VMEM(factors[k].shape, low_type) for k in tall]
        + [pltpu.VMEM(array.shape, array.dtype) for array in late]
        + [pltpu.VMEM(shape, low_type) for shape in target_shapes]
        + [pltpu.VMEM((few, width), low_type)] * free
        + [pltpu.VMEM(vec_part.shape, full)] * (free + 1)
        + [
            pltpu.VMEM(narrow, low_type),
            pltpu.VMEM(narrow, low_type),
            pltpu.VMEM((few, width), low_type),
            pltpu.VMEM(narrow, low_type),
            pltpu.VMEM((2, HALF, width), low_type),
            pltpu.VMEM((few, width), low_type),
            pltpu.VMEM((LANES, width), low_type),
            pltpu.VMEM((LANES, width), low_type),
            pltpu.VMEM((LANES, LANES), full),
            pltpu.VMEM((LANES, LANES), full),
            pltpu.VMEM((count, LANES), full),
            pltpu.VMEM((LANES, width), full),
            pltpu.VMEM(narrow, full),
            pltpu.VMEM(narrow, full),
        ],
        compiler_params=pltpu.CompilerParams(
            collective_id=1, has_side_effects=True, vmem_limit_bytes=63 * 2**20
        ),
    )(
        *kept, *factors, target_part.reshape(lead + (-1, width)), vec_part, *enc_inputs
    )
    return outs[: len(pieces)], outs[len(pieces) :]


def per_device(
    source,
    target,
    cotangent,
    src_len,
    dec_len,
    global_pos,
    enc_query,
    enc_key,
    enc_value,
    glob_query,
    glob_key,
    glob_value,
    enc_out,
    enc_attn_gain,
    enc_attn_shift,
    enc_up,
    enc_down,
    enc_ffn_gain,
    enc_ffn_shift,
    self_query,
    self_key,
    self_value,
    self_out,
    dec_self_gain,
    dec_self_shift,
    cross_query,
    cross_key,
    cross_value,
    cross_out,
    dec_cross_gain,
    dec_cross_shift,
    dec_up,
    dec_down,
    dec_ffn_gain,
    dec_ffn_shift,
):
    full = jnp.float32
    src_x = source[0]
    dec_x = target[0]
    src_count = src_x.shape[0]
    dec_count = dec_x.shape[0]
    seq_index = lax.axis_index("seq")
    peers = lax.axis_size("seq")
    src_limit = src_len[0]
    glob_places = global_pos[0]
    glob_count = glob_places.shape[0]
    src_places = seq_index * src_count + jnp.arange(src_count, dtype=jnp.int32)
    select_glob = glob_places[:, None] == src_places[None, :]
    select_low = select_glob.astype(low_type)
    norms = jnp.concatenate(
        [
            enc_attn_gain, enc_attn_shift, enc_ffn_gain, enc_ffn_shift, dec_self_gain,
            dec_self_shift, dec_cross_gain, dec_cross_shift, dec_ffn_gain, dec_ffn_shift,
        ]
    ).astype(full).reshape(10, -1)

    upward = [(i, i + 1) for i in range(peers - 1)]
    downward = [(i + 1, i) for i in range(peers - 1)]
    dec_all, glob_x, query_loc, glob_keys_loc, glob_vals_loc = start_exchange(
        dec_x,
        dot_plain(select_low, src_x).astype(low_type),
        src_x,
        (enc_query, glob_key, glob_value),
    )
    rim_x, _ = lax.optimization_barrier((src_x, glob_x))
    before = lax.ppermute(rim_x[src_count - HALF :], "seq", upward)
    after = lax.ppermute(rim_x[:HALF], "seq", downward)

    (self_k, self_v, all_cross_q, self_q, self_out_full, self_attn, self_stats, dec_first,
     self_unit, self_rate) = dec_front(
        dec_len,
        dec_all,
        (self_query, self_key, self_value, self_out, cross_query),
        norms,
        dec_count,
    )

    glob_queries = (dot_plain(glob_x, glob_query) * 0.125).astype(low_type)
    live_bias = jnp.where(src_places < src_limit, 0.0, masked_score)
    glob_acc, glob_stats = attend(
        glob_queries, glob_keys_loc, glob_vals_loc, live_bias[None, :], None, glob_count, False, 6
    )

    x_all, keys_all, vals_all = project_all((before, src_x, after, glob_x), enc_key, enc_value)
    pad_count = src_count + 2 * HALF
    pad_places = seq_index * src_count - HALF + jnp.arange(pad_count, dtype=jnp.int32)
    pad_glob = jnp.any(glob_places[:, None] == pad_places[None, :], axis=0)
    pad_use = (pad_places >= 0) & (pad_places < src_limit) & jnp.logical_not(pad_glob)
    win_use = jnp.concatenate(
        [jnp.where(pad_use, 0.0, masked_score), jnp.zeros((glob_count,), full)]
    )
    keep = jnp.where(pad_glob[HALF : HALF + src_count], 0.0, 1.0)[:, None]
    rows_block = 256
    reach = rows_block + 2 * HALF
    win_parts = [
        ((block * rows_block, reach), (pad_count, glob_count))
        for block in range(src_count // rows_block)
    ]
    win_out, win_stats, glob_out, glob_lse = window_attend(
        query_loc, keys_all, vals_all, win_use[None, :], win_parts, rows_block, glob_acc, glob_stats
    )
    (enc_attn, unit_one, rate_one, enc_first_low, enc_hidden, enc_slope, unit_two, rate_two,
     memory_low, cross_k, cross_v) = enc_front(
        win_out,
        keep,
        select_low,
        glob_out.astype(low_type),
        src_x,
        (enc_out, enc_up, enc_down, cross_key, cross_value),
        norms,
    )

    cross_acc, cross_stats = attend(
        all_cross_q, cross_k, cross_v, live_bias[None, :], None, 256, False, 2
    )
    decoded, d_res_two, all_dout, all_stats, dec_made, dec_vec = dec_middle(
        cross_acc, cross_stats, dec_first, cotangent[0], norms, (cross_out, dec_up, dec_down)
    )
    query_parts, ck_low, cv_low = attend_back(
        all_cross_q,
        cross_k,
        cross_v,
        all_dout,
        all_stats[:, : 2 * SLOT].T,
        jnp.broadcast_to(live_bias[:, None], (src_count, 512)),
        None,
        256,
        2,
    )

    enc_grads, enc_made, dec_kept, dec_begun = enc_back(
        query_parts,
        ck_low,
        cv_low,
        (unit_two, rate_two, rate_one, keep, select_low),
        (cross_key, cross_value),
        norms,
        dec_made,
        (enc_down, enc_up, enc_slope, unit_one, enc_out, win_out, enc_hidden, enc_first_low),
    )
    (d_enc_down, d_enc_pre, d_enc_res, d_attn_o, d_window, win_delta, glob_part, enc_vec,
     d_cross_sum) = enc_grads
    win_pair = (win_stats + win_delta)[:, : 2 * SLOT].T
    (d_query, d_keys_all, d_vals_all), glob_dout, kept, begun, dec_grads = window_attend_back(
        query_loc, keys_all, vals_all, d_window, win_pair, win_use[:, None], win_parts, rows_block,
        glob_part,
        [(memory_low, ck_low), (memory_low, cv_low), (enc_attn, d_attn_o)],
        enc_made,
        dec_kept,
        dec_begun,
        dec_len,
        (d_cross_sum, d_res_two, self_unit, self_rate, self_q, self_k, self_v, self_out_full,
         self_stats, cross_query, self_out, self_query, self_key, self_value, norms),
    )
    (d_cross_q, d_self_o, d_self_q, d_self_k, d_self_v, d_target_own, d_target_part,
     self_vec) = dec_grads
    vec_part = jnp.concatenate(
        [enc_vec, self_vec, dec_vec, jnp.zeros((6, enc_vec.shape[1]), full)], axis=0
    )

    own_gk, own_gv, own_gq, own_q, own_x = range(5)
    pairs = [
        (dec_first.astype(low_type), d_cross_q),
        (self_attn, d_self_o),
        (dec_x, d_self_q),
        (dec_all, d_self_k),
        (dec_all, d_self_v),
        (own_x, own_q),
        (x_all, d_keys_all),
        (x_all, d_vals_all),
        (own_x, own_gk),
        (own_x, own_gv),
        (glob_x, own_gq),
    ]
    shared, rest = last_exchange(
        kept,
        begun,
        pairs,
        (glob_queries, glob_keys_loc, glob_vals_loc, glob_dout, glob_out, glob_lse,
         live_bias[:, None], d_query, d_enc_res,
         enc_query, enc_key, enc_value, glob_query, glob_key, glob_value),
        d_target_part,
        vec_part,
    )
    d_target_sum, d_glob_x, vec_sum, from_after, from_before, d_source_own = rest
    vectors = share_vectors(vec_sum, 10)
    flags = jnp.stack([seq_index < peers - 1, seq_index > 0]).astype(jnp.int32)[None, :]
    (
        s_dec_up, s_dec_down, s_cross_out,
        s_cross_key, s_cross_value, s_enc_out, s_enc_up, s_enc_down, s_cross_query, s_self_out,
        s_self_query, s_self_key, s_self_value,
        s_enc_query, s_enc_key, s_enc_value, s_glob_key, s_glob_value, s_glob_query,
        d_source, d_target,
    ) = end_outputs(
        shared,
        (d_source_own, from_after, from_before, select_low, d_glob_x, flags),
        (d_target_own, d_target_sum),
    )
    return (
        decoded[None],
        d_source[None],
        d_target[None],
        s_enc_query,
        s_enc_key,
        s_enc_value,
        s_glob_query,
        s_glob_key,
        s_glob_value,
        s_enc_out,
        vectors[0],
        vectors[1],
        s_enc_up,
        s_enc_down,
        vectors[2],
        vectors[3],
        s_self_query,
        s_self_key,
        s_self_value,
        s_self_out,
        vectors[4],
        vectors[5],
        s_cross_query,
        s_cross_key,
        s_cross_value,
        s_cross_out,
        vectors[6],
        vectors[7],
        s_dec_up,
        s_dec_down,
        vectors[8],
        vectors[9],
    )


def swap_dp(value):
    pairs = [(i, i ^ 1) for i in range(lax.axis_size("dp"))]
    return lax.ppermute(value, "dp", pairs)


def gather_rows(value):
    rows, width = value.shape
    held = value[None]
    for bit in reversed(seq_bits()):
        other = swap(held, bit)
        upper = bit_set(bit)
        held = jnp.stack(
            [jnp.where(upper, other, held), jnp.where(upper, held, other)], axis=1
        ).reshape(2 * held.shape[0], rows, width)
    return held.reshape(-1, width)


def add_all(value):
    for bit in seq_bits():
        value = value + swap(value, bit)
    return value


def scatter_all(value):
    bits = seq_bits()
    held = value.reshape((2,) * len(bits) + (-1, value.shape[1]))
    for step, bit in enumerate(bits):
        axis = len(bits) - 1 - step
        mine = bit_set(bit).astype(jnp.int32)
        other = swap(pick_half(held, 1 - mine, axis).astype(low_type), bit)
        held = pick_half(held, mine, axis) + other.astype(jnp.float32)
    return held


def merge_body(acc_a, st_a, acc_b, st_b, acc_o, st_o):
    top_a, top_b = st_a[:, :SLOT], st_b[:, :SLOT]
    top = jnp.maximum(top_a, top_b)
    keep_a = jnp.exp(top_a - top)
    keep_b = jnp.exp(top_b - top)
    total = st_a[:, SLOT : 2 * SLOT] * keep_a + st_b[:, SLOT : 2 * SLOT] * keep_b
    spread = head_spread()
    acc_o[...] = acc_a[...] * exact_dot(keep_a, spread) + acc_b[...].astype(
        jnp.float32
    ) * exact_dot(keep_b, spread)
    rest = jnp.zeros((top.shape[0], LANES - 2 * SLOT), jnp.float32)
    st_o[...] = jnp.concatenate([top, total, rest], axis=1)


def merge_soft(held, other):
    rows = held[0].shape[0]
    return pl.pallas_call(
        merge_body,
        out_shape=[
            jax.ShapeDtypeStruct((rows, held[0].shape[1]), jnp.float32),
            jax.ShapeDtypeStruct((rows, LANES), jnp.float32),
        ],
        compiler_params=pltpu.CompilerParams(vmem_limit_bytes=vmem_bytes),
    )(*held, *other)


def merge_all(held):
    for bit in seq_bits():
        held = merge_soft(held, swap((held[0].astype(low_type), held[1]), bit))
    return held


def merge_scatter(held):
    bits = seq_bits()
    for step, bit in enumerate(bits):
        inner = len(bits) - 1 - step
        mine = bit_set(bit).astype(jnp.int32)

        def halves(value, chosen):
            split = value.reshape(1 << inner, 2, -1, value.shape[1])
            return pick_half(split, chosen, 1).reshape(-1, value.shape[1])

        away = (halves(held[0], 1 - mine).astype(low_type), halves(held[1], 1 - mine))
        held = merge_soft((halves(held[0], mine), halves(held[1], mine)), swap(away, bit))
    return held


def share_grads(grads, dp_first):
    bits = seq_bits()
    width = grads[0].shape[1]
    half = width // 2
    rows = [grad.shape[0] >> len(bits) for grad in grads]
    dp_mine = lax.axis_index("dp")
    laid = [
        grad.astype(low_type).reshape((2,) * len(bits) + (count, width))
        for grad, count in zip(grads, rows)
    ]
    steps = [(1, False)]
    rest = [(bit, False) for bit in bits[1:]]
    steps += [(0, True)] + rest if dp_first else rest[:1] + [(0, True)] + rest[1:]
    held = None
    axis = len(bits)
    for bit, is_dp in steps:
        if is_dp:
            own = lax.dynamic_slice_in_dim(held, dp_mine * half, half, held.ndim - 1)
            away = lax.dynamic_slice_in_dim(held, (1 - dp_mine) * half, half, held.ndim - 1)
            held = own + swap_dp(away)
            continue
        axis -= 1
        mine = bit_set(bit).astype(jnp.int32)
        if held is None:
            away = jnp.concatenate([pick_half(v, 1 - mine, axis) for v in laid], axis=-2)
            own = jnp.concatenate([pick_half(v, mine, axis) for v in laid], axis=-2)
        else:
            away = pick_half(held, 1 - mine, axis)
            own = pick_half(held, mine, axis)
        held = own + swap(away, bit)
    result = []
    start = 0
    for count in rows:
        result.append(held[start : start + count].astype(jnp.float32))
        start += count
    return result


def share_norms(vectors):
    stacked = jnp.concatenate([jnp.stack(vectors), jnp.zeros((6, vectors[0].shape[0]))], axis=0)
    total = add_all(stacked)
    total = total + swap_dp(total)
    length = stacked.shape[1] // lax.axis_size("seq")
    mine = lax.dynamic_slice_in_dim(total, lax.axis_index("seq") * length, length, 1)
    return [mine[k] for k in range(len(vectors))]


def per_device_wide(
    source,
    target,
    cotangent,
    src_len,
    dec_len,
    global_pos,
    enc_query,
    enc_key,
    enc_value,
    glob_query,
    glob_key,
    glob_value,
    enc_out,
    enc_attn_gain,
    enc_attn_shift,
    enc_up,
    enc_down,
    enc_ffn_gain,
    enc_ffn_shift,
    self_query,
    self_key,
    self_value,
    self_out,
    dec_self_gain,
    dec_self_shift,
    cross_query,
    cross_key,
    cross_value,
    cross_out,
    dec_cross_gain,
    dec_cross_shift,
    dec_up,
    dec_down,
    dec_ffn_gain,
    dec_ffn_shift,
):
    full = jnp.float32
    src_x = source[0]
    dec_x = target[0]
    src_count = src_x.shape[0]
    dec_count = dec_x.shape[0]
    seq_index = lax.axis_index("seq")
    peers = lax.axis_size("seq")
    src_limit = src_len[0]
    dec_limit = dec_len[0]
    glob_places = global_pos[0]
    glob_count = glob_places.shape[0]
    src_places = seq_index * src_count + jnp.arange(src_count, dtype=jnp.int32)
    select_glob = glob_places[:, None] == src_places[None, :]
    select_low = select_glob.astype(low_type)
    is_global = jnp.any(select_glob, axis=0)
    spread = head_spread()

    upward = [(i, i + 1) for i in range(peers - 1)]
    downward = [(i + 1, i) for i in range(peers - 1)]
    before = lax.ppermute(src_x[src_count - HALF :], "seq", upward)
    after = lax.ppermute(src_x[:HALF], "seq", downward)
    dec_all = gather_rows(dec_x)
    glob_x = add_all(dot_plain(select_low, src_x).astype(low_type))

    query_loc = (dot_plain(src_x, enc_query) * 0.125).astype(low_type)
    glob_keys_loc = dot_plain(src_x, glob_key).astype(low_type)
    glob_vals_loc = dot_plain(src_x, glob_value).astype(low_type)

    self_q = (dot_plain(dec_x, self_query) * 0.125).astype(low_type)
    self_k = dot_plain(dec_all, self_key).astype(low_type)
    self_v = dot_plain(dec_all, self_value).astype(low_type)
    dec_total = dec_all.shape[0]
    dec_places = seq_index * dec_count + jnp.arange(dec_count, dtype=jnp.int32)
    all_dec = jnp.arange(dec_total, dtype=jnp.int32)
    self_allowed = (all_dec[None, :] <= dec_places[:, None]) & (all_dec < dec_limit)[None, :]
    self_bias = jnp.where(self_allowed, 0.0, masked_score)
    self_out_full, self_stats = attend(self_q, self_k, self_v, self_bias, None, dec_count, True)
    self_attn = self_out_full.astype(low_type)
    dec_res_one = dec_x.astype(full) + dot_plain(self_attn, self_out)
    dec_first, dec_first_back = jax.vjp(
        layer_norm, dec_res_one, dec_self_gain.astype(full), dec_self_shift.astype(full)
    )
    dec_first_low = dec_first.astype(low_type)
    cross_q = (dot_plain(dec_first_low, cross_query) * 0.125).astype(low_type)
    all_cross_q = gather_rows(cross_q)

    glob_queries = (dot_plain(glob_x, glob_query) * 0.125).astype(low_type)
    live_bias = jnp.where(src_places < src_limit, 0.0, masked_score)
    glob_acc, glob_stats = merge_all(
        attend(
            glob_queries, glob_keys_loc, glob_vals_loc, live_bias[None, :], None, glob_count, False
        )
    )
    glob_total = glob_stats[:, SLOT : 2 * SLOT]
    glob_out = glob_acc / exact_dot(glob_total, spread)
    glob_lse = glob_stats[:, :SLOT] + jnp.log(jnp.maximum(glob_total, 1e-30))

    x_all = jnp.concatenate([before, src_x, after, glob_x], axis=0)
    keys_all = dot_plain(x_all, enc_key).astype(low_type)
    vals_all = dot_plain(x_all, enc_value).astype(low_type)
    pad_count = src_count + 2 * HALF
    pad_places = seq_index * src_count - HALF + jnp.arange(pad_count, dtype=jnp.int32)
    pad_glob = jnp.any(glob_places[:, None] == pad_places[None, :], axis=0)
    pad_use = (pad_places >= 0) & (pad_places < src_limit) & jnp.logical_not(pad_glob)
    near = jnp.abs(src_places[:, None] - pad_places[None, :]) <= HALF
    win_bias = jnp.concatenate(
        [
            jnp.where(near & pad_use[None, :], 0.0, masked_score),
            jnp.zeros((src_count, glob_count), full),
        ],
        axis=1,
    )
    near_turned = jnp.abs(src_places[None, :] - pad_places[:, None]) <= HALF
    win_bias_turned = jnp.concatenate(
        [
            jnp.where(near_turned & pad_use[:, None], 0.0, masked_score),
            jnp.zeros((glob_count, src_count), full),
        ],
        axis=0,
    )
    rows_block = 256
    reach = rows_block + 2 * HALF
    win_parts = [
        ((block * rows_block, reach), (pad_count, glob_count))
        for block in range(src_count // rows_block)
    ]
    win_out, win_stats = attend(
        query_loc, keys_all, vals_all, win_bias, win_parts, rows_block, True
    )
    placed = dot_left(select_low, glob_out.astype(low_type))
    enc_attn = jnp.where(is_global[:, None], placed, win_out).astype(low_type)
    enc_res = src_x.astype(full) + dot_plain(enc_attn, enc_out)
    enc_first, enc_first_back = jax.vjp(
        layer_norm, enc_res, enc_attn_gain.astype(full), enc_attn_shift.astype(full)
    )
    enc_first_low = enc_first.astype(low_type)
    enc_hidden, enc_slope = gelu_pair(dot_plain(enc_first_low, enc_up))
    enc_second = enc_first + dot_plain(enc_hidden, enc_down)
    memory, enc_final_back = jax.vjp(
        layer_norm, enc_second, enc_ffn_gain.astype(full), enc_ffn_shift.astype(full)
    )
    memory_low = memory.astype(low_type)

    cross_k = dot_plain(memory_low, cross_key).astype(low_type)
    cross_v = dot_plain(memory_low, cross_value).astype(low_type)
    cross_acc, cross_stats = merge_scatter(
        attend(all_cross_q, cross_k, cross_v, live_bias[None, :], None, 256, False)
    )
    cross_total = cross_stats[:, SLOT : 2 * SLOT]
    cross_out_full = cross_acc / exact_dot(cross_total, spread)
    cross_lse = cross_stats[:, :SLOT] + jnp.log(jnp.maximum(cross_total, 1e-30))
    cross_attn = cross_out_full.astype(low_type)
    dec_res_two = dec_first + dot_plain(cross_attn, cross_out)
    dec_second, dec_second_back = jax.vjp(
        layer_norm, dec_res_two, dec_cross_gain.astype(full), dec_cross_shift.astype(full)
    )
    dec_second_low = dec_second.astype(low_type)
    dec_hidden, dec_slope = gelu_pair(dot_plain(dec_second_low, dec_up))
    dec_third = dec_second + dot_plain(dec_hidden, dec_down)
    decoded, dec_final_back = jax.vjp(
        layer_norm, dec_third, dec_ffn_gain.astype(full), dec_ffn_shift.astype(full)
    )

    d_third, g_dec_ffn_gain, g_dec_ffn_shift = dec_final_back(cotangent[0].astype(full))
    d_down_low = d_third.astype(low_type)
    d_pre_low = (dot_right(d_down_low, dec_down) * dec_slope.astype(full)).astype(low_type)
    d_second = d_third + dot_right(d_pre_low, dec_up)
    d_res_two, g_dec_cross_gain, g_dec_cross_shift = dec_second_back(d_second)
    d_cross_o = d_res_two.astype(low_type)
    d_cross_attn = dot_right(d_cross_o, cross_out).astype(low_type)
    cross_delta = exact_dot(d_cross_attn.astype(full) * cross_out_full, spread.T)
    all_dout = gather_rows(d_cross_attn)
    all_stats = gather_rows(
        jnp.concatenate(
            [cross_lse, cross_delta, jnp.zeros((dec_count, LANES - 2 * SLOT), full)], axis=1
        )
    )[:, : 2 * SLOT].T
    live_turned = jnp.broadcast_to(live_bias[:, None], (src_count, 512))
    query_parts, ck_low, cv_low = attend_back(
        all_cross_q, cross_k, cross_v, all_dout, all_stats, live_turned, None, 256
    )
    d_memory = dot_right(ck_low, cross_key) + dot_right(cv_low, cross_value)

    g_dec_down = dot_left(dec_hidden, d_down_low)
    g_dec_up = dot_left(dec_second_low, d_pre_low)
    g_cross_out = dot_left(cross_attn, d_cross_o)
    g_cross_key = dot_left(memory_low, ck_low)
    g_cross_value = dot_left(memory_low, cv_low)

    d_enc_second, g_enc_ffn_gain, g_enc_ffn_shift = enc_final_back(d_memory)
    d_enc_down = d_enc_second.astype(low_type)
    d_enc_pre = (dot_right(d_enc_down, enc_down) * enc_slope.astype(full)).astype(low_type)
    d_enc_first = d_enc_second + dot_right(d_enc_pre, enc_up)
    d_enc_res, g_enc_attn_gain, g_enc_attn_shift = enc_first_back(d_enc_first)
    d_attn_o = d_enc_res.astype(low_type)
    d_attn = dot_right(d_attn_o, enc_out).astype(low_type)
    g_enc_down = dot_left(enc_hidden, d_enc_down)
    g_enc_up = dot_left(enc_first_low, d_enc_pre)
    g_enc_out = dot_left(enc_attn, d_attn_o)

    d_cross_q = scatter_all(query_parts).astype(low_type) * 0.125
    g_cross_query = dot_left(dec_first_low, d_cross_q)
    d_first = d_res_two + dot_right(d_cross_q, cross_query)
    d_res_one, g_dec_self_gain, g_dec_self_shift = dec_first_back(d_first)
    d_self_o = d_res_one.astype(low_type)
    g_self_out = dot_left(self_attn, d_self_o)
    d_self_attn = dot_right(d_self_o, self_out).astype(low_type)
    self_delta = exact_dot(d_self_attn.astype(full) * self_out_full, spread.T)
    wide = max(dec_count, LANES)
    self_pair = jnp.concatenate([self_stats[:, :SLOT], self_delta], axis=1)
    self_query_parts, d_self_k, d_self_v = attend_back(
        pad_rows(self_q, wide),
        self_k,
        self_v,
        pad_rows(d_self_attn, wide),
        pad_rows(self_pair, wide).T,
        pad_rows(self_bias, wide).T,
        None,
        wide,
    )
    d_self_q = self_query_parts[:dec_count].astype(low_type) * 0.125
    g_self_query = dot_left(dec_x, d_self_q)
    g_self_key = dot_left(dec_all, d_self_k)
    g_self_value = dot_left(dec_all, d_self_v)
    d_target = (
        d_res_one
        + dot_right(d_self_q, self_query)
        + scatter_all(dot_right(d_self_k, self_key) + dot_right(d_self_v, self_value))
    )

    glob_dout = add_all(dot_plain(select_low, d_attn).astype(low_type))
    d_window = jnp.where(is_global[:, None], jnp.zeros_like(d_attn), d_attn)
    win_delta = exact_dot(d_window.astype(full) * win_out, spread.T)
    win_pair = jnp.concatenate([win_stats[:, :SLOT], win_delta], axis=1).T
    d_query, d_keys_all, d_vals_all = attend_back(
        query_loc, keys_all, vals_all, d_window, win_pair, win_bias_turned, win_parts, rows_block
    )
    d_query_low = d_query.astype(low_type) * 0.125

    wide = max(glob_count, LANES)
    glob_delta = exact_dot(glob_dout.astype(full) * glob_out, spread.T)
    glob_pair = jnp.concatenate([glob_lse, glob_delta], axis=1)
    glob_query_parts, gk_low, gv_low = attend_back(
        pad_rows(glob_queries, wide),
        glob_keys_loc,
        glob_vals_loc,
        pad_rows(glob_dout, wide),
        pad_rows(glob_pair, wide).T,
        live_turned[:, :wide],
        None,
        wide,
    )
    d_gq = glob_query_parts[:glob_count].astype(low_type) * 0.125

    g_enc_query = dot_left(src_x, d_query_low)
    g_enc_key = dot_left(x_all, d_keys_all)
    g_enc_value = dot_left(x_all, d_vals_all)
    g_glob_query = dot_left(glob_x, d_gq)
    g_glob_key = dot_left(src_x, gk_low)
    g_glob_value = dot_left(src_x, gv_low)

    d_x_all = dot_right(d_keys_all, enc_key) + dot_right(d_vals_all, enc_value)
    from_after = lax.ppermute(d_x_all[:HALF].astype(low_type), "seq", downward)
    from_before = lax.ppermute(d_x_all[HALF + src_count : pad_count].astype(low_type), "seq", upward)
    d_glob_x = add_all((d_x_all[pad_count:] + dot_right(d_gq, glob_query)).astype(low_type))
    d_source = (
        d_enc_res
        + dot_right(d_query_low, enc_query)
        + d_x_all[HALF : HALF + src_count]
        + dot_right(gk_low, glob_key)
        + dot_right(gv_low, glob_value)
        + dot_left(select_low, d_glob_x)
    )
    d_source = d_source + jnp.pad(
        from_after.astype(full), ((src_count - HALF, 0), (0, 0))
    )
    d_source = d_source + jnp.pad(
        from_before.astype(full), ((0, src_count - HALF), (0, 0))
    )

    (s_dec_up,) = share_grads([g_dec_up], True)
    s_dec_down, s_cross_out = share_grads([g_dec_down, g_cross_out], False)
    s_cross_key, s_cross_value = share_grads([g_cross_key, g_cross_value], True)
    (s_enc_up,) = share_grads([g_enc_up], True)
    s_enc_down, s_enc_out = share_grads([g_enc_down, g_enc_out], False)
    s_self_query, s_self_key, s_self_value, s_self_out, s_cross_query = share_grads(
        [g_self_query, g_self_key, g_self_value, g_self_out, g_cross_query], False
    )
    s_enc_query, s_enc_key, s_enc_value = share_grads([g_enc_query, g_enc_key, g_enc_value], True)
    s_glob_query, s_glob_key, s_glob_value = share_grads(
        [g_glob_query, g_glob_key, g_glob_value], False
    )
    vectors = share_norms(
        [
            g_enc_attn_gain,
            g_enc_attn_shift,
            g_enc_ffn_gain,
            g_enc_ffn_shift,
            g_dec_self_gain,
            g_dec_self_shift,
            g_dec_cross_gain,
            g_dec_cross_shift,
            g_dec_ffn_gain,
            g_dec_ffn_shift,
        ]
    )
    return (
        decoded.astype(low_type)[None],
        d_source[None],
        d_target[None],
        s_enc_query,
        s_enc_key,
        s_enc_value,
        s_glob_query,
        s_glob_key,
        s_glob_value,
        s_enc_out,
        vectors[0],
        vectors[1],
        s_enc_up,
        s_enc_down,
        vectors[2],
        vectors[3],
        s_self_query,
        s_self_key,
        s_self_value,
        s_self_out,
        vectors[4],
        vectors[5],
        s_cross_query,
        s_cross_key,
        s_cross_value,
        s_cross_out,
        vectors[6],
        vectors[7],
        s_dec_up,
        s_dec_down,
        vectors[8],
        vectors[9],
    )


def solution(mesh):
    rows = P("dp", "seq", None)
    tile = P("seq", "dp")
    part = P("seq")
    layer = (tile,) * 7 + (part,) * 2 + (tile,) * 2 + (part,) * 2
    decoder = (tile,) * 4 + (part,) * 2 + (tile,) * 4 + (part,) * 2 + (tile,) * 2 + (part,) * 2
    few = mesh.shape["seq"] <= 16
    return jax.shard_map(
        per_device if few else per_device_wide,
        mesh=mesh,
        in_specs=(rows, rows, rows, P("dp"), P("dp"), P("dp", None)) + (P(),) * 29,
        out_specs=(rows, rows, rows) + layer + decoder,
        check_vma=False,
    )
```

```python
import functools

import jax
import jax.numpy as jnp
import numpy as np
from jax import lax
from jax.experimental import pallas as pl
from jax.experimental.pallas import tpu as pltpu
from jax.sharding import PartitionSpec as P

HEADS = 12
HEAD_DIM = 64
HALF = 512
PAIRS = HEADS // 2
LANES = 2 * HEAD_DIM
SLOT = 16

masked_score = -1e30
eps_norm = 1e-05
low_type = jnp.bfloat16
vmem_bytes = 56 * 2**20


def dot_plain(left, right):
    return jnp.dot(left, right, preferred_element_type=jnp.float32)


def dot_left(left, right):
    return lax.dot_general(
        left, right, (((0,), (0,)), ((), ())), preferred_element_type=jnp.float32
    )


def dot_right(left, right):
    return lax.dot_general(
        left, right, (((1,), (1,)), ((), ())), preferred_element_type=jnp.float32
    )


def exact_dot(left, right):
    return jnp.dot(
        left, right, precision=lax.Precision.HIGHEST, preferred_element_type=jnp.float32
    )


def layer_norm(value, scale_vec, shift_vec):
    average = jnp.mean(value, axis=-1, keepdims=True)
    centred = value - average
    spread = jnp.mean(centred * centred, axis=-1, keepdims=True)
    return centred * lax.rsqrt(spread + eps_norm) * scale_vec + shift_vec


def gelu_pair(value):
    cdf = 0.5 * (1.0 + lax.erf(value * 0.7071067811865476))
    slope = cdf + value * (0.3989422804014327 * jnp.exp(-0.5 * value * value))
    return (value * cdf).astype(low_type), slope.astype(low_type)


def head_spread():
    heads = lax.broadcasted_iota(jnp.int32, (SLOT, HEADS * HEAD_DIM), 0)
    columns = lax.broadcasted_iota(jnp.int32, (SLOT, HEADS * HEAD_DIM), 1)
    return (columns // HEAD_DIM == heads).astype(jnp.float32)


def head_mask(which):
    lanes = lax.broadcasted_iota(jnp.int32, (1, LANES), 1)
    return ((lanes // HEAD_DIM) == which).astype(low_type)


def attend_heads(
    first, group, parts, rows_block, blocks, normalize, q_ref, k_ref, v_ref, bias_ref, o_ref, st_ref
):
    lane = lax.broadcasted_iota(jnp.int32, (1, LANES), 1)
    for block in range(blocks):
        rows = pl.ds(block * rows_block, rows_block)
        stats = st_ref[rows, :]
        for pair in range(group):
            columns = pl.ds(pair * LANES, LANES)
            q_two = q_ref[rows, columns]
            outs = []
            for which in range(2):
                head = first + 2 * pair + which
                q_one = q_two * head_mask(which)
                scores = []
                for start, size in parts[block]:
                    keys = pl.ds(start, size)
                    bias = bias_ref[rows, keys] if bias_ref.shape[0] > 1 else bias_ref[:, keys]
                    scores.append(dot_right(q_one, k_ref[keys, columns]) + bias)
                top = functools.reduce(
                    jnp.maximum, [jnp.max(part, axis=1, keepdims=True) for part in scores]
                )
                total = jnp.zeros((rows_block, 1), jnp.float32)
                mixed = jnp.zeros((rows_block, LANES), jnp.float32)
                for (start, size), part in zip(parts[block], scores):
                    weights = jnp.exp(part - top)
                    total = total + jnp.sum(weights, axis=1, keepdims=True)
                    mixed = mixed + dot_plain(
                        weights.astype(low_type), v_ref[pl.ds(start, size), columns]
                    )
                if normalize:
                    mixed = mixed / total
                    stats = jnp.where(lane == head, top + jnp.log(total), stats)
                else:
                    stats = jnp.where(lane == head, top, stats)
                    stats = jnp.where(lane == head + SLOT, total, stats)
                outs.append(mixed)
            o_ref[rows, columns] = jnp.where(lane < HEAD_DIM, outs[0], outs[1])
        st_ref[rows, :] = stats


def forward_body(
    parts, rows_block, blocks, normalize, group, q_ref, k_ref, v_ref, bias_ref, o_ref, st_ref
):
    first = pl.program_id(1) * (2 * group)

    @pl.when(first == 0)
    def _():
        st_ref[...] = jnp.zeros_like(st_ref)

    attend_heads(
        first, group, parts, rows_block, blocks, normalize, q_ref, k_ref, v_ref, bias_ref,
        o_ref, st_ref,
    )


def attend(queries, keys, values, bias, parts, rows_block, normalize, group=1):
    count, width = queries.shape
    key_count = keys.shape[0]
    big = min(count, 512)
    blocks = big // rows_block
    parts = parts or [((0, key_count),)] * blocks
    bias_rows = bias.shape[0]
    flops = 4 * count * key_count * width
    wide = group * LANES
    return pl.pallas_call(
        functools.partial(forward_body, parts, rows_block, blocks, normalize, group),
        grid=(count // big, PAIRS // group),
        in_specs=[
            pl.BlockSpec((big, wide), lambda i, p: (i, p)),
            pl.BlockSpec((key_count, wide), lambda i, p: (0, p)),
            pl.BlockSpec((key_count, wide), lambda i, p: (0, p)),
            pl.BlockSpec(
                (min(bias_rows, big), key_count), lambda i, p: (i if bias_rows > big else 0, 0)
            ),
        ],
        out_specs=[
            pl.BlockSpec((big, wide), lambda i, p: (i, p)),
            pl.BlockSpec((big, LANES), lambda i, p: (i, 0)),
        ],
        out_shape=[
            jax.ShapeDtypeStruct((count, width), jnp.float32),
            jax.ShapeDtypeStruct((count, LANES), jnp.float32),
        ],
        compiler_params=pltpu.CompilerParams(vmem_limit_bytes=vmem_bytes),
        cost_estimate=pl.CostEstimate(
            flops=4 * flops,
            bytes_accessed=2 * (count + 2 * key_count) * width + 4 * count * width,
            transcendentals=count * key_count * HEADS,
        ),
    )(queries, keys, values, bias)


def back_heads(
    first, group, parts, rows_block, blocks, q_ref, k_ref, v_ref, d_ref, st_ref, bias_ref,
    dq_ref, key_sum, val_sum,
):
    for block in range(blocks):
        rows = pl.ds(block * rows_block, rows_block)
        for pair in range(group):
            columns = pl.ds(pair * LANES, LANES)
            q_two = q_ref[rows, columns]
            d_two = d_ref[rows, columns]
            turned = []
            for which in range(2):
                head = first + 2 * pair + which
                q_one = q_two * head_mask(which)
                d_one = d_two * head_mask(which)
                lse = st_ref[pl.ds(head, 1), rows]
                delta = st_ref[pl.ds(head + SLOT, 1), rows]
                q_grad = jnp.zeros((LANES, rows_block), jnp.float32)
                for start, size in parts[block]:
                    keys = pl.ds(start, size)
                    bias = bias_ref[keys, rows] if bias_ref.shape[1] > 1 else bias_ref[keys, :]
                    k_two = k_ref[keys, columns]
                    scores = dot_right(k_two, q_one) + bias
                    weights = jnp.exp(scores - lse)
                    slopes = dot_right(v_ref[keys, columns], d_one)
                    diffs = (weights * (slopes - delta)).astype(low_type)
                    val_sum[keys, columns] += dot_plain(weights.astype(low_type), d_one)
                    key_sum[keys, columns] += dot_plain(diffs, q_one)
                    q_grad = q_grad + dot_left(k_two, diffs)
                turned.append(q_grad[which * HEAD_DIM : (which + 1) * HEAD_DIM, :])
            dq_ref[rows, columns] = jnp.concatenate(turned, axis=0).T.astype(dq_ref.dtype)


def backward_body(
    parts, rows_block, blocks, group, q_ref, k_ref, v_ref, d_ref, st_ref, bias_ref,
    dq_ref, dk_ref, dv_ref, key_sum, val_sum,
):
    first = pl.program_id(0) * (2 * group)
    turn = pl.program_id(1)

    @pl.when(turn == 0)
    def _():
        key_sum[...] = jnp.zeros_like(key_sum)
        val_sum[...] = jnp.zeros_like(val_sum)

    back_heads(
        first, group, parts, rows_block, blocks, q_ref, k_ref, v_ref, d_ref, st_ref, bias_ref,
        dq_ref, key_sum, val_sum,
    )

    @pl.when(turn == pl.num_programs(1) - 1)
    def _():
        dk_ref[...] = key_sum[...].astype(low_type)
        dv_ref[...] = val_sum[...].astype(low_type)


def attend_back(queries, keys, values, grads, stats, bias, parts, rows_block, group=1):
    count, width = queries.shape
    key_count = keys.shape[0]
    big = min(count, 512)
    blocks = big // rows_block
    parts = parts or [((0, key_count),)] * blocks
    bias_cols = bias.shape[1]
    flops = 10 * count * key_count * width
    wide = group * LANES
    return pl.pallas_call(
        functools.partial(backward_body, parts, rows_block, blocks, group),
        grid=(PAIRS // group, count // big),
        in_specs=[
            pl.BlockSpec((big, wide), lambda p, i: (i, p)),
            pl.BlockSpec((key_count, wide), lambda p, i: (0, p)),
            pl.BlockSpec((key_count, wide), lambda p, i: (0, p)),
            pl.BlockSpec((big, wide), lambda p, i: (i, p)),
            pl.BlockSpec((2 * SLOT, big), lambda p, i: (0, i)),
            pl.BlockSpec((key_count, min(bias_cols, big)), lambda p, i: (0, 0)),
        ],
        out_specs=[
            pl.BlockSpec((big, wide), lambda p, i: (i, p)),
            pl.BlockSpec((key_count, wide), lambda p, i: (0, p)),
            pl.BlockSpec((key_count, wide), lambda p, i: (0, p)),
        ],
        out_shape=[
            jax.ShapeDtypeStruct((count, width), jnp.float32),
            jax.ShapeDtypeStruct((key_count, width), low_type),
            jax.ShapeDtypeStruct((key_count, width), low_type),
        ],
        scratch_shapes=[
            pltpu.VMEM((key_count, wide), jnp.float32),
            pltpu.VMEM((key_count, wide), jnp.float32),
        ],
        compiler_params=pltpu.CompilerParams(vmem_limit_bytes=vmem_bytes),
        cost_estimate=pl.CostEstimate(
            flops=4 * flops,
            bytes_accessed=2 * (2 * count + 4 * key_count) * width + 4 * count * width,
            transcendentals=count * key_count * HEADS,
        ),
    )(queries, keys, values, grads, stats, bias)


def seq_bits():
    count = lax.axis_size("seq")
    return [1 << k for k in range(count.bit_length() - 1)]


def swap(value, bit):
    pairs = [(i, i ^ bit) for i in range(lax.axis_size("seq"))]
    return jax.tree.map(lambda part: lax.ppermute(part, "seq", pairs), value)


def bit_set(bit):
    return (lax.axis_index("seq") & bit) != 0


def pick_half(value, chosen, axis):
    return lax.dynamic_index_in_dim(value, chosen, axis, keepdims=False)


def other_of(place, bit):
    return place + bit * (1 - 2 * ((place // bit) % 2))


def greet(partners):
    barrier = pltpu.get_barrier_semaphore()
    for partner in partners:
        pl.semaphore_signal(
            barrier, inc=1, device_id=partner, device_id_type=pl.DeviceIdType.MESH
        )
    pl.semaphore_wait(barrier, len(partners))


def remote(src, dst, sems, k, partner):
    return pltpu.make_async_remote_copy(
        src_ref=src,
        dst_ref=dst,
        send_sem=sems[0].at[k],
        recv_sem=sems[1].at[k],
        device_id=partner,
        device_id_type=pl.DeviceIdType.MESH,
    )


def piece_stages(peers, kind):
    bits = [1 << k for k in range(1, peers.bit_length() - 1)]
    if kind == "x":
        return [1, "dp"] + bits
    if kind == "y":
        return [1] + bits[:1] + ["dp"] + bits[1:]
    return [1] + bits[1:] + ["dp"] + bits[:1]


def piece_shapes(peers, rows, width, stages):
    free = peers.bit_length() - 1
    shapes = []
    for stage in stages:
        if stage == "dp":
            width = width // 2
        else:
            free -= 1
        shapes.append((2,) * free + (rows, width))
    return shapes


def bit_axis(peers, stages, s):
    rest = [bit for bit in reversed([1 << k for k in range(peers.bit_length() - 1)])]
    for stage in stages[:s]:
        if stage != "dp":
            rest.remove(stage)
    return rest.index(stages[s])


def place_bits(peers):
    me = lax.axis_index("seq")
    bits = [1 << k for k in reversed(range(peers.bit_length() - 1))]
    return bits, [(me // bit) % 2 for bit in bits]


def block_at(peers, ref, place):
    return ref.at[tuple((place // bit) % 2 for bit in place_bits(peers)[0])]


def chip_copies(peers, refs, sems, k):
    me = lax.axis_index("seq")
    half = peers // 2
    return [
        remote(
            block_at(peers, ref, me),
            block_at(peers, ref, me),
            sems,
            which * peers + k,
            {"seq": lax.rem(me + 2 * k, peers)},
        )
        for which, ref in enumerate(refs)
    ]


def core_copies(peers, refs, sems, k):
    me = lax.axis_index("seq")
    place = lax.rem(me + peers - 2 * k, peers)
    return [
        remote(
            block_at(peers, ref, place),
            block_at(peers, ref, place),
            sems,
            which * peers + peers // 2 + k,
            {"seq": other_of(me, 1)},
        )
        for which, ref in enumerate(refs)
    ]


def reach_out(peers, refs, sems):
    for k in range(1, peers // 2):
        for copy in chip_copies(peers, refs, sems, k):
            copy.start()
    for copy in core_copies(peers, refs, sems, 0):
        copy.start()


def pass_on(peers, refs, sems):
    half = peers // 2
    for k in range(1, half):
        for copy in chip_copies(peers, refs, sems, k):
            copy.wait_recv()
        for copy in core_copies(peers, refs, sems, k):
            copy.start()
    for k in range(half):
        for copy in core_copies(peers, refs, sems, k):
            copy.wait()
    for k in range(1, half):
        for copy in chip_copies(peers, refs, sems, k):
            copy.wait_send()


OWNERS = 4


def everyone(peers):
    me = lax.axis_index("seq")
    return [{"seq": lax.rem(me + k, peers)} for k in range(1, peers)]


def send_in(peers, parts, slots, sems):
    me = lax.axis_index("seq")
    apart = peers // OWNERS
    for o in range(OWNERS):
        for k, (part, slot) in enumerate(zip(parts, slots)):
            copy = pltpu.make_async_remote_copy(
                src_ref=part.at[o],
                dst_ref=slot.at[me],
                send_sem=sems[0].at[k, o],
                recv_sem=sems[1].at[k, me],
                device_id={"seq": o * apart},
                device_id_type=pl.DeviceIdType.MESH,
            )

            @pl.when(me != o * apart)
            def _():
                copy.start()

            @pl.when(me == o * apart)
            def _():
                slot[me] = part[o]


def arrive(peers, parts, slots, sems):
    me = lax.axis_index("seq")
    for j in range(peers):
        for k, (part, slot) in enumerate(zip(parts, slots)):

            @pl.when(me != j)
            def _():
                pltpu.make_async_remote_copy(
                    src_ref=part.at[0],
                    dst_ref=slot.at[j],
                    send_sem=sems[0].at[k, 0],
                    recv_sem=sems[1].at[k, j],
                    device_id={"seq": j},
                    device_id_type=pl.DeviceIdType.MESH,
                ).wait_recv()


def left(peers, parts, slots, sems):
    me = lax.axis_index("seq")
    apart = peers // OWNERS
    for o in range(OWNERS):
        for k, (part, slot) in enumerate(zip(parts, slots)):

            @pl.when(me != o * apart)
            def _():
                pltpu.make_async_remote_copy(
                    src_ref=part.at[o],
                    dst_ref=slot.at[me],
                    send_sem=sems[0].at[k, o],
                    recv_sem=sems[1].at[k, me],
                    device_id={"seq": o * apart},
                    device_id_type=pl.DeviceIdType.MESH,
                ).wait_send()


def out_copies(results, sems, o, j):
    return [
        pltpu.make_async_remote_copy(
            src_ref=result.at[o],
            dst_ref=result.at[o],
            send_sem=sems[2].at[k, j],
            recv_sem=sems[3].at[k, o],
            device_id={"seq": j},
            device_id_type=pl.DeviceIdType.MESH,
        )
        for k, result in enumerate(results)
    ]


def send_out(peers, results, sems):
    me = lax.axis_index("seq")
    apart = peers // OWNERS
    for o in range(OWNERS):
        owner = o * apart

        @pl.when(me == owner)
        def _():
            for j in range(peers):
                if j != owner:
                    for copy in out_copies(results, sems, o, j):
                        copy.start()


def take_out(peers, results, sems):
    me = lax.axis_index("seq")
    apart = peers // OWNERS
    for o in range(OWNERS):
        owner = o * apart

        @pl.when(me != owner)
        def _():
            for copy in out_copies(results, sems, o, owner):
                copy.wait_recv()

        @pl.when(me == owner)
        def _():
            for j in range(peers):
                if j != owner:
                    for copy in out_copies(results, sems, o, j):
                        copy.wait_send()


def owner_sems(peers, count):
    return [
        pltpu.SemaphoreType.DMA((count, OWNERS)),
        pltpu.SemaphoreType.DMA((count, peers)),
        pltpu.SemaphoreType.DMA((count, peers)),
        pltpu.SemaphoreType.DMA((count, OWNERS)),
    ]


def sum_at_owner(peers, part_ref, slot, sum_ref, sems):
    me = lax.axis_index("seq")
    apart = peers // OWNERS
    for o in range(OWNERS):

        @pl.when(me == o * apart)
        def _():
            arrive(peers, [part_ref], [slot], sems)
            total = slot[0].astype(jnp.float32)
            for j in range(1, peers):
                total = total + slot[j].astype(jnp.float32)
            sum_ref[o] = total.astype(low_type)


def expand_heads(stat):
    lane = lax.broadcasted_iota(jnp.int32, (1, LANES), 1)
    return jnp.concatenate(
        [
            jnp.where(lane < HEAD_DIM, stat[:, 2 * p : 2 * p + 1], stat[:, 2 * p + 1 : 2 * p + 2])
            for p in range(PAIRS)
        ],
        axis=1,
    )


def merge_parts(accs, stats):
    tops = [part[:, :SLOT] for part in stats]
    top = functools.reduce(jnp.maximum, tops)
    total = jnp.zeros_like(top)
    acc = jnp.zeros(accs[0].shape, jnp.float32)
    for part, stat, own_top in zip(accs, stats, tops):
        keep = jnp.exp(own_top - top)
        total = total + stat[:, SLOT : 2 * SLOT] * keep
        acc = acc + part.astype(jnp.float32) * expand_heads(keep)
    return acc, top, total


def finish_parts(acc, top, total):
    lanes = lax.broadcasted_iota(jnp.int32, total.shape, 1)
    total = jnp.where(lanes < HEADS, total, 1.0)
    lse = top + jnp.log(total)
    rest = jnp.zeros((top.shape[0], LANES - SLOT), jnp.float32)
    return acc * expand_heads(1.0 / total), jnp.concatenate([lse, rest], axis=1)


def window_body(
    peers, parts, rows_block, blocks, q_ref, k_ref, v_ref, use_ref, acc_ref, part_ref,
    o_ref, st_ref, out_copy, lse_copy, bias_ref, low_ref, acc_in, st_in, out_ref, lse_ref, *sems
):
    step = pl.program_id(1)
    me = lax.axis_index("seq")
    apart = peers // OWNERS

    @pl.when(step == 0)
    def _():
        greet(everyone(peers))
        low_ref[...] = acc_ref[...].astype(low_type)
        send_in(peers, [low_ref, part_ref], [acc_in, st_in], sems)
        rows = lax.broadcasted_iota(jnp.int32, bias_ref.shape, 0)
        keys = lax.broadcasted_iota(jnp.int32, bias_ref.shape, 1)
        apart_by = rows + HALF - keys
        near = (jnp.abs(apart_by) <= HALF) | (keys >= bias_ref.shape[0] + 2 * HALF)
        bias_ref[...] = jnp.where(near, use_ref[...], masked_score)

    @pl.when(step == 2)
    def _():
        for o in range(OWNERS):

            @pl.when(me == o * apart)
            def _():
                arrive(peers, [low_ref, part_ref], [acc_in, st_in], sems)
                acc, top, total = merge_parts(
                    [acc_in[j] for j in range(peers)], [st_in[j] for j in range(peers)]
                )
                out_ref[o], lse_ref[o] = finish_parts(acc, top, total)

        send_out(peers, [out_ref, lse_ref], sems)

    forward_body(
        parts, rows_block, blocks, True, 1, q_ref, k_ref, v_ref, bias_ref, o_ref, st_ref
    )

    @pl.when(step == PAIRS - 1)
    def _():
        take_out(peers, [out_ref, lse_ref], sems)
        left(peers, [low_ref, part_ref], [acc_in, st_in], sems)
        out_copy[...] = out_ref[...]
        lse_copy[...] = lse_ref[...]


def window_attend(queries, keys, values, use, parts, rows_block, glob_acc, glob_stats):
    peers = lax.axis_size("seq")
    count, width = queries.shape
    key_count = keys.shape[0]
    rows = glob_acc.shape[0] // OWNERS
    flops = 4 * count * key_count * width

    def pair_block(size):
        return pl.BlockSpec((size, LANES), lambda i, p: (0, p))

    def whole(*shape):
        return pl.BlockSpec(shape, lambda i, p: (0,) * len(shape))

    out, stats, glob_out, lse = pl.pallas_call(
        functools.partial(window_body, peers, parts, rows_block, count // rows_block),
        grid=(1, PAIRS),
        in_specs=[
            pair_block(count),
            pair_block(key_count),
            pair_block(key_count),
            whole(1, key_count),
            whole(OWNERS, rows, width),
            whole(OWNERS, rows, LANES),
        ],
        out_specs=[
            pair_block(count),
            whole(count, LANES),
            whole(OWNERS, rows, width),
            whole(OWNERS, rows, LANES),
        ],
        out_shape=[
            jax.ShapeDtypeStruct((count, width), jnp.float32),
            jax.ShapeDtypeStruct((count, LANES), jnp.float32),
            jax.ShapeDtypeStruct((OWNERS, rows, width), jnp.float32),
            jax.ShapeDtypeStruct((OWNERS, rows, LANES), jnp.float32),
        ],
        scratch_shapes=[
            pltpu.VMEM((count, key_count), jnp.float32),
            pltpu.VMEM((OWNERS, rows, width), low_type),
            pltpu.VMEM((peers, rows, width), low_type),
            pltpu.VMEM((peers, rows, LANES), jnp.float32),
            pltpu.VMEM((OWNERS, rows, width), jnp.float32),
            pltpu.VMEM((OWNERS, rows, LANES), jnp.float32),
        ]
        + owner_sems(peers, 2),
        compiler_params=pltpu.CompilerParams(
            collective_id=3, has_side_effects=True, vmem_limit_bytes=vmem_bytes
        ),
        cost_estimate=pl.CostEstimate(
            flops=4 * flops,
            bytes_accessed=2 * (count + 2 * key_count) * width + 4 * count * width,
            transcendentals=count * key_count * HEADS,
        ),
    )(
        queries, keys, values, use,
        glob_acc.reshape(OWNERS, rows, width), glob_stats.reshape(OWNERS, rows, LANES),
    )
    return out, stats, glob_out.reshape(-1, width), lse.reshape(-1, LANES)


def end_body(count, *refs):
    shared = refs[:count]
    (source_own, after, before, select, glob,
     target_own, target_sum, flags) = refs[count : count + 8]
    outs = refs[count + 8 :]
    for source, target in zip(shared, outs):
        target[...] = source[...]
    d_source, d_target = outs[count:]
    full = jnp.float32
    d_target[...] = target_own[...] + target_sum[...]
    has_after = flags[:, :1] > 0
    has_before = flags[:, 1:2] > 0
    total = source_own[...] + dot_left(select[...], glob[...])
    total = total + jnp.where(has_after, after[...].astype(full), 0.0)
    d_source[...] = total + jnp.where(has_before, before[...].astype(full), 0.0)


def end_outputs(shared, source_parts, target_parts):
    shapes = [part.shape for part in shared]
    shapes += [source_parts[0].shape, target_parts[0].shape]
    return pl.pallas_call(
        functools.partial(end_body, len(shared)),
        out_shape=[jax.ShapeDtypeStruct(shape, jnp.float32) for shape in shapes],
        compiler_params=pltpu.CompilerParams(vmem_limit_bytes=vmem_bytes),
    )(*shared, *source_parts[:5], *target_parts, source_parts[5])


def share_vectors(total, count):
    length = total.shape[1] // lax.axis_size("seq")
    mine = lax.dynamic_slice_in_dim(total, lax.axis_index("seq") * length, length, 1)
    return [mine[k] for k in range(count)]


def pad_rows(value, count):
    return jnp.pad(value, ((0, count - value.shape[0]), (0, 0)))


def fetches(fars, nears, sem):
    return [
        pltpu.make_async_copy(far, near, sem.at[k]) for k, (far, near) in enumerate(zip(fars, nears))
    ]


def bring(fars, nears, sem):
    copies = fetches(fars, nears, sem)
    for copy in copies:
        copy.start()
    return copies


class Pieces:
    def __init__(self, peers, pieces, mats, factors, kept, outs, sems, load, held, own, staging, base):
        self.peers = peers
        self.pieces = pieces
        self.mats = mats
        self.factors = factors
        self.kept = kept
        self.outs = outs
        self.sems = sems
        self.load = load
        self.held = held
        self.own = own
        self.staging = staging
        self.numbers = {}
        self.base = base
        self.me = lax.axis_index("seq")
        self.mine_dp = lax.axis_index("dp")

    def number(self, *key):
        return self.base + self.numbers.setdefault(key, len(self.numbers))

    def partner(self, stage):
        if stage == "dp":
            return {"dp": 1 - self.mine_dp}
        return {"seq": other_of(self.me, stage)}

    def halved(self, source, stages, s, mine):
        if stages[s] == "dp":
            half = source.shape[-1] // 2
            where = self.mine_dp if mine else 1 - self.mine_dp
            start = pl.multiple_of(where * half, LANES)
            return (slice(None),) * (len(source.shape) - 1) + (pl.ds(start, half),)
        digit = (self.me // stages[s]) % 2
        return (slice(None),) * bit_axis(self.peers, stages, s) + (digit if mine else 1 - digit,)

    def copy(self, name, stages, origin, target, s):
        view = origin.at[self.halved(origin, stages, s, False)]
        return remote(view, target, self.sems, self.number(name, s), self.partner(stages[s]))

    def fold(self, stages, origin, target, s, finish):
        spot = self.halved(origin, stages, s, True)
        for place in np.ndindex(*target.shape[:-2]):
            if stages[s] == "dp":
                more = origin[place + spot[-2:]]
            else:
                axis = len(spot) - 1
                more = origin[place[:axis] + spot[-1:] + place[axis:]]
            total = target[place] + more
            if finish is not None:
                if place:
                    finish[place] = total.astype(finish.dtype)
                else:
                    finish[...] = total.astype(finish.dtype)
            else:
                target[place] = total

    def origin(self, p, s):
        piece = self.pieces[p]
        if s > piece["first"]:
            return self.held[p][s - 1 - piece["first"]]
        kind, which = piece["from"]
        return {"mat": self.mats, "made": self.staging, "kept": self.kept}[kind][which]

    def target(self, p, s):
        return self.held[p][s - self.pieces[p]["first"]]

    def local(self, p, c):
        which = self.pieces[p]["from"][1]
        core = self.me % 2
        return pltpu.make_async_copy(
            self.mats[which].at[c // 2, c % 2, :, core],
            self.own[which].at[c % 2],
            self.load.at[2 * which + c % 2],
        )

    def compute(self, p):
        x, y = (self.factors[k] for k in self.pieces[p]["pair"])
        target = self.staging[self.pieces[p]["from"][1]]
        step = x.shape[1] // 2
        for block in range(2):
            product = dot_left(x[:, block * step : (block + 1) * step], y[...])
            target[block] = product.astype(low_type).reshape(target.shape[1:])

    def begin(self, p, s):
        piece = self.pieces[p]
        if s == 0 and piece["from"][0] == "mat":
            for c in range(2):
                self.local(p, c).start()
        self.copy(p, piece["stages"], self.origin(p, s), self.target(p, s), s).start()

    def end(self, p, s):
        piece = self.pieces[p]
        origin, target = self.origin(p, s), self.target(p, s)
        self.copy(p, piece["stages"], origin, target, s).wait()
        finish = self.outs[p] if s == piece["last"] else None
        if s == 0 and piece["from"][0] == "mat":
            mine = self.own[piece["from"][1]]
            for c in range(4):
                self.local(p, c).wait()
                spot = (c // 2, c % 2)
                for k in range(2):
                    target[spot + (k,)] = target[spot + (k,)] + mine[c % 2, k]
                if c < 2:
                    self.local(p, c + 2).start()
        else:
            self.fold(piece["stages"], origin, target, s, finish)

    def open(self, turn):
        for p in turn:
            if "pair" in self.pieces[p]:
                self.compute(p)
            self.begin(p, self.pieces[p]["first"])

    def move(self, turn, s):
        for p in turn:
            self.end(p, s)
            if s < self.pieces[p]["last"]:
                self.begin(p, s + 1)


def piece_plan(peers, source, rows, width, kind, first, last, pair=None):
    stages = piece_stages(peers, kind)
    shapes = piece_shapes(peers, rows, width, stages)
    plan = {"from": source, "stages": stages, "first": first, "last": last}
    if pair is not None:
        plan["pair"] = pair
    return plan, shapes[first : last + 1]


def ln_parts(value):
    average = jnp.mean(value, axis=-1, keepdims=True)
    centred = value - average
    spread = jnp.mean(centred * centred, axis=-1, keepdims=True)
    rate = lax.rsqrt(spread + eps_norm)
    return centred * rate, rate


def ln_back(grad, unit, rate, gain):
    scaled = grad * gain
    pull = jnp.mean(scaled, axis=-1, keepdims=True)
    twist = jnp.mean(scaled * unit, axis=-1, keepdims=True)
    return (
        rate * (scaled - pull - unit * twist),
        jnp.sum(grad * unit, axis=0, keepdims=True),
        jnp.sum(grad, axis=0, keepdims=True),
    )


def call_whole(body, inputs, shapes, scratch=(), **params):
    whole = pl.BlockSpec(memory_space=pltpu.VMEM)
    return pl.pallas_call(
        body,
        in_specs=[whole] * len(inputs),
        out_specs=[whole] * len(shapes),
        out_shape=[jax.ShapeDtypeStruct(shape, kind) for shape, kind in shapes],
        scratch_shapes=list(scratch),
        compiler_params=pltpu.CompilerParams(vmem_limit_bytes=vmem_bytes, **params),
    )(*inputs)


ENC_ATTN, ENC_FFN, DEC_SELF, DEC_CROSS, DEC_FFN = 0, 2, 4, 6, 8


def scale_shift(norms, which):
    return norms[which : which + 1, :], norms[which + 1 : which + 2, :]


def start_body(
    peers, dec_ref, part_ref, x_ref, wq, wgk, wgv, all_ref, glob_ref, q_ref, gk_ref, gv_ref,
    slot, send, recv, *sems
):
    bits, digits = place_bits(peers)
    greet(everyone(peers))
    send_in(peers, [part_ref], [slot], sems)
    all_ref[tuple(digits)] = dec_ref[...]
    reach_out(peers, [all_ref], (send, recv))
    x = x_ref[...]
    gk_ref[...] = dot_plain(x, wgk[...]).astype(low_type)
    sum_at_owner(peers, part_ref, slot, glob_ref, sems)
    send_out(peers, [glob_ref], sems)
    q_ref[...] = (dot_plain(x, wq[...]) * 0.125).astype(low_type)
    pass_on(peers, [all_ref], (send, recv))
    gv_ref[...] = dot_plain(x, wgv[...]).astype(low_type)
    take_out(peers, [glob_ref], sems)
    left(peers, [part_ref], [slot], sems)


def start_exchange(dec_x, glob_part, src_x, weights):
    peers = lax.axis_size("seq")
    free = peers.bit_length() - 1
    rows = glob_part.shape[0] // OWNERS
    width = dec_x.shape[1]
    dec_all, glob_x, q, gk, gv = call_whole(
        functools.partial(start_body, peers),
        [dec_x, glob_part.reshape(OWNERS, rows, width), src_x, *weights],
        [((2,) * free + dec_x.shape, dec_x.dtype), ((OWNERS, rows, width), low_type)]
        + [(src_x.shape, low_type)] * 3,
        [
            pltpu.VMEM((peers, rows, width), low_type),
            pltpu.SemaphoreType.DMA((peers,)),
            pltpu.SemaphoreType.DMA((peers,)),
        ]
        + owner_sems(peers, 1),
        collective_id=2,
        has_side_effects=True,
    )
    return dec_all.reshape(-1, width), glob_x.reshape(-1, width), q, gk, gv


def project_body(*refs):
    sources = refs[:4]
    wk, wv, x_all, k_all, v_all = refs[4:]
    start = 0
    for source in sources:
        rows = pl.ds(start, source.shape[0])
        x = source[...]
        x_all[rows, :] = x
        k_all[rows, :] = dot_plain(x, wk[...]).astype(low_type)
        v_all[rows, :] = dot_plain(x, wv[...]).astype(low_type)
        start += source.shape[0]


def project_all(sources, wk, wv):
    total = sum(source.shape[0] for source in sources)
    return call_whole(
        project_body, [*sources, wk, wv], [((total, sources[0].shape[1]), low_type)] * 3
    )


def dec_front_body(
    limit_ref, x_ref, wq, wk, wv, wo, wcq, norms, k_ref, v_ref, cq_ref, q_own, out_own, attn_own,
    st_own, first_own, low_own, unit_own, rate_own, q_ref, o_ref, st_ref, bias_ref,
):
    x = x_ref[...]
    count = x.shape[0]
    half = count // 2
    q_ref[...] = (dot_plain(x, wq[...]) * 0.125).astype(low_type)
    k_ref[...] = dot_plain(x, wk[...]).astype(low_type)
    v_ref[...] = dot_plain(x, wv[...]).astype(low_type)
    rows = lax.broadcasted_iota(jnp.int32, (count, count), 0)
    keys = lax.broadcasted_iota(jnp.int32, (count, count), 1)
    bias_ref[...] = jnp.where((keys <= rows) & (keys < limit_ref[0]), 0.0, masked_score)
    st_ref[...] = jnp.zeros_like(st_ref)
    attend_heads(
        0, PAIRS, [((0, half),), ((0, count),)], half, 2, True, q_ref, k_ref, v_ref, bias_ref,
        o_ref, st_ref,
    )
    gain, shift = scale_shift(norms, DEC_SELF)
    res = x.astype(jnp.float32) + dot_plain(o_ref[...].astype(low_type), wo[...])
    unit, _ = ln_parts(res)
    first = unit * gain + shift
    cq_ref[...] = (dot_plain(first.astype(low_type), wcq[...]) * 0.125).astype(low_type)
    mine = q_own.shape[0]
    start = pl.multiple_of(lax.axis_index("seq") * mine, mine)
    own = pl.ds(start, mine)
    q_own[...] = q_ref[own, :]
    out_own[...] = o_ref[own, :]
    attn = o_ref[own, :].astype(low_type)
    attn_own[...] = attn
    st_own[...] = st_ref[own, :]
    res_own = x_ref[own, :].astype(jnp.float32) + dot_plain(attn, wo[...])
    unit, rate = ln_parts(res_own)
    unit_own[...] = unit
    rate_own[...] = rate
    first = unit * gain + shift
    first_own[...] = first
    low_own[...] = first.astype(low_type)


def dec_front(limit, dec_all, weights, norms, mine):
    count, width = dec_all.shape
    full = jnp.float32
    whole = pl.BlockSpec(memory_space=pltpu.VMEM)
    shapes = [
        ((count, width), low_type),
        ((count, width), low_type),
        ((count, width), low_type),
        ((mine, width), low_type),
        ((mine, width), full),
        ((mine, width), low_type),
        ((mine, LANES), full),
        ((mine, width), full),
        ((mine, width), low_type),
        ((mine, width), full),
        ((mine, 1), full),
    ]
    return pl.pallas_call(
        dec_front_body,
        in_specs=[pl.BlockSpec(memory_space=pltpu.SMEM)] + [whole] * 7,
        out_specs=[whole] * len(shapes),
        out_shape=[jax.ShapeDtypeStruct(shape, kind) for shape, kind in shapes],
        scratch_shapes=[
            pltpu.VMEM((count, width), low_type),
            pltpu.VMEM((count, width), full),
            pltpu.VMEM((count, LANES), full),
            pltpu.VMEM((count, count), full),
        ],
        compiler_params=pltpu.CompilerParams(vmem_limit_bytes=vmem_bytes),
    )(limit, dec_all, *weights, norms)


def enc_front_body(
    win_ref, keep_ref, select, glob, x_ref, wo, wu_far, wd_far, wck_far, wcv_far, norms, attn_ref,
    unit_one, rate_one, low_one, hidden_ref, slope_ref, unit_two, rate_two, low_two, ck_ref, cv_ref,
    wu, wd, wck, wcv, fetch,
):
    copies = bring([wu_far, wd_far, wck_far, wcv_far], [wu, wd, wck, wcv], fetch)
    rows_block = x_ref.shape[0] // 2
    width = x_ref.shape[1]
    for block in range(2):
        rows = pl.ds(block * rows_block, rows_block)
        picked = select[:, block * rows_block : (block + 1) * rows_block]
        placed = dot_left(picked, glob[...].astype(low_type))
        attn = jnp.where(keep_ref[rows, :] > 0, win_ref[rows, :], placed).astype(low_type)
        attn_ref[rows, :] = attn
        unit, rate = ln_parts(x_ref[rows, :].astype(jnp.float32) + dot_plain(attn, wo[...]))
        unit_one[rows, :] = unit
        rate_one[rows, :] = rate
        gain, shift = scale_shift(norms, ENC_ATTN)
        second = unit * gain + shift
        first = second.astype(low_type)
        low_one[rows, :] = first
        if block == 0:
            for copy in copies[:2]:
                copy.wait()
        for k in range(wu.shape[1] // width):
            columns = pl.ds(k * width, width)
            hidden, slope = gelu_pair(dot_plain(first, wu[:, columns]))
            hidden_ref[rows, columns] = hidden
            slope_ref[rows, columns] = slope
            second = second + dot_plain(hidden, wd[columns, :])
        unit, rate = ln_parts(second)
        unit_two[rows, :] = unit
        rate_two[rows, :] = rate
        gain, shift = scale_shift(norms, ENC_FFN)
        memory = (unit * gain + shift).astype(low_type)
        low_two[rows, :] = memory
        if block == 0:
            for copy in copies[2:]:
                copy.wait()
        ck_ref[rows, :] = dot_plain(memory, wck[...]).astype(low_type)
        cv_ref[rows, :] = dot_plain(memory, wcv[...]).astype(low_type)


def enc_front(win_out, keep, select, glob, x, weights, norms):
    count, width = x.shape
    wide = weights[1].shape[1]
    full = jnp.float32
    narrow = (count, width)
    whole = pl.BlockSpec(memory_space=pltpu.VMEM)
    far = pl.BlockSpec(memory_space=pl.ANY)
    shapes = [
            (narrow, low_type),
            (narrow, full),
            ((count, 1), full),
            (narrow, low_type),
            ((count, wide), low_type),
            ((count, wide), low_type),
            (narrow, full),
            ((count, 1), full),
            (narrow, low_type),
            (narrow, low_type),
            (narrow, low_type),
        ]
    return pl.pallas_call(
        enc_front_body,
        in_specs=[whole] * 6 + [far] * 4 + [whole],
        out_specs=[whole] * len(shapes),
        out_shape=[jax.ShapeDtypeStruct(shape, kind) for shape, kind in shapes],
        scratch_shapes=[pltpu.VMEM(weight.shape, low_type) for weight in weights[1:]]
        + [pltpu.SemaphoreType.DMA((4,))],
        compiler_params=pltpu.CompilerParams(vmem_limit_bytes=vmem_bytes),
    )(win_out, keep, select, glob, x, *weights, norms)


def row_sum_steps(peers, whole_ref, out_ref, buffers, send, recv):
    me = lax.axis_index("seq")
    free = peers.bit_length() - 1
    every = slice(None)
    sends, takes, helds = buffers[:free], buffers[free : 2 * free], buffers[2 * free :]

    def source(k):
        return whole_ref if k == 0 else helds[k - 1]

    def copy(k):
        return remote(sends[k], takes[k], (send, recv), k, {"seq": other_of(me, 1 << k)})

    def begin(k):
        digit = (me // (1 << k)) % 2
        lead = (every,) * (free - 1 - k)
        sends[k][...] = source(k)[lead + (1 - digit,)].astype(low_type)
        copy(k).start()

    def end(k):
        copy(k).wait()
        digit = (me // (1 << k)) % 2
        lead = (every,) * (free - 1 - k)
        total = source(k)[lead + (digit,)] + takes[k][...].astype(jnp.float32)
        target = out_ref if k == free - 1 else helds[k]
        target[...] = total

    def step(k):
        if k > 0:
            end(k - 1)
        if k < free:
            begin(k)

    return [functools.partial(step, k) for k in range(free + 1)]


def enc_back_body(
    peers, pieces, parts_ref, g_up, g_down, g_out, dck, dcv, unit_two, rate_two, rate_one, keep_ref,
    select, wck, wcv, norms, *refs
):
    refs = list(refs)

    def take(count):
        result = refs[:count]
        del refs[:count]
        return result

    fars = take(8)
    res_ref, out_ref, window_ref, delta_ref, glob_ref, vec_ref, sum_ref = take(7)
    far_up, far_down, kept_up, kept_down, kept_out = take(5)
    send, recv, send_two, recv_two, load, fetch = take(6)
    held, own, nears = take(6), take(3), take(8)
    down_ref, pre_ref, made_up, made_down, leave = take(5)
    buffers = refs
    wd, wu, slope_ref, unit_one, wo, win_ref, hidden_ref, first_ref = nears
    work = Pieces(
        peers, pieces, [g_up, g_down, g_out], [], [], [kept_up, kept_down, kept_out],
        (send_two, recv_two), load, [held[:2], held[2:4], held[4:]], own, [], 0,
    )
    turn = [0, 1, 2]
    me = lax.axis_index("seq")
    free = peers.bit_length() - 1
    greet([{"seq": other_of(me, 1 << k)} for k in range(free)] + [work.partner("dp")])
    steps = row_sum_steps(peers, parts_ref, sum_ref, buffers, send, recv)
    steps[0]()
    work.open(turn)
    copies = bring(fars, nears, fetch)
    rows_block = dck.shape[0] // 2
    width = dck.shape[1]
    vec_ref[...] = jnp.zeros_like(vec_ref)
    glob = jnp.zeros(glob_ref.shape, jnp.float32)
    for block in range(2):
        rows = pl.ds(block * rows_block, rows_block)
        d_memory = dot_right(dck[rows, :], wck[...]) + dot_right(dcv[rows, :], wcv[...])
        gain, _ = scale_shift(norms, ENC_FFN)
        d_second, d_gain, d_shift = ln_back(d_memory, unit_two[rows, :], rate_two[rows, :], gain)
        vec_ref[2:3, :] += d_gain
        vec_ref[3:4, :] += d_shift
        d_down = d_second.astype(low_type)
        down_ref[rows, :] = d_down
        steps[2 * block + 1]()
        if block == 0:
            work.move(turn[:2], 0)
            for copy in copies[:6]:
                copy.wait()
        for k in range(wu.shape[1] // width):
            columns = pl.ds(k * width, width)
            d_hidden = dot_right(d_down, wd[columns, :])
            d_pre = (d_hidden * slope_ref[rows, columns].astype(jnp.float32)).astype(low_type)
            pre_ref[rows, columns] = d_pre
            d_second = d_second + dot_right(d_pre, wu[:, columns])
        gain, _ = scale_shift(norms, ENC_ATTN)
        d_res, d_gain, d_shift = ln_back(d_second, unit_one[rows, :], rate_one[rows, :], gain)
        vec_ref[0:1, :] += d_gain
        vec_ref[1:2, :] += d_shift
        res_ref[rows, :] = d_res
        d_out = d_res.astype(low_type)
        out_ref[rows, :] = d_out
        d_attn = dot_right(d_out, wo[...]).astype(low_type)
        glob = glob + dot_plain(
            select[:, block * rows_block : (block + 1) * rows_block], d_attn
        )
        d_window = jnp.where(keep_ref[rows, :] > 0, d_attn.astype(jnp.float32), 0.0)
        window_ref[rows, :] = d_window.astype(low_type)
        delta_ref[rows, :] = head_sums(d_window * win_ref[rows, :])
        steps[2 * block + 2]()
    work.move(turn[2:], 0)
    for copy in copies[6:]:
        copy.wait()
    for k in range(wu.shape[1] // width):
        columns = pl.ds(k * width, width)
        product = dot_left(first_ref[...], pre_ref[:, columns]).astype(low_type)
        made_up[:, :, :, :, :, columns] = product.reshape((2,) * free + (-1, width))
        product = dot_left(hidden_ref[:, columns], down_ref[...]).astype(low_type)
        made_down[k // 2, k % 2] = product.reshape(made_down.shape[2:])
    leaving = bring([made_up, made_down], [far_up, far_down], leave)
    work.move(turn, 1)
    for copy in leaving:
        copy.wait()
    glob_ref[...] = glob.astype(low_type)


def head_sums(value):
    lane = lax.broadcasted_iota(jnp.int32, (1, LANES), 1)
    result = jnp.zeros((value.shape[0], LANES), jnp.float32)
    for pair in range(PAIRS):
        two = value[:, pair * LANES : (pair + 1) * LANES]
        for which in range(2):
            inside = (lane // HEAD_DIM) == which
            total = jnp.sum(jnp.where(inside, two, 0.0), axis=1, keepdims=True)
            result = jnp.where(lane == SLOT + 2 * pair + which, total, result)
    return result


def enc_back(query_parts, dck, dcv, kept, weights, norms, made, fars):
    peers = lax.axis_size("seq")
    free = peers.bit_length() - 1
    lead = (2,) * free
    count, width = dck.shape
    full = jnp.float32
    narrow = (count, width)
    wide = fars[1].shape[1]
    glob_count = kept[-1].shape[0]
    rows = query_parts.shape[0] // peers
    shapes = [(2,) * (free - 1 - k) + (rows, width) for k in range(free)]
    plans = [
        piece_plan(peers, ("mat", k), *mat.shape[-2:], kind, 0, 1)
        for k, (mat, kind) in enumerate(zip(made, "xyz"))
    ]
    pieces = [plan for plan, _ in plans]
    whole = pl.BlockSpec(memory_space=pltpu.VMEM)
    far = pl.BlockSpec(memory_space=pl.ANY)
    sem = pltpu.SemaphoreType.DMA
    out_shapes = [
        (narrow, full),
        (narrow, low_type),
        (narrow, low_type),
        ((count, LANES), full),
        ((glob_count, width), low_type),
        ((4, width), full),
        ((rows, width), full),
        (lead + (width // peers, wide), low_type),
        (lead + (wide // peers, width), low_type),
    ] + [(shape[-1], low_type) for _, shape in plans]
    outs = pl.pallas_call(
        functools.partial(enc_back_body, peers, pieces),
        in_specs=[whole]
        + [far] * 3
        + [whole] * (3 + len(kept) + len(weights))
        + [far] * len(fars),
        out_specs=[whole] * 7 + [far] * 2 + [whole] * len(plans),
        out_shape=[jax.ShapeDtypeStruct(shape, kind) for shape, kind in out_shapes],
        scratch_shapes=[sem((free,)), sem((free,)), sem((6,)), sem((6,)), sem((6,))]
        + [sem((len(fars),))]
        + [pltpu.VMEM(one, low_type) for _, shape in plans for one in shape]
        + [pltpu.VMEM((2, 2) + mat.shape[-2:], low_type) for mat in made]
        + [pltpu.VMEM(array.shape, array.dtype) for array in fars]
        + [
            pltpu.VMEM(narrow, low_type),
            pltpu.VMEM((count, wide), low_type),
            pltpu.VMEM(lead + (width // peers, wide), low_type),
            pltpu.VMEM(lead + (wide // peers, width), low_type),
            sem((2,)),
        ]
        + [pltpu.VMEM(shape, low_type) for shape in shapes] * 2
        + [pltpu.VMEM(shape, full) for shape in shapes[:-1]],
        compiler_params=pltpu.CompilerParams(
            collective_id=8, has_side_effects=True, vmem_limit_bytes=62 * 2**20
        ),
    )(
        query_parts.reshape(lead + (rows, width)), *made, dck, dcv, *kept, *weights, norms, *fars
    )
    return outs[:7], outs[7:9], outs[9:], pieces


def turned_stats(stats, padded):
    padded[...] = jnp.zeros_like(padded)
    padded[: stats.shape[0], :] = stats
    return padded[...].T


def dec_back_body(
    limit_ref, sum_ref, res_ref, unit_ref, rate_ref, q_ref, k_ref, v_ref, o_ref, st_ref,
    wcq, wso, wsq, wsk, wsv, norms, dcq_ref, dso_ref, dsq_ref, dsk_ref, dsv_ref, own_ref,
    part_ref, vec_ref, q_pad, d_pad, st_pad, st_turned, bias_ref, dq_ref, key_sum, val_sum,
):
    full = jnp.float32
    mine = q_ref.shape[0]
    d_cq = sum_ref[...].astype(low_type) * 0.125
    dcq_ref[...] = d_cq
    gain, _ = scale_shift(norms, DEC_SELF)
    d_first = res_ref[...] + dot_right(d_cq, wcq[...])
    d_res, d_gain, d_shift = ln_back(d_first, unit_ref[...], rate_ref[...], gain)
    vec_ref[0:1, :] = d_gain
    vec_ref[1:2, :] = d_shift
    d_out = d_res.astype(low_type)
    dso_ref[...] = d_out
    d_attn = dot_right(d_out, wso[...]).astype(low_type)
    st_turned[...] = turned_stats(
        st_ref[...] + head_sums(d_attn.astype(full) * o_ref[...]), st_pad
    )
    q_pad[...] = jnp.zeros_like(q_pad)
    d_pad[...] = jnp.zeros_like(d_pad)
    q_pad[:mine, :] = q_ref[...]
    d_pad[:mine, :] = d_attn
    keys = lax.broadcasted_iota(jnp.int32, bias_ref.shape, 0)
    rows = lax.axis_index("seq") * mine + lax.broadcasted_iota(jnp.int32, bias_ref.shape, 1)
    bias_ref[...] = jnp.where((keys <= rows) & (keys < limit_ref[0]), 0.0, masked_score)
    key_sum[...] = jnp.zeros_like(key_sum)
    val_sum[...] = jnp.zeros_like(val_sum)
    back_heads(
        0, PAIRS, [((0, k_ref.shape[0]),)], LANES, 1, q_pad, k_ref, v_ref, d_pad, st_turned,
        bias_ref, dq_ref, key_sum, val_sum,
    )
    d_q = dq_ref[:mine, :].astype(low_type) * 0.125
    d_k = key_sum[...].astype(low_type)
    d_v = val_sum[...].astype(low_type)
    dsq_ref[...] = d_q
    dsk_ref[...] = d_k
    dsv_ref[...] = d_v
    own_ref[...] = d_res + dot_right(d_q, wsq[...])
    part_ref[...] = (dot_right(d_k, wsk[...]) + dot_right(d_v, wsv[...])).astype(low_type)


def enc_last_body(
    between, rims, gq_ref, gk_ref, gv_ref, gd_ref, go_ref, gs_ref, live_ref, dq_in, dk_in, dv_in, res_ref,
    wq, wk, wv, wgq, wgk, wgv, dgk_ref, dgv_ref, dgq_ref, dq_low, rim_ref, glob_ref, source_ref,
    q_pad, d_pad, st_pad, st_turned, bias_ref, dq_ref, key_sum, val_sum,
):
    full = jnp.float32
    few = gq_ref.shape[0]
    count = gk_ref.shape[0]
    q_pad[...] = jnp.zeros_like(q_pad)
    d_pad[...] = jnp.zeros_like(d_pad)
    q_pad[:few, :] = gq_ref[...]
    d_pad[:few, :] = gd_ref[...]
    st_turned[...] = turned_stats(
        gs_ref[...] + head_sums(gd_ref[...].astype(full) * go_ref[...]), st_pad
    )
    bias_ref[...] = jnp.broadcast_to(live_ref[...], bias_ref.shape)
    key_sum[...] = jnp.zeros_like(key_sum)
    val_sum[...] = jnp.zeros_like(val_sum)
    back_heads(
        0, PAIRS, [((0, count),)], LANES, 1, q_pad, gk_ref, gv_ref, d_pad, st_turned, bias_ref,
        dq_ref, key_sum, val_sum,
    )
    between()
    d_gq = dq_ref[:few, :].astype(low_type) * 0.125
    d_gk = key_sum[...].astype(low_type)
    d_gv = val_sum[...].astype(low_type)
    dgq_ref[...] = d_gq
    dgk_ref[...] = d_gk
    dgv_ref[...] = d_gv
    d_q = dq_in[...].astype(low_type) * 0.125
    dq_low[...] = d_q

    def keys_part(start, size):
        rows = pl.ds(start, size)
        return dot_right(dk_in[rows, :], wk[...]) + dot_right(dv_in[rows, :], wv[...])

    rim_ref[0] = keys_part(0, HALF).astype(low_type)
    rim_ref[1] = keys_part(HALF + count, HALF).astype(low_type)
    rims()
    glob_ref[...] = (keys_part(2 * HALF + count, few) + dot_right(d_gq, wgq[...])).astype(low_type)
    total = res_ref[...] + keys_part(HALF, count) + dot_right(d_q, wq[...])
    source_ref[...] = total + dot_right(d_gk, wgk[...]) + dot_right(d_gv, wgv[...])


def dec_middle_body(
    peers, acc_ref, st_ref, first_ref, cot_ref, norms, wo_far, wu_far, wd_far,
    decoded_ref, res_ref, dout_ref, stats_ref, g_up, g_down, g_out, vec_ref,
    wo, wu, wd, away, acc_one, st_one, low_out, st_out, acc_in, st_in,
    load, send, recv, send_two, recv_two, send_all, recv_all,
):
    full = jnp.float32
    me = lax.axis_index("seq")
    bits, digits = place_bits(peers)
    loads = [
        pltpu.make_async_copy(far, near, load.at[k])
        for k, (far, near) in enumerate(((wo_far, wo), (wu_far, wu), (wd_far, wd)))
    ]
    for copy in loads:
        copy.start()
    acc, top, total = merge_cross(
        peers, acc_ref, st_ref, away, acc_one, st_one, low_out, st_out, acc_in, st_in,
        send, recv, send_two, recv_two,
    )
    cross, lse = finish_parts(acc, top, total)
    cross_low = cross.astype(low_type)
    loads[0].wait()
    unit_one, rate_one = ln_parts(first_ref[...] + dot_plain(cross_low, wo[...]))
    gain, shift = scale_shift(norms, DEC_CROSS)
    second = unit_one * gain + shift
    second_low = second.astype(low_type)
    loads[1].wait()
    hidden, slope = gelu_pair(dot_plain(second_low, wu[...]))
    loads[2].wait()
    unit_two, rate_two = ln_parts(second + dot_plain(hidden, wd[...]))
    gain, shift = scale_shift(norms, DEC_FFN)
    decoded_ref[...] = (unit_two * gain + shift).astype(low_type)
    d_third, d_gain, d_shift = ln_back(cot_ref[...].astype(full), unit_two, rate_two, gain)
    vec_ref[2:3, :] = d_gain
    vec_ref[3:4, :] = d_shift
    d_down = d_third.astype(low_type)
    d_pre = (dot_right(d_down, wd[...]) * slope.astype(full)).astype(low_type)
    d_second = d_third + dot_right(d_pre, wu[...])
    gain, _ = scale_shift(norms, DEC_CROSS)
    d_res, d_gain, d_shift = ln_back(d_second, unit_one, rate_one, gain)
    vec_ref[0:1, :] = d_gain
    vec_ref[1:2, :] = d_shift
    res_ref[...] = d_res
    d_out = d_res.astype(low_type)
    d_cross = dot_right(d_out, wo[...]).astype(low_type)
    dout_ref[tuple(digits)] = d_cross
    stats_ref[tuple(digits)] = lse + head_sums(d_cross.astype(full) * cross)
    refs = [dout_ref, stats_ref]
    sems = (send_all, recv_all)
    reach_out(peers, refs, sems)

    width = d_out.shape[1]
    for k in range(d_pre.shape[1] // width):
        columns = pl.ds(k * width, width)
        product = dot_left(second_low, d_pre[:, k * width : (k + 1) * width]).astype(low_type)
        g_up[:, :, :, :, :, columns] = product.reshape(g_out.shape)
    pass_on(peers, refs, sems)
    for k in range(hidden.shape[1] // width):
        product = dot_left(hidden[:, k * width : (k + 1) * width], d_down).astype(low_type)
        g_down[k // 2, k % 2] = product.reshape(g_down.shape[2:])
    g_out[...] = dot_left(cross_low, d_out).astype(low_type).reshape(g_out.shape)


def merge_cross(
    peers, acc_ref, st_ref, away, acc_one, st_one, low_out, st_out, acc_in, st_in,
    send, recv, send_two, recv_two,
):
    me = lax.axis_index("seq")
    core = me % 2
    pair = me // 2
    half = peers // 2
    mate = {"seq": other_of(me, 1)}
    greet([mate] + [{"seq": lax.rem(me + 2 * k, peers)} for k in range(1, half)])
    for j in range(half):
        away[j] = acc_ref[j, 1 - core].astype(low_type)
    first = [
        remote(away, acc_one, (send, recv), 0, mate),
        remote(st_ref.at[:, 1 - core], st_one, (send, recv), 1, mate),
    ]
    for copy in first:
        copy.start()
    for copy in first:
        copy.wait()
    rest = jnp.zeros((st_one.shape[1], LANES - 2 * SLOT), jnp.float32)

    def join(j):
        acc, top, total = merge_parts([acc_ref[j, core], acc_one[j]], [st_ref[j, core], st_one[j]])
        return acc, jnp.concatenate([top, total, rest], axis=1)

    def ship(k):
        j = lax.rem(pair + k, half)
        return [
            pltpu.make_async_remote_copy(
                src_ref=source.at[j],
                dst_ref=slot.at[half - k],
                send_sem=send_two.at[which, k],
                recv_sem=recv_two.at[which, half - k],
                device_id={"seq": lax.rem(me + 2 * k, peers)},
                device_id_type=pl.DeviceIdType.MESH,
            )
            for which, (source, slot) in enumerate(((low_out, acc_in), (st_out, st_in)))
        ]

    for k in range(1, half):
        j = lax.rem(pair + k, half)
        acc, stat = join(j)
        low_out[j] = acc.astype(low_type)
        st_out[j] = stat
        for copy in ship(k):
            copy.start()
    own_acc, own_stat = join(pair)
    for k in range(1, half):
        for copy in ship(k):
            copy.wait()
    return merge_parts(
        [own_acc] + [acc_in[k] for k in range(1, half)],
        [own_stat] + [st_in[k] for k in range(1, half)],
    )


def dec_middle(acc, stats, dec_first, cotangent, norms, weights):
    peers = lax.axis_size("seq")
    free = peers.bit_length() - 1
    half = peers // 2
    rows, width = dec_first.shape
    full = jnp.float32
    whole = pl.BlockSpec(memory_space=pltpu.VMEM)
    far = pl.BlockSpec(memory_space=pl.ANY)
    wide = weights[1].shape[1]
    lead = (2,) * free
    shapes = [
        ((rows, width), low_type),
        ((rows, width), full),
        (lead + (rows, width), low_type),
        (lead + (rows, LANES), full),
        (lead + (width // peers, wide), low_type),
        (lead + (wide // peers, width), low_type),
        (lead + (width // peers, width), low_type),
        ((4, width), full),
    ]
    sem = pltpu.SemaphoreType.DMA
    decoded, d_res, dout, all_stats, g_up, g_down, g_out, vec = pl.pallas_call(
        functools.partial(dec_middle_body, peers),
        in_specs=[whole] * 5 + [far] * 3,
        out_specs=[whole] * len(shapes),
        out_shape=[jax.ShapeDtypeStruct(shape, kind) for shape, kind in shapes],
        scratch_shapes=[pltpu.VMEM(weight.shape, low_type) for weight in weights]
        + [
            pltpu.VMEM((half, rows, width), low_type),
            pltpu.VMEM((half, rows, width), low_type),
            pltpu.VMEM((half, rows, LANES), full),
            pltpu.VMEM((half, rows, width), low_type),
            pltpu.VMEM((half, rows, LANES), full),
            pltpu.VMEM((half, rows, width), low_type),
            pltpu.VMEM((half, rows, LANES), full),
            sem((3,)),
            sem((2,)),
            sem((2,)),
            sem((2, half)),
            sem((2, half)),
            sem((2 * peers,)),
            sem((2 * peers,)),
        ],
        compiler_params=pltpu.CompilerParams(
            collective_id=4, has_side_effects=True, vmem_limit_bytes=vmem_bytes
        ),
    )(
        acc.reshape(half, 2, rows, width), stats.reshape(half, 2, rows, LANES),
        dec_first, cotangent, norms, *weights,
    )
    return (
        decoded, d_res, dout.reshape(-1, width), all_stats.reshape(-1, LANES),
        (g_up, g_down, g_out), vec,
    )


def resumed(peers, piece, array, k, first, last):
    stages = piece["stages"]
    width = array.shape[-1] * (2 if "dp" in stages[:first] else 1)
    shapes = piece_shapes(peers, array.shape[-2], width, stages)
    return (
        {"from": ("kept", k), "stages": stages, "first": first, "last": last},
        shapes[first : last + 1],
    )


def window_back_body(
    peers, parts, rows_block, blocks, pieces, held_counts, turns, *refs
):
    refs = list(refs)

    def take(count):
        result = refs[:count]
        del refs[:count]
        return result

    q_ref, k_ref, v_ref, d_ref, st_ref, use_ref, part_ref = take(7)
    factors = take(5)
    kept = take(3)
    mats = take(2)
    dec_in = take(16)
    dq_ref, dk_ref, dv_ref, sum_copy = take(4)
    outs = take(len(pieces))
    dec_out = take(8)
    key_sum, val_sum, bias_ref, slot, sum_ref = take(5)
    sems = take(4)
    send, recv, load = take(3)
    held = [take(count) for count in held_counts]
    own = take(2)
    staging = take(3)
    dec_scratch = take(8)
    nears = take(5)
    (fetch,) = take(1)
    fars = dec_in[10:15]
    dec_in[10:15] = nears
    step = pl.program_id(0)
    work = Pieces(
        peers, pieces, mats, factors, kept, outs, (send, recv), load, held, own, staging, 0
    )
    for p, piece in enumerate(pieces):
        for s in range(piece["first"], piece["last"] + 1):
            work.number(p, s)

    @pl.when(step == 0)
    def _():
        greet(everyone(peers) + [work.partner("dp")])
        send_in(peers, [part_ref], [slot], sems)
        bring(fars, nears, fetch)
        work.open(turns[0])
        work.open(turns[2])
        work.open(turns[1])
        keys = lax.broadcasted_iota(jnp.int32, bias_ref.shape, 0)
        rows = lax.broadcasted_iota(jnp.int32, bias_ref.shape, 1)
        near = (jnp.abs(rows + HALF - keys) <= HALF) | (keys >= bias_ref.shape[1] + 2 * HALF)
        bias_ref[...] = jnp.where(near, use_ref[...], masked_score)

    @pl.when(step == 1)
    def _():
        work.move(turns[2], 0)
        sum_at_owner(peers, part_ref, slot, sum_ref, sems)
        send_out(peers, [sum_ref], sems)

    @pl.when(step == 2)
    def _():
        work.move(turns[1], 0)

    backward_body(
        parts, rows_block, blocks, 1, q_ref, k_ref, v_ref, d_ref, st_ref, bias_ref,
        dq_ref, dk_ref, dv_ref, key_sum, val_sum,
    )

    @pl.when(step == PAIRS - 1)
    def _():
        take_out(peers, [sum_ref], sems)
        left(peers, [part_ref], [slot], sems)
        sum_copy[...] = sum_ref[...]
        for copy in fetches(fars, nears, fetch):
            copy.wait()
        dec_back_body(*dec_in, *dec_out, *dec_scratch)
        work.move(turns[0], 2)
        work.move(turns[2], 1)
        work.move(turns[1], 1)


def window_attend_back(
    queries, keys, values, grads, stats, use, parts, rows_block, glob_part, pairs, made, kept, begun,
    limit, dec_inputs
):
    peers = lax.axis_size("seq")
    free = peers.bit_length() - 1
    lead = (2,) * free
    count, width = queries.shape
    key_count = keys.shape[0]
    rows = glob_part.shape[0] // OWNERS
    flops = 10 * count * key_count * width
    factors = []
    places = []
    for pair in pairs:
        spots = []
        for factor in pair:
            known = [k for k, other in enumerate(factors) if other is factor]
            if not known:
                factors.append(factor)
                known = [len(factors) - 1]
            spots.append(known[0])
        places.append(tuple(spots))
    mats = list(made)
    block_rows = width // peers
    plans = [resumed(peers, piece, array, k, 2, 2) for k, (piece, array) in enumerate(zip(begun, kept))]
    plans += [
        piece_plan(peers, ("made", k), block_rows, width, kind, 0, 1, pair)
        for k, (pair, kind) in enumerate(zip(places, "xyz"))
    ]
    plans += [
        piece_plan(peers, ("mat", k), *mat.shape[-2:], kind, 0, 1)
        for k, (mat, kind) in enumerate(zip(mats, "xy"))
    ]
    pieces = [plan for plan, _ in plans]
    shapes = [shape for _, shape in plans]
    sem_count = sum(len(shape) for shape in shapes)
    mine = dec_inputs[0].shape[0]
    dec_keys = dec_inputs[5].shape[0]
    full = jnp.float32
    dec_shapes = [((mine, width), low_type)] * 3 + [((dec_keys, width), low_type)] * 2
    dec_shapes += [((mine, width), full), ((dec_keys, width), low_type), ((2, width), full)]

    def pair_block(size):
        return pl.BlockSpec((size, LANES), lambda p, i: (0, p))

    def whole(*shape):
        return pl.BlockSpec(
            shape, lambda p, i: (0,) * len(shape), pipeline_mode=pl.Buffered(1)
        )

    def whole_out(*shape):
        return pl.BlockSpec(shape, lambda p, i: (0,) * len(shape))

    outs = pl.pallas_call(
        functools.partial(
            window_back_body, peers, parts, rows_block, count // rows_block, pieces,
            [len(shape) for shape in shapes], [[0, 1, 2], [3, 4, 5], [6, 7]],
        ),
        grid=(PAIRS, 1),
        in_specs=[
            pair_block(count),
            pair_block(key_count),
            pair_block(key_count),
            pair_block(count),
            whole(2 * SLOT, count),
            whole(key_count, 1),
            whole(OWNERS, rows, width),
        ]
        + [whole(*array.shape) for array in factors + list(kept)]
        + [pl.BlockSpec(memory_space=pl.ANY)] * len(mats)
        + [pl.BlockSpec(memory_space=pltpu.SMEM)]
        + [
            pl.BlockSpec(memory_space=pl.ANY) if 9 <= k < 14 else whole(*array.shape)
            for k, array in enumerate(dec_inputs)
        ],
        out_specs=[
            pair_block(count),
            pair_block(key_count),
            pair_block(key_count),
            whole_out(OWNERS, rows, width),
        ]
        + [whole_out(*shape[-1]) for shape in shapes]
        + [whole_out(*shape) for shape, _ in dec_shapes],
        out_shape=[
            jax.ShapeDtypeStruct((count, width), low_type),
            jax.ShapeDtypeStruct((key_count, width), low_type),
            jax.ShapeDtypeStruct((key_count, width), low_type),
            jax.ShapeDtypeStruct((OWNERS, rows, width), low_type),
        ]
        + [jax.ShapeDtypeStruct(shape[-1], low_type) for shape in shapes]
        + [jax.ShapeDtypeStruct(shape, kind) for shape, kind in dec_shapes],
        scratch_shapes=[
            pltpu.VMEM((key_count, LANES), jnp.float32),
            pltpu.VMEM((key_count, LANES), jnp.float32),
            pltpu.VMEM((key_count, count), jnp.float32),
            pltpu.VMEM((peers, rows, width), low_type),
            pltpu.VMEM((OWNERS, rows, width), low_type),
        ]
        + owner_sems(peers, 1)
        + [pltpu.SemaphoreType.DMA((sem_count,))] * 2
        + [pltpu.SemaphoreType.DMA((2 * len(mats),))]
        + [pltpu.VMEM(one, low_type) for shape in shapes for one in shape]
        + [pltpu.VMEM((2, 2) + mat.shape[-2:], low_type) for mat in mats]
        + [pltpu.VMEM(lead + (block_rows, width), low_type)] * 3
        + [
            pltpu.VMEM((LANES, width), low_type),
            pltpu.VMEM((LANES, width), low_type),
            pltpu.VMEM((LANES, LANES), full),
            pltpu.VMEM((LANES, LANES), full),
            pltpu.VMEM((dec_keys, LANES), full),
            pltpu.VMEM((LANES, width), full),
            pltpu.VMEM((dec_keys, width), full),
            pltpu.VMEM((dec_keys, width), full),
        ]
        + [pltpu.VMEM(array.shape, low_type) for array in dec_inputs[9:14]]
        + [pltpu.SemaphoreType.DMA((5,))],
        compiler_params=pltpu.CompilerParams(
            collective_id=7, has_side_effects=True, vmem_limit_bytes=62 * 2**20
        ),
        cost_estimate=pl.CostEstimate(
            flops=4 * flops,
            bytes_accessed=2 * (2 * count + 4 * key_count) * width + 4 * count * width,
            transcendentals=count * key_count * HEADS,
        ),
    )(
        queries, keys, values, grads, stats, use, glob_part.reshape(OWNERS, rows, width),
        *factors, *kept, *mats, limit, *dec_inputs,
    )
    last = 4 + len(pieces)
    return outs[:3], outs[3].reshape(-1, width), outs[4:last], pieces, outs[last:]


def last_body(peers, plan, *refs):
    refs = list(refs)

    def take(count):
        result = refs[:count]
        del refs[:count]
        return result

    pieces = plan["pieces"]
    kept = take(plan["kept"])
    factors = take(plan["factors"])
    target_part, vec_part = take(2)
    enc_in = take(plan["enc_in"])
    outs = take(len(pieces))
    target_out, glob_out, vec_out, from_after, from_before, source_ref = take(6)
    send, recv, fetch = take(3)
    held = [take(count) for count in plan["held"]]
    staging = take(plan["slots"])
    tall, late = plan["tall"], enc_in[8:]
    nears = take(len(tall) + len(late))
    fars = [factors[k] for k in tall] + late
    for k, near in zip(tall, nears):
        factors[k] = near
    enc_in[8:] = nears[len(tall) :]
    target_held = take(plan["free"])
    glob_held = take(plan["free"])
    vec_held = take(plan["free"] + 1)
    d_gk, d_gv, d_gq, d_q, rim, glob_part = take(6)
    enc_scratch = take(8)
    me = lax.axis_index("seq")
    bits = [1 << k for k in range(plan["free"])]
    own_x = factors[plan["rows"]].at[pl.ds(HALF, d_q.shape[0]), :]
    work = Pieces(
        peers, pieces, [], factors + [d_gk, d_gv, d_gq, d_q, own_x], kept, outs, (send, recv), None, held,
        [], staging, 0
    )
    left_one = {"seq": lax.rem(me + peers - 1, peers)}
    right_one = {"seq": lax.rem(me + 1, peers)}
    greet([work.partner(stage) for stage in bits + ["dp"]] + [left_one, right_one])
    sems = (send, recv)
    to_left = remote(rim.at[0], from_after, sems, work.number("left"), left_one)
    to_right = remote(rim.at[1], from_before, sems, work.number("right"), right_one)

    target_stages = bits
    vec_stages = bits + ["dp"]

    def target_copy(s):
        origin = target_part if s == 0 else target_held[s - 1]
        return work.copy("t", target_stages, origin, target_held[s], s), origin

    def whole_copy(name, part, result, buffers, stages, s):
        origin = part if s == 0 else result
        copy = remote(
            origin, buffers[s], sems, work.number(name, s), work.partner(stages[s])
        )
        return copy, origin

    def small_begin(s):
        if s < len(bits):
            target_copy(s)[0].start()
            whole_copy("g", glob_part, glob_out, glob_held, bits, s)[0].start()
        whole_copy("v", vec_part, vec_out, vec_held, vec_stages, s)[0].start()

    def small_end(s):
        if s < len(bits):
            copy, origin = target_copy(s)
            copy.wait()
            finish = target_out if s == len(bits) - 1 else None
            work.fold(target_stages, origin, target_held[s], s, finish)
            copy, origin = whole_copy("g", glob_part, glob_out, glob_held, bits, s)
            copy.wait()
            glob_out[...] = origin[...] + glob_held[s][...]
        copy, origin = whole_copy("v", vec_part, vec_out, vec_held, vec_stages, s)
        copy.wait()
        vec_out[...] = origin[...] + vec_held[s][...]

    turns = plan["turns"]
    work.open(turns[0])
    work.open(turns[5])
    fetched = bring(fars, nears, fetch)
    work.open(turns[1])
    work.open(turns[2])
    work.move(turns[1], 0)
    work.move(turns[2], 0)
    for copy in fetched:
        copy.wait()
    keys, vals = (factors[k] for k in plan["shared"])

    def rims():
        @pl.when(me > 0)
        def _():
            to_left.start()

        @pl.when(me < peers - 1)
        def _():
            to_right.start()

    enc_last_body(
        lambda: work.move(turns[0], 2), rims, *enc_in[:8], keys, vals, *enc_in[8:], d_gk, d_gv, d_gq, d_q,
        rim, glob_part, source_ref, *enc_scratch,
    )

    small_begin(0)
    work.move(turns[5], 3)
    work.open(turns[3])
    work.move(turns[1], 1)
    work.move(turns[3], 0)
    work.move(turns[5], 4)
    work.move(turns[2], 1)
    work.move(turns[0], 3)
    small_end(0)
    small_begin(1)
    work.open(turns[4])
    work.move(turns[1], 2)
    work.move(turns[4], 0)
    work.move(turns[3], 1)
    work.move(turns[2], 2)
    work.move(turns[0], 4)
    work.move(turns[1], 3)
    small_end(1)
    small_begin(2)
    work.move(turns[4], 1)
    work.move(turns[3], 2)
    work.move(turns[2], 3)
    work.move(turns[1], 4)
    small_end(2)
    small_begin(3)
    work.move(turns[4], 2)
    work.move(turns[3], 3)
    work.move(turns[2], 4)
    small_end(3)
    small_begin(4)
    work.move(turns[4], 3)
    work.move(turns[3], 4)
    small_end(4)
    work.move(turns[4], 4)

    @pl.when(me > 0)
    def _():
        to_left.wait_send()
        remote(rim.at[1], from_before, sems, work.number("right"), left_one).wait_recv()

    @pl.when(me < peers - 1)
    def _():
        to_right.wait_send()
        remote(rim.at[0], from_after, sems, work.number("left"), right_one).wait_recv()


KINDS = "xyxxyxxxyxx"


def last_exchange(kept, begun, pairs, enc_inputs, target_part, vec_part):
    peers = lax.axis_size("seq")
    free = peers.bit_length() - 1
    lead = (2,) * free
    full = jnp.float32
    factors = []
    spots = []
    for pair in pairs:
        spot = []
        for factor in pair:
            if isinstance(factor, int):
                spot.append(factor - 5)
                continue
            known = [k for k, other in enumerate(factors) if other is factor]
            if not known:
                factors.append(factor)
                known = [len(factors) - 1]
            spot.append(known[0])
        spots.append(tuple(spot))
    width = pairs[0][0].shape[1]
    rows = width // peers
    slots = 5
    last = free
    plans = [
        resumed(peers, piece, array, k, piece["last"] + 1, last)
        for k, (piece, array) in enumerate(zip(begun, kept))
    ]
    order = [0, 1, 2, 3, 4, 5, 6, 7, 8, 9, 10]
    for k, spot in zip(order, spots):
        slot = k % 5
        plans.append(piece_plan(peers, ("made", slot), rows, width, KINDS[k], 0, last, spot))
    pieces = [plan for plan, _ in plans]
    shapes = [shape for _, shape in plans]
    begun_count = len(begun)
    made = list(range(begun_count, len(pieces)))
    far_on = [k for k, piece in enumerate(begun) if piece["last"] == 2]
    fresh = [k for k in range(begun_count) if k not in far_on]
    turns = [fresh, made[:3], made[3:5], made[5:8], made[8:], far_on]
    target_shapes = piece_shapes(
        peers, target_part.shape[0] // peers, width, [1 << k for k in range(free)]
    )
    few = enc_inputs[0].shape[0]
    count = enc_inputs[1].shape[0]
    narrow = (count, width)
    tall = [k for k, factor in enumerate(factors) if factor.shape[0] > count]
    late = enc_inputs[8:]
    far = pl.BlockSpec(memory_space=pl.ANY)
    plan = {
        "pieces": pieces,
        "kept": begun_count,
        "factors": len(factors),
        "enc_in": len(enc_inputs),
        "held": [len(shape) for shape in shapes],
        "slots": slots,
        "turns": turns,
        "free": free,
        "shared": (spots[8][1], spots[9][1]),
        "rows": spots[8][0],
        "tall": tall,
    }
    sems = sum(len(shape) for shape in shapes) + free * 3 + 3
    whole = pl.BlockSpec(memory_space=pltpu.VMEM)
    out_shapes = [(shape[-1], full) for shape in shapes] + [
        (target_shapes[-1], full),
        ((few, width), low_type),
        (vec_part.shape, full),
        ((HALF, width), low_type),
        ((HALF, width), low_type),
        (narrow, full),
    ]
    sem = pltpu.SemaphoreType.DMA((sems,))
    outs = pl.pallas_call(
        functools.partial(last_body, peers, plan),
        in_specs=[whole] * begun_count
        + [far if k in tall else whole for k in range(len(factors))]
        + [whole] * 10
        + [far] * len(late),
        out_specs=[whole] * len(out_shapes),
        out_shape=[jax.ShapeDtypeStruct(shape, kind) for shape, kind in out_shapes],
        scratch_shapes=[sem, sem, pltpu.SemaphoreType.DMA((len(tall) + len(late),))]
        + [pltpu.VMEM(one, low_type) for shape in shapes for one in shape]
        + [pltpu.VMEM(lead + (rows, width), low_type)] * slots
        + [pltpu.VMEM(factors[k].shape, low_type) for k in tall]
        + [pltpu.VMEM(array.shape, array.dtype) for array in late]
        + [pltpu.VMEM(shape, low_type) for shape in target_shapes]
        + [pltpu.VMEM((few, width), low_type)] * free
        + [pltpu.VMEM(vec_part.shape, full)] * (free + 1)
        + [
            pltpu.VMEM(narrow, low_type),
            pltpu.VMEM(narrow, low_type),
            pltpu.VMEM((few, width), low_type),
            pltpu.VMEM(narrow, low_type),
            pltpu.VMEM((2, HALF, width), low_type),
            pltpu.VMEM((few, width), low_type),
            pltpu.VMEM((LANES, width), low_type),
            pltpu.VMEM((LANES, width), low_type),
            pltpu.VMEM((LANES, LANES), full),
            pltpu.VMEM((LANES, LANES), full),
            pltpu.VMEM((count, LANES), full),
            pltpu.VMEM((LANES, width), full),
            pltpu.VMEM(narrow, full),
            pltpu.VMEM(narrow, full),
        ],
        compiler_params=pltpu.CompilerParams(
            collective_id=1, has_side_effects=True, vmem_limit_bytes=63 * 2**20
        ),
    )(
        *kept, *factors, target_part.reshape(lead + (-1, width)), vec_part, *enc_inputs
    )
    return outs[: len(pieces)], outs[len(pieces) :]


def per_device(
    source,
    target,
    cotangent,
    src_len,
    dec_len,
    global_pos,
    enc_query,
    enc_key,
    enc_value,
    glob_query,
    glob_key,
    glob_value,
    enc_out,
    enc_attn_gain,
    enc_attn_shift,
    enc_up,
    enc_down,
    enc_ffn_gain,
    enc_ffn_shift,
    self_query,
    self_key,
    self_value,
    self_out,
    dec_self_gain,
    dec_self_shift,
    cross_query,
    cross_key,
    cross_value,
    cross_out,
    dec_cross_gain,
    dec_cross_shift,
    dec_up,
    dec_down,
    dec_ffn_gain,
    dec_ffn_shift,
):
    full = jnp.float32
    src_x = source[0]
    dec_x = target[0]
    src_count = src_x.shape[0]
    dec_count = dec_x.shape[0]
    seq_index = lax.axis_index("seq")
    peers = lax.axis_size("seq")
    src_limit = src_len[0]
    glob_places = global_pos[0]
    glob_count = glob_places.shape[0]
    src_places = seq_index * src_count + jnp.arange(src_count, dtype=jnp.int32)
    select_glob = glob_places[:, None] == src_places[None, :]
    select_low = select_glob.astype(low_type)
    norms = jnp.concatenate(
        [
            enc_attn_gain, enc_attn_shift, enc_ffn_gain, enc_ffn_shift, dec_self_gain,
            dec_self_shift, dec_cross_gain, dec_cross_shift, dec_ffn_gain, dec_ffn_shift,
        ]
    ).astype(full).reshape(10, -1)

    upward = [(i, i + 1) for i in range(peers - 1)]
    downward = [(i + 1, i) for i in range(peers - 1)]
    dec_all, glob_x, query_loc, glob_keys_loc, glob_vals_loc = start_exchange(
        dec_x,
        dot_plain(select_low, src_x).astype(low_type),
        src_x,
        (enc_query, glob_key, glob_value),
    )
    rim_x, _ = lax.optimization_barrier((src_x, glob_x))
    before = lax.ppermute(rim_x[src_count - HALF :], "seq", upward)
    after = lax.ppermute(rim_x[:HALF], "seq", downward)

    (self_k, self_v, all_cross_q, self_q, self_out_full, self_attn, self_stats, dec_first,
     dec_first_low, self_unit, self_rate) = dec_front(
        dec_len,
        dec_all,
        (self_query, self_key, self_value, self_out, cross_query),
        norms,
        dec_count,
    )

    glob_queries = (dot_plain(glob_x, glob_query) * 0.125).astype(low_type)
    live_bias = jnp.where(src_places < src_limit, 0.0, masked_score)
    glob_acc, glob_stats = attend(
        glob_queries, glob_keys_loc, glob_vals_loc, live_bias[None, :], None, glob_count, False, 6
    )

    x_all, keys_all, vals_all = project_all((before, src_x, after, glob_x), enc_key, enc_value)
    pad_count = src_count + 2 * HALF
    pad_places = seq_index * src_count - HALF + jnp.arange(pad_count, dtype=jnp.int32)
    pad_glob = jnp.any(glob_places[:, None] == pad_places[None, :], axis=0)
    pad_use = (pad_places >= 0) & (pad_places < src_limit) & jnp.logical_not(pad_glob)
    win_use = jnp.concatenate(
        [jnp.where(pad_use, 0.0, masked_score), jnp.zeros((glob_count,), full)]
    )
    keep = jnp.where(pad_glob[HALF : HALF + src_count], 0.0, 1.0)[:, None]
    rows_block = 256
    reach = rows_block + 2 * HALF
    win_parts = [
        ((block * rows_block, reach), (pad_count, glob_count))
        for block in range(src_count // rows_block)
    ]
    win_out, win_stats, glob_out, glob_lse = window_attend(
        query_loc, keys_all, vals_all, win_use[None, :], win_parts, rows_block, glob_acc, glob_stats
    )
    (enc_attn, unit_one, rate_one, enc_first_low, enc_hidden, enc_slope, unit_two, rate_two,
     memory_low, cross_k, cross_v) = enc_front(
        win_out,
        keep,
        select_low,
        glob_out,
        src_x,
        (enc_out, enc_up, enc_down, cross_key, cross_value),
        norms,
    )

    cross_acc, cross_stats = attend(
        all_cross_q, cross_k, cross_v, live_bias[None, :], None, 256, False, 2
    )
    decoded, d_res_two, all_dout, all_stats, dec_made, dec_vec = dec_middle(
        cross_acc, cross_stats, dec_first, cotangent[0], norms, (cross_out, dec_up, dec_down)
    )
    query_parts, ck_low, cv_low = attend_back(
        all_cross_q,
        cross_k,
        cross_v,
        all_dout,
        all_stats[:, : 2 * SLOT].T,
        jnp.broadcast_to(live_bias[:, None], (src_count, 512)),
        None,
        256,
        2,
    )

    enc_grads, enc_made, dec_kept, dec_begun = enc_back(
        query_parts,
        ck_low,
        cv_low,
        (unit_two, rate_two, rate_one, keep, select_low),
        (cross_key, cross_value),
        norms,
        dec_made,
        (enc_down, enc_up, enc_slope, unit_one, enc_out, win_out, enc_hidden, enc_first_low),
    )
    d_enc_res, d_attn_o, d_window, win_delta, glob_part, enc_vec, d_cross_sum = enc_grads
    win_pair = (win_stats + win_delta)[:, : 2 * SLOT].T
    (d_query, d_keys_all, d_vals_all), glob_dout, kept, begun, dec_grads = window_attend_back(
        query_loc, keys_all, vals_all, d_window, win_pair, win_use[:, None], win_parts, rows_block,
        glob_part,
        [(memory_low, ck_low), (memory_low, cv_low), (enc_attn, d_attn_o)],
        enc_made,
        dec_kept,
        dec_begun,
        dec_len,
        (d_cross_sum, d_res_two, self_unit, self_rate, self_q, self_k, self_v, self_out_full,
         self_stats, cross_query, self_out, self_query, self_key, self_value, norms),
    )
    (d_cross_q, d_self_o, d_self_q, d_self_k, d_self_v, d_target_own, d_target_part,
     self_vec) = dec_grads
    vec_part = jnp.concatenate(
        [enc_vec, self_vec, dec_vec, jnp.zeros((6, enc_vec.shape[1]), full)], axis=0
    )

    own_gk, own_gv, own_gq, own_q, own_x = range(5)
    pairs = [
        (dec_first_low, d_cross_q),
        (self_attn, d_self_o),
        (dec_x, d_self_q),
        (dec_all, d_self_k),
        (dec_all, d_self_v),
        (own_x, own_q),
        (own_x, own_gk),
        (own_x, own_gv),
        (x_all, d_keys_all),
        (x_all, d_vals_all),
        (glob_x, own_gq),
    ]
    shared, rest = last_exchange(
        kept,
        begun,
        pairs,
        (glob_queries, glob_keys_loc, glob_vals_loc, glob_dout, glob_out, glob_lse,
         live_bias[:, None], d_query, d_enc_res,
         enc_query, enc_key, enc_value, glob_query, glob_key, glob_value),
        d_target_part,
        vec_part,
    )
    d_target_sum, d_glob_x, vec_sum, from_after, from_before, d_source_own = rest
    vectors = share_vectors(vec_sum, 10)
    flags = jnp.stack([seq_index < peers - 1, seq_index > 0]).astype(jnp.int32)[None, :]
    (
        s_dec_up, s_dec_down, s_cross_out,
        s_cross_key, s_cross_value, s_enc_out, s_enc_up, s_enc_down, s_cross_query, s_self_out,
        s_self_query, s_self_key, s_self_value,
        s_enc_query, s_glob_key, s_glob_value, s_enc_key, s_enc_value, s_glob_query,
        d_source, d_target,
    ) = end_outputs(
        shared,
        (d_source_own, from_after, from_before, select_low, d_glob_x, flags),
        (d_target_own, d_target_sum),
    )
    return (
        decoded[None],
        d_source[None],
        d_target[None],
        s_enc_query,
        s_enc_key,
        s_enc_value,
        s_glob_query,
        s_glob_key,
        s_glob_value,
        s_enc_out,
        vectors[0],
        vectors[1],
        s_enc_up,
        s_enc_down,
        vectors[2],
        vectors[3],
        s_self_query,
        s_self_key,
        s_self_value,
        s_self_out,
        vectors[4],
        vectors[5],
        s_cross_query,
        s_cross_key,
        s_cross_value,
        s_cross_out,
        vectors[6],
        vectors[7],
        s_dec_up,
        s_dec_down,
        vectors[8],
        vectors[9],
    )


def swap_dp(value):
    pairs = [(i, i ^ 1) for i in range(lax.axis_size("dp"))]
    return lax.ppermute(value, "dp", pairs)


def gather_rows(value):
    rows, width = value.shape
    held = value[None]
    for bit in reversed(seq_bits()):
        other = swap(held, bit)
        upper = bit_set(bit)
        held = jnp.stack(
            [jnp.where(upper, other, held), jnp.where(upper, held, other)], axis=1
        ).reshape(2 * held.shape[0], rows, width)
    return held.reshape(-1, width)


def add_all(value):
    for bit in seq_bits():
        value = value + swap(value, bit)
    return value


def scatter_all(value):
    bits = seq_bits()
    held = value.reshape((2,) * len(bits) + (-1, value.shape[1]))
    for step, bit in enumerate(bits):
        axis = len(bits) - 1 - step
        mine = bit_set(bit).astype(jnp.int32)
        other = swap(pick_half(held, 1 - mine, axis).astype(low_type), bit)
        held = pick_half(held, mine, axis) + other.astype(jnp.float32)
    return held


def merge_body(acc_a, st_a, acc_b, st_b, acc_o, st_o):
    top_a, top_b = st_a[:, :SLOT], st_b[:, :SLOT]
    top = jnp.maximum(top_a, top_b)
    keep_a = jnp.exp(top_a - top)
    keep_b = jnp.exp(top_b - top)
    total = st_a[:, SLOT : 2 * SLOT] * keep_a + st_b[:, SLOT : 2 * SLOT] * keep_b
    spread = head_spread()
    acc_o[...] = acc_a[...] * exact_dot(keep_a, spread) + acc_b[...].astype(
        jnp.float32
    ) * exact_dot(keep_b, spread)
    rest = jnp.zeros((top.shape[0], LANES - 2 * SLOT), jnp.float32)
    st_o[...] = jnp.concatenate([top, total, rest], axis=1)


def merge_soft(held, other):
    rows = held[0].shape[0]
    return pl.pallas_call(
        merge_body,
        out_shape=[
            jax.ShapeDtypeStruct((rows, held[0].shape[1]), jnp.float32),
            jax.ShapeDtypeStruct((rows, LANES), jnp.float32),
        ],
        compiler_params=pltpu.CompilerParams(vmem_limit_bytes=vmem_bytes),
    )(*held, *other)


def merge_all(held):
    for bit in seq_bits():
        held = merge_soft(held, swap((held[0].astype(low_type), held[1]), bit))
    return held


def merge_scatter(held):
    bits = seq_bits()
    for step, bit in enumerate(bits):
        inner = len(bits) - 1 - step
        mine = bit_set(bit).astype(jnp.int32)

        def halves(value, chosen):
            split = value.reshape(1 << inner, 2, -1, value.shape[1])
            return pick_half(split, chosen, 1).reshape(-1, value.shape[1])

        away = (halves(held[0], 1 - mine).astype(low_type), halves(held[1], 1 - mine))
        held = merge_soft((halves(held[0], mine), halves(held[1], mine)), swap(away, bit))
    return held


def share_grads(grads, dp_first):
    bits = seq_bits()
    width = grads[0].shape[1]
    half = width // 2
    rows = [grad.shape[0] >> len(bits) for grad in grads]
    dp_mine = lax.axis_index("dp")
    laid = [
        grad.astype(low_type).reshape((2,) * len(bits) + (count, width))
        for grad, count in zip(grads, rows)
    ]
    steps = [(1, False)]
    rest = [(bit, False) for bit in bits[1:]]
    steps += [(0, True)] + rest if dp_first else rest[:1] + [(0, True)] + rest[1:]
    held = None
    axis = len(bits)
    for bit, is_dp in steps:
        if is_dp:
            own = lax.dynamic_slice_in_dim(held, dp_mine * half, half, held.ndim - 1)
            away = lax.dynamic_slice_in_dim(held, (1 - dp_mine) * half, half, held.ndim - 1)
            held = own + swap_dp(away)
            continue
        axis -= 1
        mine = bit_set(bit).astype(jnp.int32)
        if held is None:
            away = jnp.concatenate([pick_half(v, 1 - mine, axis) for v in laid], axis=-2)
            own = jnp.concatenate([pick_half(v, mine, axis) for v in laid], axis=-2)
        else:
            away = pick_half(held, 1 - mine, axis)
            own = pick_half(held, mine, axis)
        held = own + swap(away, bit)
    result = []
    start = 0
    for count in rows:
        result.append(held[start : start + count].astype(jnp.float32))
        start += count
    return result


def share_norms(vectors):
    stacked = jnp.concatenate([jnp.stack(vectors), jnp.zeros((6, vectors[0].shape[0]))], axis=0)
    total = add_all(stacked)
    total = total + swap_dp(total)
    length = stacked.shape[1] // lax.axis_size("seq")
    mine = lax.dynamic_slice_in_dim(total, lax.axis_index("seq") * length, length, 1)
    return [mine[k] for k in range(len(vectors))]


def per_device_wide(
    source,
    target,
    cotangent,
    src_len,
    dec_len,
    global_pos,
    enc_query,
    enc_key,
    enc_value,
    glob_query,
    glob_key,
    glob_value,
    enc_out,
    enc_attn_gain,
    enc_attn_shift,
    enc_up,
    enc_down,
    enc_ffn_gain,
    enc_ffn_shift,
    self_query,
    self_key,
    self_value,
    self_out,
    dec_self_gain,
    dec_self_shift,
    cross_query,
    cross_key,
    cross_value,
    cross_out,
    dec_cross_gain,
    dec_cross_shift,
    dec_up,
    dec_down,
    dec_ffn_gain,
    dec_ffn_shift,
):
    full = jnp.float32
    src_x = source[0]
    dec_x = target[0]
    src_count = src_x.shape[0]
    dec_count = dec_x.shape[0]
    seq_index = lax.axis_index("seq")
    peers = lax.axis_size("seq")
    src_limit = src_len[0]
    dec_limit = dec_len[0]
    glob_places = global_pos[0]
    glob_count = glob_places.shape[0]
    src_places = seq_index * src_count + jnp.arange(src_count, dtype=jnp.int32)
    select_glob = glob_places[:, None] == src_places[None, :]
    select_low = select_glob.astype(low_type)
    is_global = jnp.any(select_glob, axis=0)
    spread = head_spread()

    upward = [(i, i + 1) for i in range(peers - 1)]
    downward = [(i + 1, i) for i in range(peers - 1)]
    before = lax.ppermute(src_x[src_count - HALF :], "seq", upward)
    after = lax.ppermute(src_x[:HALF], "seq", downward)
    dec_all = gather_rows(dec_x)
    glob_x = add_all(dot_plain(select_low, src_x).astype(low_type))

    query_loc = (dot_plain(src_x, enc_query) * 0.125).astype(low_type)
    glob_keys_loc = dot_plain(src_x, glob_key).astype(low_type)
    glob_vals_loc = dot_plain(src_x, glob_value).astype(low_type)

    self_q = (dot_plain(dec_x, self_query) * 0.125).astype(low_type)
    self_k = dot_plain(dec_all, self_key).astype(low_type)
    self_v = dot_plain(dec_all, self_value).astype(low_type)
    dec_total = dec_all.shape[0]
    dec_places = seq_index * dec_count + jnp.arange(dec_count, dtype=jnp.int32)
    all_dec = jnp.arange(dec_total, dtype=jnp.int32)
    self_allowed = (all_dec[None, :] <= dec_places[:, None]) & (all_dec < dec_limit)[None, :]
    self_bias = jnp.where(self_allowed, 0.0, masked_score)
    self_out_full, self_stats = attend(self_q, self_k, self_v, self_bias, None, dec_count, True)
    self_attn = self_out_full.astype(low_type)
    dec_res_one = dec_x.astype(full) + dot_plain(self_attn, self_out)
    dec_first, dec_first_back = jax.vjp(
        layer_norm, dec_res_one, dec_self_gain.astype(full), dec_self_shift.astype(full)
    )
    dec_first_low = dec_first.astype(low_type)
    cross_q = (dot_plain(dec_first_low, cross_query) * 0.125).astype(low_type)
    all_cross_q = gather_rows(cross_q)

    glob_queries = (dot_plain(glob_x, glob_query) * 0.125).astype(low_type)
    live_bias = jnp.where(src_places < src_limit, 0.0, masked_score)
    glob_acc, glob_stats = merge_all(
        attend(
            glob_queries, glob_keys_loc, glob_vals_loc, live_bias[None, :], None, glob_count, False
        )
    )
    glob_total = glob_stats[:, SLOT : 2 * SLOT]
    glob_out = glob_acc / exact_dot(glob_total, spread)
    glob_lse = glob_stats[:, :SLOT] + jnp.log(jnp.maximum(glob_total, 1e-30))

    x_all = jnp.concatenate([before, src_x, after, glob_x], axis=0)
    keys_all = dot_plain(x_all, enc_key).astype(low_type)
    vals_all = dot_plain(x_all, enc_value).astype(low_type)
    pad_count = src_count + 2 * HALF
    pad_places = seq_index * src_count - HALF + jnp.arange(pad_count, dtype=jnp.int32)
    pad_glob = jnp.any(glob_places[:, None] == pad_places[None, :], axis=0)
    pad_use = (pad_places >= 0) & (pad_places < src_limit) & jnp.logical_not(pad_glob)
    near = jnp.abs(src_places[:, None] - pad_places[None, :]) <= HALF
    win_bias = jnp.concatenate(
        [
            jnp.where(near & pad_use[None, :], 0.0, masked_score),
            jnp.zeros((src_count, glob_count), full),
        ],
        axis=1,
    )
    near_turned = jnp.abs(src_places[None, :] - pad_places[:, None]) <= HALF
    win_bias_turned = jnp.concatenate(
        [
            jnp.where(near_turned & pad_use[:, None], 0.0, masked_score),
            jnp.zeros((glob_count, src_count), full),
        ],
        axis=0,
    )
    rows_block = 256
    reach = rows_block + 2 * HALF
    win_parts = [
        ((block * rows_block, reach), (pad_count, glob_count))
        for block in range(src_count // rows_block)
    ]
    win_out, win_stats = attend(
        query_loc, keys_all, vals_all, win_bias, win_parts, rows_block, True
    )
    placed = dot_left(select_low, glob_out.astype(low_type))
    enc_attn = jnp.where(is_global[:, None], placed, win_out).astype(low_type)
    enc_res = src_x.astype(full) + dot_plain(enc_attn, enc_out)
    enc_first, enc_first_back = jax.vjp(
        layer_norm, enc_res, enc_attn_gain.astype(full), enc_attn_shift.astype(full)
    )
    enc_first_low = enc_first.astype(low_type)
    enc_hidden, enc_slope = gelu_pair(dot_plain(enc_first_low, enc_up))
    enc_second = enc_first + dot_plain(enc_hidden, enc_down)
    memory, enc_final_back = jax.vjp(
        layer_norm, enc_second, enc_ffn_gain.astype(full), enc_ffn_shift.astype(full)
    )
    memory_low = memory.astype(low_type)

    cross_k = dot_plain(memory_low, cross_key).astype(low_type)
    cross_v = dot_plain(memory_low, cross_value).astype(low_type)
    cross_acc, cross_stats = merge_scatter(
        attend(all_cross_q, cross_k, cross_v, live_bias[None, :], None, 256, False)
    )
    cross_total = cross_stats[:, SLOT : 2 * SLOT]
    cross_out_full = cross_acc / exact_dot(cross_total, spread)
    cross_lse = cross_stats[:, :SLOT] + jnp.log(jnp.maximum(cross_total, 1e-30))
    cross_attn = cross_out_full.astype(low_type)
    dec_res_two = dec_first + dot_plain(cross_attn, cross_out)
    dec_second, dec_second_back = jax.vjp(
        layer_norm, dec_res_two, dec_cross_gain.astype(full), dec_cross_shift.astype(full)
    )
    dec_second_low = dec_second.astype(low_type)
    dec_hidden, dec_slope = gelu_pair(dot_plain(dec_second_low, dec_up))
    dec_third = dec_second + dot_plain(dec_hidden, dec_down)
    decoded, dec_final_back = jax.vjp(
        layer_norm, dec_third, dec_ffn_gain.astype(full), dec_ffn_shift.astype(full)
    )

    d_third, g_dec_ffn_gain, g_dec_ffn_shift = dec_final_back(cotangent[0].astype(full))
    d_down_low = d_third.astype(low_type)
    d_pre_low = (dot_right(d_down_low, dec_down) * dec_slope.astype(full)).astype(low_type)
    d_second = d_third + dot_right(d_pre_low, dec_up)
    d_res_two, g_dec_cross_gain, g_dec_cross_shift = dec_second_back(d_second)
    d_cross_o = d_res_two.astype(low_type)
    d_cross_attn = dot_right(d_cross_o, cross_out).astype(low_type)
    cross_delta = exact_dot(d_cross_attn.astype(full) * cross_out_full, spread.T)
    all_dout = gather_rows(d_cross_attn)
    all_stats = gather_rows(
        jnp.concatenate(
            [cross_lse, cross_delta, jnp.zeros((dec_count, LANES - 2 * SLOT), full)], axis=1
        )
    )[:, : 2 * SLOT].T
    live_turned = jnp.broadcast_to(live_bias[:, None], (src_count, 512))
    query_parts, ck_low, cv_low = attend_back(
        all_cross_q, cross_k, cross_v, all_dout, all_stats, live_turned, None, 256
    )
    d_memory = dot_right(ck_low, cross_key) + dot_right(cv_low, cross_value)

    g_dec_down = dot_left(dec_hidden, d_down_low)
    g_dec_up = dot_left(dec_second_low, d_pre_low)
    g_cross_out = dot_left(cross_attn, d_cross_o)
    g_cross_key = dot_left(memory_low, ck_low)
    g_cross_value = dot_left(memory_low, cv_low)

    d_enc_second, g_enc_ffn_gain, g_enc_ffn_shift = enc_final_back(d_memory)
    d_enc_down = d_enc_second.astype(low_type)
    d_enc_pre = (dot_right(d_enc_down, enc_down) * enc_slope.astype(full)).astype(low_type)
    d_enc_first = d_enc_second + dot_right(d_enc_pre, enc_up)
    d_enc_res, g_enc_attn_gain, g_enc_attn_shift = enc_first_back(d_enc_first)
    d_attn_o = d_enc_res.astype(low_type)
    d_attn = dot_right(d_attn_o, enc_out).astype(low_type)
    g_enc_down = dot_left(enc_hidden, d_enc_down)
    g_enc_up = dot_left(enc_first_low, d_enc_pre)
    g_enc_out = dot_left(enc_attn, d_attn_o)

    d_cross_q = scatter_all(query_parts).astype(low_type) * 0.125
    g_cross_query = dot_left(dec_first_low, d_cross_q)
    d_first = d_res_two + dot_right(d_cross_q, cross_query)
    d_res_one, g_dec_self_gain, g_dec_self_shift = dec_first_back(d_first)
    d_self_o = d_res_one.astype(low_type)
    g_self_out = dot_left(self_attn, d_self_o)
    d_self_attn = dot_right(d_self_o, self_out).astype(low_type)
    self_delta = exact_dot(d_self_attn.astype(full) * self_out_full, spread.T)
    wide = max(dec_count, LANES)
    self_pair = jnp.concatenate([self_stats[:, :SLOT], self_delta], axis=1)
    self_query_parts, d_self_k, d_self_v = attend_back(
        pad_rows(self_q, wide),
        self_k,
        self_v,
        pad_rows(d_self_attn, wide),
        pad_rows(self_pair, wide).T,
        pad_rows(self_bias, wide).T,
        None,
        wide,
    )
    d_self_q = self_query_parts[:dec_count].astype(low_type) * 0.125
    g_self_query = dot_left(dec_x, d_self_q)
    g_self_key = dot_left(dec_all, d_self_k)
    g_self_value = dot_left(dec_all, d_self_v)
    d_target = (
        d_res_one
        + dot_right(d_self_q, self_query)
        + scatter_all(dot_right(d_self_k, self_key) + dot_right(d_self_v, self_value))
    )

    glob_dout = add_all(dot_plain(select_low, d_attn).astype(low_type))
    d_window = jnp.where(is_global[:, None], jnp.zeros_like(d_attn), d_attn)
    win_delta = exact_dot(d_window.astype(full) * win_out, spread.T)
    win_pair = jnp.concatenate([win_stats[:, :SLOT], win_delta], axis=1).T
    d_query, d_keys_all, d_vals_all = attend_back(
        query_loc, keys_all, vals_all, d_window, win_pair, win_bias_turned, win_parts, rows_block
    )
    d_query_low = d_query.astype(low_type) * 0.125

    wide = max(glob_count, LANES)
    glob_delta = exact_dot(glob_dout.astype(full) * glob_out, spread.T)
    glob_pair = jnp.concatenate([glob_lse, glob_delta], axis=1)
    glob_query_parts, gk_low, gv_low = attend_back(
        pad_rows(glob_queries, wide),
        glob_keys_loc,
        glob_vals_loc,
        pad_rows(glob_dout, wide),
        pad_rows(glob_pair, wide).T,
        live_turned[:, :wide],
        None,
        wide,
    )
    d_gq = glob_query_parts[:glob_count].astype(low_type) * 0.125

    g_enc_query = dot_left(src_x, d_query_low)
    g_enc_key = dot_left(x_all, d_keys_all)
    g_enc_value = dot_left(x_all, d_vals_all)
    g_glob_query = dot_left(glob_x, d_gq)
    g_glob_key = dot_left(src_x, gk_low)
    g_glob_value = dot_left(src_x, gv_low)

    d_x_all = dot_right(d_keys_all, enc_key) + dot_right(d_vals_all, enc_value)
    from_after = lax.ppermute(d_x_all[:HALF].astype(low_type), "seq", downward)
    from_before = lax.ppermute(d_x_all[HALF + src_count : pad_count].astype(low_type), "seq", upward)
    d_glob_x = add_all((d_x_all[pad_count:] + dot_right(d_gq, glob_query)).astype(low_type))
    d_source = (
        d_enc_res
        + dot_right(d_query_low, enc_query)
        + d_x_all[HALF : HALF + src_count]
        + dot_right(gk_low, glob_key)
        + dot_right(gv_low, glob_value)
        + dot_left(select_low, d_glob_x)
    )
    d_source = d_source + jnp.pad(
        from_after.astype(full), ((src_count - HALF, 0), (0, 0))
    )
    d_source = d_source + jnp.pad(
        from_before.astype(full), ((0, src_count - HALF), (0, 0))
    )

    (s_dec_up,) = share_grads([g_dec_up], True)
    s_dec_down, s_cross_out = share_grads([g_dec_down, g_cross_out], False)
    s_cross_key, s_cross_value = share_grads([g_cross_key, g_cross_value], True)
    (s_enc_up,) = share_grads([g_enc_up], True)
    s_enc_down, s_enc_out = share_grads([g_enc_down, g_enc_out], False)
    s_self_query, s_self_key, s_self_value, s_self_out, s_cross_query = share_grads(
        [g_self_query, g_self_key, g_self_value, g_self_out, g_cross_query], False
    )
    s_enc_query, s_enc_key, s_enc_value = share_grads([g_enc_query, g_enc_key, g_enc_value], True)
    s_glob_query, s_glob_key, s_glob_value = share_grads(
        [g_glob_query, g_glob_key, g_glob_value], False
    )
    vectors = share_norms(
        [
            g_enc_attn_gain,
            g_enc_attn_shift,
            g_enc_ffn_gain,
            g_enc_ffn_shift,
            g_dec_self_gain,
            g_dec_self_shift,
            g_dec_cross_gain,
            g_dec_cross_shift,
            g_dec_ffn_gain,
            g_dec_ffn_shift,
        ]
    )
    return (
        decoded.astype(low_type)[None],
        d_source[None],
        d_target[None],
        s_enc_query,
        s_enc_key,
        s_enc_value,
        s_glob_query,
        s_glob_key,
        s_glob_value,
        s_enc_out,
        vectors[0],
        vectors[1],
        s_enc_up,
        s_enc_down,
        vectors[2],
        vectors[3],
        s_self_query,
        s_self_key,
        s_self_value,
        s_self_out,
        vectors[4],
        vectors[5],
        s_cross_query,
        s_cross_key,
        s_cross_value,
        s_cross_out,
        vectors[6],
        vectors[7],
        s_dec_up,
        s_dec_down,
        vectors[8],
        vectors[9],
    )


def solution(mesh):
    rows = P("dp", "seq", None)
    tile = P("seq", "dp")
    part = P("seq")
    layer = (tile,) * 7 + (part,) * 2 + (tile,) * 2 + (part,) * 2
    decoder = (tile,) * 4 + (part,) * 2 + (tile,) * 4 + (part,) * 2 + (tile,) * 2 + (part,) * 2
    few = mesh.shape["seq"] <= 16
    return jax.shard_map(
        per_device if few else per_device_wide,
        mesh=mesh,
        in_specs=(rows, rows, rows, P("dp"), P("dp"), P("dp", None)) + (P(),) * 29,
        out_specs=(rows, rows, rows) + layer + decoder,
        check_vma=False,
    )
```

```python
import functools

import jax
import jax.numpy as jnp
import numpy as np
from jax import lax
from jax.experimental import pallas as pl
from jax.experimental.pallas import tpu as pltpu
from jax.sharding import PartitionSpec as P

HEADS = 12
HEAD_DIM = 64
HALF = 512
PAIRS = HEADS // 2
LANES = 2 * HEAD_DIM
SLOT = 16

masked_score = -1e30
eps_norm = 1e-05
low_type = jnp.bfloat16
vmem_bytes = 56 * 2**20


def dot_plain(left, right):
    return jnp.dot(left, right, preferred_element_type=jnp.float32)


def dot_left(left, right):
    return lax.dot_general(
        left, right, (((0,), (0,)), ((), ())), preferred_element_type=jnp.float32
    )


def dot_right(left, right):
    return lax.dot_general(
        left, right, (((1,), (1,)), ((), ())), preferred_element_type=jnp.float32
    )


def exact_dot(left, right):
    return jnp.dot(
        left, right, precision=lax.Precision.HIGHEST, preferred_element_type=jnp.float32
    )


def layer_norm(value, scale_vec, shift_vec):
    average = jnp.mean(value, axis=-1, keepdims=True)
    centred = value - average
    spread = jnp.mean(centred * centred, axis=-1, keepdims=True)
    return centred * lax.rsqrt(spread + eps_norm) * scale_vec + shift_vec


def gelu_pair(value):
    cdf = 0.5 * (1.0 + lax.erf(value * 0.7071067811865476))
    slope = cdf + value * (0.3989422804014327 * jnp.exp(-0.5 * value * value))
    return (value * cdf).astype(low_type), slope.astype(low_type)


def head_spread():
    heads = lax.broadcasted_iota(jnp.int32, (SLOT, HEADS * HEAD_DIM), 0)
    columns = lax.broadcasted_iota(jnp.int32, (SLOT, HEADS * HEAD_DIM), 1)
    return (columns // HEAD_DIM == heads).astype(jnp.float32)


def head_mask(which):
    lanes = lax.broadcasted_iota(jnp.int32, (1, LANES), 1)
    return ((lanes // HEAD_DIM) == which).astype(low_type)


def attend_heads(
    first, group, parts, rows_block, blocks, normalize, q_ref, k_ref, v_ref, bias_ref, o_ref, st_ref
):
    lane = lax.broadcasted_iota(jnp.int32, (1, LANES), 1)
    for block in range(blocks):
        rows = pl.ds(block * rows_block, rows_block)
        stats = st_ref[rows, :]
        for pair in range(group):
            columns = pl.ds(pair * LANES, LANES)
            q_two = q_ref[rows, columns]
            outs = []
            for which in range(2):
                head = first + 2 * pair + which
                q_one = q_two * head_mask(which)
                scores = []
                for start, size in parts[block]:
                    keys = pl.ds(start, size)
                    bias = bias_ref[rows, keys] if bias_ref.shape[0] > 1 else bias_ref[:, keys]
                    scores.append(dot_right(q_one, k_ref[keys, columns]) + bias)
                top = functools.reduce(
                    jnp.maximum, [jnp.max(part, axis=1, keepdims=True) for part in scores]
                )
                total = jnp.zeros((rows_block, 1), jnp.float32)
                mixed = jnp.zeros((rows_block, LANES), jnp.float32)
                for (start, size), part in zip(parts[block], scores):
                    weights = jnp.exp(part - top)
                    total = total + jnp.sum(weights, axis=1, keepdims=True)
                    mixed = mixed + dot_plain(
                        weights.astype(low_type), v_ref[pl.ds(start, size), columns]
                    )
                if normalize:
                    mixed = mixed / total
                    stats = jnp.where(lane == head, top + jnp.log(total), stats)
                else:
                    stats = jnp.where(lane == head, top, stats)
                    stats = jnp.where(lane == head + SLOT, total, stats)
                outs.append(mixed)
            o_ref[rows, columns] = jnp.where(lane < HEAD_DIM, outs[0], outs[1])
        st_ref[rows, :] = stats


def forward_body(
    parts, rows_block, blocks, normalize, group, q_ref, k_ref, v_ref, bias_ref, o_ref, st_ref
):
    first = pl.program_id(1) * (2 * group)

    @pl.when(first == 0)
    def _():
        st_ref[...] = jnp.zeros_like(st_ref)

    attend_heads(
        first, group, parts, rows_block, blocks, normalize, q_ref, k_ref, v_ref, bias_ref,
        o_ref, st_ref,
    )


def attend(queries, keys, values, bias, parts, rows_block, normalize, group=1):
    count, width = queries.shape
    key_count = keys.shape[0]
    big = min(count, 512)
    blocks = big // rows_block
    parts = parts or [((0, key_count),)] * blocks
    bias_rows = bias.shape[0]
    flops = 4 * count * key_count * width
    wide = group * LANES
    return pl.pallas_call(
        functools.partial(forward_body, parts, rows_block, blocks, normalize, group),
        grid=(count // big, PAIRS // group),
        in_specs=[
            pl.BlockSpec((big, wide), lambda i, p: (i, p)),
            pl.BlockSpec((key_count, wide), lambda i, p: (0, p)),
            pl.BlockSpec((key_count, wide), lambda i, p: (0, p)),
            pl.BlockSpec(
                (min(bias_rows, big), key_count), lambda i, p: (i if bias_rows > big else 0, 0)
            ),
        ],
        out_specs=[
            pl.BlockSpec((big, wide), lambda i, p: (i, p)),
            pl.BlockSpec((big, LANES), lambda i, p: (i, 0)),
        ],
        out_shape=[
            jax.ShapeDtypeStruct((count, width), jnp.float32),
            jax.ShapeDtypeStruct((count, LANES), jnp.float32),
        ],
        compiler_params=pltpu.CompilerParams(vmem_limit_bytes=vmem_bytes),
        cost_estimate=pl.CostEstimate(
            flops=4 * flops,
            bytes_accessed=2 * (count + 2 * key_count) * width + 4 * count * width,
            transcendentals=count * key_count * HEADS,
        ),
    )(queries, keys, values, bias)


def back_heads(
    first, group, parts, rows_block, blocks, q_ref, k_ref, v_ref, d_ref, st_ref, bias_ref,
    dq_ref, key_sum, val_sum,
):
    for block in range(blocks):
        rows = pl.ds(block * rows_block, rows_block)
        for pair in range(group):
            columns = pl.ds(pair * LANES, LANES)
            q_two = q_ref[rows, columns]
            d_two = d_ref[rows, columns]
            turned = []
            for which in range(2):
                head = first + 2 * pair + which
                q_one = q_two * head_mask(which)
                d_one = d_two * head_mask(which)
                lse = st_ref[pl.ds(head, 1), rows]
                delta = st_ref[pl.ds(head + SLOT, 1), rows]
                q_grad = jnp.zeros((LANES, rows_block), jnp.float32)
                for start, size in parts[block]:
                    keys = pl.ds(start, size)
                    bias = bias_ref[keys, rows] if bias_ref.shape[1] > 1 else bias_ref[keys, :]
                    k_two = k_ref[keys, columns]
                    scores = dot_right(k_two, q_one) + bias
                    weights = jnp.exp(scores - lse)
                    slopes = dot_right(v_ref[keys, columns], d_one)
                    diffs = (weights * (slopes - delta)).astype(low_type)
                    val_sum[keys, columns] += dot_plain(weights.astype(low_type), d_one)
                    key_sum[keys, columns] += dot_plain(diffs, q_one)
                    q_grad = q_grad + dot_left(k_two, diffs)
                turned.append(q_grad[which * HEAD_DIM : (which + 1) * HEAD_DIM, :])
            dq_ref[rows, columns] = jnp.concatenate(turned, axis=0).T.astype(dq_ref.dtype)


def backward_body(
    parts, rows_block, blocks, group, q_ref, k_ref, v_ref, d_ref, st_ref, bias_ref,
    dq_ref, dk_ref, dv_ref, key_sum, val_sum,
):
    first = pl.program_id(0) * (2 * group)
    turn = pl.program_id(1)

    @pl.when(turn == 0)
    def _():
        key_sum[...] = jnp.zeros_like(key_sum)
        val_sum[...] = jnp.zeros_like(val_sum)

    back_heads(
        first, group, parts, rows_block, blocks, q_ref, k_ref, v_ref, d_ref, st_ref, bias_ref,
        dq_ref, key_sum, val_sum,
    )

    @pl.when(turn == pl.num_programs(1) - 1)
    def _():
        dk_ref[...] = key_sum[...].astype(low_type)
        dv_ref[...] = val_sum[...].astype(low_type)


def attend_back(queries, keys, values, grads, stats, bias, parts, rows_block, group=1):
    count, width = queries.shape
    key_count = keys.shape[0]
    big = min(count, 512)
    blocks = big // rows_block
    parts = parts or [((0, key_count),)] * blocks
    bias_cols = bias.shape[1]
    flops = 10 * count * key_count * width
    wide = group * LANES
    return pl.pallas_call(
        functools.partial(backward_body, parts, rows_block, blocks, group),
        grid=(PAIRS // group, count // big),
        in_specs=[
            pl.BlockSpec((big, wide), lambda p, i: (i, p)),
            pl.BlockSpec((key_count, wide), lambda p, i: (0, p)),
            pl.BlockSpec((key_count, wide), lambda p, i: (0, p)),
            pl.BlockSpec((big, wide), lambda p, i: (i, p)),
            pl.BlockSpec((2 * SLOT, big), lambda p, i: (0, i)),
            pl.BlockSpec((key_count, min(bias_cols, big)), lambda p, i: (0, 0)),
        ],
        out_specs=[
            pl.BlockSpec((big, wide), lambda p, i: (i, p)),
            pl.BlockSpec((key_count, wide), lambda p, i: (0, p)),
            pl.BlockSpec((key_count, wide), lambda p, i: (0, p)),
        ],
        out_shape=[
            jax.ShapeDtypeStruct((count, width), jnp.float32),
            jax.ShapeDtypeStruct((key_count, width), low_type),
            jax.ShapeDtypeStruct((key_count, width), low_type),
        ],
        scratch_shapes=[
            pltpu.VMEM((key_count, wide), jnp.float32),
            pltpu.VMEM((key_count, wide), jnp.float32),
        ],
        compiler_params=pltpu.CompilerParams(vmem_limit_bytes=vmem_bytes),
        cost_estimate=pl.CostEstimate(
            flops=4 * flops,
            bytes_accessed=2 * (2 * count + 4 * key_count) * width + 4 * count * width,
            transcendentals=count * key_count * HEADS,
        ),
    )(queries, keys, values, grads, stats, bias)


def seq_bits():
    count = lax.axis_size("seq")
    return [1 << k for k in range(count.bit_length() - 1)]


def swap(value, bit):
    pairs = [(i, i ^ bit) for i in range(lax.axis_size("seq"))]
    return jax.tree.map(lambda part: lax.ppermute(part, "seq", pairs), value)


def bit_set(bit):
    return (lax.axis_index("seq") & bit) != 0


def pick_half(value, chosen, axis):
    return lax.dynamic_index_in_dim(value, chosen, axis, keepdims=False)


def other_of(place, bit):
    return place + bit * (1 - 2 * ((place // bit) % 2))


def greet(partners):
    barrier = pltpu.get_barrier_semaphore()
    for partner in partners:
        pl.semaphore_signal(
            barrier, inc=1, device_id=partner, device_id_type=pl.DeviceIdType.MESH
        )
    pl.semaphore_wait(barrier, len(partners))


def remote(src, dst, sems, k, partner):
    return pltpu.make_async_remote_copy(
        src_ref=src,
        dst_ref=dst,
        send_sem=sems[0].at[k],
        recv_sem=sems[1].at[k],
        device_id=partner,
        device_id_type=pl.DeviceIdType.MESH,
    )


def piece_stages(peers, kind):
    bits = [1 << k for k in range(1, peers.bit_length() - 1)]
    if kind == "x":
        return [1, "dp"] + bits
    if kind == "y":
        return [1] + bits[:1] + ["dp"] + bits[1:]
    return [1] + bits[1:] + ["dp"] + bits[:1]


def piece_shapes(peers, rows, width, stages):
    free = peers.bit_length() - 1
    shapes = []
    for stage in stages:
        if stage == "dp":
            width = width // 2
        else:
            free -= 1
        shapes.append((2,) * free + (rows, width))
    return shapes


def bit_axis(peers, stages, s):
    rest = [bit for bit in reversed([1 << k for k in range(peers.bit_length() - 1)])]
    for stage in stages[:s]:
        if stage != "dp":
            rest.remove(stage)
    return rest.index(stages[s])


def place_bits(peers):
    me = lax.axis_index("seq")
    bits = [1 << k for k in reversed(range(peers.bit_length() - 1))]
    return bits, [(me // bit) % 2 for bit in bits]


def block_at(peers, ref, place):
    return ref.at[tuple((place // bit) % 2 for bit in place_bits(peers)[0])]


def chip_copies(peers, refs, sems, k):
    me = lax.axis_index("seq")
    half = peers // 2
    return [
        remote(
            block_at(peers, ref, me),
            block_at(peers, ref, me),
            sems,
            which * peers + k,
            {"seq": lax.rem(me + 2 * k, peers)},
        )
        for which, ref in enumerate(refs)
    ]


def core_copies(peers, refs, sems, k):
    me = lax.axis_index("seq")
    place = lax.rem(me + peers - 2 * k, peers)
    return [
        remote(
            block_at(peers, ref, place),
            block_at(peers, ref, place),
            sems,
            which * peers + peers // 2 + k,
            {"seq": other_of(me, 1)},
        )
        for which, ref in enumerate(refs)
    ]


def reach_out(peers, refs, sems):
    for k in range(1, peers // 2):
        for copy in chip_copies(peers, refs, sems, k):
            copy.start()
    for copy in core_copies(peers, refs, sems, 0):
        copy.start()


def pass_on(peers, refs, sems):
    half = peers // 2
    for k in range(1, half):
        for copy in chip_copies(peers, refs, sems, k):
            copy.wait_recv()
        for copy in core_copies(peers, refs, sems, k):
            copy.start()
    for k in range(half):
        for copy in core_copies(peers, refs, sems, k):
            copy.wait()
    for k in range(1, half):
        for copy in chip_copies(peers, refs, sems, k):
            copy.wait_send()


OWNERS = 4


def everyone(peers):
    me = lax.axis_index("seq")
    return [{"seq": lax.rem(me + k, peers)} for k in range(1, peers)]


def send_in(peers, parts, slots, sems):
    me = lax.axis_index("seq")
    apart = peers // OWNERS
    for o in range(OWNERS):
        for k, (part, slot) in enumerate(zip(parts, slots)):
            copy = pltpu.make_async_remote_copy(
                src_ref=part.at[o],
                dst_ref=slot.at[me],
                send_sem=sems[0].at[k, o],
                recv_sem=sems[1].at[k, me],
                device_id={"seq": o * apart},
                device_id_type=pl.DeviceIdType.MESH,
            )

            @pl.when(me != o * apart)
            def _():
                copy.start()

            @pl.when(me == o * apart)
            def _():
                slot[me] = part[o]


def arrive(peers, parts, slots, sems):
    me = lax.axis_index("seq")
    for j in range(peers):
        for k, (part, slot) in enumerate(zip(parts, slots)):

            @pl.when(me != j)
            def _():
                pltpu.make_async_remote_copy(
                    src_ref=part.at[0],
                    dst_ref=slot.at[j],
                    send_sem=sems[0].at[k, 0],
                    recv_sem=sems[1].at[k, j],
                    device_id={"seq": j},
                    device_id_type=pl.DeviceIdType.MESH,
                ).wait_recv()


def left(peers, parts, slots, sems):
    me = lax.axis_index("seq")
    apart = peers // OWNERS
    for o in range(OWNERS):
        for k, (part, slot) in enumerate(zip(parts, slots)):

            @pl.when(me != o * apart)
            def _():
                pltpu.make_async_remote_copy(
                    src_ref=part.at[o],
                    dst_ref=slot.at[me],
                    send_sem=sems[0].at[k, o],
                    recv_sem=sems[1].at[k, me],
                    device_id={"seq": o * apart},
                    device_id_type=pl.DeviceIdType.MESH,
                ).wait_send()


def out_copies(results, sems, o, j):
    return [
        pltpu.make_async_remote_copy(
            src_ref=result.at[o],
            dst_ref=result.at[o],
            send_sem=sems[2].at[k, j],
            recv_sem=sems[3].at[k, o],
            device_id={"seq": j},
            device_id_type=pl.DeviceIdType.MESH,
        )
        for k, result in enumerate(results)
    ]


def send_out(peers, results, sems):
    me = lax.axis_index("seq")
    apart = peers // OWNERS
    for o in range(OWNERS):
        owner = o * apart

        @pl.when(me == owner)
        def _():
            for j in range(peers):
                if j != owner:
                    for copy in out_copies(results, sems, o, j):
                        copy.start()


def take_out(peers, results, sems):
    me = lax.axis_index("seq")
    apart = peers // OWNERS
    for o in range(OWNERS):
        owner = o * apart

        @pl.when(me != owner)
        def _():
            for copy in out_copies(results, sems, o, owner):
                copy.wait_recv()

        @pl.when(me == owner)
        def _():
            for j in range(peers):
                if j != owner:
                    for copy in out_copies(results, sems, o, j):
                        copy.wait_send()


def owner_sems(peers, count):
    return [
        pltpu.SemaphoreType.DMA((count, OWNERS)),
        pltpu.SemaphoreType.DMA((count, peers)),
        pltpu.SemaphoreType.DMA((count, peers)),
        pltpu.SemaphoreType.DMA((count, OWNERS)),
    ]


def sum_at_owner(peers, part_ref, slot, sum_ref, sems):
    me = lax.axis_index("seq")
    apart = peers // OWNERS
    for o in range(OWNERS):

        @pl.when(me == o * apart)
        def _():
            arrive(peers, [part_ref], [slot], sems)
            total = slot[0].astype(jnp.float32)
            for j in range(1, peers):
                total = total + slot[j].astype(jnp.float32)
            sum_ref[o] = total.astype(low_type)


def expand_heads(stat):
    lane = lax.broadcasted_iota(jnp.int32, (1, LANES), 1)
    return jnp.concatenate(
        [
            jnp.where(lane < HEAD_DIM, stat[:, 2 * p : 2 * p + 1], stat[:, 2 * p + 1 : 2 * p + 2])
            for p in range(PAIRS)
        ],
        axis=1,
    )


def merge_parts(accs, stats):
    tops = [part[:, :SLOT] for part in stats]
    top = functools.reduce(jnp.maximum, tops)
    total = jnp.zeros_like(top)
    acc = jnp.zeros(accs[0].shape, jnp.float32)
    for part, stat, own_top in zip(accs, stats, tops):
        keep = jnp.exp(own_top - top)
        total = total + stat[:, SLOT : 2 * SLOT] * keep
        acc = acc + part.astype(jnp.float32) * expand_heads(keep)
    return acc, top, total


def finish_parts(acc, top, total):
    lanes = lax.broadcasted_iota(jnp.int32, total.shape, 1)
    total = jnp.where(lanes < HEADS, total, 1.0)
    lse = top + jnp.log(total)
    rest = jnp.zeros((top.shape[0], LANES - SLOT), jnp.float32)
    return acc * expand_heads(1.0 / total), jnp.concatenate([lse, rest], axis=1)


def window_body(
    peers, parts, rows_block, blocks, q_ref, k_ref, v_ref, use_ref, acc_ref, part_ref,
    o_ref, st_ref, out_copy, lse_copy, bias_ref, low_ref, acc_in, st_in, out_ref, lse_ref, *sems
):
    step = pl.program_id(1)
    me = lax.axis_index("seq")
    apart = peers // OWNERS

    @pl.when(step == 0)
    def _():
        greet(everyone(peers))
        low_ref[...] = acc_ref[...].astype(low_type)
        send_in(peers, [low_ref, part_ref], [acc_in, st_in], sems)
        rows = lax.broadcasted_iota(jnp.int32, bias_ref.shape, 0)
        keys = lax.broadcasted_iota(jnp.int32, bias_ref.shape, 1)
        apart_by = rows + HALF - keys
        near = (jnp.abs(apart_by) <= HALF) | (keys >= bias_ref.shape[0] + 2 * HALF)
        bias_ref[...] = jnp.where(near, use_ref[...], masked_score)

    @pl.when(step == 2)
    def _():
        for o in range(OWNERS):

            @pl.when(me == o * apart)
            def _():
                arrive(peers, [low_ref, part_ref], [acc_in, st_in], sems)
                acc, top, total = merge_parts(
                    [acc_in[j] for j in range(peers)], [st_in[j] for j in range(peers)]
                )
                mixed, lse_ref[o] = finish_parts(acc, top, total)
                out_ref[o] = mixed.astype(low_type)

        send_out(peers, [out_ref, lse_ref], sems)

    forward_body(
        parts, rows_block, blocks, True, 1, q_ref, k_ref, v_ref, bias_ref, o_ref, st_ref
    )

    @pl.when(step == PAIRS - 1)
    def _():
        take_out(peers, [out_ref, lse_ref], sems)
        left(peers, [low_ref, part_ref], [acc_in, st_in], sems)
        out_copy[...] = out_ref[...]
        lse_copy[...] = lse_ref[...]


def window_attend(queries, keys, values, use, parts, rows_block, glob_acc, glob_stats):
    peers = lax.axis_size("seq")
    count, width = queries.shape
    key_count = keys.shape[0]
    rows = glob_acc.shape[0] // OWNERS
    flops = 4 * count * key_count * width

    def pair_block(size):
        return pl.BlockSpec((size, LANES), lambda i, p: (0, p))

    def whole(*shape):
        return pl.BlockSpec(shape, lambda i, p: (0,) * len(shape))

    out, stats, glob_out, lse = pl.pallas_call(
        functools.partial(window_body, peers, parts, rows_block, count // rows_block),
        grid=(1, PAIRS),
        in_specs=[
            pair_block(count),
            pair_block(key_count),
            pair_block(key_count),
            whole(1, key_count),
            whole(OWNERS, rows, width),
            whole(OWNERS, rows, LANES),
        ],
        out_specs=[
            pair_block(count),
            whole(count, LANES),
            whole(OWNERS, rows, width),
            whole(OWNERS, rows, LANES),
        ],
        out_shape=[
            jax.ShapeDtypeStruct((count, width), jnp.float32),
            jax.ShapeDtypeStruct((count, LANES), jnp.float32),
            jax.ShapeDtypeStruct((OWNERS, rows, width), low_type),
            jax.ShapeDtypeStruct((OWNERS, rows, LANES), jnp.float32),
        ],
        scratch_shapes=[
            pltpu.VMEM((count, key_count), jnp.float32),
            pltpu.VMEM((OWNERS, rows, width), low_type),
            pltpu.VMEM((peers, rows, width), low_type),
            pltpu.VMEM((peers, rows, LANES), jnp.float32),
            pltpu.VMEM((OWNERS, rows, width), low_type),
            pltpu.VMEM((OWNERS, rows, LANES), jnp.float32),
        ]
        + owner_sems(peers, 2),
        compiler_params=pltpu.CompilerParams(
            collective_id=3, has_side_effects=True, vmem_limit_bytes=vmem_bytes
        ),
        cost_estimate=pl.CostEstimate(
            flops=4 * flops,
            bytes_accessed=2 * (count + 2 * key_count) * width + 4 * count * width,
            transcendentals=count * key_count * HEADS,
        ),
    )(
        queries, keys, values, use,
        glob_acc.reshape(OWNERS, rows, width), glob_stats.reshape(OWNERS, rows, LANES),
    )
    return out, stats, glob_out.reshape(-1, width), lse.reshape(-1, LANES)


def end_body(count, *refs):
    shared = refs[:count]
    (source_own, after, before, select, glob,
     target_own, target_sum, flags) = refs[count : count + 8]
    outs = refs[count + 8 :]
    for source, target in zip(shared, outs):
        target[...] = source[...]
    d_source, d_target = outs[count:]
    full = jnp.float32
    d_target[...] = target_own[...] + target_sum[...]
    has_after = flags[:, :1] > 0
    has_before = flags[:, 1:2] > 0
    total = source_own[...] + dot_left(select[...], glob[...])
    total = total + jnp.where(has_after, after[...].astype(full), 0.0)
    d_source[...] = total + jnp.where(has_before, before[...].astype(full), 0.0)


def end_outputs(shared, source_parts, target_parts):
    shapes = [part.shape for part in shared]
    shapes += [source_parts[0].shape, target_parts[0].shape]
    return pl.pallas_call(
        functools.partial(end_body, len(shared)),
        out_shape=[jax.ShapeDtypeStruct(shape, jnp.float32) for shape in shapes],
        compiler_params=pltpu.CompilerParams(vmem_limit_bytes=vmem_bytes),
    )(*shared, *source_parts[:5], *target_parts, source_parts[5])


def share_vectors(total, count):
    length = total.shape[1] // lax.axis_size("seq")
    mine = lax.dynamic_slice_in_dim(total, lax.axis_index("seq") * length, length, 1)
    return [mine[k] for k in range(count)]


def pad_rows(value, count):
    return jnp.pad(value, ((0, count - value.shape[0]), (0, 0)))


def fetches(fars, nears, sem):
    return [
        pltpu.make_async_copy(far, near, sem.at[k]) for k, (far, near) in enumerate(zip(fars, nears))
    ]


def bring(fars, nears, sem):
    copies = fetches(fars, nears, sem)
    for copy in copies:
        copy.start()
    return copies


class Pieces:
    def __init__(self, peers, pieces, mats, factors, kept, outs, sems, load, held, own, staging, base):
        self.peers = peers
        self.pieces = pieces
        self.mats = mats
        self.factors = factors
        self.kept = kept
        self.outs = outs
        self.sems = sems
        self.load = load
        self.held = held
        self.own = own
        self.staging = staging
        self.numbers = {}
        self.base = base
        self.me = lax.axis_index("seq")
        self.mine_dp = lax.axis_index("dp")

    def number(self, *key):
        return self.base + self.numbers.setdefault(key, len(self.numbers))

    def partner(self, stage):
        if stage == "dp":
            return {"dp": 1 - self.mine_dp}
        return {"seq": other_of(self.me, stage)}

    def halved(self, source, stages, s, mine):
        if stages[s] == "dp":
            half = source.shape[-1] // 2
            where = self.mine_dp if mine else 1 - self.mine_dp
            start = pl.multiple_of(where * half, LANES)
            return (slice(None),) * (len(source.shape) - 1) + (pl.ds(start, half),)
        digit = (self.me // stages[s]) % 2
        return (slice(None),) * bit_axis(self.peers, stages, s) + (digit if mine else 1 - digit,)

    def copy(self, name, stages, origin, target, s):
        view = origin.at[self.halved(origin, stages, s, False)]
        return remote(view, target, self.sems, self.number(name, s), self.partner(stages[s]))

    def fold(self, stages, origin, target, s, finish):
        spot = self.halved(origin, stages, s, True)
        for place in np.ndindex(*target.shape[:-2]):
            if stages[s] == "dp":
                more = origin[place + spot[-2:]]
            else:
                axis = len(spot) - 1
                more = origin[place[:axis] + spot[-1:] + place[axis:]]
            total = target[place] + more
            if finish is not None:
                if place:
                    finish[place] = total.astype(finish.dtype)
                else:
                    finish[...] = total.astype(finish.dtype)
            else:
                target[place] = total

    def origin(self, p, s):
        piece = self.pieces[p]
        if s > piece["first"]:
            return self.held[p][s - 1 - piece["first"]]
        kind, which = piece["from"]
        return {"mat": self.mats, "made": self.staging, "kept": self.kept}[kind][which]

    def target(self, p, s):
        return self.held[p][s - self.pieces[p]["first"]]

    def local(self, p, c):
        which = self.pieces[p]["from"][1]
        core = self.me % 2
        return pltpu.make_async_copy(
            self.mats[which].at[c // 2, c % 2, :, core],
            self.own[which].at[c % 2],
            self.load.at[2 * which + c % 2],
        )

    def compute(self, p):
        x, y = (self.factors[k] for k in self.pieces[p]["pair"])
        target = self.staging[self.pieces[p]["from"][1]]
        step = x.shape[1] // 2
        for block in range(2):
            product = dot_left(x[:, block * step : (block + 1) * step], y[...])
            target[block] = product.astype(low_type).reshape(target.shape[1:])

    def begin(self, p, s):
        piece = self.pieces[p]
        if s == 0 and piece["from"][0] == "mat":
            for c in range(2):
                self.local(p, c).start()
        self.copy(p, piece["stages"], self.origin(p, s), self.target(p, s), s).start()

    def end(self, p, s):
        piece = self.pieces[p]
        origin, target = self.origin(p, s), self.target(p, s)
        self.copy(p, piece["stages"], origin, target, s).wait()
        finish = self.outs[p] if s == piece["last"] else None
        if s == 0 and piece["from"][0] == "mat":
            mine = self.own[piece["from"][1]]
            for c in range(4):
                self.local(p, c).wait()
                spot = (c // 2, c % 2)
                for k in range(2):
                    target[spot + (k,)] = target[spot + (k,)] + mine[c % 2, k]
                if c < 2:
                    self.local(p, c + 2).start()
        else:
            self.fold(piece["stages"], origin, target, s, finish)

    def open(self, turn):
        for p in turn:
            if "pair" in self.pieces[p]:
                self.compute(p)
            self.begin(p, self.pieces[p]["first"])

    def move(self, turn, s):
        for p in turn:
            self.end(p, s)
            if s < self.pieces[p]["last"]:
                self.begin(p, s + 1)


def piece_plan(peers, source, rows, width, kind, first, last, pair=None):
    stages = piece_stages(peers, kind)
    shapes = piece_shapes(peers, rows, width, stages)
    plan = {"from": source, "stages": stages, "first": first, "last": last}
    if pair is not None:
        plan["pair"] = pair
    return plan, shapes[first : last + 1]


def ln_parts(value):
    average = jnp.mean(value, axis=-1, keepdims=True)
    centred = value - average
    spread = jnp.mean(centred * centred, axis=-1, keepdims=True)
    rate = lax.rsqrt(spread + eps_norm)
    return centred * rate, rate


def ln_back(grad, unit, rate, gain):
    scaled = grad * gain
    pull = jnp.mean(scaled, axis=-1, keepdims=True)
    twist = jnp.mean(scaled * unit, axis=-1, keepdims=True)
    return (
        rate * (scaled - pull - unit * twist),
        jnp.sum(grad * unit, axis=0, keepdims=True),
        jnp.sum(grad, axis=0, keepdims=True),
    )


def call_whole(body, inputs, shapes, scratch=(), **params):
    whole = pl.BlockSpec(memory_space=pltpu.VMEM)
    return pl.pallas_call(
        body,
        in_specs=[whole] * len(inputs),
        out_specs=[whole] * len(shapes),
        out_shape=[jax.ShapeDtypeStruct(shape, kind) for shape, kind in shapes],
        scratch_shapes=list(scratch),
        compiler_params=pltpu.CompilerParams(vmem_limit_bytes=vmem_bytes, **params),
    )(*inputs)


ENC_ATTN, ENC_FFN, DEC_SELF, DEC_CROSS, DEC_FFN = 0, 2, 4, 6, 8


def scale_shift(norms, which):
    return norms[which : which + 1, :], norms[which + 1 : which + 2, :]


def start_body(
    peers, dec_ref, part_ref, x_ref, wq, wgk, wgv, all_ref, glob_ref, q_ref, gk_ref, gv_ref,
    slot, send, recv, *sems
):
    bits, digits = place_bits(peers)
    greet(everyone(peers))
    send_in(peers, [part_ref], [slot], sems)
    all_ref[tuple(digits)] = dec_ref[...]
    reach_out(peers, [all_ref], (send, recv))
    x = x_ref[...]
    gk_ref[...] = dot_plain(x, wgk[...]).astype(low_type)
    sum_at_owner(peers, part_ref, slot, glob_ref, sems)
    send_out(peers, [glob_ref], sems)
    q_ref[...] = (dot_plain(x, wq[...]) * 0.125).astype(low_type)
    pass_on(peers, [all_ref], (send, recv))
    gv_ref[...] = dot_plain(x, wgv[...]).astype(low_type)
    take_out(peers, [glob_ref], sems)
    left(peers, [part_ref], [slot], sems)


def start_exchange(dec_x, glob_part, src_x, weights):
    peers = lax.axis_size("seq")
    free = peers.bit_length() - 1
    rows = glob_part.shape[0] // OWNERS
    width = dec_x.shape[1]
    dec_all, glob_x, q, gk, gv = call_whole(
        functools.partial(start_body, peers),
        [dec_x, glob_part.reshape(OWNERS, rows, width), src_x, *weights],
        [((2,) * free + dec_x.shape, dec_x.dtype), ((OWNERS, rows, width), low_type)]
        + [(src_x.shape, low_type)] * 3,
        [
            pltpu.VMEM((peers, rows, width), low_type),
            pltpu.SemaphoreType.DMA((peers,)),
            pltpu.SemaphoreType.DMA((peers,)),
        ]
        + owner_sems(peers, 1),
        collective_id=2,
        has_side_effects=True,
    )
    return dec_all.reshape(-1, width), glob_x.reshape(-1, width), q, gk, gv


def project_body(*refs):
    sources = refs[:4]
    wk, wv, x_all, k_all, v_all = refs[4:]
    start = 0
    for source in sources:
        rows = pl.ds(start, source.shape[0])
        x = source[...]
        x_all[rows, :] = x
        k_all[rows, :] = dot_plain(x, wk[...]).astype(low_type)
        v_all[rows, :] = dot_plain(x, wv[...]).astype(low_type)
        start += source.shape[0]


def project_all(sources, wk, wv):
    total = sum(source.shape[0] for source in sources)
    return call_whole(
        project_body, [*sources, wk, wv], [((total, sources[0].shape[1]), low_type)] * 3
    )


def dec_front_body(
    limit_ref, x_ref, wq, wk, wv, wo, wcq, norms, k_ref, v_ref, cq_ref, q_own, out_own, attn_own,
    st_own, first_own, low_own, unit_own, rate_own, q_ref, o_ref, st_ref, bias_ref,
):
    x = x_ref[...]
    count = x.shape[0]
    half = count // 2
    q_ref[...] = (dot_plain(x, wq[...]) * 0.125).astype(low_type)
    k_ref[...] = dot_plain(x, wk[...]).astype(low_type)
    v_ref[...] = dot_plain(x, wv[...]).astype(low_type)
    rows = lax.broadcasted_iota(jnp.int32, (count, count), 0)
    keys = lax.broadcasted_iota(jnp.int32, (count, count), 1)
    bias_ref[...] = jnp.where((keys <= rows) & (keys < limit_ref[0]), 0.0, masked_score)
    st_ref[...] = jnp.zeros_like(st_ref)
    attend_heads(
        0, PAIRS, [((0, half),), ((0, count),)], half, 2, True, q_ref, k_ref, v_ref, bias_ref,
        o_ref, st_ref,
    )
    gain, shift = scale_shift(norms, DEC_SELF)
    res = x.astype(jnp.float32) + dot_plain(o_ref[...].astype(low_type), wo[...])
    unit, _ = ln_parts(res)
    first = unit * gain + shift
    cq_ref[...] = (dot_plain(first.astype(low_type), wcq[...]) * 0.125).astype(low_type)
    mine = q_own.shape[0]
    start = pl.multiple_of(lax.axis_index("seq") * mine, mine)
    own = pl.ds(start, mine)
    q_own[...] = q_ref[own, :]
    out_own[...] = o_ref[own, :]
    attn = o_ref[own, :].astype(low_type)
    attn_own[...] = attn
    st_own[...] = st_ref[own, :]
    res_own = x_ref[own, :].astype(jnp.float32) + dot_plain(attn, wo[...])
    unit, rate = ln_parts(res_own)
    unit_own[...] = unit
    rate_own[...] = rate
    first = unit * gain + shift
    first_own[...] = first
    low_own[...] = first.astype(low_type)


def dec_front(limit, dec_all, weights, norms, mine):
    count, width = dec_all.shape
    full = jnp.float32
    whole = pl.BlockSpec(memory_space=pltpu.VMEM)
    shapes = [
        ((count, width), low_type),
        ((count, width), low_type),
        ((count, width), low_type),
        ((mine, width), low_type),
        ((mine, width), full),
        ((mine, width), low_type),
        ((mine, LANES), full),
        ((mine, width), full),
        ((mine, width), low_type),
        ((mine, width), full),
        ((mine, 1), full),
    ]
    return pl.pallas_call(
        dec_front_body,
        in_specs=[pl.BlockSpec(memory_space=pltpu.SMEM)] + [whole] * 7,
        out_specs=[whole] * len(shapes),
        out_shape=[jax.ShapeDtypeStruct(shape, kind) for shape, kind in shapes],
        scratch_shapes=[
            pltpu.VMEM((count, width), low_type),
            pltpu.VMEM((count, width), full),
            pltpu.VMEM((count, LANES), full),
            pltpu.VMEM((count, count), full),
        ],
        compiler_params=pltpu.CompilerParams(vmem_limit_bytes=vmem_bytes),
    )(limit, dec_all, *weights, norms)


def enc_front_body(
    win_ref, keep_ref, select, glob, x_ref, wo, wu_far, wd_far, wck_far, wcv_far, norms, attn_ref,
    unit_one, rate_one, low_one, hidden_ref, slope_ref, unit_two, rate_two, low_two, ck_ref, cv_ref,
    wu, wd, wck, wcv, fetch,
):
    copies = bring([wu_far, wd_far, wck_far, wcv_far], [wu, wd, wck, wcv], fetch)
    rows_block = x_ref.shape[0] // 2
    width = x_ref.shape[1]
    for block in range(2):
        rows = pl.ds(block * rows_block, rows_block)
        picked = select[:, block * rows_block : (block + 1) * rows_block]
        placed = dot_left(picked, glob[...].astype(low_type))
        attn = jnp.where(keep_ref[rows, :] > 0, win_ref[rows, :], placed).astype(low_type)
        attn_ref[rows, :] = attn
        unit, rate = ln_parts(x_ref[rows, :].astype(jnp.float32) + dot_plain(attn, wo[...]))
        unit_one[rows, :] = unit
        rate_one[rows, :] = rate
        gain, shift = scale_shift(norms, ENC_ATTN)
        second = unit * gain + shift
        first = second.astype(low_type)
        low_one[rows, :] = first
        if block == 0:
            for copy in copies[:2]:
                copy.wait()
        for k in range(wu.shape[1] // width):
            columns = pl.ds(k * width, width)
            hidden, slope = gelu_pair(dot_plain(first, wu[:, columns]))
            hidden_ref[rows, columns] = hidden
            slope_ref[rows, columns] = slope
            second = second + dot_plain(hidden, wd[columns, :])
        unit, rate = ln_parts(second)
        unit_two[rows, :] = unit
        rate_two[rows, :] = rate
        gain, shift = scale_shift(norms, ENC_FFN)
        memory = (unit * gain + shift).astype(low_type)
        low_two[rows, :] = memory
        if block == 0:
            for copy in copies[2:]:
                copy.wait()
        ck_ref[rows, :] = dot_plain(memory, wck[...]).astype(low_type)
        cv_ref[rows, :] = dot_plain(memory, wcv[...]).astype(low_type)


def enc_front(win_out, keep, select, glob, x, weights, norms):
    count, width = x.shape
    wide = weights[1].shape[1]
    full = jnp.float32
    narrow = (count, width)
    whole = pl.BlockSpec(memory_space=pltpu.VMEM)
    far = pl.BlockSpec(memory_space=pl.ANY)
    shapes = [
            (narrow, low_type),
            (narrow, full),
            ((count, 1), full),
            (narrow, low_type),
            ((count, wide), low_type),
            ((count, wide), low_type),
            (narrow, full),
            ((count, 1), full),
            (narrow, low_type),
            (narrow, low_type),
            (narrow, low_type),
        ]
    return pl.pallas_call(
        enc_front_body,
        in_specs=[whole] * 6 + [far] * 4 + [whole],
        out_specs=[whole] * len(shapes),
        out_shape=[jax.ShapeDtypeStruct(shape, kind) for shape, kind in shapes],
        scratch_shapes=[pltpu.VMEM(weight.shape, low_type) for weight in weights[1:]]
        + [pltpu.SemaphoreType.DMA((4,))],
        compiler_params=pltpu.CompilerParams(vmem_limit_bytes=vmem_bytes),
    )(win_out, keep, select, glob, x, *weights, norms)


def row_sum_steps(peers, whole_ref, out_ref, buffers, send, recv):
    me = lax.axis_index("seq")
    free = peers.bit_length() - 1
    every = slice(None)
    sends, takes, helds = buffers[:free], buffers[free : 2 * free], buffers[2 * free :]

    def source(k):
        return whole_ref if k == 0 else helds[k - 1]

    def copy(k):
        return remote(sends[k], takes[k], (send, recv), k, {"seq": other_of(me, 1 << k)})

    def begin(k):
        digit = (me // (1 << k)) % 2
        lead = (every,) * (free - 1 - k)
        sends[k][...] = source(k)[lead + (1 - digit,)].astype(low_type)
        copy(k).start()

    def end(k):
        copy(k).wait()
        digit = (me // (1 << k)) % 2
        lead = (every,) * (free - 1 - k)
        total = source(k)[lead + (digit,)] + takes[k][...].astype(jnp.float32)
        target = out_ref if k == free - 1 else helds[k]
        target[...] = total

    def step(k):
        if k > 0:
            end(k - 1)
        if k < free:
            begin(k)

    return [functools.partial(step, k) for k in range(free + 1)]


def enc_back_body(
    peers, pieces, parts_ref, g_up, g_down, g_out, dck, dcv, unit_two, rate_two, rate_one, keep_ref,
    select, wck, wcv, norms, *refs
):
    refs = list(refs)

    def take(count):
        result = refs[:count]
        del refs[:count]
        return result

    fars = take(8)
    res_ref, out_ref, window_ref, delta_ref, glob_ref, vec_ref, sum_ref = take(7)
    far_up, far_down, kept_up, kept_down, kept_out = take(5)
    send, recv, send_two, recv_two, load, fetch = take(6)
    held, own, nears = take(6), take(3), take(8)
    down_ref, pre_ref, made_up, made_down, leave = take(5)
    buffers = refs
    wd, wu, slope_ref, unit_one, wo, win_ref, hidden_ref, first_ref = nears
    work = Pieces(
        peers, pieces, [g_up, g_down, g_out], [], [], [kept_up, kept_down, kept_out],
        (send_two, recv_two), load, [held[:2], held[2:4], held[4:]], own, [], 0,
    )
    turn = [0, 1, 2]
    me = lax.axis_index("seq")
    free = peers.bit_length() - 1
    greet([{"seq": other_of(me, 1 << k)} for k in range(free)] + [work.partner("dp")])
    steps = row_sum_steps(peers, parts_ref, sum_ref, buffers, send, recv)
    steps[0]()
    work.open(turn)
    copies = bring(fars, nears, fetch)
    rows_block = dck.shape[0] // 2
    width = dck.shape[1]
    vec_ref[...] = jnp.zeros_like(vec_ref)
    glob = jnp.zeros(glob_ref.shape, jnp.float32)
    for block in range(2):
        rows = pl.ds(block * rows_block, rows_block)
        d_memory = dot_right(dck[rows, :], wck[...]) + dot_right(dcv[rows, :], wcv[...])
        gain, _ = scale_shift(norms, ENC_FFN)
        d_second, d_gain, d_shift = ln_back(d_memory, unit_two[rows, :], rate_two[rows, :], gain)
        vec_ref[2:3, :] += d_gain
        vec_ref[3:4, :] += d_shift
        d_down = d_second.astype(low_type)
        down_ref[rows, :] = d_down
        steps[2 * block + 1]()
        if block == 0:
            work.move(turn[:2], 0)
            for copy in copies[:6]:
                copy.wait()
        for k in range(wu.shape[1] // width):
            columns = pl.ds(k * width, width)
            d_hidden = dot_right(d_down, wd[columns, :])
            d_pre = (d_hidden * slope_ref[rows, columns].astype(jnp.float32)).astype(low_type)
            pre_ref[rows, columns] = d_pre
            d_second = d_second + dot_right(d_pre, wu[:, columns])
        gain, _ = scale_shift(norms, ENC_ATTN)
        d_res, d_gain, d_shift = ln_back(d_second, unit_one[rows, :], rate_one[rows, :], gain)
        vec_ref[0:1, :] += d_gain
        vec_ref[1:2, :] += d_shift
        res_ref[rows, :] = d_res
        d_out = d_res.astype(low_type)
        out_ref[rows, :] = d_out
        d_attn = dot_right(d_out, wo[...]).astype(low_type)
        glob = glob + dot_plain(
            select[:, block * rows_block : (block + 1) * rows_block], d_attn
        )
        d_window = jnp.where(keep_ref[rows, :] > 0, d_attn.astype(jnp.float32), 0.0)
        window_ref[rows, :] = d_window.astype(low_type)
        delta_ref[rows, :] = head_sums(d_window * win_ref[rows, :])
        steps[2 * block + 2]()
    work.move(turn[2:], 0)
    for copy in copies[6:]:
        copy.wait()
    for k in range(wu.shape[1] // width):
        columns = pl.ds(k * width, width)
        product = dot_left(first_ref[...], pre_ref[:, columns]).astype(low_type)
        made_up[:, :, :, :, :, columns] = product.reshape((2,) * free + (-1, width))
        product = dot_left(hidden_ref[:, columns], down_ref[...]).astype(low_type)
        made_down[k // 2, k % 2] = product.reshape(made_down.shape[2:])
    leaving = bring([made_up, made_down], [far_up, far_down], leave)
    work.move(turn, 1)
    for copy in leaving:
        copy.wait()
    glob_ref[...] = glob.astype(low_type)


def head_sums(value):
    lane = lax.broadcasted_iota(jnp.int32, (1, LANES), 1)
    result = jnp.zeros((value.shape[0], LANES), jnp.float32)
    for pair in range(PAIRS):
        two = value[:, pair * LANES : (pair + 1) * LANES]
        for which in range(2):
            inside = (lane // HEAD_DIM) == which
            total = jnp.sum(jnp.where(inside, two, 0.0), axis=1, keepdims=True)
            result = jnp.where(lane == SLOT + 2 * pair + which, total, result)
    return result


def enc_back(query_parts, dck, dcv, kept, weights, norms, made, fars):
    peers = lax.axis_size("seq")
    free = peers.bit_length() - 1
    lead = (2,) * free
    count, width = dck.shape
    full = jnp.float32
    narrow = (count, width)
    wide = fars[1].shape[1]
    glob_count = kept[-1].shape[0]
    rows = query_parts.shape[0] // peers
    shapes = [(2,) * (free - 1 - k) + (rows, width) for k in range(free)]
    plans = [
        piece_plan(peers, ("mat", k), *mat.shape[-2:], kind, 0, 1)
        for k, (mat, kind) in enumerate(zip(made, "xyz"))
    ]
    pieces = [plan for plan, _ in plans]
    whole = pl.BlockSpec(memory_space=pltpu.VMEM)
    far = pl.BlockSpec(memory_space=pl.ANY)
    sem = pltpu.SemaphoreType.DMA
    out_shapes = [
        (narrow, full),
        (narrow, low_type),
        (narrow, low_type),
        ((count, LANES), full),
        ((glob_count, width), low_type),
        ((4, width), full),
        ((rows, width), full),
        (lead + (width // peers, wide), low_type),
        (lead + (wide // peers, width), low_type),
    ] + [(shape[-1], low_type) for _, shape in plans]
    outs = pl.pallas_call(
        functools.partial(enc_back_body, peers, pieces),
        in_specs=[whole]
        + [far] * 3
        + [whole] * (3 + len(kept) + len(weights))
        + [far] * len(fars),
        out_specs=[whole] * 7 + [far] * 2 + [whole] * len(plans),
        out_shape=[jax.ShapeDtypeStruct(shape, kind) for shape, kind in out_shapes],
        scratch_shapes=[sem((free,)), sem((free,)), sem((6,)), sem((6,)), sem((6,))]
        + [sem((len(fars),))]
        + [pltpu.VMEM(one, low_type) for _, shape in plans for one in shape]
        + [pltpu.VMEM((2, 2) + mat.shape[-2:], low_type) for mat in made]
        + [pltpu.VMEM(array.shape, array.dtype) for array in fars]
        + [
            pltpu.VMEM(narrow, low_type),
            pltpu.VMEM((count, wide), low_type),
            pltpu.VMEM(lead + (width // peers, wide), low_type),
            pltpu.VMEM(lead + (wide // peers, width), low_type),
            sem((2,)),
        ]
        + [pltpu.VMEM(shape, low_type) for shape in shapes] * 2
        + [pltpu.VMEM(shape, full) for shape in shapes[:-1]],
        compiler_params=pltpu.CompilerParams(
            collective_id=8, has_side_effects=True, vmem_limit_bytes=62 * 2**20
        ),
    )(
        query_parts.reshape(lead + (rows, width)), *made, dck, dcv, *kept, *weights, norms, *fars
    )
    return outs[:7], outs[7:9], outs[9:], pieces


def turned_stats(stats, padded):
    padded[...] = jnp.zeros_like(padded)
    padded[: stats.shape[0], :] = stats
    return padded[...].T


def dec_back_body(
    limit_ref, sum_ref, res_ref, unit_ref, rate_ref, q_ref, k_ref, v_ref, o_ref, st_ref,
    wcq, wso, wsq, wsk, wsv, norms, dcq_ref, dso_ref, dsq_ref, dsk_ref, dsv_ref, own_ref,
    part_ref, vec_ref, q_pad, d_pad, st_pad, st_turned, bias_ref, dq_ref, key_sum, val_sum,
):
    full = jnp.float32
    mine = q_ref.shape[0]
    d_cq = sum_ref[...].astype(low_type) * 0.125
    dcq_ref[...] = d_cq
    gain, _ = scale_shift(norms, DEC_SELF)
    d_first = res_ref[...] + dot_right(d_cq, wcq[...])
    d_res, d_gain, d_shift = ln_back(d_first, unit_ref[...], rate_ref[...], gain)
    vec_ref[0:1, :] = d_gain
    vec_ref[1:2, :] = d_shift
    d_out = d_res.astype(low_type)
    dso_ref[...] = d_out
    d_attn = dot_right(d_out, wso[...]).astype(low_type)
    st_turned[...] = turned_stats(
        st_ref[...] + head_sums(d_attn.astype(full) * o_ref[...]), st_pad
    )
    q_pad[...] = jnp.zeros_like(q_pad)
    d_pad[...] = jnp.zeros_like(d_pad)
    q_pad[:mine, :] = q_ref[...]
    d_pad[:mine, :] = d_attn
    keys = lax.broadcasted_iota(jnp.int32, bias_ref.shape, 0)
    rows = lax.axis_index("seq") * mine + lax.broadcasted_iota(jnp.int32, bias_ref.shape, 1)
    bias_ref[...] = jnp.where((keys <= rows) & (keys < limit_ref[0]), 0.0, masked_score)
    key_sum[...] = jnp.zeros_like(key_sum)
    val_sum[...] = jnp.zeros_like(val_sum)
    back_heads(
        0, PAIRS, [((0, k_ref.shape[0]),)], LANES, 1, q_pad, k_ref, v_ref, d_pad, st_turned,
        bias_ref, dq_ref, key_sum, val_sum,
    )
    d_q = dq_ref[:mine, :].astype(low_type) * 0.125
    d_k = key_sum[...].astype(low_type)
    d_v = val_sum[...].astype(low_type)
    dsq_ref[...] = d_q
    dsk_ref[...] = d_k
    dsv_ref[...] = d_v
    own_ref[...] = d_res + dot_right(d_q, wsq[...])
    part_ref[...] = (dot_right(d_k, wsk[...]) + dot_right(d_v, wsv[...])).astype(low_type)


def enc_last_body(
    between, rims, gq_ref, gk_ref, gv_ref, gd_ref, go_ref, gs_ref, live_ref, dq_in, dk_in, dv_in, res_ref,
    wq, wk, wv, wgq, wgk, wgv, dgk_ref, dgv_ref, dgq_ref, dq_low, rim_ref, glob_ref, source_ref,
    q_pad, d_pad, st_pad, st_turned, bias_ref, dq_ref, key_sum, val_sum,
):
    full = jnp.float32
    few = gq_ref.shape[0]
    count = gk_ref.shape[0]
    q_pad[...] = jnp.zeros_like(q_pad)
    d_pad[...] = jnp.zeros_like(d_pad)
    q_pad[:few, :] = gq_ref[...]
    d_pad[:few, :] = gd_ref[...]
    st_turned[...] = turned_stats(
        gs_ref[...] + head_sums(gd_ref[...].astype(full) * go_ref[...]), st_pad
    )
    bias_ref[...] = jnp.broadcast_to(live_ref[...], bias_ref.shape)
    key_sum[...] = jnp.zeros_like(key_sum)
    val_sum[...] = jnp.zeros_like(val_sum)
    back_heads(
        0, PAIRS, [((0, count),)], LANES, 1, q_pad, gk_ref, gv_ref, d_pad, st_turned, bias_ref,
        dq_ref, key_sum, val_sum,
    )
    between()
    d_gq = dq_ref[:few, :].astype(low_type) * 0.125
    d_gk = key_sum[...].astype(low_type)
    d_gv = val_sum[...].astype(low_type)
    dgq_ref[...] = d_gq
    dgk_ref[...] = d_gk
    dgv_ref[...] = d_gv
    d_q = dq_in[...].astype(low_type) * 0.125
    dq_low[...] = d_q

    def keys_part(start, size):
        rows = pl.ds(start, size)
        return dot_right(dk_in[rows, :], wk[...]) + dot_right(dv_in[rows, :], wv[...])

    rim_ref[0] = keys_part(0, HALF).astype(low_type)
    rim_ref[1] = keys_part(HALF + count, HALF).astype(low_type)
    rims()
    glob_ref[...] = (keys_part(2 * HALF + count, few) + dot_right(d_gq, wgq[...])).astype(low_type)
    total = res_ref[...] + keys_part(HALF, count) + dot_right(d_q, wq[...])
    source_ref[...] = total + dot_right(d_gk, wgk[...]) + dot_right(d_gv, wgv[...])


def dec_middle_body(
    peers, acc_ref, st_ref, first_ref, cot_ref, norms, wo_far, wu_far, wd_far,
    decoded_ref, res_ref, dout_ref, stats_ref, g_up, g_down, g_out, vec_ref,
    wo, wu, wd, away, acc_one, st_one, low_out, st_out, acc_in, st_in,
    load, send, recv, send_two, recv_two, send_all, recv_all,
):
    full = jnp.float32
    me = lax.axis_index("seq")
    bits, digits = place_bits(peers)
    loads = [
        pltpu.make_async_copy(far, near, load.at[k])
        for k, (far, near) in enumerate(((wo_far, wo), (wu_far, wu), (wd_far, wd)))
    ]
    for copy in loads:
        copy.start()
    acc, top, total = merge_cross(
        peers, acc_ref, st_ref, away, acc_one, st_one, low_out, st_out, acc_in, st_in,
        send, recv, send_two, recv_two,
    )
    cross, lse = finish_parts(acc, top, total)
    cross_low = cross.astype(low_type)
    loads[0].wait()
    unit_one, rate_one = ln_parts(first_ref[...] + dot_plain(cross_low, wo[...]))
    gain, shift = scale_shift(norms, DEC_CROSS)
    second = unit_one * gain + shift
    second_low = second.astype(low_type)
    loads[1].wait()
    hidden, slope = gelu_pair(dot_plain(second_low, wu[...]))
    loads[2].wait()
    unit_two, rate_two = ln_parts(second + dot_plain(hidden, wd[...]))
    gain, shift = scale_shift(norms, DEC_FFN)
    decoded_ref[...] = (unit_two * gain + shift).astype(low_type)
    d_third, d_gain, d_shift = ln_back(cot_ref[...].astype(full), unit_two, rate_two, gain)
    vec_ref[2:3, :] = d_gain
    vec_ref[3:4, :] = d_shift
    d_down = d_third.astype(low_type)
    d_pre = (dot_right(d_down, wd[...]) * slope.astype(full)).astype(low_type)
    d_second = d_third + dot_right(d_pre, wu[...])
    gain, _ = scale_shift(norms, DEC_CROSS)
    d_res, d_gain, d_shift = ln_back(d_second, unit_one, rate_one, gain)
    vec_ref[0:1, :] = d_gain
    vec_ref[1:2, :] = d_shift
    res_ref[...] = d_res
    d_out = d_res.astype(low_type)
    d_cross = dot_right(d_out, wo[...]).astype(low_type)
    dout_ref[tuple(digits)] = d_cross
    stats_ref[tuple(digits)] = lse + head_sums(d_cross.astype(full) * cross)
    refs = [dout_ref, stats_ref]
    sems = (send_all, recv_all)
    reach_out(peers, refs, sems)

    width = d_out.shape[1]
    for k in range(d_pre.shape[1] // width):
        columns = pl.ds(k * width, width)
        product = dot_left(second_low, d_pre[:, k * width : (k + 1) * width]).astype(low_type)
        g_up[:, :, :, :, :, columns] = product.reshape(g_out.shape)
    pass_on(peers, refs, sems)
    for k in range(hidden.shape[1] // width):
        product = dot_left(hidden[:, k * width : (k + 1) * width], d_down).astype(low_type)
        g_down[k // 2, k % 2] = product.reshape(g_down.shape[2:])
    g_out[...] = dot_left(cross_low, d_out).astype(low_type).reshape(g_out.shape)


def merge_cross(
    peers, acc_ref, st_ref, away, acc_one, st_one, low_out, st_out, acc_in, st_in,
    send, recv, send_two, recv_two,
):
    me = lax.axis_index("seq")
    core = me % 2
    pair = me // 2
    half = peers // 2
    mate = {"seq": other_of(me, 1)}
    greet([mate] + [{"seq": lax.rem(me + 2 * k, peers)} for k in range(1, half)])
    for j in range(half):
        away[j] = acc_ref[j, 1 - core].astype(low_type)
    first = [
        remote(away, acc_one, (send, recv), 0, mate),
        remote(st_ref.at[:, 1 - core], st_one, (send, recv), 1, mate),
    ]
    for copy in first:
        copy.start()
    for copy in first:
        copy.wait()
    rest = jnp.zeros((st_one.shape[1], LANES - 2 * SLOT), jnp.float32)

    def join(j):
        acc, top, total = merge_parts([acc_ref[j, core], acc_one[j]], [st_ref[j, core], st_one[j]])
        return acc, jnp.concatenate([top, total, rest], axis=1)

    def ship(k):
        j = lax.rem(pair + k, half)
        return [
            pltpu.make_async_remote_copy(
                src_ref=source.at[j],
                dst_ref=slot.at[half - k],
                send_sem=send_two.at[which, k],
                recv_sem=recv_two.at[which, half - k],
                device_id={"seq": lax.rem(me + 2 * k, peers)},
                device_id_type=pl.DeviceIdType.MESH,
            )
            for which, (source, slot) in enumerate(((low_out, acc_in), (st_out, st_in)))
        ]

    for k in range(1, half):
        j = lax.rem(pair + k, half)
        acc, stat = join(j)
        low_out[j] = acc.astype(low_type)
        st_out[j] = stat
        for copy in ship(k):
            copy.start()
    own_acc, own_stat = join(pair)
    for k in range(1, half):
        for copy in ship(k):
            copy.wait()
    return merge_parts(
        [own_acc] + [acc_in[k] for k in range(1, half)],
        [own_stat] + [st_in[k] for k in range(1, half)],
    )


def dec_middle(acc, stats, dec_first, cotangent, norms, weights):
    peers = lax.axis_size("seq")
    free = peers.bit_length() - 1
    half = peers // 2
    rows, width = dec_first.shape
    full = jnp.float32
    whole = pl.BlockSpec(memory_space=pltpu.VMEM)
    far = pl.BlockSpec(memory_space=pl.ANY)
    wide = weights[1].shape[1]
    lead = (2,) * free
    shapes = [
        ((rows, width), low_type),
        ((rows, width), full),
        (lead + (rows, width), low_type),
        (lead + (rows, LANES), full),
        (lead + (width // peers, wide), low_type),
        (lead + (wide // peers, width), low_type),
        (lead + (width // peers, width), low_type),
        ((4, width), full),
    ]
    sem = pltpu.SemaphoreType.DMA
    decoded, d_res, dout, all_stats, g_up, g_down, g_out, vec = pl.pallas_call(
        functools.partial(dec_middle_body, peers),
        in_specs=[whole] * 5 + [far] * 3,
        out_specs=[whole] * len(shapes),
        out_shape=[jax.ShapeDtypeStruct(shape, kind) for shape, kind in shapes],
        scratch_shapes=[pltpu.VMEM(weight.shape, low_type) for weight in weights]
        + [
            pltpu.VMEM((half, rows, width), low_type),
            pltpu.VMEM((half, rows, width), low_type),
            pltpu.VMEM((half, rows, LANES), full),
            pltpu.VMEM((half, rows, width), low_type),
            pltpu.VMEM((half, rows, LANES), full),
            pltpu.VMEM((half, rows, width), low_type),
            pltpu.VMEM((half, rows, LANES), full),
            sem((3,)),
            sem((2,)),
            sem((2,)),
            sem((2, half)),
            sem((2, half)),
            sem((2 * peers,)),
            sem((2 * peers,)),
        ],
        compiler_params=pltpu.CompilerParams(
            collective_id=4, has_side_effects=True, vmem_limit_bytes=vmem_bytes
        ),
    )(
        acc.reshape(half, 2, rows, width), stats.reshape(half, 2, rows, LANES),
        dec_first, cotangent, norms, *weights,
    )
    return (
        decoded, d_res, dout.reshape(-1, width), all_stats.reshape(-1, LANES),
        (g_up, g_down, g_out), vec,
    )


def resumed(peers, piece, array, k, first, last):
    stages = piece["stages"]
    width = array.shape[-1] * (2 if "dp" in stages[:first] else 1)
    shapes = piece_shapes(peers, array.shape[-2], width, stages)
    return (
        {"from": ("kept", k), "stages": stages, "first": first, "last": last},
        shapes[first : last + 1],
    )


def window_back_body(
    peers, parts, rows_block, blocks, pieces, held_counts, turns, *refs
):
    refs = list(refs)

    def take(count):
        result = refs[:count]
        del refs[:count]
        return result

    q_ref, k_ref, v_ref, d_ref, st_ref, use_ref, part_ref = take(7)
    factors = take(5)
    kept = take(3)
    mats = take(2)
    dec_in = take(16)
    dq_ref, dk_ref, dv_ref, sum_copy = take(4)
    outs = take(len(pieces))
    dec_out = take(8)
    key_sum, val_sum, bias_ref, slot, sum_ref = take(5)
    sems = take(4)
    send, recv, load = take(3)
    held = [take(count) for count in held_counts]
    own = take(2)
    staging = take(3)
    dec_scratch = take(8)
    nears = take(5)
    (fetch,) = take(1)
    fars = dec_in[10:15]
    dec_in[10:15] = nears
    step = pl.program_id(0)
    work = Pieces(
        peers, pieces, mats, factors, kept, outs, (send, recv), load, held, own, staging, 0
    )
    for p, piece in enumerate(pieces):
        for s in range(piece["first"], piece["last"] + 1):
            work.number(p, s)

    @pl.when(step == 0)
    def _():
        greet(everyone(peers) + [work.partner("dp")])
        send_in(peers, [part_ref], [slot], sems)
        bring(fars, nears, fetch)
        work.open(turns[0])
        work.open(turns[2])
        work.open(turns[1])
        keys = lax.broadcasted_iota(jnp.int32, bias_ref.shape, 0)
        rows = lax.broadcasted_iota(jnp.int32, bias_ref.shape, 1)
        near = (jnp.abs(rows + HALF - keys) <= HALF) | (keys >= bias_ref.shape[1] + 2 * HALF)
        bias_ref[...] = jnp.where(near, use_ref[...], masked_score)

    @pl.when(step == 1)
    def _():
        work.move(turns[2], 0)
        sum_at_owner(peers, part_ref, slot, sum_ref, sems)
        send_out(peers, [sum_ref], sems)

    @pl.when(step == 2)
    def _():
        work.move(turns[1], 0)

    backward_body(
        parts, rows_block, blocks, 1, q_ref, k_ref, v_ref, d_ref, st_ref, bias_ref,
        dq_ref, dk_ref, dv_ref, key_sum, val_sum,
    )

    @pl.when(step == PAIRS - 1)
    def _():
        take_out(peers, [sum_ref], sems)
        left(peers, [part_ref], [slot], sems)
        sum_copy[...] = sum_ref[...]
        for copy in fetches(fars, nears, fetch):
            copy.wait()
        dec_back_body(*dec_in, *dec_out, *dec_scratch)
        work.move(turns[0], 2)
        work.move(turns[2], 1)
        work.move(turns[1], 1)


def window_attend_back(
    queries, keys, values, grads, stats, use, parts, rows_block, glob_part, pairs, made, kept, begun,
    limit, dec_inputs
):
    peers = lax.axis_size("seq")
    free = peers.bit_length() - 1
    lead = (2,) * free
    count, width = queries.shape
    key_count = keys.shape[0]
    rows = glob_part.shape[0] // OWNERS
    flops = 10 * count * key_count * width
    factors = []
    places = []
    for pair in pairs:
        spots = []
        for factor in pair:
            known = [k for k, other in enumerate(factors) if other is factor]
            if not known:
                factors.append(factor)
                known = [len(factors) - 1]
            spots.append(known[0])
        places.append(tuple(spots))
    mats = list(made)
    block_rows = width // peers
    plans = [resumed(peers, piece, array, k, 2, 2) for k, (piece, array) in enumerate(zip(begun, kept))]
    plans += [
        piece_plan(peers, ("made", k), block_rows, width, kind, 0, 1, pair)
        for k, (pair, kind) in enumerate(zip(places, "xyz"))
    ]
    plans += [
        piece_plan(peers, ("mat", k), *mat.shape[-2:], kind, 0, 1)
        for k, (mat, kind) in enumerate(zip(mats, "xy"))
    ]
    pieces = [plan for plan, _ in plans]
    shapes = [shape for _, shape in plans]
    sem_count = sum(len(shape) for shape in shapes)
    mine = dec_inputs[0].shape[0]
    dec_keys = dec_inputs[5].shape[0]
    full = jnp.float32
    dec_shapes = [((mine, width), low_type)] * 3 + [((dec_keys, width), low_type)] * 2
    dec_shapes += [((mine, width), full), ((dec_keys, width), low_type), ((2, width), full)]

    def pair_block(size):
        return pl.BlockSpec((size, LANES), lambda p, i: (0, p))

    def whole(*shape):
        return pl.BlockSpec(
            shape, lambda p, i: (0,) * len(shape), pipeline_mode=pl.Buffered(1)
        )

    def whole_out(*shape):
        return pl.BlockSpec(shape, lambda p, i: (0,) * len(shape))

    outs = pl.pallas_call(
        functools.partial(
            window_back_body, peers, parts, rows_block, count // rows_block, pieces,
            [len(shape) for shape in shapes], [[0, 1, 2], [3, 4, 5], [6, 7]],
        ),
        grid=(PAIRS, 1),
        in_specs=[
            pair_block(count),
            pair_block(key_count),
            pair_block(key_count),
            pair_block(count),
            whole(2 * SLOT, count),
            whole(key_count, 1),
            whole(OWNERS, rows, width),
        ]
        + [whole(*array.shape) for array in factors + list(kept)]
        + [pl.BlockSpec(memory_space=pl.ANY)] * len(mats)
        + [pl.BlockSpec(memory_space=pltpu.SMEM)]
        + [
            pl.BlockSpec(memory_space=pl.ANY) if 9 <= k < 14 else whole(*array.shape)
            for k, array in enumerate(dec_inputs)
        ],
        out_specs=[
            pair_block(count),
            pair_block(key_count),
            pair_block(key_count),
            whole_out(OWNERS, rows, width),
        ]
        + [whole_out(*shape[-1]) for shape in shapes]
        + [whole_out(*shape) for shape, _ in dec_shapes],
        out_shape=[
            jax.ShapeDtypeStruct((count, width), low_type),
            jax.ShapeDtypeStruct((key_count, width), low_type),
            jax.ShapeDtypeStruct((key_count, width), low_type),
            jax.ShapeDtypeStruct((OWNERS, rows, width), low_type),
        ]
        + [jax.ShapeDtypeStruct(shape[-1], low_type) for shape in shapes]
        + [jax.ShapeDtypeStruct(shape, kind) for shape, kind in dec_shapes],
        scratch_shapes=[
            pltpu.VMEM((key_count, LANES), jnp.float32),
            pltpu.VMEM((key_count, LANES), jnp.float32),
            pltpu.VMEM((key_count, count), jnp.float32),
            pltpu.VMEM((peers, rows, width), low_type),
            pltpu.VMEM((OWNERS, rows, width), low_type),
        ]
        + owner_sems(peers, 1)
        + [pltpu.SemaphoreType.DMA((sem_count,))] * 2
        + [pltpu.SemaphoreType.DMA((2 * len(mats),))]
        + [pltpu.VMEM(one, low_type) for shape in shapes for one in shape]
        + [pltpu.VMEM((2, 2) + mat.shape[-2:], low_type) for mat in mats]
        + [pltpu.VMEM(lead + (block_rows, width), low_type)] * 3
        + [
            pltpu.VMEM((LANES, width), low_type),
            pltpu.VMEM((LANES, width), low_type),
            pltpu.VMEM((LANES, LANES), full),
            pltpu.VMEM((LANES, LANES), full),
            pltpu.VMEM((dec_keys, LANES), full),
            pltpu.VMEM((LANES, width), full),
            pltpu.VMEM((dec_keys, width), full),
            pltpu.VMEM((dec_keys, width), full),
        ]
        + [pltpu.VMEM(array.shape, low_type) for array in dec_inputs[9:14]]
        + [pltpu.SemaphoreType.DMA((5,))],
        compiler_params=pltpu.CompilerParams(
            collective_id=7, has_side_effects=True, vmem_limit_bytes=62 * 2**20
        ),
        cost_estimate=pl.CostEstimate(
            flops=4 * flops,
            bytes_accessed=2 * (2 * count + 4 * key_count) * width + 4 * count * width,
            transcendentals=count * key_count * HEADS,
        ),
    )(
        queries, keys, values, grads, stats, use, glob_part.reshape(OWNERS, rows, width),
        *factors, *kept, *mats, limit, *dec_inputs,
    )
    last = 4 + len(pieces)
    return outs[:3], outs[3].reshape(-1, width), outs[4:last], pieces, outs[last:]


def last_body(peers, plan, *refs):
    refs = list(refs)

    def take(count):
        result = refs[:count]
        del refs[:count]
        return result

    pieces = plan["pieces"]
    kept = take(plan["kept"])
    factors = take(plan["factors"])
    target_part, vec_part = take(2)
    enc_in = take(plan["enc_in"])
    outs = take(len(pieces))
    target_out, glob_out, vec_out, from_after, from_before, source_ref = take(6)
    send, recv, fetch = take(3)
    held = [take(count) for count in plan["held"]]
    staging = take(plan["slots"])
    tall, late = plan["tall"], enc_in[8:]
    nears = take(len(tall) + len(late))
    fars = [factors[k] for k in tall] + late
    for k, near in zip(tall, nears):
        factors[k] = near
    enc_in[8:] = nears[len(tall) :]
    target_held = take(plan["free"])
    glob_held = take(plan["free"])
    vec_held = take(plan["free"] + 1)
    d_gk, d_gv, d_gq, d_q, rim, glob_part = take(6)
    enc_scratch = take(8)
    me = lax.axis_index("seq")
    bits = [1 << k for k in range(plan["free"])]
    own_x = factors[plan["rows"]].at[pl.ds(HALF, d_q.shape[0]), :]
    work = Pieces(
        peers, pieces, [], factors + [d_gk, d_gv, d_gq, d_q, own_x], kept, outs, (send, recv), None, held,
        [], staging, 0
    )
    left_one = {"seq": lax.rem(me + peers - 1, peers)}
    right_one = {"seq": lax.rem(me + 1, peers)}
    greet([work.partner(stage) for stage in bits + ["dp"]] + [left_one, right_one])
    sems = (send, recv)
    to_left = remote(rim.at[0], from_after, sems, work.number("left"), left_one)
    to_right = remote(rim.at[1], from_before, sems, work.number("right"), right_one)

    target_stages = bits
    vec_stages = bits + ["dp"]

    def target_copy(s):
        origin = target_part if s == 0 else target_held[s - 1]
        return work.copy("t", target_stages, origin, target_held[s], s), origin

    def whole_copy(name, part, result, buffers, stages, s):
        origin = part if s == 0 else result
        copy = remote(
            origin, buffers[s], sems, work.number(name, s), work.partner(stages[s])
        )
        return copy, origin

    def small_begin(s):
        if s < len(bits):
            target_copy(s)[0].start()
            whole_copy("g", glob_part, glob_out, glob_held, bits, s)[0].start()
        whole_copy("v", vec_part, vec_out, vec_held, vec_stages, s)[0].start()

    def small_end(s):
        if s < len(bits):
            copy, origin = target_copy(s)
            copy.wait()
            finish = target_out if s == len(bits) - 1 else None
            work.fold(target_stages, origin, target_held[s], s, finish)
            copy, origin = whole_copy("g", glob_part, glob_out, glob_held, bits, s)
            copy.wait()
            glob_out[...] = origin[...] + glob_held[s][...]
        copy, origin = whole_copy("v", vec_part, vec_out, vec_held, vec_stages, s)
        copy.wait()
        vec_out[...] = origin[...] + vec_held[s][...]

    turns = plan["turns"]
    work.open(turns[0])
    work.open(turns[5])
    fetched = bring(fars, nears, fetch)
    work.open(turns[1])
    work.open(turns[2])
    work.move(turns[1], 0)
    work.move(turns[2], 0)
    for copy in fetched:
        copy.wait()
    keys, vals = (factors[k] for k in plan["shared"])

    def rims():
        @pl.when(me > 0)
        def _():
            to_left.start()

        @pl.when(me < peers - 1)
        def _():
            to_right.start()

    enc_last_body(
        lambda: work.move(turns[0], 2), rims, *enc_in[:8], keys, vals, *enc_in[8:], d_gk, d_gv, d_gq, d_q,
        rim, glob_part, source_ref, *enc_scratch,
    )

    small_begin(0)
    work.move(turns[5], 3)
    work.open(turns[3])
    work.move(turns[1], 1)
    work.move(turns[3], 0)
    work.move(turns[5], 4)
    work.move(turns[2], 1)
    work.move(turns[0], 3)
    small_end(0)
    small_begin(1)
    work.open(turns[4])
    work.move(turns[1], 2)
    work.move(turns[4], 0)
    work.move(turns[3], 1)
    work.move(turns[2], 2)
    work.move(turns[0], 4)
    work.move(turns[1], 3)
    small_end(1)
    small_begin(2)
    work.move(turns[4], 1)
    work.move(turns[3], 2)
    work.move(turns[2], 3)
    work.move(turns[1], 4)
    small_end(2)
    small_begin(3)
    work.move(turns[4], 2)
    work.move(turns[3], 3)
    work.move(turns[2], 4)
    small_end(3)
    small_begin(4)
    work.move(turns[4], 3)
    work.move(turns[3], 4)
    small_end(4)
    work.move(turns[4], 4)

    @pl.when(me > 0)
    def _():
        to_left.wait_send()
        remote(rim.at[1], from_before, sems, work.number("right"), left_one).wait_recv()

    @pl.when(me < peers - 1)
    def _():
        to_right.wait_send()
        remote(rim.at[0], from_after, sems, work.number("left"), right_one).wait_recv()


KINDS = "xyxxyxxxyxx"


def last_exchange(kept, begun, pairs, enc_inputs, target_part, vec_part):
    peers = lax.axis_size("seq")
    free = peers.bit_length() - 1
    lead = (2,) * free
    full = jnp.float32
    factors = []
    spots = []
    for pair in pairs:
        spot = []
        for factor in pair:
            if isinstance(factor, int):
                spot.append(factor - 5)
                continue
            known = [k for k, other in enumerate(factors) if other is factor]
            if not known:
                factors.append(factor)
                known = [len(factors) - 1]
            spot.append(known[0])
        spots.append(tuple(spot))
    width = pairs[0][0].shape[1]
    rows = width // peers
    slots = 5
    last = free
    plans = [
        resumed(peers, piece, array, k, piece["last"] + 1, last)
        for k, (piece, array) in enumerate(zip(begun, kept))
    ]
    order = [0, 1, 2, 3, 4, 5, 6, 7, 8, 9, 10]
    for k, spot in zip(order, spots):
        slot = k % 5
        plans.append(piece_plan(peers, ("made", slot), rows, width, KINDS[k], 0, last, spot))
    pieces = [plan for plan, _ in plans]
    shapes = [shape for _, shape in plans]
    begun_count = len(begun)
    made = list(range(begun_count, len(pieces)))
    far_on = [k for k, piece in enumerate(begun) if piece["last"] == 2]
    fresh = [k for k in range(begun_count) if k not in far_on]
    turns = [fresh, made[:3], made[3:5], made[5:8], made[8:], far_on]
    target_shapes = piece_shapes(
        peers, target_part.shape[0] // peers, width, [1 << k for k in range(free)]
    )
    few = enc_inputs[0].shape[0]
    count = enc_inputs[1].shape[0]
    narrow = (count, width)
    tall = [k for k, factor in enumerate(factors) if factor.shape[0] > count]
    late = enc_inputs[8:]
    far = pl.BlockSpec(memory_space=pl.ANY)
    plan = {
        "pieces": pieces,
        "kept": begun_count,
        "factors": len(factors),
        "enc_in": len(enc_inputs),
        "held": [len(shape) for shape in shapes],
        "slots": slots,
        "turns": turns,
        "free": free,
        "shared": (spots[8][1], spots[9][1]),
        "rows": spots[8][0],
        "tall": tall,
    }
    sems = sum(len(shape) for shape in shapes) + free * 3 + 3
    whole = pl.BlockSpec(memory_space=pltpu.VMEM)
    out_shapes = [(shape[-1], full) for shape in shapes] + [
        (target_shapes[-1], full),
        ((few, width), low_type),
        (vec_part.shape, full),
        ((HALF, width), low_type),
        ((HALF, width), low_type),
        (narrow, full),
    ]
    sem = pltpu.SemaphoreType.DMA((sems,))
    outs = pl.pallas_call(
        functools.partial(last_body, peers, plan),
        in_specs=[whole] * begun_count
        + [far if k in tall else whole for k in range(len(factors))]
        + [whole] * 10
        + [far] * len(late),
        out_specs=[whole] * len(out_shapes),
        out_shape=[jax.ShapeDtypeStruct(shape, kind) for shape, kind in out_shapes],
        scratch_shapes=[sem, sem, pltpu.SemaphoreType.DMA((len(tall) + len(late),))]
        + [pltpu.VMEM(one, low_type) for shape in shapes for one in shape]
        + [pltpu.VMEM(lead + (rows, width), low_type)] * slots
        + [pltpu.VMEM(factors[k].shape, low_type) for k in tall]
        + [pltpu.VMEM(array.shape, array.dtype) for array in late]
        + [pltpu.VMEM(shape, low_type) for shape in target_shapes]
        + [pltpu.VMEM((few, width), low_type)] * free
        + [pltpu.VMEM(vec_part.shape, full)] * (free + 1)
        + [
            pltpu.VMEM(narrow, low_type),
            pltpu.VMEM(narrow, low_type),
            pltpu.VMEM((few, width), low_type),
            pltpu.VMEM(narrow, low_type),
            pltpu.VMEM((2, HALF, width), low_type),
            pltpu.VMEM((few, width), low_type),
            pltpu.VMEM((LANES, width), low_type),
            pltpu.VMEM((LANES, width), low_type),
            pltpu.VMEM((LANES, LANES), full),
            pltpu.VMEM((LANES, LANES), full),
            pltpu.VMEM((count, LANES), full),
            pltpu.VMEM((LANES, width), full),
            pltpu.VMEM(narrow, full),
            pltpu.VMEM(narrow, full),
        ],
        compiler_params=pltpu.CompilerParams(
            collective_id=1, has_side_effects=True, vmem_limit_bytes=63 * 2**20
        ),
    )(
        *kept, *factors, target_part.reshape(lead + (-1, width)), vec_part, *enc_inputs
    )
    return outs[: len(pieces)], outs[len(pieces) :]


def per_device(
    source,
    target,
    cotangent,
    src_len,
    dec_len,
    global_pos,
    enc_query,
    enc_key,
    enc_value,
    glob_query,
    glob_key,
    glob_value,
    enc_out,
    enc_attn_gain,
    enc_attn_shift,
    enc_up,
    enc_down,
    enc_ffn_gain,
    enc_ffn_shift,
    self_query,
    self_key,
    self_value,
    self_out,
    dec_self_gain,
    dec_self_shift,
    cross_query,
    cross_key,
    cross_value,
    cross_out,
    dec_cross_gain,
    dec_cross_shift,
    dec_up,
    dec_down,
    dec_ffn_gain,
    dec_ffn_shift,
):
    full = jnp.float32
    src_x = source[0]
    dec_x = target[0]
    src_count = src_x.shape[0]
    dec_count = dec_x.shape[0]
    seq_index = lax.axis_index("seq")
    peers = lax.axis_size("seq")
    src_limit = src_len[0]
    glob_places = global_pos[0]
    glob_count = glob_places.shape[0]
    src_places = seq_index * src_count + jnp.arange(src_count, dtype=jnp.int32)
    select_glob = glob_places[:, None] == src_places[None, :]
    select_low = select_glob.astype(low_type)
    norms = jnp.concatenate(
        [
            enc_attn_gain, enc_attn_shift, enc_ffn_gain, enc_ffn_shift, dec_self_gain,
            dec_self_shift, dec_cross_gain, dec_cross_shift, dec_ffn_gain, dec_ffn_shift,
        ]
    ).astype(full).reshape(10, -1)

    upward = [(i, i + 1) for i in range(peers - 1)]
    downward = [(i + 1, i) for i in range(peers - 1)]
    dec_all, glob_x, query_loc, glob_keys_loc, glob_vals_loc = start_exchange(
        dec_x,
        dot_plain(select_low, src_x).astype(low_type),
        src_x,
        (enc_query, glob_key, glob_value),
    )
    rim_x, _ = lax.optimization_barrier((src_x, glob_x))
    before = lax.ppermute(rim_x[src_count - HALF :], "seq", upward)
    after = lax.ppermute(rim_x[:HALF], "seq", downward)

    (self_k, self_v, all_cross_q, self_q, self_out_full, self_attn, self_stats, dec_first,
     dec_first_low, self_unit, self_rate) = dec_front(
        dec_len,
        dec_all,
        (self_query, self_key, self_value, self_out, cross_query),
        norms,
        dec_count,
    )

    glob_queries = (dot_plain(glob_x, glob_query) * 0.125).astype(low_type)
    live_bias = jnp.where(src_places < src_limit, 0.0, masked_score)
    glob_acc, glob_stats = attend(
        glob_queries, glob_keys_loc, glob_vals_loc, live_bias[None, :], None, glob_count, False, 6
    )

    x_all, keys_all, vals_all = project_all((before, src_x, after, glob_x), enc_key, enc_value)
    pad_count = src_count + 2 * HALF
    pad_places = seq_index * src_count - HALF + jnp.arange(pad_count, dtype=jnp.int32)
    pad_glob = jnp.any(glob_places[:, None] == pad_places[None, :], axis=0)
    pad_use = (pad_places >= 0) & (pad_places < src_limit) & jnp.logical_not(pad_glob)
    win_use = jnp.concatenate(
        [jnp.where(pad_use, 0.0, masked_score), jnp.zeros((glob_count,), full)]
    )
    keep = jnp.where(pad_glob[HALF : HALF + src_count], 0.0, 1.0)[:, None]
    rows_block = 256
    reach = rows_block + 2 * HALF
    win_parts = [
        ((block * rows_block, reach), (pad_count, glob_count))
        for block in range(src_count // rows_block)
    ]
    win_out, win_stats, glob_out, glob_lse = window_attend(
        query_loc, keys_all, vals_all, win_use[None, :], win_parts, rows_block, glob_acc, glob_stats
    )
    (enc_attn, unit_one, rate_one, enc_first_low, enc_hidden, enc_slope, unit_two, rate_two,
     memory_low, cross_k, cross_v) = enc_front(
        win_out,
        keep,
        select_low,
        glob_out,
        src_x,
        (enc_out, enc_up, enc_down, cross_key, cross_value),
        norms,
    )

    cross_acc, cross_stats = attend(
        all_cross_q, cross_k, cross_v, live_bias[None, :], None, 256, False, 2
    )
    decoded, d_res_two, all_dout, all_stats, dec_made, dec_vec = dec_middle(
        cross_acc, cross_stats, dec_first, cotangent[0], norms, (cross_out, dec_up, dec_down)
    )
    query_parts, ck_low, cv_low = attend_back(
        all_cross_q,
        cross_k,
        cross_v,
        all_dout,
        all_stats[:, : 2 * SLOT].T,
        jnp.broadcast_to(live_bias[:, None], (src_count, 512)),
        None,
        256,
        2,
    )

    enc_grads, enc_made, dec_kept, dec_begun = enc_back(
        query_parts,
        ck_low,
        cv_low,
        (unit_two, rate_two, rate_one, keep, select_low),
        (cross_key, cross_value),
        norms,
        dec_made,
        (enc_down, enc_up, enc_slope, unit_one, enc_out, win_out, enc_hidden, enc_first_low),
    )
    d_enc_res, d_attn_o, d_window, win_delta, glob_part, enc_vec, d_cross_sum = enc_grads
    win_pair = (win_stats + win_delta)[:, : 2 * SLOT].T
    (d_query, d_keys_all, d_vals_all), glob_dout, kept, begun, dec_grads = window_attend_back(
        query_loc, keys_all, vals_all, d_window, win_pair, win_use[:, None], win_parts, rows_block,
        glob_part,
        [(memory_low, ck_low), (memory_low, cv_low), (enc_attn, d_attn_o)],
        enc_made,
        dec_kept,
        dec_begun,
        dec_len,
        (d_cross_sum, d_res_two, self_unit, self_rate, self_q, self_k, self_v, self_out_full,
         self_stats, cross_query, self_out, self_query, self_key, self_value, norms),
    )
    (d_cross_q, d_self_o, d_self_q, d_self_k, d_self_v, d_target_own, d_target_part,
     self_vec) = dec_grads
    vec_part = jnp.concatenate(
        [enc_vec, self_vec, dec_vec, jnp.zeros((6, enc_vec.shape[1]), full)], axis=0
    )

    own_gk, own_gv, own_gq, own_q, own_x = range(5)
    pairs = [
        (dec_first_low, d_cross_q),
        (self_attn, d_self_o),
        (dec_x, d_self_q),
        (dec_all, d_self_k),
        (dec_all, d_self_v),
        (own_x, own_q),
        (own_x, own_gk),
        (own_x, own_gv),
        (x_all, d_keys_all),
        (x_all, d_vals_all),
        (glob_x, own_gq),
    ]
    shared, rest = last_exchange(
        kept,
        begun,
        pairs,
        (glob_queries, glob_keys_loc, glob_vals_loc, glob_dout, glob_out, glob_lse,
         live_bias[:, None], d_query, d_enc_res,
         enc_query, enc_key, enc_value, glob_query, glob_key, glob_value),
        d_target_part,
        vec_part,
    )
    d_target_sum, d_glob_x, vec_sum, from_after, from_before, d_source_own = rest
    vectors = share_vectors(vec_sum, 10)
    flags = jnp.stack([seq_index < peers - 1, seq_index > 0]).astype(jnp.int32)[None, :]
    (
        s_dec_up, s_dec_down, s_cross_out,
        s_cross_key, s_cross_value, s_enc_out, s_enc_up, s_enc_down, s_cross_query, s_self_out,
        s_self_query, s_self_key, s_self_value,
        s_enc_query, s_glob_key, s_glob_value, s_enc_key, s_enc_value, s_glob_query,
        d_source, d_target,
    ) = end_outputs(
        shared,
        (d_source_own, from_after, from_before, select_low, d_glob_x, flags),
        (d_target_own, d_target_sum),
    )
    return (
        decoded[None],
        d_source[None],
        d_target[None],
        s_enc_query,
        s_enc_key,
        s_enc_value,
        s_glob_query,
        s_glob_key,
        s_glob_value,
        s_enc_out,
        vectors[0],
        vectors[1],
        s_enc_up,
        s_enc_down,
        vectors[2],
        vectors[3],
        s_self_query,
        s_self_key,
        s_self_value,
        s_self_out,
        vectors[4],
        vectors[5],
        s_cross_query,
        s_cross_key,
        s_cross_value,
        s_cross_out,
        vectors[6],
        vectors[7],
        s_dec_up,
        s_dec_down,
        vectors[8],
        vectors[9],
    )


def swap_dp(value):
    pairs = [(i, i ^ 1) for i in range(lax.axis_size("dp"))]
    return lax.ppermute(value, "dp", pairs)


def gather_rows(value):
    rows, width = value.shape
    held = value[None]
    for bit in reversed(seq_bits()):
        other = swap(held, bit)
        upper = bit_set(bit)
        held = jnp.stack(
            [jnp.where(upper, other, held), jnp.where(upper, held, other)], axis=1
        ).reshape(2 * held.shape[0], rows, width)
    return held.reshape(-1, width)


def add_all(value):
    for bit in seq_bits():
        value = value + swap(value, bit)
    return value


def scatter_all(value):
    bits = seq_bits()
    held = value.reshape((2,) * len(bits) + (-1, value.shape[1]))
    for step, bit in enumerate(bits):
        axis = len(bits) - 1 - step
        mine = bit_set(bit).astype(jnp.int32)
        other = swap(pick_half(held, 1 - mine, axis).astype(low_type), bit)
        held = pick_half(held, mine, axis) + other.astype(jnp.float32)
    return held


def merge_body(acc_a, st_a, acc_b, st_b, acc_o, st_o):
    top_a, top_b = st_a[:, :SLOT], st_b[:, :SLOT]
    top = jnp.maximum(top_a, top_b)
    keep_a = jnp.exp(top_a - top)
    keep_b = jnp.exp(top_b - top)
    total = st_a[:, SLOT : 2 * SLOT] * keep_a + st_b[:, SLOT : 2 * SLOT] * keep_b
    spread = head_spread()
    acc_o[...] = acc_a[...] * exact_dot(keep_a, spread) + acc_b[...].astype(
        jnp.float32
    ) * exact_dot(keep_b, spread)
    rest = jnp.zeros((top.shape[0], LANES - 2 * SLOT), jnp.float32)
    st_o[...] = jnp.concatenate([top, total, rest], axis=1)


def merge_soft(held, other):
    rows = held[0].shape[0]
    return pl.pallas_call(
        merge_body,
        out_shape=[
            jax.ShapeDtypeStruct((rows, held[0].shape[1]), jnp.float32),
            jax.ShapeDtypeStruct((rows, LANES), jnp.float32),
        ],
        compiler_params=pltpu.CompilerParams(vmem_limit_bytes=vmem_bytes),
    )(*held, *other)


def merge_all(held):
    for bit in seq_bits():
        held = merge_soft(held, swap((held[0].astype(low_type), held[1]), bit))
    return held


def merge_scatter(held):
    bits = seq_bits()
    for step, bit in enumerate(bits):
        inner = len(bits) - 1 - step
        mine = bit_set(bit).astype(jnp.int32)

        def halves(value, chosen):
            split = value.reshape(1 << inner, 2, -1, value.shape[1])
            return pick_half(split, chosen, 1).reshape(-1, value.shape[1])

        away = (halves(held[0], 1 - mine).astype(low_type), halves(held[1], 1 - mine))
        held = merge_soft((halves(held[0], mine), halves(held[1], mine)), swap(away, bit))
    return held


def share_grads(grads, dp_first):
    bits = seq_bits()
    width = grads[0].shape[1]
    half = width // 2
    rows = [grad.shape[0] >> len(bits) for grad in grads]
    dp_mine = lax.axis_index("dp")
    laid = [
        grad.astype(low_type).reshape((2,) * len(bits) + (count, width))
        for grad, count in zip(grads, rows)
    ]
    steps = [(1, False)]
    rest = [(bit, False) for bit in bits[1:]]
    steps += [(0, True)] + rest if dp_first else rest[:1] + [(0, True)] + rest[1:]
    held = None
    axis = len(bits)
    for bit, is_dp in steps:
        if is_dp:
            own = lax.dynamic_slice_in_dim(held, dp_mine * half, half, held.ndim - 1)
            away = lax.dynamic_slice_in_dim(held, (1 - dp_mine) * half, half, held.ndim - 1)
            held = own + swap_dp(away)
            continue
        axis -= 1
        mine = bit_set(bit).astype(jnp.int32)
        if held is None:
            away = jnp.concatenate([pick_half(v, 1 - mine, axis) for v in laid], axis=-2)
            own = jnp.concatenate([pick_half(v, mine, axis) for v in laid], axis=-2)
        else:
            away = pick_half(held, 1 - mine, axis)
            own = pick_half(held, mine, axis)
        held = own + swap(away, bit)
    result = []
    start = 0
    for count in rows:
        result.append(held[start : start + count].astype(jnp.float32))
        start += count
    return result


def share_norms(vectors):
    stacked = jnp.concatenate([jnp.stack(vectors), jnp.zeros((6, vectors[0].shape[0]))], axis=0)
    total = add_all(stacked)
    total = total + swap_dp(total)
    length = stacked.shape[1] // lax.axis_size("seq")
    mine = lax.dynamic_slice_in_dim(total, lax.axis_index("seq") * length, length, 1)
    return [mine[k] for k in range(len(vectors))]


def per_device_wide(
    source,
    target,
    cotangent,
    src_len,
    dec_len,
    global_pos,
    enc_query,
    enc_key,
    enc_value,
    glob_query,
    glob_key,
    glob_value,
    enc_out,
    enc_attn_gain,
    enc_attn_shift,
    enc_up,
    enc_down,
    enc_ffn_gain,
    enc_ffn_shift,
    self_query,
    self_key,
    self_value,
    self_out,
    dec_self_gain,
    dec_self_shift,
    cross_query,
    cross_key,
    cross_value,
    cross_out,
    dec_cross_gain,
    dec_cross_shift,
    dec_up,
    dec_down,
    dec_ffn_gain,
    dec_ffn_shift,
):
    full = jnp.float32
    src_x = source[0]
    dec_x = target[0]
    src_count = src_x.shape[0]
    dec_count = dec_x.shape[0]
    seq_index = lax.axis_index("seq")
    peers = lax.axis_size("seq")
    src_limit = src_len[0]
    dec_limit = dec_len[0]
    glob_places = global_pos[0]
    glob_count = glob_places.shape[0]
    src_places = seq_index * src_count + jnp.arange(src_count, dtype=jnp.int32)
    select_glob = glob_places[:, None] == src_places[None, :]
    select_low = select_glob.astype(low_type)
    is_global = jnp.any(select_glob, axis=0)
    spread = head_spread()

    upward = [(i, i + 1) for i in range(peers - 1)]
    downward = [(i + 1, i) for i in range(peers - 1)]
    before = lax.ppermute(src_x[src_count - HALF :], "seq", upward)
    after = lax.ppermute(src_x[:HALF], "seq", downward)
    dec_all = gather_rows(dec_x)
    glob_x = add_all(dot_plain(select_low, src_x).astype(low_type))

    query_loc = (dot_plain(src_x, enc_query) * 0.125).astype(low_type)
    glob_keys_loc = dot_plain(src_x, glob_key).astype(low_type)
    glob_vals_loc = dot_plain(src_x, glob_value).astype(low_type)

    self_q = (dot_plain(dec_x, self_query) * 0.125).astype(low_type)
    self_k = dot_plain(dec_all, self_key).astype(low_type)
    self_v = dot_plain(dec_all, self_value).astype(low_type)
    dec_total = dec_all.shape[0]
    dec_places = seq_index * dec_count + jnp.arange(dec_count, dtype=jnp.int32)
    all_dec = jnp.arange(dec_total, dtype=jnp.int32)
    self_allowed = (all_dec[None, :] <= dec_places[:, None]) & (all_dec < dec_limit)[None, :]
    self_bias = jnp.where(self_allowed, 0.0, masked_score)
    self_out_full, self_stats = attend(self_q, self_k, self_v, self_bias, None, dec_count, True)
    self_attn = self_out_full.astype(low_type)
    dec_res_one = dec_x.astype(full) + dot_plain(self_attn, self_out)
    dec_first, dec_first_back = jax.vjp(
        layer_norm, dec_res_one, dec_self_gain.astype(full), dec_self_shift.astype(full)
    )
    dec_first_low = dec_first.astype(low_type)
    cross_q = (dot_plain(dec_first_low, cross_query) * 0.125).astype(low_type)
    all_cross_q = gather_rows(cross_q)

    glob_queries = (dot_plain(glob_x, glob_query) * 0.125).astype(low_type)
    live_bias = jnp.where(src_places < src_limit, 0.0, masked_score)
    glob_acc, glob_stats = merge_all(
        attend(
            glob_queries, glob_keys_loc, glob_vals_loc, live_bias[None, :], None, glob_count, False
        )
    )
    glob_total = glob_stats[:, SLOT : 2 * SLOT]
    glob_out = glob_acc / exact_dot(glob_total, spread)
    glob_lse = glob_stats[:, :SLOT] + jnp.log(jnp.maximum(glob_total, 1e-30))

    x_all = jnp.concatenate([before, src_x, after, glob_x], axis=0)
    keys_all = dot_plain(x_all, enc_key).astype(low_type)
    vals_all = dot_plain(x_all, enc_value).astype(low_type)
    pad_count = src_count + 2 * HALF
    pad_places = seq_index * src_count - HALF + jnp.arange(pad_count, dtype=jnp.int32)
    pad_glob = jnp.any(glob_places[:, None] == pad_places[None, :], axis=0)
    pad_use = (pad_places >= 0) & (pad_places < src_limit) & jnp.logical_not(pad_glob)
    near = jnp.abs(src_places[:, None] - pad_places[None, :]) <= HALF
    win_bias = jnp.concatenate(
        [
            jnp.where(near & pad_use[None, :], 0.0, masked_score),
            jnp.zeros((src_count, glob_count), full),
        ],
        axis=1,
    )
    near_turned = jnp.abs(src_places[None, :] - pad_places[:, None]) <= HALF
    win_bias_turned = jnp.concatenate(
        [
            jnp.where(near_turned & pad_use[:, None], 0.0, masked_score),
            jnp.zeros((glob_count, src_count), full),
        ],
        axis=0,
    )
    rows_block = 256
    reach = rows_block + 2 * HALF
    win_parts = [
        ((block * rows_block, reach), (pad_count, glob_count))
        for block in range(src_count // rows_block)
    ]
    win_out, win_stats = attend(
        query_loc, keys_all, vals_all, win_bias, win_parts, rows_block, True
    )
    placed = dot_left(select_low, glob_out.astype(low_type))
    enc_attn = jnp.where(is_global[:, None], placed, win_out).astype(low_type)
    enc_res = src_x.astype(full) + dot_plain(enc_attn, enc_out)
    enc_first, enc_first_back = jax.vjp(
        layer_norm, enc_res, enc_attn_gain.astype(full), enc_attn_shift.astype(full)
    )
    enc_first_low = enc_first.astype(low_type)
    enc_hidden, enc_slope = gelu_pair(dot_plain(enc_first_low, enc_up))
    enc_second = enc_first + dot_plain(enc_hidden, enc_down)
    memory, enc_final_back = jax.vjp(
        layer_norm, enc_second, enc_ffn_gain.astype(full), enc_ffn_shift.astype(full)
    )
    memory_low = memory.astype(low_type)

    cross_k = dot_plain(memory_low, cross_key).astype(low_type)
    cross_v = dot_plain(memory_low, cross_value).astype(low_type)
    cross_acc, cross_stats = merge_scatter(
        attend(all_cross_q, cross_k, cross_v, live_bias[None, :], None, 256, False)
    )
    cross_total = cross_stats[:, SLOT : 2 * SLOT]
    cross_out_full = cross_acc / exact_dot(cross_total, spread)
    cross_lse = cross_stats[:, :SLOT] + jnp.log(jnp.maximum(cross_total, 1e-30))
    cross_attn = cross_out_full.astype(low_type)
    dec_res_two = dec_first + dot_plain(cross_attn, cross_out)
    dec_second, dec_second_back = jax.vjp(
        layer_norm, dec_res_two, dec_cross_gain.astype(full), dec_cross_shift.astype(full)
    )
    dec_second_low = dec_second.astype(low_type)
    dec_hidden, dec_slope = gelu_pair(dot_plain(dec_second_low, dec_up))
    dec_third = dec_second + dot_plain(dec_hidden, dec_down)
    decoded, dec_final_back = jax.vjp(
        layer_norm, dec_third, dec_ffn_gain.astype(full), dec_ffn_shift.astype(full)
    )

    d_third, g_dec_ffn_gain, g_dec_ffn_shift = dec_final_back(cotangent[0].astype(full))
    d_down_low = d_third.astype(low_type)
    d_pre_low = (dot_right(d_down_low, dec_down) * dec_slope.astype(full)).astype(low_type)
    d_second = d_third + dot_right(d_pre_low, dec_up)
    d_res_two, g_dec_cross_gain, g_dec_cross_shift = dec_second_back(d_second)
    d_cross_o = d_res_two.astype(low_type)
    d_cross_attn = dot_right(d_cross_o, cross_out).astype(low_type)
    cross_delta = exact_dot(d_cross_attn.astype(full) * cross_out_full, spread.T)
    all_dout = gather_rows(d_cross_attn)
    all_stats = gather_rows(
        jnp.concatenate(
            [cross_lse, cross_delta, jnp.zeros((dec_count, LANES - 2 * SLOT), full)], axis=1
        )
    )[:, : 2 * SLOT].T
    live_turned = jnp.broadcast_to(live_bias[:, None], (src_count, 512))
    query_parts, ck_low, cv_low = attend_back(
        all_cross_q, cross_k, cross_v, all_dout, all_stats, live_turned, None, 256
    )
    d_memory = dot_right(ck_low, cross_key) + dot_right(cv_low, cross_value)

    g_dec_down = dot_left(dec_hidden, d_down_low)
    g_dec_up = dot_left(dec_second_low, d_pre_low)
    g_cross_out = dot_left(cross_attn, d_cross_o)
    g_cross_key = dot_left(memory_low, ck_low)
    g_cross_value = dot_left(memory_low, cv_low)

    d_enc_second, g_enc_ffn_gain, g_enc_ffn_shift = enc_final_back(d_memory)
    d_enc_down = d_enc_second.astype(low_type)
    d_enc_pre = (dot_right(d_enc_down, enc_down) * enc_slope.astype(full)).astype(low_type)
    d_enc_first = d_enc_second + dot_right(d_enc_pre, enc_up)
    d_enc_res, g_enc_attn_gain, g_enc_attn_shift = enc_first_back(d_enc_first)
    d_attn_o = d_enc_res.astype(low_type)
    d_attn = dot_right(d_attn_o, enc_out).astype(low_type)
    g_enc_down = dot_left(enc_hidden, d_enc_down)
    g_enc_up = dot_left(enc_first_low, d_enc_pre)
    g_enc_out = dot_left(enc_attn, d_attn_o)

    d_cross_q = scatter_all(query_parts).astype(low_type) * 0.125
    g_cross_query = dot_left(dec_first_low, d_cross_q)
    d_first = d_res_two + dot_right(d_cross_q, cross_query)
    d_res_one, g_dec_self_gain, g_dec_self_shift = dec_first_back(d_first)
    d_self_o = d_res_one.astype(low_type)
    g_self_out = dot_left(self_attn, d_self_o)
    d_self_attn = dot_right(d_self_o, self_out).astype(low_type)
    self_delta = exact_dot(d_self_attn.astype(full) * self_out_full, spread.T)
    wide = max(dec_count, LANES)
    self_pair = jnp.concatenate([self_stats[:, :SLOT], self_delta], axis=1)
    self_query_parts, d_self_k, d_self_v = attend_back(
        pad_rows(self_q, wide),
        self_k,
        self_v,
        pad_rows(d_self_attn, wide),
        pad_rows(self_pair, wide).T,
        pad_rows(self_bias, wide).T,
        None,
        wide,
    )
    d_self_q = self_query_parts[:dec_count].astype(low_type) * 0.125
    g_self_query = dot_left(dec_x, d_self_q)
    g_self_key = dot_left(dec_all, d_self_k)
    g_self_value = dot_left(dec_all, d_self_v)
    d_target = (
        d_res_one
        + dot_right(d_self_q, self_query)
        + scatter_all(dot_right(d_self_k, self_key) + dot_right(d_self_v, self_value))
    )

    glob_dout = add_all(dot_plain(select_low, d_attn).astype(low_type))
    d_window = jnp.where(is_global[:, None], jnp.zeros_like(d_attn), d_attn)
    win_delta = exact_dot(d_window.astype(full) * win_out, spread.T)
    win_pair = jnp.concatenate([win_stats[:, :SLOT], win_delta], axis=1).T
    d_query, d_keys_all, d_vals_all = attend_back(
        query_loc, keys_all, vals_all, d_window, win_pair, win_bias_turned, win_parts, rows_block
    )
    d_query_low = d_query.astype(low_type) * 0.125

    wide = max(glob_count, LANES)
    glob_delta = exact_dot(glob_dout.astype(full) * glob_out, spread.T)
    glob_pair = jnp.concatenate([glob_lse, glob_delta], axis=1)
    glob_query_parts, gk_low, gv_low = attend_back(
        pad_rows(glob_queries, wide),
        glob_keys_loc,
        glob_vals_loc,
        pad_rows(glob_dout, wide),
        pad_rows(glob_pair, wide).T,
        live_turned[:, :wide],
        None,
        wide,
    )
    d_gq = glob_query_parts[:glob_count].astype(low_type) * 0.125

    g_enc_query = dot_left(src_x, d_query_low)
    g_enc_key = dot_left(x_all, d_keys_all)
    g_enc_value = dot_left(x_all, d_vals_all)
    g_glob_query = dot_left(glob_x, d_gq)
    g_glob_key = dot_left(src_x, gk_low)
    g_glob_value = dot_left(src_x, gv_low)

    d_x_all = dot_right(d_keys_all, enc_key) + dot_right(d_vals_all, enc_value)
    from_after = lax.ppermute(d_x_all[:HALF].astype(low_type), "seq", downward)
    from_before = lax.ppermute(d_x_all[HALF + src_count : pad_count].astype(low_type), "seq", upward)
    d_glob_x = add_all((d_x_all[pad_count:] + dot_right(d_gq, glob_query)).astype(low_type))
    d_source = (
        d_enc_res
        + dot_right(d_query_low, enc_query)
        + d_x_all[HALF : HALF + src_count]
        + dot_right(gk_low, glob_key)
        + dot_right(gv_low, glob_value)
        + dot_left(select_low, d_glob_x)
    )
    d_source = d_source + jnp.pad(
        from_after.astype(full), ((src_count - HALF, 0), (0, 0))
    )
    d_source = d_source + jnp.pad(
        from_before.astype(full), ((0, src_count - HALF), (0, 0))
    )

    (s_dec_up,) = share_grads([g_dec_up], True)
    s_dec_down, s_cross_out = share_grads([g_dec_down, g_cross_out], False)
    s_cross_key, s_cross_value = share_grads([g_cross_key, g_cross_value], True)
    (s_enc_up,) = share_grads([g_enc_up], True)
    s_enc_down, s_enc_out = share_grads([g_enc_down, g_enc_out], False)
    s_self_query, s_self_key, s_self_value, s_self_out, s_cross_query = share_grads(
        [g_self_query, g_self_key, g_self_value, g_self_out, g_cross_query], False
    )
    s_enc_query, s_enc_key, s_enc_value = share_grads([g_enc_query, g_enc_key, g_enc_value], True)
    s_glob_query, s_glob_key, s_glob_value = share_grads(
        [g_glob_query, g_glob_key, g_glob_value], False
    )
    vectors = share_norms(
        [
            g_enc_attn_gain,
            g_enc_attn_shift,
            g_enc_ffn_gain,
            g_enc_ffn_shift,
            g_dec_self_gain,
            g_dec_self_shift,
            g_dec_cross_gain,
            g_dec_cross_shift,
            g_dec_ffn_gain,
            g_dec_ffn_shift,
        ]
    )
    return (
        decoded.astype(low_type)[None],
        d_source[None],
        d_target[None],
        s_enc_query,
        s_enc_key,
        s_enc_value,
        s_glob_query,
        s_glob_key,
        s_glob_value,
        s_enc_out,
        vectors[0],
        vectors[1],
        s_enc_up,
        s_enc_down,
        vectors[2],
        vectors[3],
        s_self_query,
        s_self_key,
        s_self_value,
        s_self_out,
        vectors[4],
        vectors[5],
        s_cross_query,
        s_cross_key,
        s_cross_value,
        s_cross_out,
        vectors[6],
        vectors[7],
        s_dec_up,
        s_dec_down,
        vectors[8],
        vectors[9],
    )


def solution(mesh):
    rows = P("dp", "seq", None)
    tile = P("seq", "dp")
    part = P("seq")
    layer = (tile,) * 7 + (part,) * 2 + (tile,) * 2 + (part,) * 2
    decoder = (tile,) * 4 + (part,) * 2 + (tile,) * 4 + (part,) * 2 + (tile,) * 2 + (part,) * 2
    few = mesh.shape["seq"] <= 16
    return jax.shard_map(
        per_device if few else per_device_wide,
        mesh=mesh,
        in_specs=(rows, rows, rows, P("dp"), P("dp"), P("dp", None)) + (P(),) * 29,
        out_specs=(rows, rows, rows) + layer + decoder,
        check_vma=False,
    )
```
